128 devices in a mesh: dp: 8 (over x, core), fsdp: 16 (over z, y).
Axes of the slice: x: 4, y: 4, z: 4, core: 2. Of those that a mesh axis runs over, the one named last changes fastest.
Arguments:
- token_ids: int32 [48, 2048], P('dp', 'fsdp'), may hold values from 0 to 30521
- splits: int32 [48], P('dp'), may hold values from 512 to 1535
- valid_mask: int32 [48, 2048], P('dp', 'fsdp'), may hold values from 0 to 1, as said below
- embed_table: bfloat16 [30522, 128], replicated, may hold values from -6 to 6
- embed_proj: bfloat16 [384, 512], replicated, may hold values from -0.3125 to 0.3125
- embed_bias: float32 [512], replicated, may hold values from -1.75 to 1.75
- type_table: float32 [2, 512], replicated, may hold values from -3 to 3
- teach_in: bfloat16 [512, 1024], replicated, may hold values from -0.25 to 0.25
- teach_qkv: bfloat16 [1024, 3072], replicated, may hold values from -0.1875 to 0.1875
- teach_att: bfloat16 [1024, 1024], replicated, may hold values from -2 to 2
- teach_up: bfloat16 [1024, 4096], replicated, may hold values from -0.1875 to 0.1875
- teach_down: bfloat16 [4096, 1024], replicated, may hold values from -0.09375 to 0.09375
- teach_out: bfloat16 [1024, 512], replicated, may hold values from -0.1875 to 0.1875
- teach_bias: float32 [10752], replicated, may hold values from -0.625 to 0.625
- teach_gain: float32 [2560], replicated, may hold values from 0.5 to 1.5
- teach_shift: float32 [2560], replicated, may hold values from -1.75 to 1.75
- matrices: float32 [720896], P(('dp', 'fsdp'))
- vectors: float32 [6016], P(('dp', 'fsdp'))
- matrix_first: float32 [720896], P(('dp', 'fsdp')), may hold values from -3.8146973e-05 to 3.8146973e-05
- matrix_second: float32 [720896], P(('dp', 'fsdp')), may hold values from 3.439206e-12 to 1.3756824e-11
- vector_first: float32 [6016], P(('dp', 'fsdp')), may hold values from -0.00015258789 to 0.00015258789
- vector_second: float32 [6016], P(('dp', 'fsdp')), may hold values from 5.5027295e-11 to 2.2010918e-10
Outputs:
- loss_sum: float32 [], replicated
- query_count: float32 [], replicated
- grad_norm: float32 [], replicated
- new_matrices: float32 [720896], P(('dp', 'fsdp'))
- new_matrix_first: float32 [720896], P(('dp', 'fsdp'))
- new_matrix_second: float32 [720896], P(('dp', 'fsdp'))
- new_vectors: float32 [6016], P(('dp', 'fsdp'))
- new_vector_first: float32 [6016], P(('dp', 'fsdp'))
- new_vector_second: float32 [6016], P(('dp', 'fsdp'))
The draws below stay inside these ranges and needn't reach their ends.
Inputs may be any that keep to these rules, and one draw needn't show every extreme that they name: `valid_mask`: 1 marks a query whose loss counts. `splits`: first token of the second segment of a row.
All inputs are finite; a program needn't handle non-finite values.
Results may differ from the reference program's by a relative error of at most 0.0076.
The reference program's roundings to bfloat16 on the way count: a program that leaves them out, or rounds other values in their place, can miss the bound.
Values may be sent and summed in bfloat16 or wider, within the bound.
A program may use at most 320 MiB of HBM per device.

```python
import math
import jax
import jax.numpy as jnp
import numpy as np
from jax import lax

D_E = 512
D_T = 1024
FF_T = 4096
D_S = 128
FF_S = 512
HEADS = 4
FFN_COUNT = 4
VOCAB = 30522
EMB_DIM = 128
STEP = 5
HEAD_T = 256
HEAD_S = 32
SEQ = 2048
ROWS = 48
MAT_TOTAL = 720896
VEC_TOTAL = 6016


def draw_matrices(key, part):
    key = jax.random.fold_in(key, 11)
    noise = jax.random.normal(key, (MAT_TOTAL,), jnp.float32)
    amounts = [D_E * D_S, 3 * D_S * D_S, D_S * D_S, FFN_COUNT * D_S * FF_S, FFN_COUNT * FF_S * D_S, D_S * D_E]
    factors = [D_E ** (-0.5), D_S ** (-0.5), 0.35 * (SEQ / D_S) ** 0.5 * D_S ** (-0.5) * D_S ** 0.5 / D_S ** 0.5, D_S ** (-0.5), FF_S ** (-0.5), D_S ** (-0.5)]
    scales = jnp.concatenate([jnp.full((amount,), factor, jnp.float32) for amount, factor in zip(amounts, factors)])
    return noise * scales


def draw_vectors(key, part):
    key = jax.random.fold_in(key, 12)
    noise = jax.random.normal(key, (VEC_TOTAL,), jnp.float32)
    jitter = jax.random.uniform(jax.random.fold_in(key, 5), (VEC_TOTAL,), jnp.float32, -1.0, 1.0)
    layout = [(D_S, 0, D_S), (3 * D_S, 0, D_S), (D_S, 0, D_S), (D_S, 1, D_S), (D_S, 0, D_S), (FFN_COUNT * FF_S, 0, FF_S), (FFN_COUNT * D_S, 0, D_S), (FFN_COUNT * D_S, 1, D_S), (FFN_COUNT * D_S, 0, D_S), (D_E, 0, D_E), (D_E, 1, D_E), (D_E, 0, D_E)]
    pieces = []
    offset = 0
    for amount, is_gain, width in layout:
        place = (jnp.arange(amount) % width).astype(jnp.float32) / width
        if is_gain:
            pieces.append(0.5 + place + 0.1 * jitter[offset:offset + amount])
        else:
            pieces.append(0.2 * noise[offset:offset + amount])
        offset += amount
    return jnp.concatenate(pieces)


def draw_valid_mask(key, part):
    key = jax.random.fold_in(key, 13)
    row_index = jnp.arange(ROWS, dtype=jnp.int32)[:, None]
    places = jnp.arange(SEQ, dtype=jnp.int32)[None, :]
    row_span = max(ROWS - 1, 1)
    limit = 100 * (SEQ + 2 * places) * (row_span + 2 * row_index) // (SEQ * row_span)
    rolled = jax.random.randint(key, (ROWS, SEQ), 0, 1000)
    return (rolled < limit).astype(jnp.int32)


def with_ends(drawn, rng, least, top_value):
    spot = [jax.random.randint(jax.random.fold_in(rng, axis), (), 0, length) for axis, length in enumerate(drawn.shape)]
    main_axis = drawn.shape.index(max(drawn.shape))
    beside = spot[:main_axis] + [(spot[main_axis] + 1) % drawn.shape[main_axis]] + spot[main_axis + 1:]
    return drawn.at[tuple(spot)].set(least).at[tuple(beside)].set(top_value)


def shard_levels(rng, shape, shards, low, largest):
    loudness = 1.0
    for dim, parts in shards:
        heights = jax.random.uniform(jax.random.fold_in(jax.random.fold_in(rng, 6), dim), (parts,), jnp.float32, low / len(shards), largest / len(shards))
        loudness = loudness * jnp.repeat(jnp.exp(heights), shape[dim] // parts).reshape((-1,) + (1,) * (len(shape) - 1 - dim))
    return loudness


def cumulative_ranks(number_of, slope):
    weights = [(1 << 20) // math.isqrt(grade ** slope) + 1 for grade in range(1, number_of + 1)]
    scale = 1 + sum(weights) // (1 << 30)
    return np.cumsum(np.array([max(1, weight // scale) for weight in weights]))


def skewed_ids(key, shape, count, skew):
    grid = cumulative_ranks(count, skew)
    ticket = jax.random.randint(jax.random.fold_in(key, 1), shape, 0, int(grid[count - 1]))
    grade = jnp.searchsorted(jnp.asarray(grid, jnp.int32), ticket, side="right")
    return jax.random.permutation(jax.random.fold_in(key, 2), count)[grade].astype(jnp.int32)


def centred(key, dims, scale, most, split=(), held_as=jnp.bfloat16):
    loudness = shard_levels(key, dims, split, -0.22, 0.18) if split else 1.0
    drawn = jax.random.normal(key, dims, jnp.float32) * scale * loudness
    return jnp.minimum(jnp.maximum(drawn, -most), most).astype(held_as)


def setup_inputs(seed: int = 0) -> dict:
    key_of = jax.random.split(jax.random.key(seed), 23)
    token_ids = with_ends(skewed_ids(key_of[0], (ROWS, SEQ), VOCAB, 2), jax.random.fold_in(key_of[0], 3), 0, VOCAB - 1).astype(jnp.int32)
    splits = with_ends(jax.random.randint(key_of[1], (ROWS,), SEQ // 4, 3 * SEQ // 4), jax.random.fold_in(key_of[1], 1), SEQ // 4, (3 * SEQ // 4) - 1).astype(jnp.int32)
    valid_mask = draw_valid_mask(jax.random.fold_in(key_of[22], 71), 0)
    embed_table = centred(key_of[3], (VOCAB, EMB_DIM), 1.0, 6.0)
    embed_proj = centred(key_of[4], (3 * EMB_DIM, D_E), (3 * EMB_DIM) ** -0.5, 0.3125)
    embed_bias = centred(key_of[5], (D_E,), 0.3, 1.75, (), jnp.float32)
    type_table = centred(key_of[6], (2, D_E), 0.5, 3.0, (), jnp.float32)
    teach_in = centred(key_of[7], (D_E, D_T), D_E ** -0.5, 0.25)
    teach_qkv = centred(key_of[8], (D_T, 3 * D_T), D_T ** -0.5, 0.1875)
    teach_att = centred(key_of[9], (D_T, D_T), (max(1, 16 * D_T // SEQ)) ** -0.5, 2.0)
    teach_up = centred(key_of[10], (D_T, FF_T), D_T ** -0.5, 0.1875)
    teach_down = centred(key_of[11], (FF_T, D_T), FF_T ** -0.5, 0.09375)
    teach_out = centred(key_of[12], (D_T, D_E), D_T ** -0.5, 0.1875)
    teach_bias = centred(key_of[13], (6 * D_T + FF_T + D_E,), 0.1, 0.625, (), jnp.float32)
    teach_gain = jnp.clip(1.0 + 0.1 * jax.random.normal(key_of[14], (2 * D_T + D_E,), jnp.float32), 0.5, 1.5)
    teach_shift = centred(key_of[15], (2 * D_T + D_E,), 0.3, 1.75, (), jnp.float32)
    matrices = draw_matrices(jax.random.fold_in(key_of[22], 71), 0)
    vectors = draw_vectors(jax.random.fold_in(key_of[22], 71), 0)
    matrix_first = centred(key_of[18], (MAT_TOTAL,), (0.00555 * (MAT_TOTAL + VEC_TOTAL) ** -0.5), 3.814697265625e-05, ((0, 128),), jnp.float32)
    matrix_second = jnp.clip(jnp.exp(math.log(1.3756823805111118e-11) - 1.3862944 * jax.random.uniform(key_of[19], (MAT_TOTAL,), jnp.float32) ** shard_levels(key_of[19], (MAT_TOTAL,), ((0, 128),), -0.2, 0.2)), 3.4392059512777795e-12, 1.3756823805111118e-11)
    vector_first = centred(key_of[20], (VEC_TOTAL,), (0.0222 * (MAT_TOTAL + VEC_TOTAL) ** -0.5), 0.00015258789, ((0, 128),), jnp.float32)
    vector_second = jnp.clip(jnp.exp(math.log(2.201091808817779e-10) - 1.3862944 * jax.random.uniform(key_of[21], (VEC_TOTAL,), jnp.float32) ** shard_levels(key_of[21], (VEC_TOTAL,), ((0, 128),), -0.2, 0.2)), 5.502729522044447e-11, 2.201091808817779e-10)
    return {"token_ids": token_ids, "splits": splits, "valid_mask": valid_mask, "embed_table": embed_table, "embed_proj": embed_proj, "embed_bias": embed_bias, "type_table": type_table, "teach_in": teach_in, "teach_qkv": teach_qkv, "teach_att": teach_att, "teach_up": teach_up, "teach_down": teach_down, "teach_out": teach_out, "teach_bias": teach_bias, "teach_gain": teach_gain, "teach_shift": teach_shift, "matrices": matrices, "vectors": vectors, "matrix_first": matrix_first, "matrix_second": matrix_second, "vector_first": vector_first, "vector_second": vector_second}


CLIP_NORM = 0.05
BETA_ONE = 0.9
BETA_TWO = 0.999
LEARN_RATE = 0.3
WEIGHT_DECAY = 0.01
ADAM_EPS = 1e-06

@jax.custom_vjp
def low(v):
    return lax.optimization_barrier(v.astype(jnp.bfloat16)).astype(jnp.float32)

@jax.custom_vjp
def low_back(v):
    return v

def low_keep(v):
    return (low(v), None)

def low_pass(kept, grad):
    return (grad,)

def back_keep(v):
    return (v, None)

def back_low(kept, grad):
    return (low(grad),)
low.defvjp(low_keep, low_pass)
low_back.defvjp(back_keep, back_low)

def precise_dot(left, right):
    return jnp.dot(left, right, precision=lax.Precision.HIGHEST)

def precise_sum(form, left, right):
    return jnp.einsum(form, left, right, precision=lax.Precision.HIGHEST)

def mat_layouts():
    return [(D_E, D_S), (D_S, 3 * D_S), (D_S, D_S), (FFN_COUNT, D_S, FF_S), (FFN_COUNT, FF_S, D_S), (D_S, D_E)]

def vec_layouts():
    return [(D_S,), (3 * D_S,), (D_S,), (D_S,), (D_S,), (FFN_COUNT, FF_S), (FFN_COUNT, D_S), (FFN_COUNT, D_S), (FFN_COUNT, D_S), (D_E,), (D_E,), (D_E,)]

def split_flat(flat, layouts):
    pieces = []
    offset = 0
    for layout in layouts:
        amount = math.prod(layout)
        pieces.append(flat[offset:offset + amount].reshape(layout))
        offset += amount
    return pieces

def layer_norm(values, gain, shift):
    center = values - lax.optimization_barrier(jnp.mean(values, -1, keepdims=True))
    spread = lax.optimization_barrier(jnp.mean(center * center, -1, keepdims=True))
    return center * lax.rsqrt(spread + 1e-05) * gain + shift

def embed_row(ids_row, split_row, table, proj, bias, types):
    places = jnp.arange(SEQ)
    padded = jnp.pad(ids_row, 1)
    left = jnp.where((places > 0)[:, None], table[padded[:-2]], 0.0)
    right = jnp.where((places < SEQ - 1)[:, None], table[padded[2:]], 0.0)
    trigram = jnp.concatenate([left, table[ids_row], right], -1)
    typed = jnp.where((places >= split_row)[:, None], types[1], types[0])
    return low(precise_dot(trigram, proj) + bias + typed)

def teacher_row(embedded, mats, biases, gains, shifts):
    w_in, w_qkv, w_att, w_up, w_down, w_out = mats
    hidden = precise_dot(embedded, w_in) + biases[0]
    qkv = low(precise_dot(low(hidden), w_qkv) + biases[1])
    queries = qkv[:, :D_T].reshape(SEQ, HEADS, HEAD_T)
    keys = qkv[:, D_T:2 * D_T].reshape(SEQ, HEADS, HEAD_T)
    values = qkv[:, 2 * D_T:].reshape(SEQ, HEADS, HEAD_T)
    scores = precise_sum('qhd,khd->hqk', queries, keys) * HEAD_T ** (-0.5)
    probs = jax.nn.softmax(scores, -1)
    mixed = low(precise_sum('hqk,khd->qhd', low(probs), values).reshape(SEQ, D_T))
    normed = layer_norm(hidden + precise_dot(mixed, w_att) + biases[2], gains[0], shifts[0])
    active = low(jax.nn.gelu(precise_dot(low(normed), w_up) + biases[3], approximate=False))
    normed = layer_norm(normed + precise_dot(active, w_down) + biases[4], gains[1], shifts[1])
    target = layer_norm(embedded + precise_dot(low(normed), w_out) + biases[5], gains[2], shifts[2])
    return (queries, keys, target)

def student_row(matrices, vectors, embedded, t_query, t_key, target, weights):
    w_in, w_qkv, w_att, w_up, w_down, w_out = split_flat(low(matrices), mat_layouts())
    in_bias, qkv_bias, att_bias, att_gain, att_shift, up_bias, down_bias, ffn_gain, ffn_shift, out_bias, out_gain, out_shift = split_flat(low(vectors), vec_layouts())
    first = low_back(precise_dot(embedded, w_in) + in_bias)
    qkv = low(low_back(precise_dot(low(first), w_qkv) + qkv_bias))
    queries = qkv[:, :D_S].reshape(SEQ, HEADS, HEAD_S)
    keys = qkv[:, D_S:2 * D_S].reshape(SEQ, HEADS, HEAD_S)
    values = qkv[:, 2 * D_S:].reshape(SEQ, HEADS, HEAD_S)
    scores = low_back(precise_sum('qhd,khd->hqk', queries, keys) * HEAD_S ** (-0.5))
    probs = jax.nn.softmax(scores, -1)
    mixed = low(low_back(precise_sum('hqk,khd->qhd', low(probs), values).reshape(SEQ, D_S)))
    branch = low_back(precise_dot(mixed, w_att) + att_bias)
    state = att_gain * (first + branch) + att_shift
    for index in range(FFN_COUNT):
        inner = low_back(precise_dot(low(state), w_up[index]) + up_bias[index])
        outer = low_back(precise_dot(low(jax.nn.gelu(inner, approximate=False)), w_down[index]) + down_bias[index])
        state = ffn_gain[index] * (state + outer) + ffn_shift[index]
    output = low_back(precise_dot(low(state), w_out) + out_bias)
    result = out_gain * (embedded + output) + out_shift
    t_scores = precise_sum('qhd,khd->hqk', t_query, t_key) * HEAD_T ** (-0.5)
    t_probs = jax.nn.softmax(t_scores, -1)
    kl_terms = lax.optimization_barrier(jnp.sum(t_probs * (t_scores - scores), -1)) - jax.nn.logsumexp(t_scores, -1) + jax.nn.logsumexp(scores, -1)
    diff = result - target
    per_query = lax.optimization_barrier(jnp.mean(kl_terms, 0)) + lax.optimization_barrier(jnp.mean(diff * diff, -1))
    return jnp.sum(weights * per_query)

def adam_parts(grad, first, second, master, decay, factor):
    grad = grad * factor
    first = BETA_ONE * first + (1.0 - BETA_ONE) * grad
    second = BETA_TWO * second + (1.0 - BETA_TWO) * grad * grad
    ratio = first / (1.0 - BETA_ONE ** STEP) / (jnp.sqrt(second / (1.0 - BETA_TWO ** STEP)) + ADAM_EPS) + decay * master
    return (first, second, ratio)

def reference(token_ids, splits, valid_mask, embed_table, embed_proj, embed_bias, type_table, teach_in, teach_qkv, teach_att, teach_up, teach_down, teach_out, teach_bias, teach_gain, teach_shift, matrices, vectors, matrix_first, matrix_second, vector_first, vector_second):
    table = embed_table.astype(jnp.float32)
    proj = embed_proj.astype(jnp.float32)
    teach_mats = [w.astype(jnp.float32) for w in (teach_in, teach_qkv, teach_att, teach_up, teach_down, teach_out)]
    biases = split_flat(teach_bias, [(D_T,), (3 * D_T,), (D_T,), (FF_T,), (D_T,), (D_E,)])
    gains = split_flat(teach_gain, [(D_T,), (D_T,), (D_E,)])
    shifts = split_flat(teach_shift, [(D_T,), (D_T,), (D_E,)])

    def teacher_pass(row):
        embedded = embed_row(row[0], row[1], table, proj, embed_bias, type_table)
        queries, keys, target = teacher_row(embedded, teach_mats, biases, gains, shifts)
        return (embedded, queries, keys, target)
    embedded, t_query, t_key, target = lax.map(teacher_pass, (token_ids, splits))
    weights = valid_mask.astype(jnp.float32)
    query_count = jnp.sum(weights)
    row_loss = jax.checkpoint(student_row)

    def total_loss(mats_in, vecs_in):

        def add_row(carry, row):
            return (carry + row_loss(mats_in, vecs_in, *row), None)
        total, _ = lax.scan(add_row, jnp.zeros((), jnp.float32), (embedded, t_query, t_key, target, weights))
        return total
    loss_sum, pullback = jax.vjp(total_loss, matrices, vectors)
    grad_mats, grad_vecs = pullback(1.0 / query_count)
    grad_norm = jnp.sqrt(jnp.sum(grad_mats * grad_mats) + jnp.sum(grad_vecs * grad_vecs))
    factor = CLIP_NORM / jnp.maximum(grad_norm, CLIP_NORM)
    mat_first, mat_second, mat_ratio = adam_parts(grad_mats, matrix_first, matrix_second, matrices, WEIGHT_DECAY, factor)
    scaled = []
    for master, ratio in zip(split_flat(matrices, mat_layouts()), split_flat(mat_ratio, mat_layouts())):
        trust = jnp.sqrt(jnp.sum(master * master)) / jnp.sqrt(jnp.sum(ratio * ratio))
        scaled.append((trust * ratio).reshape(-1))
    new_matrices = matrices - LEARN_RATE * jnp.concatenate(scaled)
    vec_first, vec_second, vec_ratio = adam_parts(grad_vecs, vector_first, vector_second, vectors, 0.0, factor)
    new_vectors = vectors - LEARN_RATE * vec_ratio
    return (loss_sum, query_count, grad_norm, new_matrices, mat_first, mat_second, new_vectors, vec_first, vec_second)
```

```python
import functools
import math

import jax
import jax.numpy as jnp
from jax import lax
from jax.experimental import pallas as pl
from jax.experimental.pallas import tpu as pltpu
from jax.sharding import PartitionSpec as P

D_E = 512
D_T = 1024
FF_T = 4096
D_S = 128
FF_S = 512
HEADS = 4
FFN_COUNT = 4
STEP = 5
HEAD_T = 256
HEAD_S = 32
SEQ = 2048
QB = 256
OWN = 3 * QB
SLOTS = 2 * SEQ

CLIP_NORM = 0.05
BETA_ONE = 0.9
BETA_TWO = 0.999
LEARN_RATE = 0.3
WEIGHT_DECAY = 0.01
ADAM_EPS = 1e-06

F32 = jnp.float32
BF16 = jnp.bfloat16
LOG2E = 1.4426950408889634
MESH = pl.DeviceIdType.MESH
BIG_VMEM = 60 * 2**20

MAT_ROWS = (512, 384, 128, 2048, 2048, 512)
SHARD = 44
BLOCK = 48
(V_IN, V_QKV, V_ATT, V_AGAIN, V_ASHIFT, V_UP, V_DOWN, V_FGAIN, V_FSHIFT, V_OUT, V_OGAIN, V_OSHIFT) = (
    0, 1, 4, 5, 6, 7, 23, 27, 31, 35, 39, 43)


def dot(left, right):
    return jnp.dot(left, right, preferred_element_type=F32)


def dot_nt(left, right):
    return lax.dot_general(left, right, (((1,), (1,)), ((), ())), preferred_element_type=F32)


def dot_tn(left, right):
    return lax.dot_general(left, right, (((0,), (0,)), ((), ())), preferred_element_type=F32)


def layer_norm(values, gain, shift):
    center = values - jnp.mean(values, -1, keepdims=True)
    spread = jnp.mean(center * center, -1, keepdims=True)
    return center * lax.rsqrt(spread + 1e-05) * gain + shift


def gelu(values):
    return 0.5 * values * (1.0 + lax.erf(values * 0.7071067811865476))


def params(**more):
    return pltpu.CompilerParams(vmem_limit_bytes=BIG_VMEM, **more)


def whole(*shape):
    return pl.BlockSpec(shape, lambda *_: (0,) * len(shape))


def rows_of(place):
    i, g = place % 8, place // 8
    return 3 * g + (3 * i) // 8, 3 * g + (3 * i + 2) // 8


def spread_kernel(e_ref, mask_ref, all_ref, weight_ref, masks, send, recv):
    dp, me = lax.axis_index("dp"), lax.axis_index("fsdp")
    barrier = pltpu.get_barrier_semaphore()

    def greet(k, _):
        pl.semaphore_signal(barrier, inc=1, device_id=(dp, (me + k) % 16), device_id_type=MESH)
        return 0

    lax.fori_loop(1, 16, greet, 0)
    r0, r1 = rows_of(me)
    all_ref[0, me] = e_ref[r0]
    masks[me] = mask_ref[...]

    @pl.when(r1 == r0)
    def _():
        all_ref[1] = jnp.zeros_like(all_ref[1])

    @pl.when(r1 != r0)
    def _():
        all_ref[1, me] = e_ref[r1]

    pl.semaphore_wait(barrier, 15)

    def copies(k):
        peer = (me + k) % 16
        s0, s1 = rows_of(peer)
        where = dict(device_id=(dp, peer), device_id_type=MESH)
        return (
            pltpu.make_async_remote_copy(e_ref.at[s0], all_ref.at[0, me], send.at[k, 0], recv.at[k, 0], **where),
            pltpu.make_async_remote_copy(e_ref.at[s1], all_ref.at[1, me], send.at[k, 1], recv.at[k, 1], **where),
            pltpu.make_async_remote_copy(mask_ref, masks.at[me], send.at[k, 2], recv.at[k, 2], **where),
            s0 != s1,
        )

    def start(k, _):
        first, second, third, two = copies(k)
        first.start()
        third.start()

        @pl.when(two)
        def _():
            second.start()

        return 0

    lax.fori_loop(1, 16, start, 0)

    def finish(k, _):
        first, second, third, two = copies(k)
        first.wait_send()
        third.wait_send()

        @pl.when(two)
        def _():
            second.wait_send()

        source = (me + 16 - k) % 16
        here = dict(device_id=(dp, source), device_id_type=MESH)
        pltpu.make_async_remote_copy(e_ref.at[r0], all_ref.at[0, source], send.at[k, 0], recv.at[k, 0], **here).wait_recv()
        pltpu.make_async_remote_copy(mask_ref, masks.at[source], send.at[k, 2], recv.at[k, 2], **here).wait_recv()

        @pl.when(r1 != r0)
        def _():
            pltpu.make_async_remote_copy(
                e_ref.at[r1], all_ref.at[1, source], send.at[k, 1], recv.at[k, 1], **here
            ).wait_recv()

        return 0

    lax.fori_loop(1, 16, finish, 0)
    first_block = (3 * (me % 8)) % 8
    for j in range(3):
        t = first_block + j
        row = lax.select(t >= 8, r1, r0)
        for half in range(2):
            line = masks[2 * (t % 8) + half, pl.ds(row, 1), :]
            weight_ref[j, :, half * 128 : half * 128 + 128] = line.astype(F32)


def spread(rows, mask):
    vmem = pl.BlockSpec(memory_space=pltpu.VMEM)
    return pl.pallas_call(
        spread_kernel,
        in_specs=[vmem] * 2,
        out_specs=[vmem] * 2,
        out_shape=[
            jax.ShapeDtypeStruct((2, 16, 128, 128), BF16),
            jax.ShapeDtypeStruct((3, 1, QB), F32),
        ],
        scratch_shapes=[
            pltpu.VMEM((16, 8, 128), jnp.int32),
            pltpu.SemaphoreType.DMA((16, 3)),
            pltpu.SemaphoreType.DMA((16, 3)),
        ],
        compiler_params=params(collective_id=0, has_side_effects=True),
        name="spread",
    )(rows, mask)


PT = 512


def project_kernel(meta, e_ref, proj_ref, ebias_ref, types_ref, win_ref, wkv_ref, bias_ref, emb_ref, k_ref, vt_ref):
    t = pl.program_id(0)
    per = SEQ // PT
    s, p = t // per, t % per
    base = t * PT
    mid = e_ref[pl.ds(pl.multiple_of(base, PT), PT), :]
    lo, hi = jnp.maximum(base - 16, 0), jnp.minimum(base + PT, SLOTS - 16)
    before = e_ref[pl.ds(pl.multiple_of(lo, 16), 16), :].astype(F32)[15:16]
    after = e_ref[pl.ds(pl.multiple_of(hi, 16), 16), :].astype(F32)[0:1]
    before = jnp.where(p == 0, 0.0, before)
    after = jnp.where(p == per - 1, 0.0, after)
    wide = mid.astype(F32)
    row = lax.broadcasted_iota(jnp.int32, (PT, 1), 0)
    left = jnp.where(row == 0, before, pltpu.roll(wide, 1, 0)).astype(BF16)
    right = jnp.where(row == PT - 1, after, pltpu.roll(wide, PT - 1, 0)).astype(BF16)
    trigram = jnp.concatenate([left, mid, right], 1)
    split = jnp.where(s == 0, meta[0], meta[1])
    typed = jnp.where(row + p * PT >= split, types_ref[1:2, :], types_ref[0:1, :])
    emb = (dot(trigram, proj_ref[...]) + ebias_ref[...] + typed).astype(BF16)
    emb_ref[...] = emb
    hidden = (dot(emb, win_ref[...]) + bias_ref[:, :D_T]).astype(BF16)
    k_ref[...] = (dot(hidden, wkv_ref[:, D_T : 2 * D_T]) + bias_ref[:, 2 * D_T : 3 * D_T]).astype(BF16)
    values = (dot(hidden, wkv_ref[:, 2 * D_T :]) + bias_ref[:, 3 * D_T : 4 * D_T]).astype(BF16)
    vt_ref[...] = values.T


def project(meta, e, proj, ebias, types, win, wqkv, bias):
    return pl.pallas_call(
        project_kernel,
        grid_spec=pltpu.PrefetchScalarGridSpec(
            num_scalar_prefetch=1,
            grid=(SLOTS // PT,),
            in_specs=[
                whole(SLOTS, 128),
                whole(3 * 128, D_E),
                whole(1, D_E),
                whole(2, D_E),
                whole(D_E, D_T),
                whole(D_T, 3 * D_T),
                whole(1, 10752),
            ],
            out_specs=[
                pl.BlockSpec((PT, D_E), lambda t, m: (t, 0)),
                pl.BlockSpec((PT, D_T), lambda t, m: (t, 0)),
                pl.BlockSpec((D_T, PT), lambda t, m: (0, t)),
            ],
        ),
        out_shape=[
            jax.ShapeDtypeStruct((SLOTS, D_E), BF16),
            jax.ShapeDtypeStruct((SLOTS, D_T), BF16),
            jax.ShapeDtypeStruct((D_T, SLOTS), BF16),
        ],
        compiler_params=params(),
        name="project",
    )(meta, e, proj, ebias, types, win, wqkv, bias)


def own_kernel(meta, emb_all, win_ref, wqkv_ref, bias_ref, emb_ref, hid_ref, q_ref, sem):
    copy = pltpu.make_async_copy(emb_all.at[pl.ds(pl.multiple_of(meta[2] * QB, QB), OWN)], emb_ref, sem)
    copy.start()
    copy.wait()
    hidden = dot(emb_ref[...], win_ref[...]) + bias_ref[:, :D_T]
    hid_ref[...] = hidden
    queries = (dot(hidden.astype(BF16), wqkv_ref[...]) + bias_ref[:, D_T : 2 * D_T]).astype(BF16)
    q_ref[...] = queries * jnp.asarray(HEAD_T**-0.5, BF16)


def own_queries(meta, emb, win, wqkv, bias):
    return pl.pallas_call(
        own_kernel,
        grid_spec=pltpu.PrefetchScalarGridSpec(
            num_scalar_prefetch=1,
            grid=(1,),
            in_specs=[
                pl.BlockSpec(memory_space=pl.ANY),
                whole(D_E, D_T),
                whole(D_T, D_T),
                whole(1, 10752),
            ],
            out_specs=[whole(OWN, D_E), whole(OWN, D_T), whole(OWN, D_T)],
            scratch_shapes=[pltpu.SemaphoreType.DMA],
        ),
        out_shape=[
            jax.ShapeDtypeStruct((OWN, D_E), BF16),
            jax.ShapeDtypeStruct((OWN, D_T), F32),
            jax.ShapeDtypeStruct((OWN, D_T), BF16),
        ],
        compiler_params=params(),
        name="own_queries",
    )(meta, emb, win, wqkv, bias)


ST = 1024


def student_in_kernel(emb_ref, win_ref, wqkv_ref, vec_ref, first_ref, q_ref, k_ref, v_ref, kt_ref, vt_ref):
    first = (dot(emb_ref[...], win_ref[...]) + vec_ref[V_IN : V_IN + 1, :]).astype(BF16)
    first_ref[...] = first
    qkv = dot(first, wqkv_ref[...])
    q_ref[...] = (qkv[:, :D_S] + vec_ref[V_QKV : V_QKV + 1, :]).astype(BF16)
    keys = (qkv[:, D_S : 2 * D_S] + vec_ref[V_QKV + 1 : V_QKV + 2, :]).astype(BF16)
    values = (qkv[:, 2 * D_S :] + vec_ref[V_QKV + 2 : V_QKV + 3, :]).astype(BF16)
    k_ref[...] = keys
    v_ref[...] = values
    kt_ref[...] = keys.T
    vt_ref[...] = values.T


def student_in(emb, win, wqkv, vecs):
    tall = jax.ShapeDtypeStruct((SLOTS, D_S), BF16)
    flat = jax.ShapeDtypeStruct((D_S, SLOTS), BF16)
    down = pl.BlockSpec((ST, D_S), lambda t: (t, 0))
    across = pl.BlockSpec((D_S, ST), lambda t: (0, t))
    return pl.pallas_call(
        student_in_kernel,
        grid=(SLOTS // ST,),
        in_specs=[pl.BlockSpec((ST, D_E), lambda t: (t, 0)), whole(D_E, D_S), whole(D_S, 3 * D_S), whole(48, 128)],
        out_specs=[down, down, down, down, across, across],
        out_shape=[tall, tall, tall, tall, flat, flat],
        compiler_params=params(),
        name="student_in",
    )(emb, win, wqkv, vecs)


CK = 64


def head_lanes(values, head):
    lane = lax.broadcasted_iota(jnp.int32, (1, D_S), 1)
    return jnp.where(lane // HEAD_S == head, values, jnp.zeros_like(values))


def attend_kernel(meta, tq_ref, tk_ref, tvt_ref, sq_ref, sk_ref, svt_ref, et_ref, es_ref, tmix_ref, smix_ref, stat_ref, ts, ss):
    head = pl.program_id(1)
    s_scale = HEAD_S**-0.5
    queries = tq_ref[...]
    s_queries = head_lanes(sq_ref[...], head)
    t_max = jnp.full((8, QB), -jnp.inf, F32)
    s_max = jnp.full((8, QB), -jnp.inf, F32)
    for c in range(SEQ // 256):
        part = pl.ds(c * 256, 256)
        t_part = dot_nt(tk_ref[part, :], queries)
        ts[part, :] = t_part
        t_max = jnp.maximum(t_max, jnp.max(t_part.reshape(32, 8, QB), 0))
        s_part = dot_nt(sk_ref[part, :], s_queries)
        ss[part, :] = s_part
        s_max = jnp.maximum(s_max, jnp.max(s_part.reshape(32, 8, QB), 0))
    t_top = jnp.max(t_max, 0, keepdims=True)
    s_top = jnp.max(s_max, 0, keepdims=True)
    t_off, s_off = t_top * LOG2E, s_top * (s_scale * LOG2E)

    def step(c, carry):
        t_sum, s_sum, kl = carry
        part = pl.ds(pl.multiple_of(c * CK, CK), CK)
        t_part, s_part = ts[part, :], ss[part, :]
        t_exp = jnp.exp2(t_part * LOG2E - t_off)
        s_exp = jnp.exp2(s_part * (s_scale * LOG2E) - s_off)
        et_ref[0, 0, part, :] = t_exp.astype(BF16)
        es_ref[0, 0, part, :] = s_exp.astype(BF16)
        fold = lambda v: jnp.sum(v.reshape(CK // 8, 8, QB), 0)
        return (
            t_sum + fold(t_exp),
            s_sum + fold(s_exp),
            kl + fold(t_exp * (t_part - s_part * s_scale)),
        )

    zero = jnp.zeros((8, QB), F32)
    t_sum, s_sum, kl = lax.fori_loop(0, SEQ // CK, step, (zero, zero, zero), unroll=2)
    t_sum = jnp.sum(t_sum, 0, keepdims=True)
    s_sum = jnp.sum(s_sum, 0, keepdims=True)
    kl = jnp.sum(kl, 0, keepdims=True)
    t_inv, s_inv = 1.0 / t_sum, 1.0 / s_sum
    kl = kl * t_inv - (t_top + jnp.log(t_sum)) + (s_top * s_scale + jnp.log(s_sum))
    stat_ref[0, 0, 0:1, :] = t_inv
    stat_ref[0, 0, 1:2, :] = s_inv
    stat_ref[0, 0, 2:3, :] = kl
    stat_ref[0, 0, 3:8, :] = jnp.zeros((5, QB), F32)
    t_mixed = dot(tvt_ref[...], et_ref[0, 0]) * t_inv
    tmix_ref[...] = t_mixed.T.astype(BF16)
    smix_ref[0] = dot(svt_ref[...], es_ref[0, 0]) * s_inv


def attend(meta, tq, tk, tvt, sq, sk, svt):
    slot = lambda j, m: (m[2] + j) // 8
    return pl.pallas_call(
        attend_kernel,
        grid_spec=pltpu.PrefetchScalarGridSpec(
            num_scalar_prefetch=1,
            grid=(3, HEADS),
            in_specs=[
                pl.BlockSpec((QB, HEAD_T), lambda j, h, m: (j, h)),
                pl.BlockSpec((SEQ, HEAD_T), lambda j, h, m: (slot(j, m), h)),
                pl.BlockSpec((HEAD_T, SEQ), lambda j, h, m: (h, slot(j, m))),
                pl.BlockSpec((QB, D_S), lambda j, h, m: (m[2] + j, 0)),
                pl.BlockSpec((SEQ, D_S), lambda j, h, m: (slot(j, m), 0)),
                pl.BlockSpec((HEAD_S, SEQ), lambda j, h, m: (h, slot(j, m))),
            ],
            out_specs=[
                pl.BlockSpec((1, 1, SEQ, QB), lambda j, h, m: (j, h, 0, 0)),
                pl.BlockSpec((1, 1, SEQ, QB), lambda j, h, m: (j, h, 0, 0)),
                pl.BlockSpec((QB, HEAD_T), lambda j, h, m: (j, h)),
                pl.BlockSpec((1, HEAD_S, QB), lambda j, h, m: (j, h, 0)),
                pl.BlockSpec((1, 1, 8, QB), lambda j, h, m: (j, h, 0, 0)),
            ],
            scratch_shapes=[pltpu.VMEM((SEQ, QB), F32), pltpu.VMEM((SEQ, QB), F32)],
        ),
        out_shape=[
            jax.ShapeDtypeStruct((3, HEADS, SEQ, QB), BF16),
            jax.ShapeDtypeStruct((3, HEADS, SEQ, QB), BF16),
            jax.ShapeDtypeStruct((OWN, D_T), BF16),
            jax.ShapeDtypeStruct((3, D_S, QB), F32),
            jax.ShapeDtypeStruct((3, HEADS, 8, QB), F32),
        ],
        compiler_params=params(),
        name="attend",
    )(meta, tq, tk, tvt, sq, sk, svt)


FC = 1024


def teacher_kernel(mix_ref, hid_ref, emb_ref, att_ref, up_ref, down_ref, out_ref, bias_ref, up_bias_ref, gain_ref, shift_ref, target_ref, norm, low, acc):
    c = pl.program_id(0)

    @pl.when(c == 0)
    def _():
        summed = hid_ref[...] + dot(mix_ref[...], att_ref[...]) + bias_ref[:, 4096:5120]
        one = layer_norm(summed, gain_ref[:, :D_T], shift_ref[:, :D_T])
        norm[...] = one
        low[...] = one.astype(BF16)

    act = gelu(dot(low[...], up_ref[...]) + up_bias_ref[...]).astype(BF16)
    part = dot(act, down_ref[...])

    @pl.when(c == 0)
    def _():
        acc[...] = part

    @pl.when(c > 0)
    def _():
        acc[...] += part

    @pl.when(c == pl.num_programs(0) - 1)
    def _():
        summed = norm[...] + acc[...] + bias_ref[:, 9216:10240]
        two = layer_norm(summed, gain_ref[:, D_T : 2 * D_T], shift_ref[:, D_T : 2 * D_T])
        last = emb_ref[...].astype(F32) + dot(two.astype(BF16), out_ref[...]) + bias_ref[:, 10240:]
        target_ref[...] = layer_norm(last, gain_ref[:, 2 * D_T :], shift_ref[:, 2 * D_T :])


def teacher(mix, hid, emb, att, up, down, out, bias, gain, shift):
    return pl.pallas_call(
        teacher_kernel,
        grid=(FF_T // FC,),
        in_specs=[
            whole(OWN, D_T),
            whole(OWN, D_T),
            whole(OWN, D_E),
            whole(D_T, D_T),
            pl.BlockSpec((D_T, FC), lambda c: (0, c)),
            pl.BlockSpec((FC, D_T), lambda c: (c, 0)),
            whole(D_T, D_E),
            whole(1, 10752),
            pl.BlockSpec((1, FC), lambda c: (0, 5120 // FC + c)),
            whole(1, 2560),
            whole(1, 2560),
        ],
        out_specs=whole(OWN, D_E),
        out_shape=jax.ShapeDtypeStruct((OWN, D_E), F32),
        scratch_shapes=[pltpu.VMEM((OWN, D_T), F32), pltpu.VMEM((OWN, D_T), BF16), pltpu.VMEM((OWN, D_T), F32)],
        compiler_params=params(),
        name="teacher",
    )(mix, hid, emb, att, up, down, out, bias, bias, gain, shift)


def student_kernel(emb_ref, smix_ref, target_ref, weight_ref, stat_ref, win_ref, watt_ref, wup_ref, wdown_ref, wout_ref, vec_ref,
                   grad_ref, vgrad_ref, dsum_ref, dmix_ref, part_ref, states, inners, outers):
    line = lambda r, n=1: jnp.concatenate([vec_ref[r + i : r + i + 1, :] for i in range(n)], 1) if n > 1 else vec_ref[r : r + 1, :]

    def put(r, value):
        for i in range(value.shape[1] // 128):
            vgrad_ref[r + i : r + i + 1, :] = value[:, i * 128 : i * 128 + 128]

    total = lambda v: jnp.sum(v.astype(F32), 0, keepdims=True)
    emb = emb_ref[...]
    source = emb.astype(F32)
    first = dot(emb, win_ref[...]) + line(V_IN)
    mixed = jnp.concatenate([smix_ref[j].T for j in range(3)], 0).astype(BF16)
    branch = dot(mixed, watt_ref[...]) + line(V_ATT)
    state = line(V_AGAIN) * (first + branch) + line(V_ASHIFT)
    for i in range(FFN_COUNT):
        states[i] = state
        inner = dot(state.astype(BF16), wup_ref[i]) + line(V_UP + 4 * i, 4)
        inners[i] = inner
        act = gelu(inner).astype(BF16)
        pre = state + dot(act, wdown_ref[i]) + line(V_DOWN + i)
        outers[i] = pre
        state = line(V_FGAIN + i) * pre + line(V_FSHIFT + i)
    state_low = state.astype(BF16)
    summed = source + dot(state_low, wout_ref[...]) + line(V_OUT, 4)
    diff = line(V_OGAIN, 4) * summed + line(V_OSHIFT, 4) - target_ref[...]
    weight = weight_ref[...]
    loss = jnp.sum(weight * jnp.sum(diff * diff, 1, keepdims=True)) * (1.0 / D_E)
    count = jnp.sum(weight)
    d_result = (weight * (2.0 / D_E)) * diff
    put(V_OGAIN, total(d_result * summed))
    put(V_OSHIFT, total(d_result))
    d_output = (d_result * line(V_OGAIN, 4)).astype(BF16)
    out_g = dot_tn(state_low, d_output)
    for n in range(4):
        grad_ref[pl.ds(4224 + n, 128, stride=4), :] = out_g[:, n * 128 : n * 128 + 128]
    put(V_OUT, total(d_output))
    d_state = dot_nt(d_output, wout_ref[...])
    for i in reversed(range(FFN_COUNT)):
        inner = inners[i]
        put(V_FGAIN + i, total(d_state * outers[i]))
        put(V_FSHIFT + i, total(d_state))
        d_sum = d_state * line(V_FGAIN + i)
        d_outer = d_sum.astype(BF16)
        half = 0.5 * (1.0 + lax.erf(inner * 0.7071067811865476))
        act = (inner * half).astype(BF16)
        slope = half + inner * jnp.exp(-0.5 * inner * inner) * 0.3989422804014327
        grad_ref[2176 + 512 * i : 2176 + 512 * (i + 1), :] = dot_tn(act, d_outer)
        d_inner = (dot_nt(d_outer, wdown_ref[i]) * slope).astype(BF16)
        up_g = dot_tn(states[i].astype(BF16), d_inner)
        for n in range(4):
            grad_ref[pl.ds(128 + 512 * i + n, 128, stride=4), :] = up_g[:, n * 128 : n * 128 + 128]
        put(V_UP + 4 * i, total(d_inner))
        put(V_DOWN + i, total(d_outer))
        d_state = d_sum + dot_nt(d_inner, wup_ref[i])
    put(V_AGAIN, total(d_state * (first + branch)))
    put(V_ASHIFT, total(d_state))
    d_sum = d_state * line(V_AGAIN)
    d_branch = d_sum.astype(BF16)
    grad_ref[0:128, :] = dot_tn(mixed, d_branch)
    put(V_ATT, total(d_branch))
    dsum_ref[...] = d_sum
    dmix_ref[...] = dot_nt(d_branch, watt_ref[...]).astype(BF16)
    for r in (0, 1, 2, 3, 47):
        vgrad_ref[r : r + 1, :] = jnp.zeros((1, 128), F32)
    kl = jnp.zeros((1, QB), F32)
    row = lax.broadcasted_iota(jnp.int32, (8, 128), 0)
    lane = lax.broadcasted_iota(jnp.int32, (8, 128), 1)
    part_ref[...] = jnp.where((row == 0) & (lane == 0), loss, 0.0) + jnp.where((row == 0) & (lane == 1), count, 0.0)


def student(emb, smix, target, weight, stat, win, watt, wup, wdown, wout, vecs):
    return pl.pallas_call(
        student_kernel,
        grid=(1,),
        in_specs=[
            whole(OWN, D_E),
            whole(3, D_S, QB),
            whole(OWN, D_E),
            whole(OWN, 1),
            whole(3, HEADS, 8, QB),
            whole(D_E, D_S),
            whole(D_S, D_S),
            whole(FFN_COUNT, D_S, FF_S),
            whole(FFN_COUNT, FF_S, D_S),
            whole(D_S, D_E),
            whole(48, 128),
        ],
        out_specs=[whole(4736, 128), whole(48, 128), whole(OWN, D_S), whole(OWN, D_S), whole(8, 128)],
        out_shape=[
            jax.ShapeDtypeStruct((4736, 128), F32),
            jax.ShapeDtypeStruct((48, 128), F32),
            jax.ShapeDtypeStruct((OWN, D_S), F32),
            jax.ShapeDtypeStruct((OWN, D_S), BF16),
            jax.ShapeDtypeStruct((8, 128), F32),
        ],
        scratch_shapes=[
            pltpu.VMEM((FFN_COUNT, OWN, D_S), F32),
            pltpu.VMEM((FFN_COUNT, OWN, FF_S), F32),
            pltpu.VMEM((FFN_COUNT, OWN, D_S), F32),
        ],
        compiler_params=params(),
        name="student",
    )(emb, smix, target, weight, stat, win, watt, wup, wdown, wout, vecs)


def back_kernel(meta, et_ref, es_ref, stat_ref, smix_ref, dmix_ref, weight_ref, sq_ref, sk_unused, sv_ref, skt_ref, dsum_ref,
                emb_ref, first_ref, wqkv_ref, grad_ref, vgrad_ref, kl_ref, dkv, dqt, ds, dq, dfirst):
    j, head = pl.program_id(0), pl.program_id(1)
    s_scale = HEAD_S**-0.5

    @pl.when((j == 0) & (head == 0))
    def _():
        dkv[...] = jnp.zeros_like(dkv)
        kl_ref[...] = jnp.zeros_like(kl_ref)

    t_inv, s_inv = stat_ref[0, 0, 0:1, :], stat_ref[0, 0, 1:2, :]
    weight = weight_ref[0]
    kl_ref[0:1, :] += weight * stat_ref[0, 0, 2:3, :] * (1.0 / HEADS)
    quarter = weight * (1.0 / HEADS)
    dmix_t = dmix_ref[...].astype(F32).T
    place = lax.broadcasted_iota(jnp.int32, (D_S, 1), 0) // HEAD_S
    dmix_t = jnp.where(place == head, dmix_t, 0.0)
    mix = smix_ref[0]
    row_dot = jnp.sum(dmix_t * jnp.concatenate([mix] * HEADS, 0), 0, keepdims=True)
    offset = row_dot - quarter
    t_part = quarter * t_inv
    dmix_low = dmix_t.astype(BF16)
    for c in range(SEQ // 256):
        part = pl.ds(c * 256, 256)
        d_probs = dot(sv_ref[part, :], dmix_low)
        es = es_ref[0, 0, part, :].astype(F32)
        et = et_ref[0, 0, part, :].astype(F32)
        ds[part, :] = ((d_probs - offset) * s_inv * es - et * t_part).astype(BF16)
    slot = pl.multiple_of((meta[2] + j) // 8 * SEQ, SEQ)
    s_queries = head_lanes(sq_ref[...], head)
    dmix_z = (dmix_t * s_inv).astype(BF16)
    for c in range(SEQ // 256):
        part = pl.ds(c * 256, 256)
        rows = pl.ds(slot + c * 256, 256)
        dkv[rows, :D_S] += dot(ds[part, :], s_queries)
        dkv[rows, D_S:] += dot_nt(es_ref[0, 0, part, :], dmix_z)
    dqt[pl.ds(pl.multiple_of(head * HEAD_S, HEAD_S), HEAD_S), :] = dot(skt_ref[...], ds[...]) * s_scale

    @pl.when(head == HEADS - 1)
    def _():
        dq[pl.ds(pl.multiple_of(j * QB, QB), QB), :] = dqt[...].T

    @pl.when((j == 2) & (head == HEADS - 1))
    def _():
        qkv_w = wqkv_ref[...]
        dq_low = dq[...].astype(BF16)
        own = pl.ds(pl.multiple_of(meta[2] * QB, QB), OWN)
        q_grad = dot_tn(first_ref[own, :], dq_low)
        own_part = dsum_ref[...] + dot_nt(dq_low, qkv_w[:, :D_S])
        kv_grad = jnp.zeros((D_S, 2 * D_S), F32)
        kv_bias = jnp.zeros((1, 2 * D_S), F32)
        for c in range(8):
            part = pl.ds(c * 512, 512)
            wide = dkv[part, :]
            low = jnp.concatenate([(wide[:, :D_S] * s_scale).astype(BF16), wide[:, D_S:].astype(BF16)], 1)
            kv_grad += dot_tn(first_ref[part, :], low)
            kv_bias += jnp.sum(low.astype(F32), 0, keepdims=True)
            dfirst[part, :] = dot_nt(low, qkv_w[:, D_S:])
        dfirst[own, :] += own_part
        in_grad = jnp.zeros((D_S, D_E), F32)
        in_bias = jnp.zeros((1, D_S), F32)
        for c in range(8):
            part = pl.ds(c * 512, 512)
            low = dfirst[part, :].astype(BF16)
            in_grad += dot_tn(low, emb_ref[part, :])
            in_bias += jnp.sum(low.astype(F32), 0, keepdims=True)
        grad_ref[0:512, :] = in_grad.T
        grad_ref[pl.ds(512, 128, stride=3), :] = q_grad
        grad_ref[pl.ds(513, 128, stride=3), :] = kv_grad[:, :D_S]
        grad_ref[pl.ds(514, 128, stride=3), :] = kv_grad[:, D_S:]
        vgrad_ref[...] = jnp.zeros((8, 128), F32)
        vgrad_ref[0:1, :] = in_bias
        vgrad_ref[1:2, :] = jnp.sum(dq_low.astype(F32), 0, keepdims=True)
        vgrad_ref[2:3, :] = kv_bias[:, :D_S]
        vgrad_ref[3:4, :] = kv_bias[:, D_S:]


def back(meta, et, es, stat, smix, dmix, weight, sq, sk, sv, skt, dsum, emb, first, wqkv):
    slot = lambda j, m: (m[2] + j) // 8
    return pl.pallas_call(
        back_kernel,
        grid_spec=pltpu.PrefetchScalarGridSpec(
            num_scalar_prefetch=1,
            grid=(3, HEADS),
            in_specs=[
                pl.BlockSpec((1, 1, SEQ, QB), lambda j, h, m: (j, h, 0, 0)),
                pl.BlockSpec((1, 1, SEQ, QB), lambda j, h, m: (j, h, 0, 0)),
                pl.BlockSpec((1, 1, 8, QB), lambda j, h, m: (j, h, 0, 0)),
                pl.BlockSpec((1, HEAD_S, QB), lambda j, h, m: (j, h, 0)),
                pl.BlockSpec((QB, D_S), lambda j, h, m: (j, 0)),
                pl.BlockSpec((1, 1, QB), lambda j, h, m: (j, 0, 0)),
                pl.BlockSpec((QB, D_S), lambda j, h, m: (m[2] + j, 0)),
                pl.BlockSpec((SEQ, D_S), lambda j, h, m: (slot(j, m), 0)),
                pl.BlockSpec((SEQ, D_S), lambda j, h, m: (slot(j, m), 0)),
                pl.BlockSpec((HEAD_S, SEQ), lambda j, h, m: (h, slot(j, m))),
                whole(OWN, D_S),
                whole(SLOTS, D_E),
                whole(SLOTS, D_S),
                whole(D_S, 3 * D_S),
            ],
            out_specs=[whole(896, 128), whole(8, 128), whole(8, QB)],
            scratch_shapes=[
                pltpu.VMEM((SLOTS, 2 * D_S), F32),
                pltpu.VMEM((D_S, QB), F32),
                pltpu.VMEM((SEQ, QB), BF16),
                pltpu.VMEM((OWN, D_S), F32),
                pltpu.VMEM((SLOTS, D_S), F32),
            ],
        ),
        out_shape=[
            jax.ShapeDtypeStruct((896, 128), F32),
            jax.ShapeDtypeStruct((8, 128), F32),
            jax.ShapeDtypeStruct((8, QB), F32),
        ],
        compiler_params=params(),
        name="back",
    )(meta, et, es, stat, smix, dmix, weight, sq, sk, sv, skt, dsum, emb, first, wqkv)


def update_kernel(g_ref, part_ref, master_ref, first_ref, second_ref, new_ref, newf_ref, news_ref, scal_ref,
                  half_out, half_in, mine, block_out, blocks_in, tile_out, tiles_f, tiles_d,
                  half_sems, block_send, block_recv, f_send, f_recv, d_send, d_recv):
    dp, fs = lax.axis_index("dp"), lax.axis_index("fsdp")
    x, core = dp // 2, dp % 2
    sibling = (2 * x + 1 - core, fs)
    barrier = pltpu.get_barrier_semaphore()

    def chip(k):
        return (2 * ((x + k // 16) % 4) + core, (fs + k) % 16)

    def greet(k, _):
        pl.semaphore_signal(barrier, inc=1, device_id=chip(k), device_id_type=MESH)
        return 0

    lax.fori_loop(1, 64, greet, 0)
    for k in range(4):
        other = (2 * ((x + k) % 4) + 1 - core, fs)
        pl.semaphore_signal(barrier, inc=1, device_id=other, device_id_type=MESH)

    def split(i, _):
        half_out[i] = g_ref[i // 16, 1 - core, i % 16].astype(BF16)
        return 0

    lax.fori_loop(0, 64, split, 0)
    pl.semaphore_wait(barrier, 67)
    swap = pltpu.make_async_remote_copy(
        half_out, half_in, half_sems.at[0], half_sems.at[1], device_id=sibling, device_id_type=MESH
    )
    swap.start()
    swap.wait()

    def join(i, _):
        summed = g_ref[i // 16, core, i % 16] + half_in[i].astype(F32)
        block_out[i] = summed.astype(BF16)
        return 0

    lax.fori_loop(0, 64, join, 0)
    my_chip = x * 16 + fs
    mine[...] = g_ref[x, core, fs] + half_in[my_chip].astype(F32)

    def block_copy(k):
        xk, fk = (x + k // 16) % 4, (fs + k) % 16
        return pltpu.make_async_remote_copy(
            block_out.at[xk * 16 + fk], blocks_in.at[k], block_send.at[k], block_recv.at[k],
            device_id=(2 * xk + core, fk), device_id_type=MESH,
        )

    def start(k, _):
        block_copy(k).start()
        return 0

    lax.fori_loop(1, 64, start, 0)

    def gather(k, _):
        block_copy(k).wait()
        mine[...] += blocks_in[k].astype(F32)
        return 0

    lax.fori_loop(1, 64, gather, 0)

    row = lax.broadcasted_iota(jnp.int32, (BLOCK, 128), 0)
    lane8 = lax.broadcasted_iota(jnp.int32, (8, 128), 1)
    row8 = lax.broadcasted_iota(jnp.int32, (8, 128), 0)
    place = (dp * 16 + fs) * SHARD + row
    is_matrix = row < SHARD
    bounds = [0]
    for rows in MAT_ROWS:
        bounds.append(bounds[-1] + rows)
    members = [is_matrix & (place >= bounds[i]) & (place < bounds[i + 1]) for i in range(6)]

    def everyone(tile, turn):
        tile_out[turn, 0] = tile
        tiles_f[turn, fs] = tile

        def f_copy(k):
            return pltpu.make_async_remote_copy(
                tile_out.at[turn, 0], tiles_f.at[turn, fs], f_send.at[turn, k], f_recv.at[turn, k],
                device_id=(dp, (fs + k) % 16), device_id_type=MESH,
            )

        def d_copy(k):
            return pltpu.make_async_remote_copy(
                tile_out.at[turn, 1], tiles_d.at[turn, dp], d_send.at[turn, k], d_recv.at[turn, k],
                device_id=((dp + k) % 8, fs), device_id_type=MESH,
            )

        for k in range(1, 16):
            f_copy(k).start()
        for k in range(1, 16):
            f_copy(k).wait()
        total = tiles_f[turn, 0]
        for k in range(1, 16):
            total = total + tiles_f[turn, k]
        tile_out[turn, 1] = total
        tiles_d[turn, dp] = total
        for k in range(1, 8):
            d_copy(k).start()
        for k in range(1, 8):
            d_copy(k).wait()
        total = tiles_d[turn, 0]
        for k in range(1, 8):
            total = total + tiles_d[turn, k]
        return total

    def entry(tile, i):
        return jnp.sum(jnp.where((row8 == 0) & (lane8 == i), tile, 0.0), keepdims=True)

    def tile_of(values):
        tile = jnp.zeros((8, 128), F32)
        for i, value in values:
            tile += jnp.where((row8 == 0) & (lane8 == i), value, 0.0)
        return tile

    grad = mine[...]
    master = master_ref[...]
    squares = master * master
    tile = part_ref[...] + tile_of(
        [(2, jnp.sum(grad * grad, keepdims=True))]
        + [(3 + i, jnp.sum(jnp.where(members[i], squares, 0.0), keepdims=True)) for i in range(6)]
    )
    tile = everyone(tile, 0)
    loss, count = entry(tile, 0), entry(tile, 1)
    inverse = 1.0 / count
    norm = jnp.sqrt(entry(tile, 2)) * inverse
    factor = CLIP_NORM / jnp.maximum(norm, CLIP_NORM)
    grad = grad * inverse * factor
    first = BETA_ONE * first_ref[...] + (1.0 - BETA_ONE) * grad
    second = BETA_TWO * second_ref[...] + (1.0 - BETA_TWO) * grad * grad
    newf_ref[...] = first
    news_ref[...] = second
    ratio = first / (1.0 - BETA_ONE**STEP) / (jnp.sqrt(second / (1.0 - BETA_TWO**STEP)) + ADAM_EPS)
    ratio = ratio + jnp.where(is_matrix, WEIGHT_DECAY * master, 0.0)
    squares = ratio * ratio
    steps = everyone(tile_of([(3 + i, jnp.sum(jnp.where(members[i], squares, 0.0), keepdims=True)) for i in range(6)]), 1)
    trust = jnp.ones((BLOCK, 128), F32)
    for i in range(6):
        trust = jnp.where(members[i], jnp.sqrt(entry(tile, 3 + i)) / jnp.sqrt(entry(steps, 3 + i)), trust)
    new_ref[...] = master - LEARN_RATE * (trust * ratio)
    scal_ref[...] = tile_of([(0, loss), (1, count), (2, norm)])


def update(grads, part, master, first, second):
    vmem = pl.BlockSpec(memory_space=pltpu.VMEM)
    block = jax.ShapeDtypeStruct((BLOCK, 128), F32)
    dma = pltpu.SemaphoreType.DMA
    return pl.pallas_call(
        update_kernel,
        in_specs=[vmem] * 5,
        out_specs=[vmem] * 4,
        out_shape=[block, block, block, jax.ShapeDtypeStruct((8, 128), F32)],
        scratch_shapes=[
            pltpu.VMEM((64, BLOCK, 128), BF16),
            pltpu.VMEM((64, BLOCK, 128), BF16),
            pltpu.VMEM((BLOCK, 128), F32),
            pltpu.VMEM((64, BLOCK, 128), BF16),
            pltpu.VMEM((64, BLOCK, 128), BF16),
            pltpu.VMEM((2, 2, 8, 128), F32),
            pltpu.VMEM((2, 16, 8, 128), F32),
            pltpu.VMEM((2, 8, 8, 128), F32),
            dma((2,)),
            dma((64,)),
            dma((64,)),
            dma((2, 16)),
            dma((2, 16)),
            dma((2, 8)),
            dma((2, 8)),
        ],
        compiler_params=params(collective_id=1, has_side_effects=True),
        name="update",
    )(grads, part, master, first, second)


def pack(mats, vecs):
    return jnp.concatenate(
        [mats.reshape(SHARD, 128), jnp.pad(vecs, (0, 128 - 47)).reshape(1, 128), jnp.zeros((BLOCK - SHARD - 1, 128), mats.dtype)]
    )


def per_device(
    token_ids,
    splits,
    valid_mask,
    embed_table,
    embed_proj,
    embed_bias,
    type_table,
    teach_in,
    teach_qkv,
    teach_att,
    teach_up,
    teach_down,
    teach_out,
    teach_bias,
    teach_gain,
    teach_shift,
    matrices,
    vectors,
    matrix_first,
    matrix_second,
    vector_first,
    vector_second,
):
    master = pack(matrices, vectors)
    gathered = lax.all_gather(master.astype(BF16), ("dp", "fsdp"), axis=0, tiled=False)
    place = lax.axis_index("fsdp")
    r0, r1 = rows_of(place)
    meta = jnp.stack([splits[r0], splits[r1], (3 * (place % 8)) % 8, jnp.zeros((), jnp.int32)]).astype(jnp.int32)
    spread_rows, weights = spread(embed_table[token_ids], jnp.pad(valid_mask, ((0, 2), (0, 0))))
    bias = teach_bias.reshape(1, -1)
    emb, t_keys, t_values = project(
        meta, spread_rows.reshape(SLOTS, 128), embed_proj, embed_bias.reshape(1, -1), type_table, teach_in, teach_qkv, bias
    )
    own_emb, hidden, t_queries = own_queries(meta, emb, teach_in, teach_qkv, bias)

    flat = gathered[:, :SHARD].reshape(5632, 128)
    vecs = jnp.pad(gathered[:, SHARD, :47].reshape(47, 128).astype(F32), ((0, 1), (0, 0)))
    in_w, qkv_w, att_w = flat[:512], flat[512:896].reshape(128, 384), flat[896:1024]
    up_w = flat[1024:3072].reshape(FFN_COUNT, D_S, FF_S)
    down_w = flat[3072:5120].reshape(FFN_COUNT, FF_S, D_S)
    out_w = flat[5120:].reshape(D_S, D_E)
    first, s_q, s_k, s_v, s_kt, s_vt = student_in(emb, in_w, qkv_w, vecs)
    et, es, t_mixed, s_mixed, stat = attend(meta, t_queries, t_keys, t_values, s_q, s_k, s_vt)
    target = teacher(
        t_mixed, hidden, own_emb, teach_att, teach_up, teach_down, teach_out, bias,
        teach_gain.reshape(1, -1), teach_shift.reshape(1, -1),
    )
    grads_c, vgrads_c, d_sum, d_mixed, part = student(
        own_emb, s_mixed, target, weights.reshape(OWN, 1), stat, in_w, att_w, up_w, down_w, out_w, vecs
    )
    grads_d, vgrads_d, kl = back(
        meta, et, es, stat, s_mixed, d_mixed, weights, s_q, s_k, s_v, s_kt, d_sum, emb, first, qkv_w
    )
    part = part.at[0, 0].add(jnp.sum(kl))
    grads = jnp.concatenate([grads_d, grads_c]).reshape(128, SHARD, 128)
    vgrads = jnp.concatenate([vgrads_d[:4], vgrads_c[4:47]]).reshape(128, 1, 47)
    grads = jnp.concatenate(
        [grads, jnp.pad(vgrads, ((0, 0), (0, 0), (0, 81))), jnp.zeros((128, BLOCK - SHARD - 1, 128), F32)], 1
    ).reshape(4, 2, 16, BLOCK, 128)
    new, new_first, new_second, scalars = update(
        grads, part, master, pack(matrix_first, vector_first), pack(matrix_second, vector_second)
    )
    mats = lambda v: v[:SHARD].reshape(-1)
    vecs_of = lambda v: v[SHARD, :47]
    return (
        scalars[0, 0],
        scalars[0, 1],
        scalars[0, 2],
        mats(new),
        mats(new_first),
        mats(new_second),
        vecs_of(new),
        vecs_of(new_first),
        vecs_of(new_second),
    )


def solution(mesh):
    both = P(("dp", "fsdp"))
    return jax.shard_map(
        per_device,
        mesh=mesh,
        in_specs=(P("dp", "fsdp"), P("dp"), P("dp", "fsdp")) + (P(),) * 13 + (both,) * 6,
        out_specs=(P(), P(), P(), both, both, both, both, both, both),
        check_vma=False,
    )
```

```python
import functools
import math

import jax
import jax.numpy as jnp
from jax import lax
from jax.experimental import pallas as pl
from jax.experimental.pallas import tpu as pltpu
from jax.sharding import PartitionSpec as P

D_E = 512
D_T = 1024
FF_T = 4096
D_S = 128
FF_S = 512
HEADS = 4
FFN_COUNT = 4
STEP = 5
HEAD_T = 256
HEAD_S = 32
SEQ = 2048
QB = 256
OWN = 3 * QB
SLOTS = 2 * SEQ

CLIP_NORM = 0.05
BETA_ONE = 0.9
BETA_TWO = 0.999
LEARN_RATE = 0.3
WEIGHT_DECAY = 0.01
ADAM_EPS = 1e-06

F32 = jnp.float32
BF16 = jnp.bfloat16
LOG2E = 1.4426950408889634
MESH = pl.DeviceIdType.MESH
BIG_VMEM = 60 * 2**20

MAT_ROWS = (512, 384, 128, 2048, 2048, 512)
SHARD = 44
BLOCK = 48
(V_IN, V_QKV, V_ATT, V_AGAIN, V_ASHIFT, V_UP, V_DOWN, V_FGAIN, V_FSHIFT, V_OUT, V_OGAIN, V_OSHIFT) = (
    0, 1, 4, 5, 6, 7, 23, 27, 31, 35, 39, 43)


def dot(left, right):
    return jnp.dot(left, right, preferred_element_type=F32)


def dot_nt(left, right):
    return lax.dot_general(left, right, (((1,), (1,)), ((), ())), preferred_element_type=F32)


def dot_tn(left, right):
    return lax.dot_general(left, right, (((0,), (0,)), ((), ())), preferred_element_type=F32)


def layer_norm(values, gain, shift):
    center = values - jnp.mean(values, -1, keepdims=True)
    spread = jnp.mean(center * center, -1, keepdims=True)
    return center * lax.rsqrt(spread + 1e-05) * gain + shift


def gelu(values):
    return 0.5 * values * (1.0 + lax.erf(values * 0.7071067811865476))


def params(**more):
    return pltpu.CompilerParams(vmem_limit_bytes=BIG_VMEM, **more)


def whole(*shape):
    return pl.BlockSpec(shape, lambda *_: (0,) * len(shape))


def line(ref, row, count=1):
    if count == 1:
        return ref[row : row + 1, :]
    return jnp.concatenate([ref[row + i : row + i + 1, :] for i in range(count)], 1)


def fold(values, op=jnp.sum):
    return op(values.reshape(values.shape[0] // 8, 8, values.shape[1]), 0)


def rows_of(place):
    i, g = place % 8, place // 8
    return 3 * g + (3 * i) // 8, 3 * g + (3 * i + 2) // 8


def first_block():
    return (3 * (lax.axis_index("fsdp") % 8)) % 8


def slot_of(j):
    return (first_block() + j) // 8


def spread_kernel(e_ref, mask_in, mats_ref, vecs_ref, all_ref, weight_ref, params_ref, mask_ref, masks, wide, block, send, recv, p_send, p_recv, s_send, s_recv):
    dp, me = lax.axis_index("dp"), lax.axis_index("fsdp")
    x, core = dp // 2, dp % 2
    sibling = (2 * x + 1 - core, me)
    barrier = pltpu.get_barrier_semaphore()

    def chip(k):
        return (2 * ((x + k // 16) % 4) + core, (me + k) % 16)

    def greet(k, _):
        pl.semaphore_signal(barrier, inc=1, device_id=chip(k), device_id_type=MESH)
        return 0

    lax.fori_loop(1, 64, greet, 0)
    pl.semaphore_signal(barrier, inc=1, device_id=sibling, device_id_type=MESH)
    r0, r1 = rows_of(me)
    all_ref[0, me] = e_ref[r0]
    mask_ref[0:6] = mask_in[...]
    mask_ref[6:8] = jnp.zeros((2, 128), jnp.int32)
    masks[me] = mask_ref[...]
    wide[...] = jnp.zeros((BLOCK, 128), F32)
    wide[0:SHARD, :] = mats_ref[...]
    wide[SHARD : SHARD + 1, 0:47] = vecs_ref[...]
    block[...] = wide[...].astype(BF16)
    params_ref[dp * 16 + me] = block[...]

    @pl.when(r1 == r0)
    def _():
        all_ref[1] = jnp.zeros_like(all_ref[1])

    @pl.when(r1 != r0)
    def _():
        all_ref[1, me] = e_ref[r1]

    pl.semaphore_wait(barrier, 64)

    def copies(k):
        peer = (me + k) % 16
        s0, s1 = rows_of(peer)
        where = dict(device_id=(dp, peer), device_id_type=MESH)
        return (
            pltpu.make_async_remote_copy(e_ref.at[s0], all_ref.at[0, me], send.at[k, 0], recv.at[k, 0], **where),
            pltpu.make_async_remote_copy(e_ref.at[s1], all_ref.at[1, me], send.at[k, 1], recv.at[k, 1], **where),
            pltpu.make_async_remote_copy(mask_ref, masks.at[me], send.at[k, 2], recv.at[k, 2], **where),
            s0 != s1,
        )

    def start(k, _):
        first, second, third, two = copies(k)
        first.start()
        third.start()

        @pl.when(two)
        def _():
            second.start()

        return 0

    lax.fori_loop(1, 16, start, 0)

    def param_copy(k):
        return pltpu.make_async_remote_copy(
            block, params_ref.at[dp * 16 + me], p_send.at[k], p_recv.at[k], device_id=chip(k), device_id_type=MESH
        )

    def param_start(k, _):
        param_copy(k).start()
        return 0

    lax.fori_loop(1, 64, param_start, 0)

    def to_sibling(k):
        source = 2 * ((x + 4 - k // 16) % 4) + core
        place = source * 16 + (me + 64 - k) % 16
        return pltpu.make_async_remote_copy(
            params_ref.at[place], params_ref.at[place], s_send.at[k], s_recv.at[k], device_id=sibling, device_id_type=MESH
        )

    to_sibling(0).start()

    def finish(k, _):
        first, second, third, two = copies(k)
        first.wait_send()
        third.wait_send()

        @pl.when(two)
        def _():
            second.wait_send()

        source = (me + 16 - k) % 16
        here = dict(device_id=(dp, source), device_id_type=MESH)
        pltpu.make_async_remote_copy(e_ref.at[r0], all_ref.at[0, source], send.at[k, 0], recv.at[k, 0], **here).wait_recv()
        pltpu.make_async_remote_copy(mask_ref, masks.at[source], send.at[k, 2], recv.at[k, 2], **here).wait_recv()

        @pl.when(r1 != r0)
        def _():
            pltpu.make_async_remote_copy(
                e_ref.at[r1], all_ref.at[1, source], send.at[k, 1], recv.at[k, 1], **here
            ).wait_recv()

        return 0

    lax.fori_loop(1, 16, finish, 0)

    def forward(k, _):
        param_copy(k).wait()
        to_sibling(k).start()
        return 0

    lax.fori_loop(1, 64, forward, 0)

    def forwarded(k, _):
        to_sibling(k).wait()
        return 0

    lax.fori_loop(0, 64, forwarded, 0)
    for j in range(3):
        t = first_block() + j
        row = lax.select(t >= 8, r1, r0)
        for half in range(2):
            line = masks[2 * (t % 8) + half, pl.ds(row, 1), :]
            weight_ref[j, :, half * 128 : half * 128 + 128] = line.astype(F32)


def spread(rows, mask, mats, vecs):
    vmem = pl.BlockSpec(memory_space=pltpu.VMEM)
    dma = pltpu.SemaphoreType.DMA
    return pl.pallas_call(
        spread_kernel,
        in_specs=[vmem] * 4,
        out_specs=[vmem] * 3,
        out_shape=[
            jax.ShapeDtypeStruct((2, 16, 128, 128), BF16),
            jax.ShapeDtypeStruct((3, 1, QB), F32),
            jax.ShapeDtypeStruct((128, BLOCK, 128), BF16),
        ],
        scratch_shapes=[
            pltpu.VMEM((8, 128), jnp.int32),
            pltpu.VMEM((16, 8, 128), jnp.int32),
            pltpu.VMEM((BLOCK, 128), F32),
            pltpu.VMEM((BLOCK, 128), BF16),
            dma((16, 3)),
            dma((16, 3)),
            dma((64,)),
            dma((64,)),
            dma((64,)),
            dma((64,)),
        ],
        compiler_params=params(collective_id=0, has_side_effects=True),
        name="spread",
    )(rows, mask, mats, vecs)


PT = 512
TILES = SLOTS // PT


def unpack(packed_ref, flat, win_ref, wqkv_ref, watt_ref, wup_ref, wdown_ref, wout_ref, vec_ref):
    lane = lax.broadcasted_iota(jnp.int32, (1, 128), 1)
    vec_ref[...] = jnp.zeros((48, 128), F32)
    for pair in range(64):
        both = [packed_ref[2 * pair + i].astype(F32) for i in range(2)]
        flat[88 * pair : 88 * pair + 88, :] = jnp.concatenate([b[:SHARD] for b in both], 0)
        for i in range(2):
            row, shift = divmod(47 * (2 * pair + i), 128)
            entries = both[i][SHARD : SHARD + 1, :]
            moved = pltpu.roll(entries, shift, 1) if shift else entries
            vec_ref[row : row + 1, :] += jnp.where(lane >= shift, moved, 0.0)
            if shift + 47 > 128:
                vec_ref[row + 1 : row + 2, :] += jnp.where(lane < shift, moved, 0.0)
    win_ref[...] = flat[0:512, :].astype(BF16)
    for n in range(3):
        wqkv_ref[:, n * 128 : n * 128 + 128] = flat[pl.ds(512 + n, 128, stride=3), :].astype(BF16)
    watt_ref[...] = flat[896:1024, :].astype(BF16)
    for i in range(FFN_COUNT):
        for n in range(4):
            wup_ref[i, :, n * 128 : n * 128 + 128] = flat[pl.ds(1024 + 512 * i + n, 128, stride=4), :].astype(BF16)
        wdown_ref[i] = flat[3072 + 512 * i : 3584 + 512 * i, :].astype(BF16)
    for n in range(4):
        wout_ref[:, n * 128 : n * 128 + 128] = flat[pl.ds(5120 + n, 128, stride=4), :].astype(BF16)


def project_kernel(splits_ref, e_ref, packed_ref, proj_ref, ebias_ref, types_ref, twin_ref, twqkv_ref, bias_ref,
                   emb_ref, k_ref, vt_ref, first_ref, sq_ref, sk_ref, sv_ref, skt_ref, svt_ref,
                   own_ref, hid_ref, tq_ref, win_ref, wqkv_ref, watt_ref, wup_ref, wdown_ref, wout_ref, vec_ref, flat):
    t = pl.program_id(0)

    @pl.when(t == 0)
    def _():
        unpack(packed_ref, flat, win_ref, wqkv_ref, watt_ref, wup_ref, wdown_ref, wout_ref, vec_ref)

    @pl.when(t < TILES)
    def _():
        per = SEQ // PT
        s, p = t // per, t % per
        base = t * PT
        mid = e_ref[pl.ds(pl.multiple_of(base, PT), PT), :]
        lo, hi = jnp.maximum(base - 16, 0), jnp.minimum(base + PT, SLOTS - 16)
        before = e_ref[pl.ds(pl.multiple_of(lo, 16), 16), :].astype(F32)[15:16]
        after = e_ref[pl.ds(pl.multiple_of(hi, 16), 16), :].astype(F32)[0:1]
        before = jnp.where(p == 0, 0.0, before)
        after = jnp.where(p == per - 1, 0.0, after)
        wide = mid.astype(F32)
        row = lax.broadcasted_iota(jnp.int32, (PT, 1), 0)
        left = jnp.where(row == 0, before, pltpu.roll(wide, 1, 0)).astype(BF16)
        right = jnp.where(row == PT - 1, after, pltpu.roll(wide, PT - 1, 0)).astype(BF16)
        trigram = jnp.concatenate([left, mid, right], 1)
        r0, r1 = rows_of(lax.axis_index("fsdp"))
        split = splits_ref[jnp.where(s == 0, r0, r1)]
        typed = jnp.where(row + p * PT >= split, types_ref[1:2, :], types_ref[0:1, :])
        emb = (dot(trigram, proj_ref[...]) + line(ebias_ref, 0, 4) + typed).astype(BF16)
        emb_ref[pl.ds(pl.multiple_of(base, PT), PT), :] = emb
        hidden = (dot(emb, twin_ref[...]) + line(bias_ref, 0, 8)).astype(BF16)
        k_ref[...] = (dot(hidden, twqkv_ref[:, D_T : 2 * D_T]) + line(bias_ref, 16, 8)).astype(BF16)
        values = (dot(hidden, twqkv_ref[:, 2 * D_T :]) + line(bias_ref, 24, 8)).astype(BF16)
        vt_ref[...] = values.T
        first = (dot(emb, win_ref[...]) + line(vec_ref, V_IN)).astype(BF16)
        first_ref[...] = first
        qkv = dot(first, wqkv_ref[...])
        sq_ref[...] = (qkv[:, :D_S] + line(vec_ref, V_QKV)).astype(BF16)
        s_keys = (qkv[:, D_S : 2 * D_S] + line(vec_ref, V_QKV + 1)).astype(BF16)
        s_values = (qkv[:, 2 * D_S :] + line(vec_ref, V_QKV + 2)).astype(BF16)
        sk_ref[...] = s_keys
        sv_ref[...] = s_values
        skt_ref[...] = s_keys.T
        svt_ref[...] = s_values.T

    @pl.when(t == TILES)
    def _():
        emb = emb_ref[pl.ds(pl.multiple_of(first_block() * QB, QB), OWN), :]
        own_ref[...] = emb
        hidden = dot(emb, twin_ref[...]) + line(bias_ref, 0, 8)
        hid_ref[...] = hidden
        queries = (dot(hidden.astype(BF16), twqkv_ref[:, :D_T]) + line(bias_ref, 8, 8)).astype(BF16)
        tq_ref[...] = queries * jnp.asarray(HEAD_T**-0.5, BF16)


def project(splits, e, packed, proj, ebias, types, win, wqkv, bias):
    tall = jax.ShapeDtypeStruct((SLOTS, D_S), BF16)
    flat = jax.ShapeDtypeStruct((D_S, SLOTS), BF16)
    tile = lambda t: jnp.minimum(t, TILES - 1)
    down = pl.BlockSpec((PT, D_S), lambda t: (tile(t), 0))
    across = pl.BlockSpec((D_S, PT), lambda t: (0, tile(t)))
    made = [
        ((OWN, D_E), BF16),
        ((OWN, D_T), F32),
        ((OWN, D_T), BF16),
        ((D_E, D_S), BF16),
        ((D_S, 3 * D_S), BF16),
        ((D_S, D_S), BF16),
        ((FFN_COUNT, D_S, FF_S), BF16),
        ((FFN_COUNT, FF_S, D_S), BF16),
        ((D_S, D_E), BF16),
        ((48, 128), F32),
    ]
    return pl.pallas_call(
        project_kernel,
        grid=(TILES + 1,),
        in_specs=[
            pl.BlockSpec(memory_space=pltpu.SMEM),
            whole(SLOTS, 128),
            whole(128, BLOCK, 128),
            whole(3 * 128, D_E),
            whole(4, 128),
            whole(2, D_E),
            whole(D_E, D_T),
            whole(D_T, 3 * D_T),
            whole(84, 128),
        ],
        out_specs=[
            whole(SLOTS, D_E),
            pl.BlockSpec((PT, D_T), lambda t: (tile(t), 0)),
            pl.BlockSpec((D_T, PT), lambda t: (0, tile(t))),
        ]
        + [down] * 4
        + [across] * 2
        + [whole(*shape) for shape, _ in made],
        out_shape=[
            jax.ShapeDtypeStruct((SLOTS, D_E), BF16),
            jax.ShapeDtypeStruct((SLOTS, D_T), BF16),
            jax.ShapeDtypeStruct((D_T, SLOTS), BF16),
        ]
        + [tall] * 4
        + [flat] * 2
        + [jax.ShapeDtypeStruct(*entry) for entry in made],
        scratch_shapes=[pltpu.VMEM((5632, 128), F32)],
        compiler_params=params(),
        name="project",
    )(splits, e, packed, proj, ebias, types, win, wqkv, bias)


CB = 256
SUB = 64
STEPS = 3 * HEADS


def head_lanes(values, head):
    lane = lax.broadcasted_iota(jnp.int32, (1, D_S), 1)
    return jnp.where(lane // HEAD_S == head, values, jnp.zeros_like(values))


def attend_kernel(tq_ref, tk_ref, tvt_ref, sq_ref, sk_ref, svt_ref, et_ref, es_ref, tmix_ref, smix_ref, stat_ref,
                  ts0, ts1, ss0, ss1, mx0, mx1):
    n = pl.program_id(0)
    s_factor = HEAD_S**-0.5 * LOG2E

    def work(ts, ss, mx, tr, sr, mr, scores, mixes):
        if scores:
            queries, s_queries = tq_ref[...], head_lanes(sq_ref[...], n % HEADS)
            t_max = s_max = jnp.full((8, QB), -jnp.inf, F32)
        if mixes:
            t_top, s_top = jnp.max(mr[0], 0, keepdims=True), jnp.max(mr[1], 0, keepdims=True)
            t_off, s_off = t_top * LOG2E, s_top * s_factor
            t_sum = s_sum = kl = jnp.zeros((8, QB), F32)
            t_mix, s_mix = jnp.zeros((HEAD_T, QB), F32), jnp.zeros((HEAD_S, QB), F32)
        for c in range(SEQ // CB):
            part = slice(c * CB, c * CB + CB)
            if scores:
                t_part = dot_nt(tk_ref[part, :], queries)
                ts[part, :] = t_part
                s_part = dot_nt(sk_ref[part, :], s_queries)
                ss[part, :] = s_part
                t_max = jnp.maximum(t_max, fold(t_part, jnp.max))
                s_max = jnp.maximum(s_max, fold(s_part, jnp.max))
            if mixes:
                for u in range(c * CB, c * CB + CB, SUB):
                    some = slice(u, u + SUB)
                    t_log = tr[some, :] * LOG2E - t_off
                    s_log = sr[some, :] * s_factor - s_off
                    t_exp, s_exp = jnp.exp2(t_log), jnp.exp2(s_log)
                    et_ref[0, some, :] = t_exp.astype(BF16)
                    es_ref[0, some, :] = s_exp.astype(BF16)
                    t_sum, s_sum = t_sum + fold(t_exp), s_sum + fold(s_exp)
                    kl = kl + fold(t_exp * (t_log - s_log))
                t_mix += dot(tvt_ref[:, part], et_ref[0, part, :])
                s_mix += dot(svt_ref[:, part], es_ref[0, part, :])
        if scores:
            mx[0], mx[1] = t_max, s_max
        if mixes:
            t_sum, s_sum, kl = (jnp.sum(v, 0, keepdims=True) for v in (t_sum, s_sum, kl))
            t_inv, s_inv = 1.0 / t_sum, 1.0 / s_sum
            stat_ref[0, 0, 0:1, :] = t_inv
            stat_ref[0, 0, 1:2, :] = s_inv
            stat_ref[0, 0, 2:3, :] = kl * t_inv * (1.0 / LOG2E) - jnp.log(t_sum) + jnp.log(s_sum)
            stat_ref[0, 0, 3:8, :] = jnp.zeros((5, QB), F32)
            tmix_ref[...] = (t_mix * t_inv).T.astype(BF16)
            smix_ref[0] = s_mix * s_inv

    even, odd = (ts0, ss0, mx0), (ts1, ss1, mx1)
    pl.when(n == 0)(lambda: work(*even, *odd, True, False))
    pl.when((n > 0) & (n < STEPS) & (n % 2 == 0))(lambda: work(*even, *odd, True, True))
    pl.when((n > 0) & (n < STEPS) & (n % 2 == 1))(lambda: work(*odd, *even, True, True))
    pl.when(n == STEPS)(lambda: work(*even, *odd, False, True))


def attend(tq, tk, tvt, sq, sk, svt):
    now = lambda n: jnp.minimum(n, STEPS - 1)
    last = lambda n: jnp.maximum(n - 1, 0)
    block = lambda n: n // HEADS
    head = lambda n: n % HEADS
    return pl.pallas_call(
        attend_kernel,
        grid=(STEPS + 1,),
        in_specs=[
            pl.BlockSpec((QB, HEAD_T), lambda n: (block(now(n)), head(now(n)))),
            pl.BlockSpec((SEQ, HEAD_T), lambda n: (slot_of(block(now(n))), head(now(n)))),
            pl.BlockSpec((HEAD_T, SEQ), lambda n: (head(last(n)), slot_of(block(last(n))))),
            pl.BlockSpec((QB, D_S), lambda n: (first_block() + block(now(n)), 0)),
            pl.BlockSpec((SEQ, D_S), lambda n: (slot_of(block(now(n))), 0)),
            pl.BlockSpec((HEAD_S, SEQ), lambda n: (head(last(n)), slot_of(block(last(n))))),
        ],
        out_specs=[
            pl.BlockSpec((1, SEQ, QB), lambda n: (block(last(n)), 0, head(last(n)))),
            pl.BlockSpec((1, SEQ, QB), lambda n: (block(last(n)), 0, head(last(n)))),
            pl.BlockSpec((QB, HEAD_T), lambda n: (block(last(n)), head(last(n)))),
            pl.BlockSpec((1, HEAD_S, QB), lambda n: (block(last(n)), head(last(n)), 0)),
            pl.BlockSpec((1, 1, 8, QB), lambda n: (block(last(n)), head(last(n)), 0, 0)),
        ],
        out_shape=[
            jax.ShapeDtypeStruct((3, SEQ, HEADS * QB), BF16),
            jax.ShapeDtypeStruct((3, SEQ, HEADS * QB), BF16),
            jax.ShapeDtypeStruct((OWN, D_T), BF16),
            jax.ShapeDtypeStruct((3, D_S, QB), F32),
            jax.ShapeDtypeStruct((3, HEADS, 8, QB), F32),
        ],
        scratch_shapes=[pltpu.VMEM((SEQ, QB), F32)] * 4 + [pltpu.VMEM((2, 8, QB), F32)] * 2,
        compiler_params=params(),
        name="attend",
    )(tq, tk, tvt, sq, sk, svt)


FC = 1024


def teacher_kernel(mix_ref, hid_ref, emb_ref, att_ref, up_ref, down_ref, out_ref, bias_ref, gain_ref, shift_ref, target_ref, norm, low, acc):
    c = pl.program_id(0)

    @pl.when(c == 0)
    def _():
        summed = hid_ref[...] + dot(mix_ref[...], att_ref[...]) + line(bias_ref, 32, 8)
        one = layer_norm(summed, line(gain_ref, 0, 8), line(shift_ref, 0, 8))
        norm[...] = one
        low[...] = one.astype(BF16)

    rows = FC // 128
    up_bias = bias_ref[pl.ds(pl.multiple_of(40 + rows * c, 8), rows), :]
    act = gelu(dot(low[...], up_ref[...]) + line(up_bias, 0, rows)).astype(BF16)
    part = dot(act, down_ref[...])

    @pl.when(c == 0)
    def _():
        acc[...] = part

    @pl.when(c > 0)
    def _():
        acc[...] += part

    @pl.when(c == pl.num_programs(0) - 1)
    def _():
        summed = norm[...] + acc[...] + line(bias_ref, 72, 8)
        two = layer_norm(summed, line(gain_ref, 8, 8), line(shift_ref, 8, 8))
        last = emb_ref[...].astype(F32) + dot(two.astype(BF16), out_ref[...]) + line(bias_ref, 80, 4)
        target_ref[...] = layer_norm(last, line(gain_ref, 16, 4), line(shift_ref, 16, 4))


def teacher(mix, hid, emb, att, up, down, out, bias, gain, shift):
    return pl.pallas_call(
        teacher_kernel,
        grid=(FF_T // FC,),
        in_specs=[
            whole(OWN, D_T),
            whole(OWN, D_T),
            whole(OWN, D_E),
            whole(D_T, D_T),
            pl.BlockSpec((D_T, FC), lambda c: (0, c)),
            pl.BlockSpec((FC, D_T), lambda c: (c, 0)),
            whole(D_T, D_E),
            whole(84, 128),
            whole(20, 128),
            whole(20, 128),
        ],
        out_specs=whole(OWN, D_E),
        out_shape=jax.ShapeDtypeStruct((OWN, D_E), F32),
        scratch_shapes=[pltpu.VMEM((OWN, D_T), F32), pltpu.VMEM((OWN, D_T), BF16), pltpu.VMEM((OWN, D_T), F32)],
        compiler_params=params(),
        name="teacher",
    )(mix, hid, emb, att, up, down, out, bias, gain, shift)


def student_kernel(emb_ref, smix_ref, target_ref, weight_ref, win_ref, watt_ref, wup_ref, wdown_ref, wout_ref, vec_ref,
                   grad_ref, vgrad_ref, dsum_ref, dmix_ref, part_ref, states, inners, outers):

    def put(r, value):
        for i in range(value.shape[1] // 128):
            vgrad_ref[r + i : r + i + 1, :] = value[:, i * 128 : i * 128 + 128]

    total = lambda v: jnp.sum(v.astype(F32), 0, keepdims=True)
    emb = emb_ref[...]
    source = emb.astype(F32)
    first = dot(emb, win_ref[...]) + line(vec_ref, V_IN)
    mixed = jnp.concatenate([smix_ref[j].T for j in range(3)], 0).astype(BF16)
    branch = dot(mixed, watt_ref[...]) + line(vec_ref, V_ATT)
    state = line(vec_ref, V_AGAIN) * (first + branch) + line(vec_ref, V_ASHIFT)
    for i in range(FFN_COUNT):
        states[i] = state
        inner = dot(state.astype(BF16), wup_ref[i]) + line(vec_ref, V_UP + 4 * i, 4)
        inners[i] = inner
        act = gelu(inner).astype(BF16)
        pre = state + dot(act, wdown_ref[i]) + line(vec_ref, V_DOWN + i)
        outers[i] = pre
        state = line(vec_ref, V_FGAIN + i) * pre + line(vec_ref, V_FSHIFT + i)
    state_low = state.astype(BF16)
    summed = source + dot(state_low, wout_ref[...]) + line(vec_ref, V_OUT, 4)
    diff = line(vec_ref, V_OGAIN, 4) * summed + line(vec_ref, V_OSHIFT, 4) - target_ref[...]
    weight = jnp.concatenate([jnp.broadcast_to(weight_ref[j], (8, QB)).T[:, 0:1] for j in range(3)], 0)
    loss = jnp.sum(weight * jnp.sum(diff * diff, 1, keepdims=True)) * (1.0 / D_E)
    count = jnp.sum(weight)
    d_result = (weight * (2.0 / D_E)) * diff
    put(V_OGAIN, total(d_result * summed))
    put(V_OSHIFT, total(d_result))
    d_output = (d_result * line(vec_ref, V_OGAIN, 4)).astype(BF16)
    out_g = dot_tn(state_low, d_output)
    for n in range(4):
        grad_ref[pl.ds(4224 + n, 128, stride=4), :] = out_g[:, n * 128 : n * 128 + 128]
    put(V_OUT, total(d_output))
    d_state = dot_nt(d_output, wout_ref[...])
    for i in reversed(range(FFN_COUNT)):
        inner = inners[i]
        put(V_FGAIN + i, total(d_state * outers[i]))
        put(V_FSHIFT + i, total(d_state))
        d_sum = d_state * line(vec_ref, V_FGAIN + i)
        d_outer = d_sum.astype(BF16)
        half = 0.5 * (1.0 + lax.erf(inner * 0.7071067811865476))
        act = (inner * half).astype(BF16)
        slope = half + inner * jnp.exp(-0.5 * inner * inner) * 0.3989422804014327
        grad_ref[2176 + 512 * i : 2176 + 512 * (i + 1), :] = dot_tn(act, d_outer)
        d_inner = (dot_nt(d_outer, wdown_ref[i]) * slope).astype(BF16)
        up_g = dot_tn(states[i].astype(BF16), d_inner)
        for n in range(4):
            grad_ref[pl.ds(128 + 512 * i + n, 128, stride=4), :] = up_g[:, n * 128 : n * 128 + 128]
        put(V_UP + 4 * i, total(d_inner))
        put(V_DOWN + i, total(d_outer))
        d_state = d_sum + dot_nt(d_inner, wup_ref[i])
    put(V_AGAIN, total(d_state * (first + branch)))
    put(V_ASHIFT, total(d_state))
    d_sum = d_state * line(vec_ref, V_AGAIN)
    d_branch = d_sum.astype(BF16)
    grad_ref[0:128, :] = dot_tn(mixed, d_branch)
    put(V_ATT, total(d_branch))
    dsum_ref[...] = d_sum
    dmix_ref[...] = dot_nt(d_branch, watt_ref[...]).astype(BF16)
    for r in (0, 1, 2, 3, 47):
        vgrad_ref[r : r + 1, :] = jnp.zeros((1, 128), F32)
    row = lax.broadcasted_iota(jnp.int32, (8, 128), 0)
    lane = lax.broadcasted_iota(jnp.int32, (8, 128), 1)
    part_ref[...] = jnp.where((row == 0) & (lane == 0), loss, 0.0) + jnp.where((row == 0) & (lane == 1), count, 0.0)


def student(emb, smix, target, weight, win, watt, wup, wdown, wout, vecs):
    return pl.pallas_call(
        student_kernel,
        grid=(1,),
        in_specs=[
            whole(OWN, D_E),
            whole(3, D_S, QB),
            whole(OWN, D_E),
            whole(3, 1, QB),
            whole(D_E, D_S),
            whole(D_S, D_S),
            whole(FFN_COUNT, D_S, FF_S),
            whole(FFN_COUNT, FF_S, D_S),
            whole(D_S, D_E),
            whole(48, 128),
        ],
        out_specs=[whole(4736, 128), whole(48, 128), whole(OWN, D_S), whole(OWN, D_S), whole(8, 128)],
        out_shape=[
            jax.ShapeDtypeStruct((4736, 128), F32),
            jax.ShapeDtypeStruct((48, 128), F32),
            jax.ShapeDtypeStruct((OWN, D_S), F32),
            jax.ShapeDtypeStruct((OWN, D_S), BF16),
            jax.ShapeDtypeStruct((8, 128), F32),
        ],
        scratch_shapes=[
            pltpu.VMEM((FFN_COUNT, OWN, D_S), F32),
            pltpu.VMEM((FFN_COUNT, OWN, FF_S), F32),
            pltpu.VMEM((FFN_COUNT, OWN, D_S), F32),
        ],
        compiler_params=params(),
        name="student",
    )(emb, smix, target, weight, win, watt, wup, wdown, wout, vecs)


KB = 512


def back_kernel(et_ref, es_ref, stat_ref, smix_ref, dmix_ref, weight_ref, sq_ref, sv_ref, skt_ref, dsum_ref, emb_ref, first_ref,
                wqkv_ref, vgrad_ref, part_in, late_ref, block_ref, part_ref,
                dkv, dqt, ds, dq, dfirst, dmt, dmz, sqd, rows, flat, vecs, kls, sem):
    j, kb = pl.program_id(0), pl.program_id(1)
    s_scale = HEAD_S**-0.5
    late = pltpu.make_async_copy(late_ref, flat.at[896:5632], sem)

    @pl.when((j == 0) & (kb == 0))
    def _():
        late.start()
        dkv[...] = jnp.zeros_like(dkv)
        kls[...] = jnp.zeros_like(kls)

    @pl.when(kb == 0)
    def _():
        quarter = weight_ref[0] * (1.0 / HEADS)
        wide = dmix_ref[...].astype(F32)
        tall = wide.T
        place = lax.broadcasted_iota(jnp.int32, (D_S, 1), 0) // HEAD_S
        for h in range(HEADS):
            own = slice(h * HEAD_S, h * HEAD_S + HEAD_S)
            mine = slice(h * QB, h * QB + QB)
            t_inv, s_inv = stat_ref[0, h, 0:1, :], stat_ref[0, h, 1:2, :]
            kls[0:1, :] += quarter * stat_ref[0, h, 2:3, :]
            row_dot = jnp.sum(tall[own] * smix_ref[0, own, :], 0, keepdims=True)
            rows[h, 0:1, :] = row_dot - quarter
            rows[h, 1:2, :] = s_inv
            rows[h, 2:3, :] = quarter * t_inv
            dmt[h] = jnp.where(place == h, tall, 0.0).astype(BF16)
            dmz[mine, :] = head_lanes(wide * stat_ref[0, h].T[:, 1:2], h).astype(BF16)
            sqd[mine, :] = head_lanes(sq_ref[...], h)
        dqt[...] = jnp.zeros_like(dqt)

    here = pl.ds(pl.multiple_of(slot_of(j) * SEQ + kb * KB, KB), KB)
    dkv[here, D_S:] += dot(es_ref[0], dmz[...])
    for h in range(HEADS):
        lanes = slice(h * QB, h * QB + QB)
        for c in range(KB // 256):
            part = slice(c * 256, c * 256 + 256)
            d_probs = dot(sv_ref[part, :], dmt[h])
            s_exp, t_exp = es_ref[0, part, lanes].astype(F32), et_ref[0, part, lanes].astype(F32)
            d_scores = (d_probs - rows[h, 0:1, :]) * rows[h, 1:2, :] * s_exp - t_exp * rows[h, 2:3, :]
            ds[part, lanes] = d_scores.astype(BF16)
        own = slice(h * HEAD_S, h * HEAD_S + HEAD_S)
        dqt[own, :] += dot(skt_ref[own, :], ds[:, lanes])
    dkv[here, :D_S] += dot(ds[...], sqd[...])

    @pl.when(kb == pl.num_programs(1) - 1)
    def _():
        dq[pl.ds(pl.multiple_of(j * QB, QB), QB), :] = (dqt[...] * s_scale).T

    @pl.when((j == 2) & (kb == pl.num_programs(1) - 1))
    def _():
        qkv_w = wqkv_ref[...]
        dq_low = dq[...].astype(BF16)
        own = pl.ds(pl.multiple_of(first_block() * QB, QB), OWN)
        q_grad = dot_tn(first_ref[own, :], dq_low)
        own_part = dsum_ref[...] + dot_nt(dq_low, qkv_w[:, :D_S])
        kv_grad = jnp.zeros((D_S, 2 * D_S), F32)
        kv_bias = jnp.zeros((1, 2 * D_S), F32)
        for c in range(8):
            part = pl.ds(c * 512, 512)
            wide = dkv[part, :]
            low = jnp.concatenate([(wide[:, :D_S] * s_scale).astype(BF16), wide[:, D_S:].astype(BF16)], 1)
            kv_grad += dot_tn(first_ref[part, :], low)
            kv_bias += jnp.sum(low.astype(F32), 0, keepdims=True)
            dfirst[part, :] = dot_nt(low, qkv_w[:, D_S:])
        dfirst[own, :] += own_part
        in_grad = jnp.zeros((D_S, D_E), F32)
        in_bias = jnp.zeros((1, D_S), F32)
        for c in range(8):
            part = pl.ds(c * 512, 512)
            low = dfirst[part, :].astype(BF16)
            in_grad += dot_tn(low, emb_ref[part, :])
            in_bias += jnp.sum(low.astype(F32), 0, keepdims=True)
        flat[0:512, :] = in_grad.T
        flat[pl.ds(512, 128, stride=3), :] = q_grad
        flat[pl.ds(513, 128, stride=3), :] = kv_grad[:, :D_S]
        flat[pl.ds(514, 128, stride=3), :] = kv_grad[:, D_S:]
        vecs[...] = vgrad_ref[...]
        vecs[0:1, :] = in_bias
        vecs[1:2, :] = jnp.sum(dq_low.astype(F32), 0, keepdims=True)
        vecs[2:3, :] = kv_bias[:, :D_S]
        vecs[3:4, :] = kv_bias[:, D_S:]
        late.wait()
        lane = lax.broadcasted_iota(jnp.int32, (1, 128), 1)
        rest = jnp.zeros((BLOCK - SHARD - 1, 128), F32)
        for pair in range(64):
            both = flat[88 * pair : 88 * pair + 88, :]
            for i in range(2):
                owner = 2 * pair + i
                row, shift = divmod(47 * owner, 128)
                entries = vecs[row : row + 1, :]
                if shift + 47 > 128:
                    entries = jnp.where(lane >= shift, entries, vecs[row + 1 : row + 2, :])
                if shift:
                    entries = pltpu.roll(entries, 128 - shift, 1)
                entries = jnp.where(lane < 47, entries, 0.0)
                mine = both[SHARD * i : SHARD * (i + 1)]
                block_ref[owner // 32, owner // 16 % 2, owner % 16] = jnp.concatenate([mine, entries, rest], 0).astype(BF16)
        kl = jnp.sum(kls[0:1, :], keepdims=True)
        corner = (lax.broadcasted_iota(jnp.int32, (8, 128), 0) == 0) & (lax.broadcasted_iota(jnp.int32, (8, 128), 1) == 0)
        part_ref[...] = part_in[...] + jnp.where(corner, kl, 0.0)


def back(et, es, stat, smix, dmix, weight, sq, sv, skt, dsum, emb, first, wqkv, vgrad, part, late):
    count = SEQ // KB
    place = lambda j, k: slot_of(j) * count + k
    return pl.pallas_call(
        back_kernel,
        grid=(3, count),
        in_specs=[
            pl.BlockSpec((1, KB, HEADS * QB), lambda j, k: (j, k, 0)),
            pl.BlockSpec((1, KB, HEADS * QB), lambda j, k: (j, k, 0)),
            pl.BlockSpec((1, HEADS, 8, QB), lambda j, k: (j, 0, 0, 0)),
            pl.BlockSpec((1, D_S, QB), lambda j, k: (j, 0, 0)),
            pl.BlockSpec((QB, D_S), lambda j, k: (j, 0)),
            pl.BlockSpec((1, 1, QB), lambda j, k: (j, 0, 0)),
            pl.BlockSpec((QB, D_S), lambda j, k: (first_block() + j, 0)),
            pl.BlockSpec((KB, D_S), lambda j, k: (place(j, k), 0)),
            pl.BlockSpec((D_S, KB), lambda j, k: (0, place(j, k))),
            whole(OWN, D_S),
            whole(SLOTS, D_E),
            whole(SLOTS, D_S),
            whole(D_S, 3 * D_S),
            whole(48, 128),
            whole(8, 128),
            pl.BlockSpec(memory_space=pl.ANY),
        ],
        out_specs=[whole(4, 2, 16, BLOCK, 128), whole(8, 128)],
        out_shape=[
            jax.ShapeDtypeStruct((4, 2, 16, BLOCK, 128), BF16),
            jax.ShapeDtypeStruct((8, 128), F32),
        ],
        scratch_shapes=[
            pltpu.VMEM((SLOTS, 2 * D_S), F32),
            pltpu.VMEM((D_S, QB), F32),
            pltpu.VMEM((KB, HEADS * QB), BF16),
            pltpu.VMEM((OWN, D_S), F32),
            pltpu.VMEM((SLOTS, D_S), F32),
            pltpu.VMEM((HEADS, D_S, QB), BF16),
            pltpu.VMEM((HEADS * QB, D_S), BF16),
            pltpu.VMEM((HEADS * QB, D_S), BF16),
            pltpu.VMEM((HEADS, 8, QB), F32),
            pltpu.VMEM((5632, 128), F32),
            pltpu.VMEM((48, 128), F32),
            pltpu.VMEM((8, QB), F32),
            pltpu.SemaphoreType.DMA,
        ],
        compiler_params=params(),
        name="back",
    )(et, es, stat, smix, dmix, weight, sq, sv, skt, dsum, emb, first, wqkv, vgrad, part, late)


def update_kernel(g_ref, part_ref, master_mat, master_vec, first_mat, first_vec, second_mat, second_vec,
                  new_ref, newf_ref, news_ref, scal_ref, packs, half_in, mine, block_out, blocks_in, tile_out, tiles_f, tiles_d,
                  half_sems, block_send, block_recv, f_send, f_recv, d_send, d_recv):
    dp, fs = lax.axis_index("dp"), lax.axis_index("fsdp")
    x, core = dp // 2, dp % 2
    sibling = (2 * x + 1 - core, fs)
    barrier = pltpu.get_barrier_semaphore()

    def chip(k):
        return (2 * ((x + k // 16) % 4) + core, (fs + k) % 16)

    def greet(k, _):
        pl.semaphore_signal(barrier, inc=1, device_id=chip(k), device_id_type=MESH)
        return 0

    lax.fori_loop(1, 64, greet, 0)
    for k in range(4):
        other = (2 * ((x + k) % 4) + 1 - core, fs)
        pl.semaphore_signal(barrier, inc=1, device_id=other, device_id_type=MESH)

    packs[...] = jnp.zeros_like(packs)
    for i, (mat, vec) in enumerate([(master_mat, master_vec), (first_mat, first_vec), (second_mat, second_vec)]):
        packs[i, 0:SHARD, :] = mat[...]
        packs[i, SHARD : SHARD + 1, 0:47] = vec[...]
    pl.semaphore_wait(barrier, 67)
    swap = pltpu.make_async_remote_copy(
        g_ref.at[:, 1 - core], half_in, half_sems.at[0], half_sems.at[1], device_id=sibling, device_id_type=MESH
    )
    swap.start()
    swap.wait()

    def join(i, _):
        summed = g_ref[i // 16, core, i % 16].astype(F32) + half_in[i // 16, i % 16].astype(F32)
        block_out[i] = summed.astype(BF16)
        return 0

    lax.fori_loop(0, 64, join, 0)
    mine[...] = g_ref[x, core, fs].astype(F32) + half_in[x, fs].astype(F32)

    def block_copy(k):
        xk, fk = (x + k // 16) % 4, (fs + k) % 16
        return pltpu.make_async_remote_copy(
            block_out.at[xk * 16 + fk], blocks_in.at[k], block_send.at[k], block_recv.at[k],
            device_id=(2 * xk + core, fk), device_id_type=MESH,
        )

    def start(k, _):
        block_copy(k).start()
        return 0

    lax.fori_loop(1, 64, start, 0)

    def gather(k, _):
        block_copy(k).wait()
        mine[...] += blocks_in[k].astype(F32)
        return 0

    lax.fori_loop(1, 64, gather, 0)

    row = lax.broadcasted_iota(jnp.int32, (BLOCK, 128), 0)
    lane8 = lax.broadcasted_iota(jnp.int32, (8, 128), 1)
    row8 = lax.broadcasted_iota(jnp.int32, (8, 128), 0)
    place = (dp * 16 + fs) * SHARD + row
    is_matrix = row < SHARD
    bounds = [0]
    for rows in MAT_ROWS:
        bounds.append(bounds[-1] + rows)
    members = [is_matrix & (place >= bounds[i]) & (place < bounds[i + 1]) for i in range(6)]

    def everyone(tile, turn):
        tile_out[turn, 0] = tile
        tiles_f[turn, fs] = tile

        def f_copy(k):
            return pltpu.make_async_remote_copy(
                tile_out.at[turn, 0], tiles_f.at[turn, fs], f_send.at[turn, k], f_recv.at[turn, k],
                device_id=(dp, (fs + k) % 16), device_id_type=MESH,
            )

        def d_copy(k):
            return pltpu.make_async_remote_copy(
                tile_out.at[turn, 1], tiles_d.at[turn, dp], d_send.at[turn, k], d_recv.at[turn, k],
                device_id=((dp + k) % 8, fs), device_id_type=MESH,
            )

        for k in range(1, 16):
            f_copy(k).start()
        for k in range(1, 16):
            f_copy(k).wait()
        total = tiles_f[turn, 0]
        for k in range(1, 16):
            total = total + tiles_f[turn, k]
        tile_out[turn, 1] = total
        tiles_d[turn, dp] = total
        for k in range(1, 8):
            d_copy(k).start()
        for k in range(1, 8):
            d_copy(k).wait()
        total = tiles_d[turn, 0]
        for k in range(1, 8):
            total = total + tiles_d[turn, k]
        return total

    def entry(tile, i):
        return jnp.sum(jnp.where((row8 == 0) & (lane8 == i), tile, 0.0), keepdims=True)

    def tile_of(values):
        tile = jnp.zeros((8, 128), F32)
        for i, value in values:
            tile += jnp.where((row8 == 0) & (lane8 == i), value, 0.0)
        return tile

    grad = mine[...]
    master = packs[0]
    squares = master * master
    tile = part_ref[...] + tile_of(
        [(2, jnp.sum(grad * grad, keepdims=True))]
        + [(3 + i, jnp.sum(jnp.where(members[i], squares, 0.0), keepdims=True)) for i in range(6)]
    )
    tile = everyone(tile, 0)
    loss, count = entry(tile, 0), entry(tile, 1)
    inverse = 1.0 / count
    norm = jnp.sqrt(entry(tile, 2)) * inverse
    factor = CLIP_NORM / jnp.maximum(norm, CLIP_NORM)
    grad = grad * inverse * factor
    first = BETA_ONE * packs[1] + (1.0 - BETA_ONE) * grad
    second = BETA_TWO * packs[2] + (1.0 - BETA_TWO) * grad * grad
    newf_ref[...] = first
    news_ref[...] = second
    ratio = first / (1.0 - BETA_ONE**STEP) / (jnp.sqrt(second / (1.0 - BETA_TWO**STEP)) + ADAM_EPS)
    ratio = ratio + jnp.where(is_matrix, WEIGHT_DECAY * master, 0.0)
    squares = ratio * ratio
    steps = everyone(tile_of([(3 + i, jnp.sum(jnp.where(members[i], squares, 0.0), keepdims=True)) for i in range(6)]), 1)
    trust = jnp.ones((BLOCK, 128), F32)
    for i in range(6):
        trust = jnp.where(members[i], jnp.sqrt(entry(tile, 3 + i)) / jnp.sqrt(entry(steps, 3 + i)), trust)
    new_ref[...] = master - LEARN_RATE * (trust * ratio)
    scal_ref[...] = tile_of([(0, loss), (1, count), (2, norm)])


def update(grads, part, *state):
    vmem = pl.BlockSpec(memory_space=pltpu.VMEM)
    block = jax.ShapeDtypeStruct((BLOCK, 128), F32)
    dma = pltpu.SemaphoreType.DMA
    return pl.pallas_call(
        update_kernel,
        in_specs=[vmem] * 8,
        out_specs=[vmem] * 4,
        out_shape=[block, block, block, jax.ShapeDtypeStruct((8, 128), F32)],
        scratch_shapes=[
            pltpu.VMEM((3, BLOCK, 128), F32),
            pltpu.VMEM((4, 16, BLOCK, 128), BF16),
            pltpu.VMEM((BLOCK, 128), F32),
            pltpu.VMEM((64, BLOCK, 128), BF16),
            pltpu.VMEM((64, BLOCK, 128), BF16),
            pltpu.VMEM((2, 2, 8, 128), F32),
            pltpu.VMEM((2, 16, 8, 128), F32),
            pltpu.VMEM((2, 8, 8, 128), F32),
            dma((2,)),
            dma((64,)),
            dma((64,)),
            dma((2, 16)),
            dma((2, 16)),
            dma((2, 8)),
            dma((2, 8)),
        ],
        compiler_params=params(collective_id=1, has_side_effects=True),
        name="update",
    )(grads, part, *state)


def finish_kernel(new_ref, newf_ref, news_ref, scal_ref, loss, count, norm, m0, m1, m2, v0, v1, v2):
    for source, mat, vec in ((new_ref, m0, v0), (newf_ref, m1, v1), (news_ref, m2, v2)):
        mat[...] = source[0:SHARD, :]
        vec[...] = source[SHARD : SHARD + 1, 0:47]
    for i, out in enumerate((loss, count, norm)):
        out[...] = scal_ref[0:1, i : i + 1]


def finish(*made):
    vmem = pl.BlockSpec(memory_space=pltpu.VMEM)
    shape = lambda *dims: jax.ShapeDtypeStruct(dims, F32)
    return pl.pallas_call(
        finish_kernel,
        in_specs=[vmem] * 4,
        out_specs=[vmem] * 9,
        out_shape=[shape(1, 1)] * 3 + [shape(SHARD, 128)] * 3 + [shape(1, 47)] * 3,
        name="finish",
    )(*made)


def per_device(
    token_ids,
    splits,
    valid_mask,
    embed_table,
    embed_proj,
    embed_bias,
    type_table,
    teach_in,
    teach_qkv,
    teach_att,
    teach_up,
    teach_down,
    teach_out,
    teach_bias,
    teach_gain,
    teach_shift,
    matrices,
    vectors,
    matrix_first,
    matrix_second,
    vector_first,
    vector_second,
):
    mat = lambda v: v.reshape(SHARD, 128)
    vec = lambda v: v.reshape(1, 47)
    rows_128 = lambda v: v.reshape(-1, 128)
    bias = rows_128(teach_bias)
    spread_rows, weights, packed = spread(embed_table[token_ids], valid_mask, mat(matrices), vec(vectors))
    (
        emb, t_keys, t_values, first, s_q, s_k, s_v, s_kt, s_vt, own_emb, hidden, t_queries,
        in_w, qkv_w, att_w, up_w, down_w, out_w, vecs,
    ) = project(
        splits, spread_rows.reshape(SLOTS, 128), packed, embed_proj, rows_128(embed_bias), type_table, teach_in, teach_qkv, bias
    )
    et, es, t_mixed, s_mixed, stat = attend(t_queries, t_keys, t_values, s_q, s_k, s_vt)
    target = teacher(
        t_mixed, hidden, own_emb, teach_att, teach_up, teach_down, teach_out, bias, rows_128(teach_gain), rows_128(teach_shift)
    )
    late, vgrads, d_sum, d_mixed, part = student(
        own_emb, s_mixed, target, weights, in_w, att_w, up_w, down_w, out_w, vecs
    )
    blocks, part = back(
        et, es, stat, s_mixed, d_mixed, weights, s_q, s_v, s_kt, d_sum, emb, first, qkv_w, vgrads, part, late
    )
    made = update(
        blocks, part, mat(matrices), vec(vectors), mat(matrix_first), vec(vector_first), mat(matrix_second), vec(vector_second)
    )
    loss, count, norm, m0, m1, m2, v0, v1, v2 = finish(*made)
    flat = lambda v: v.reshape(-1)
    scalar = lambda v: v.reshape(())
    return (
        scalar(loss), scalar(count), scalar(norm), flat(m0), flat(m1), flat(m2), flat(v0), flat(v1), flat(v2),
    )


def solution(mesh):
    both = P(("dp", "fsdp"))
    return jax.shard_map(
        per_device,
        mesh=mesh,
        in_specs=(P("dp", "fsdp"), P("dp"), P("dp", "fsdp")) + (P(),) * 13 + (both,) * 6,
        out_specs=(P(), P(), P(), both, both, both, both, both, both),
        check_vma=False,
    )
```

```python
import functools
import math

import jax
import jax.numpy as jnp
from jax import lax
from jax.experimental import pallas as pl
from jax.experimental.pallas import tpu as pltpu
from jax.sharding import PartitionSpec as P

D_E = 512
D_T = 1024
FF_T = 4096
D_S = 128
FF_S = 512
HEADS = 4
FFN_COUNT = 4
STEP = 5
HEAD_T = 256
HEAD_S = 32
SEQ = 2048
QB = 256
OWN = 3 * QB
SLOTS = 2 * SEQ

CLIP_NORM = 0.05
BETA_ONE = 0.9
BETA_TWO = 0.999
LEARN_RATE = 0.3
WEIGHT_DECAY = 0.01
ADAM_EPS = 1e-06

F32 = jnp.float32
BF16 = jnp.bfloat16
LOG2E = 1.4426950408889634
MESH = pl.DeviceIdType.MESH
BIG_VMEM = 60 * 2**20

MAT_ROWS = (512, 384, 128, 2048, 2048, 512)
SHARD = 44
BLOCK = 48
(V_IN, V_QKV, V_ATT, V_AGAIN, V_ASHIFT, V_UP, V_DOWN, V_FGAIN, V_FSHIFT, V_OUT, V_OGAIN, V_OSHIFT) = (
    0, 1, 4, 5, 6, 7, 23, 27, 31, 35, 39, 43)


def dot(left, right):
    return jnp.dot(left, right, preferred_element_type=F32)


def dot_nt(left, right):
    return lax.dot_general(left, right, (((1,), (1,)), ((), ())), preferred_element_type=F32)


def dot_tn(left, right):
    return lax.dot_general(left, right, (((0,), (0,)), ((), ())), preferred_element_type=F32)


def layer_norm(values, gain, shift):
    center = values - jnp.mean(values, -1, keepdims=True)
    spread = jnp.mean(center * center, -1, keepdims=True)
    return center * lax.rsqrt(spread + 1e-05) * gain + shift


def gelu(values):
    return 0.5 * values * (1.0 + lax.erf(values * 0.7071067811865476))


def params(**more):
    return pltpu.CompilerParams(vmem_limit_bytes=BIG_VMEM, **more)


def whole(*shape):
    return pl.BlockSpec(shape, lambda *_: (0,) * len(shape))


def line(ref, row, count=1):
    if count == 1:
        return ref[row : row + 1, :]
    return jnp.concatenate([ref[row + i : row + i + 1, :] for i in range(count)], 1)


def fold(values, op=jnp.sum):
    return op(values.reshape(values.shape[0] // 8, 8, values.shape[1]), 0)


def spots():
    dp, fs = lax.axis_index("dp"), lax.axis_index("fsdp")
    return dp // 2, dp % 2, fs // 4, fs % 4


def place_in_group():
    _, core, _, y = spots()
    return 2 * y + core


def first_block():
    return (3 * place_in_group()) % 8


def slot_of(j):
    return (first_block() + j) // 8


def has_two():
    i = place_in_group()
    return (i == 2) | (i == 5)


PT = 512
TILES = SEQ // PT


def front_kernel(e_ref, mask_ref, splits_ref, mats_ref, vecs_ref, proj_hbm, win_hbm, wqkv_hbm, ebias_ref, types_ref, bias_ref,
                 emb_hbm, k_hbm, vt_hbm, own_ref, hid_ref, tq_ref, weight_ref, params_ref,
                 note, notes, wide, block, e_all, proj_ref, win_ref, wqkv_ref, emb_t, k_t, vt_t,
                 load, e_send, e_recv, n_send, n_recv, a_send, a_recv, b_send, b_recv, c_send, c_recv,
                 out, s_send, s_recv, own_sem):
    dp, me = lax.axis_index("dp"), lax.axis_index("fsdp")
    x, core, z, y = spots()
    i = 2 * y + core
    sibling = (2 * x + 1 - core, me)
    source_dp = 2 * x + z // 2
    is_source = z // 2 == core
    loads = [
        pltpu.make_async_copy(hbm, ref, load.at[n])
        for n, (hbm, ref) in enumerate([(proj_hbm, proj_ref), (win_hbm, win_ref), (wqkv_hbm, wqkv_ref)])
    ]
    barrier = pltpu.get_barrier_semaphore()

    def signal(device):
        pl.semaphore_signal(barrier, inc=1, device_id=device, device_id_type=MESH)

    def greet_source(f, _):
        @pl.when(jnp.logical_not(is_source & (f == me)))
        def _():
            signal((source_dp, f))

        return 0

    def greet_plane(k, _):
        signal((dp, (me + k) % 16))
        return 0

    lax.fori_loop(0, 16, greet_source, 0)
    lax.fori_loop(1, 16, greet_plane, 0)
    for k in range(1, 4):
        signal((2 * ((x + k) % 4) + core, me))
    signal(sibling)
    for copy in loads:
        copy.start()

    lane = lax.broadcasted_iota(jnp.int32, (1, 128), 1)
    note[0:6, :] = mask_ref[...]
    line_of_splits = jnp.zeros((1, 128), jnp.int32)
    for r in range(6):
        line_of_splits = jnp.where(lane == r, splits_ref[r], line_of_splits)
    note[6:7, :] = line_of_splits
    note[7:8, :] = jnp.zeros((1, 128), jnp.int32)
    wide[...] = jnp.zeros((BLOCK, 128), F32)
    wide[0:SHARD, :] = mats_ref[...]
    wide[SHARD : SHARD + 1, 0:47] = vecs_ref[...]
    block[...] = wide[...].astype(BF16)
    params_ref[dp * 16 + me] = block[...]
    main = (3 * i + 1) // 8

    @pl.when(is_source)
    def _():
        e_all[pl.ds(pl.multiple_of(me * 128, 128), 128), :] = e_ref[3 * (z % 2) + main]
        notes[me] = note[...]

    pl.semaphore_wait(barrier, jnp.where(is_source, 15, 16) + 15 + 3 + 1)

    def e_copies(d):
        zd, yd, cd = 2 * core + d // 8, d // 2 % 4, d % 2
        row = 3 * (d // 8) + (3 * (2 * yd + cd) + 1) // 8
        where = dict(device_id=(2 * x + cd, 4 * zd + yd), device_id_type=MESH)
        here = pl.ds(pl.multiple_of(me * 128, 128), 128)
        other = jnp.logical_not((zd == z) & (yd == y) & (cd == core))
        return other, (
            pltpu.make_async_remote_copy(e_ref.at[row], e_all.at[here], e_send.at[d], e_recv.at[me], **where),
            pltpu.make_async_remote_copy(note, notes.at[me], n_send.at[d], n_recv.at[me], **where),
        )

    def e_start(d, _):
        other, copies = e_copies(d)

        @pl.when(other)
        def _():
            for copy in copies:
                copy.start()

        return 0

    lax.fori_loop(0, 16, e_start, 0)

    def e_sent(d, _):
        other, copies = e_copies(d)

        @pl.when(other)
        def _():
            for copy in copies:
                copy.wait_send()

        return 0

    def e_arrived(f, _):
        @pl.when(jnp.logical_not(is_source & (f == me)))
        def _():
            where = dict(device_id=(source_dp, f), device_id_type=MESH)
            there = pl.ds(pl.multiple_of(f * 128, 128), 128)
            pltpu.make_async_remote_copy(e_ref.at[0], e_all.at[there], e_send.at[0], e_recv.at[f], **where).wait_recv()
            pltpu.make_async_remote_copy(note, notes.at[f], n_send.at[0], n_recv.at[f], **where).wait_recv()

        return 0

    def a_copy(k):
        return pltpu.make_async_remote_copy(
            block, params_ref.at[dp * 16 + me], a_send.at[k], a_recv.at[k], device_id=(dp, (me + k) % 16), device_id_type=MESH
        )

    def b_copy(k):
        mine = params_ref.at[pl.ds(dp * 16, 16)]
        return pltpu.make_async_remote_copy(
            mine, mine, b_send.at[k], b_recv.at[k], device_id=(2 * ((x + k) % 4) + core, me), device_id_type=MESH
        )

    def c_copy(k):
        mine = params_ref.at[pl.ds((2 * k + core) * 16, 16)]
        return pltpu.make_async_remote_copy(mine, mine, c_send.at[k], c_recv.at[k], device_id=sibling, device_id_type=MESH)

    def a_start(k, _):
        a_copy(k).start()
        return 0

    def a_wait(k, _):
        a_copy(k).wait()
        return 0

    lax.fori_loop(1, 16, a_start, 0)

    gives = ((y == 1) & (core == 1)) | ((y == 2) & (core == 0))
    takes = has_two()
    main_slot = jnp.where(i == 5, 1, 0)
    his_slot = jnp.where(y == 1, 1, 0)

    def out_copies(t):
        b = t % 2
        rows = pl.ds(pl.multiple_of(main_slot * SEQ + t * PT, PT), PT)
        return (
            pltpu.make_async_copy(emb_t.at[b], emb_hbm.at[rows], out.at[0, b]),
            pltpu.make_async_copy(k_t.at[b], k_hbm.at[rows], out.at[1, b]),
            pltpu.make_async_copy(vt_t.at[b], vt_hbm.at[:, rows], out.at[2, b]),
        )

    def give_copies(t):
        b = t % 2
        rows = pl.ds(pl.multiple_of(his_slot * SEQ + t * PT, PT), PT)
        where = dict(device_id=sibling, device_id_type=MESH)
        return (
            pltpu.make_async_remote_copy(emb_t.at[b], emb_hbm.at[rows], s_send.at[0, t], s_recv.at[0, t], **where),
            pltpu.make_async_remote_copy(k_t.at[b], k_hbm.at[rows], s_send.at[1, t], s_recv.at[1, t], **where),
            pltpu.make_async_remote_copy(vt_t.at[b], vt_hbm.at[:, rows], s_send.at[2, t], s_recv.at[2, t], **where),
        )

    def settle(t):
        for copy in out_copies(t):
            copy.wait()

        @pl.when(gives)
        def _():
            for copy in give_copies(t):
                copy.wait_send()

    per = SEQ // PT
    row = lax.broadcasted_iota(jnp.int32, (PT, 1), 0)
    for t in range(TILES):
        b = t % 2
        lax.fori_loop(4 * t + (1 if t else 0), min(4 * t + 5, 16), e_arrived, 0)
        if t == 0:
            loads[0].wait()
            split = jnp.sum(jnp.where(lane == 3 * (z % 2) + main, notes[0, 6:7, :], 0), keepdims=True)
        mid = e_all[t * PT : t * PT + PT, :]
        if t:
            before = e_all[t * PT - 16 : t * PT, :].astype(F32)[15:16]
        else:
            before = jnp.zeros((1, 128), F32)
        if t < TILES - 1:
            after = e_all[t * PT + PT : t * PT + PT + 16, :].astype(F32)[0:1]
        else:
            after = jnp.zeros((1, 128), F32)
        broad = mid.astype(F32)
        left = jnp.where(row == 0, before, pltpu.roll(broad, 1, 0)).astype(BF16)
        right = jnp.where(row == PT - 1, after, pltpu.roll(broad, PT - 1, 0)).astype(BF16)
        trigram = jnp.concatenate([left, mid, right], 1)
        typed = jnp.where(row + t * PT >= split, types_ref[1:2, :], types_ref[0:1, :])
        emb = (dot(trigram, proj_ref[...]) + line(ebias_ref, 0, 4) + typed).astype(BF16)
        if t == 0:
            loads[1].wait()
        hidden = (dot(emb, win_ref[...]) + line(bias_ref, 0, 8)).astype(BF16)
        if t == 0:
            loads[2].wait()
        keys = (dot(hidden, wqkv_ref[:, D_T : 2 * D_T]) + line(bias_ref, 16, 8)).astype(BF16)
        values = (dot(hidden, wqkv_ref[:, 2 * D_T :]) + line(bias_ref, 24, 8)).astype(BF16)
        if t >= 2:
            settle(t - 2)
        emb_t[b] = emb
        k_t[b] = keys
        vt_t[b] = values.T
        for copy in out_copies(t):
            copy.start()

        @pl.when(gives)
        def _(t=t):
            for copy in give_copies(t):
                copy.start()

        if t == 0:
            lax.fori_loop(1, 16, a_wait, 0)
            for k in range(1, 4):
                b_copy(k).start()
        if t == 2:
            for k in range(1, 4):
                b_copy(k).wait()
            for k in range(4):
                c_copy(k).start()
    for t in range(TILES - 2, TILES):
        settle(t)

    @pl.when(takes)
    def _():
        for t in range(TILES):
            give_copies_in = give_copies(t)
            for copy in give_copies_in:
                copy.wait_recv()

    own = pltpu.make_async_copy(emb_hbm.at[pl.ds(pl.multiple_of(first_block() * QB, QB), OWN)], own_ref, own_sem)
    own.start()
    for j in range(3):
        t = first_block() + j
        local = 3 * (z % 2) + (3 * i + j) // 8
        for half in range(2):
            weight_ref[j, :, half * 128 : half * 128 + 128] = notes[2 * (t % 8) + half, pl.ds(local, 1), :].astype(F32)
    own.wait()
    hidden = dot(own_ref[...], win_ref[...]) + line(bias_ref, 0, 8)
    hid_ref[...] = hidden
    queries = (dot(hidden.astype(BF16), wqkv_ref[:, :D_T]) + line(bias_ref, 8, 8)).astype(BF16)
    tq_ref[...] = queries * jnp.asarray(HEAD_T**-0.5, BF16)
    lax.fori_loop(0, 16, e_sent, 0)
    for k in range(4):
        c_copy(k).wait()


def front(e, mask, splits, mats, vecs, proj, win, wqkv, ebias, types, bias):
    vmem = pl.BlockSpec(memory_space=pltpu.VMEM)
    hbm = pl.BlockSpec(memory_space=pl.ANY)
    dma = pltpu.SemaphoreType.DMA
    return pl.pallas_call(
        front_kernel,
        in_specs=[vmem, vmem, pl.BlockSpec(memory_space=pltpu.SMEM), vmem, vmem, hbm, hbm, hbm, vmem, vmem, vmem],
        out_specs=[hbm, hbm, hbm, vmem, vmem, vmem, vmem, vmem],
        out_shape=[
            jax.ShapeDtypeStruct((SLOTS, D_E), BF16),
            jax.ShapeDtypeStruct((SLOTS, D_T), BF16),
            jax.ShapeDtypeStruct((D_T, SLOTS), BF16),
            jax.ShapeDtypeStruct((OWN, D_E), BF16),
            jax.ShapeDtypeStruct((OWN, D_T), F32),
            jax.ShapeDtypeStruct((OWN, D_T), BF16),
            jax.ShapeDtypeStruct((3, 1, QB), F32),
            jax.ShapeDtypeStruct((128, BLOCK, 128), BF16),
        ],
        scratch_shapes=[
            pltpu.VMEM((8, 128), jnp.int32),
            pltpu.VMEM((16, 8, 128), jnp.int32),
            pltpu.VMEM((BLOCK, 128), F32),
            pltpu.VMEM((BLOCK, 128), BF16),
            pltpu.VMEM((SEQ, 128), BF16),
            pltpu.VMEM((3 * 128, D_E), BF16),
            pltpu.VMEM((D_E, D_T), BF16),
            pltpu.VMEM((D_T, 3 * D_T), BF16),
            pltpu.VMEM((2, PT, D_E), BF16),
            pltpu.VMEM((2, PT, D_T), BF16),
            pltpu.VMEM((2, D_T, PT), BF16),
            dma((3,)),
            dma((16,)),
            dma((16,)),
            dma((16,)),
            dma((16,)),
            dma((16,)),
            dma((16,)),
            dma((4,)),
            dma((4,)),
            dma((4,)),
            dma((4,)),
            dma((3, 2)),
            dma((3, TILES)),
            dma((3, TILES)),
            dma,
        ],
        compiler_params=params(collective_id=0, has_side_effects=True),
        name="front",
    )(e, mask, splits, mats, vecs, proj, win, wqkv, ebias, types, bias)


def unpack(packed_ref, flat, win_ref, wqkv_ref, watt_ref, wup_ref, wdown_ref, wout_ref, vec_ref):
    lane = lax.broadcasted_iota(jnp.int32, (1, 128), 1)
    vec_ref[...] = jnp.zeros((48, 128), F32)
    for pair in range(64):
        both = [packed_ref[2 * pair + i].astype(F32) for i in range(2)]
        flat[88 * pair : 88 * pair + 88, :] = jnp.concatenate([b[:SHARD] for b in both], 0)
        for i in range(2):
            row, shift = divmod(47 * (2 * pair + i), 128)
            entries = both[i][SHARD : SHARD + 1, :]
            moved = pltpu.roll(entries, shift, 1) if shift else entries
            vec_ref[row : row + 1, :] += jnp.where(lane >= shift, moved, 0.0)
            if shift + 47 > 128:
                vec_ref[row + 1 : row + 2, :] += jnp.where(lane < shift, moved, 0.0)
    win_ref[...] = flat[0:512, :].astype(BF16)
    for n in range(3):
        wqkv_ref[:, n * 128 : n * 128 + 128] = flat[pl.ds(512 + n, 128, stride=3), :].astype(BF16)
    watt_ref[...] = flat[896:1024, :].astype(BF16)
    for i in range(FFN_COUNT):
        for n in range(4):
            wup_ref[i, :, n * 128 : n * 128 + 128] = flat[pl.ds(1024 + 512 * i + n, 128, stride=4), :].astype(BF16)
        wdown_ref[i] = flat[3072 + 512 * i : 3584 + 512 * i, :].astype(BF16)
    for n in range(4):
        wout_ref[:, n * 128 : n * 128 + 128] = flat[pl.ds(5120 + n, 128, stride=4), :].astype(BF16)


ST = 1024


def student_in_kernel(emb_ref, packed_ref, first_ref, sq_ref, sk_ref, sv_ref, skt_ref, svt_ref,
                      win_ref, wqkv_ref, watt_ref, wup_ref, wdown_ref, wout_ref, vec_ref, flat):
    t = pl.program_id(0)

    @pl.when(t == 0)
    def _():
        unpack(packed_ref, flat, win_ref, wqkv_ref, watt_ref, wup_ref, wdown_ref, wout_ref, vec_ref)

    emb = emb_ref[...]
    emb = jnp.where((t < SEQ // ST) | has_two(), emb, jnp.zeros_like(emb))
    first = (dot(emb, win_ref[...]) + line(vec_ref, V_IN)).astype(BF16)
    first_ref[...] = first
    qkv = dot(first, wqkv_ref[...])
    sq_ref[...] = (qkv[:, :D_S] + line(vec_ref, V_QKV)).astype(BF16)
    s_keys = (qkv[:, D_S : 2 * D_S] + line(vec_ref, V_QKV + 1)).astype(BF16)
    s_values = (qkv[:, 2 * D_S :] + line(vec_ref, V_QKV + 2)).astype(BF16)
    sk_ref[...] = s_keys
    sv_ref[...] = s_values
    skt_ref[...] = s_keys.T
    svt_ref[...] = s_values.T


def student_in(emb, packed):
    tall = jax.ShapeDtypeStruct((SLOTS, D_S), BF16)
    flat = jax.ShapeDtypeStruct((D_S, SLOTS), BF16)
    down = pl.BlockSpec((ST, D_S), lambda t: (t, 0))
    across = pl.BlockSpec((D_S, ST), lambda t: (0, t))
    made = [
        ((D_E, D_S), BF16),
        ((D_S, 3 * D_S), BF16),
        ((D_S, D_S), BF16),
        ((FFN_COUNT, D_S, FF_S), BF16),
        ((FFN_COUNT, FF_S, D_S), BF16),
        ((D_S, D_E), BF16),
        ((48, 128), F32),
    ]
    return pl.pallas_call(
        student_in_kernel,
        grid=(SLOTS // ST,),
        in_specs=[pl.BlockSpec((ST, D_E), lambda t: (t, 0)), whole(128, BLOCK, 128)],
        out_specs=[down] * 4 + [across] * 2 + [whole(*shape) for shape, _ in made],
        out_shape=[tall] * 4 + [flat] * 2 + [jax.ShapeDtypeStruct(*entry) for entry in made],
        scratch_shapes=[pltpu.VMEM((5632, 128), F32)],
        compiler_params=params(),
        name="student_in",
    )(emb, packed)


CB = 256
SUB = 64
STEPS = 3 * HEADS


def head_lanes(values, head):
    lane = lax.broadcasted_iota(jnp.int32, (1, D_S), 1)
    return jnp.where(lane // HEAD_S == head, values, jnp.zeros_like(values))


def attend_kernel(tq_ref, tk_ref, tvt_ref, sq_ref, sk_ref, svt_ref, et_ref, es_ref, tmix_ref, smix_ref, stat_ref,
                  ts0, ts1, ss0, ss1, mx0, mx1):
    n = pl.program_id(0)
    s_factor = HEAD_S**-0.5 * LOG2E

    def work(ts, ss, mx, tr, sr, mr, scores, mixes):
        if scores:
            queries, s_queries = tq_ref[...], head_lanes(sq_ref[...], n % HEADS)
            t_max = s_max = jnp.full((8, QB), -jnp.inf, F32)
        if mixes:
            t_top, s_top = jnp.max(mr[0], 0, keepdims=True), jnp.max(mr[1], 0, keepdims=True)
            t_off, s_off = t_top * LOG2E, s_top * s_factor
            t_sum = s_sum = kl = jnp.zeros((8, QB), F32)
            t_mix, s_mix = jnp.zeros((HEAD_T, QB), F32), jnp.zeros((HEAD_S, QB), F32)
        for c in range(SEQ // CB):
            part = slice(c * CB, c * CB + CB)
            if scores:
                t_part = dot_nt(tk_ref[part, :], queries)
                ts[part, :] = t_part
                s_part = dot_nt(sk_ref[part, :], s_queries)
                ss[part, :] = s_part
                t_max = jnp.maximum(t_max, fold(t_part, jnp.max))
                s_max = jnp.maximum(s_max, fold(s_part, jnp.max))
            if mixes:
                for u in range(c * CB, c * CB + CB, SUB):
                    some = slice(u, u + SUB)
                    t_log = tr[some, :] * LOG2E - t_off
                    s_log = sr[some, :] * s_factor - s_off
                    t_exp, s_exp = jnp.exp2(t_log), jnp.exp2(s_log)
                    et_ref[0, some, :] = t_exp.astype(BF16)
                    es_ref[0, some, :] = s_exp.astype(BF16)
                    t_sum, s_sum = t_sum + fold(t_exp), s_sum + fold(s_exp)
                    kl = kl + fold(t_exp * (t_log - s_log))
                t_mix += dot(tvt_ref[:, part], et_ref[0, part, :])
                s_mix += dot(svt_ref[:, part], es_ref[0, part, :])
        if scores:
            mx[0], mx[1] = t_max, s_max
        if mixes:
            t_sum, s_sum, kl = (jnp.sum(v, 0, keepdims=True) for v in (t_sum, s_sum, kl))
            t_inv, s_inv = 1.0 / t_sum, 1.0 / s_sum
            stat_ref[0, 0, 0:1, :] = t_inv
            stat_ref[0, 0, 1:2, :] = s_inv
            stat_ref[0, 0, 2:3, :] = kl * t_inv * (1.0 / LOG2E) - jnp.log(t_sum) + jnp.log(s_sum)
            stat_ref[0, 0, 3:8, :] = jnp.zeros((5, QB), F32)
            tmix_ref[...] = (t_mix * t_inv).T.astype(BF16)
            smix_ref[0] = s_mix * s_inv

    even, odd = (ts0, ss0, mx0), (ts1, ss1, mx1)
    pl.when(n == 0)(lambda: work(*even, *odd, True, False))
    pl.when((n > 0) & (n < STEPS) & (n % 2 == 0))(lambda: work(*even, *odd, True, True))
    pl.when((n > 0) & (n < STEPS) & (n % 2 == 1))(lambda: work(*odd, *even, True, True))
    pl.when(n == STEPS)(lambda: work(*even, *odd, False, True))


def attend(tq, tk, tvt, sq, sk, svt):
    now = lambda n: jnp.minimum(n, STEPS - 1)
    last = lambda n: jnp.maximum(n - 1, 0)
    block = lambda n: n // HEADS
    head = lambda n: n % HEADS
    return pl.pallas_call(
        attend_kernel,
        grid=(STEPS + 1,),
        in_specs=[
            pl.BlockSpec((QB, HEAD_T), lambda n: (block(now(n)), head(now(n)))),
            pl.BlockSpec((SEQ, HEAD_T), lambda n: (slot_of(block(now(n))), head(now(n)))),
            pl.BlockSpec((HEAD_T, SEQ), lambda n: (head(last(n)), slot_of(block(last(n))))),
            pl.BlockSpec((QB, D_S), lambda n: (first_block() + block(now(n)), 0)),
            pl.BlockSpec((SEQ, D_S), lambda n: (slot_of(block(now(n))), 0)),
            pl.BlockSpec((HEAD_S, SEQ), lambda n: (head(last(n)), slot_of(block(last(n))))),
        ],
        out_specs=[
            pl.BlockSpec((1, SEQ, QB), lambda n: (block(last(n)), 0, head(last(n)))),
            pl.BlockSpec((1, SEQ, QB), lambda n: (block(last(n)), 0, head(last(n)))),
            pl.BlockSpec((QB, HEAD_T), lambda n: (block(last(n)), head(last(n)))),
            pl.BlockSpec((1, HEAD_S, QB), lambda n: (block(last(n)), head(last(n)), 0)),
            pl.BlockSpec((1, 1, 8, QB), lambda n: (block(last(n)), head(last(n)), 0, 0)),
        ],
        out_shape=[
            jax.ShapeDtypeStruct((3, SEQ, HEADS * QB), BF16),
            jax.ShapeDtypeStruct((3, SEQ, HEADS * QB), BF16),
            jax.ShapeDtypeStruct((OWN, D_T), BF16),
            jax.ShapeDtypeStruct((3, D_S, QB), F32),
            jax.ShapeDtypeStruct((3, HEADS, 8, QB), F32),
        ],
        scratch_shapes=[pltpu.VMEM((SEQ, QB), F32)] * 4 + [pltpu.VMEM((2, 8, QB), F32)] * 2,
        compiler_params=params(),
        name="attend",
    )(tq, tk, tvt, sq, sk, svt)


FC = 1024


def teacher_kernel(mix_ref, hid_ref, emb_ref, att_ref, up_ref, down_ref, out_ref, bias_ref, gain_ref, shift_ref, target_ref, norm, low, acc):
    c = pl.program_id(0)

    @pl.when(c == 0)
    def _():
        summed = hid_ref[...] + dot(mix_ref[...], att_ref[...]) + line(bias_ref, 32, 8)
        one = layer_norm(summed, line(gain_ref, 0, 8), line(shift_ref, 0, 8))
        norm[...] = one
        low[...] = one.astype(BF16)

    rows = FC // 128
    up_bias = bias_ref[pl.ds(pl.multiple_of(40 + rows * c, 8), rows), :]
    act = gelu(dot(low[...], up_ref[...]) + line(up_bias, 0, rows)).astype(BF16)
    part = dot(act, down_ref[...])

    @pl.when(c == 0)
    def _():
        acc[...] = part

    @pl.when(c > 0)
    def _():
        acc[...] += part

    @pl.when(c == pl.num_programs(0) - 1)
    def _():
        summed = norm[...] + acc[...] + line(bias_ref, 72, 8)
        two = layer_norm(summed, line(gain_ref, 8, 8), line(shift_ref, 8, 8))
        last = emb_ref[...].astype(F32) + dot(two.astype(BF16), out_ref[...]) + line(bias_ref, 80, 4)
        target_ref[...] = layer_norm(last, line(gain_ref, 16, 4), line(shift_ref, 16, 4))


def teacher(mix, hid, emb, att, up, down, out, bias, gain, shift):
    return pl.pallas_call(
        teacher_kernel,
        grid=(FF_T // FC,),
        in_specs=[
            whole(OWN, D_T),
            whole(OWN, D_T),
            whole(OWN, D_E),
            whole(D_T, D_T),
            pl.BlockSpec((D_T, FC), lambda c: (0, c)),
            pl.BlockSpec((FC, D_T), lambda c: (c, 0)),
            whole(D_T, D_E),
            whole(84, 128),
            whole(20, 128),
            whole(20, 128),
        ],
        out_specs=whole(OWN, D_E),
        out_shape=jax.ShapeDtypeStruct((OWN, D_E), F32),
        scratch_shapes=[pltpu.VMEM((OWN, D_T), F32), pltpu.VMEM((OWN, D_T), BF16), pltpu.VMEM((OWN, D_T), F32)],
        compiler_params=params(),
        name="teacher",
    )(mix, hid, emb, att, up, down, out, bias, gain, shift)


def student_kernel(emb_ref, smix_ref, target_ref, weight_ref, win_ref, watt_ref, wup_ref, wdown_ref, wout_ref, vec_ref,
                   grad_ref, vgrad_ref, dsum_ref, dmix_ref, part_ref, states, inners, outers):

    def put(r, value):
        for i in range(value.shape[1] // 128):
            vgrad_ref[r + i : r + i + 1, :] = value[:, i * 128 : i * 128 + 128]

    total = lambda v: jnp.sum(v.astype(F32), 0, keepdims=True)
    emb = emb_ref[...]
    source = emb.astype(F32)
    first = dot(emb, win_ref[...]) + line(vec_ref, V_IN)
    mixed = jnp.concatenate([smix_ref[j].T for j in range(3)], 0).astype(BF16)
    branch = dot(mixed, watt_ref[...]) + line(vec_ref, V_ATT)
    state = line(vec_ref, V_AGAIN) * (first + branch) + line(vec_ref, V_ASHIFT)
    for i in range(FFN_COUNT):
        states[i] = state
        inner = dot(state.astype(BF16), wup_ref[i]) + line(vec_ref, V_UP + 4 * i, 4)
        inners[i] = inner
        act = gelu(inner).astype(BF16)
        pre = state + dot(act, wdown_ref[i]) + line(vec_ref, V_DOWN + i)
        outers[i] = pre
        state = line(vec_ref, V_FGAIN + i) * pre + line(vec_ref, V_FSHIFT + i)
    state_low = state.astype(BF16)
    summed = source + dot(state_low, wout_ref[...]) + line(vec_ref, V_OUT, 4)
    diff = line(vec_ref, V_OGAIN, 4) * summed + line(vec_ref, V_OSHIFT, 4) - target_ref[...]
    weight = jnp.concatenate([jnp.broadcast_to(weight_ref[j], (8, QB)).T[:, 0:1] for j in range(3)], 0)
    loss = jnp.sum(weight * jnp.sum(diff * diff, 1, keepdims=True)) * (1.0 / D_E)
    count = jnp.sum(weight)
    d_result = (weight * (2.0 / D_E)) * diff
    put(V_OGAIN, total(d_result * summed))
    put(V_OSHIFT, total(d_result))
    d_output = (d_result * line(vec_ref, V_OGAIN, 4)).astype(BF16)
    out_g = dot_tn(state_low, d_output)
    for n in range(4):
        grad_ref[pl.ds(4224 + n, 128, stride=4), :] = out_g[:, n * 128 : n * 128 + 128]
    put(V_OUT, total(d_output))
    d_state = dot_nt(d_output, wout_ref[...])
    for i in reversed(range(FFN_COUNT)):
        inner = inners[i]
        put(V_FGAIN + i, total(d_state * outers[i]))
        put(V_FSHIFT + i, total(d_state))
        d_sum = d_state * line(vec_ref, V_FGAIN + i)
        d_outer = d_sum.astype(BF16)
        half = 0.5 * (1.0 + lax.erf(inner * 0.7071067811865476))
        act = (inner * half).astype(BF16)
        slope = half + inner * jnp.exp(-0.5 * inner * inner) * 0.3989422804014327
        grad_ref[2176 + 512 * i : 2176 + 512 * (i + 1), :] = dot_tn(act, d_outer)
        d_inner = (dot_nt(d_outer, wdown_ref[i]) * slope).astype(BF16)
        up_g = dot_tn(states[i].astype(BF16), d_inner)
        for n in range(4):
            grad_ref[pl.ds(128 + 512 * i + n, 128, stride=4), :] = up_g[:, n * 128 : n * 128 + 128]
        put(V_UP + 4 * i, total(d_inner))
        put(V_DOWN + i, total(d_outer))
        d_state = d_sum + dot_nt(d_inner, wup_ref[i])
    put(V_AGAIN, total(d_state * (first + branch)))
    put(V_ASHIFT, total(d_state))
    d_sum = d_state * line(vec_ref, V_AGAIN)
    d_branch = d_sum.astype(BF16)
    grad_ref[0:128, :] = dot_tn(mixed, d_branch)
    put(V_ATT, total(d_branch))
    dsum_ref[...] = d_sum
    dmix_ref[...] = dot_nt(d_branch, watt_ref[...]).astype(BF16)
    for r in (0, 1, 2, 3, 47):
        vgrad_ref[r : r + 1, :] = jnp.zeros((1, 128), F32)
    row = lax.broadcasted_iota(jnp.int32, (8, 128), 0)
    lane = lax.broadcasted_iota(jnp.int32, (8, 128), 1)
    part_ref[...] = jnp.where((row == 0) & (lane == 0), loss, 0.0) + jnp.where((row == 0) & (lane == 1), count, 0.0)


def student(emb, smix, target, weight, win, watt, wup, wdown, wout, vecs):
    return pl.pallas_call(
        student_kernel,
        grid=(1,),
        in_specs=[
            whole(OWN, D_E),
            whole(3, D_S, QB),
            whole(OWN, D_E),
            whole(3, 1, QB),
            whole(D_E, D_S),
            whole(D_S, D_S),
            whole(FFN_COUNT, D_S, FF_S),
            whole(FFN_COUNT, FF_S, D_S),
            whole(D_S, D_E),
            whole(48, 128),
        ],
        out_specs=[whole(4736, 128), whole(48, 128), whole(OWN, D_S), whole(OWN, D_S), whole(8, 128)],
        out_shape=[
            jax.ShapeDtypeStruct((4736, 128), F32),
            jax.ShapeDtypeStruct((48, 128), F32),
            jax.ShapeDtypeStruct((OWN, D_S), F32),
            jax.ShapeDtypeStruct((OWN, D_S), BF16),
            jax.ShapeDtypeStruct((8, 128), F32),
        ],
        scratch_shapes=[
            pltpu.VMEM((FFN_COUNT, OWN, D_S), F32),
            pltpu.VMEM((FFN_COUNT, OWN, FF_S), F32),
            pltpu.VMEM((FFN_COUNT, OWN, D_S), F32),
        ],
        compiler_params=params(),
        name="student",
    )(emb, smix, target, weight, win, watt, wup, wdown, wout, vecs)


KB = 512


def back_kernel(et_ref, es_ref, stat_ref, smix_ref, dmix_ref, weight_ref, sq_ref, sv_ref, skt_ref, dsum_ref, emb_ref, first_ref,
                wqkv_ref, vgrad_ref, part_in, late_ref, block_ref, part_ref,
                dkv, dqt, ds, dq, dfirst, dmt, dmz, sqd, rows, flat, vecs, kls, sem):
    j, kb = pl.program_id(0), pl.program_id(1)
    s_scale = HEAD_S**-0.5
    late = pltpu.make_async_copy(late_ref, flat.at[896:5632], sem)

    @pl.when((j == 0) & (kb == 0))
    def _():
        late.start()
        dkv[...] = jnp.zeros_like(dkv)
        kls[...] = jnp.zeros_like(kls)

    @pl.when(kb == 0)
    def _():
        quarter = weight_ref[0] * (1.0 / HEADS)
        wide = dmix_ref[...].astype(F32)
        tall = wide.T
        place = lax.broadcasted_iota(jnp.int32, (D_S, 1), 0) // HEAD_S
        for h in range(HEADS):
            own = slice(h * HEAD_S, h * HEAD_S + HEAD_S)
            mine = slice(h * QB, h * QB + QB)
            t_inv, s_inv = stat_ref[0, h, 0:1, :], stat_ref[0, h, 1:2, :]
            kls[0:1, :] += quarter * stat_ref[0, h, 2:3, :]
            row_dot = jnp.sum(tall[own] * smix_ref[0, own, :], 0, keepdims=True)
            rows[h, 0:1, :] = row_dot - quarter
            rows[h, 1:2, :] = s_inv
            rows[h, 2:3, :] = quarter * t_inv
            dmt[h] = jnp.where(place == h, tall, 0.0).astype(BF16)
            dmz[mine, :] = head_lanes(wide * stat_ref[0, h].T[:, 1:2], h).astype(BF16)
            sqd[mine, :] = head_lanes(sq_ref[...], h)
        dqt[...] = jnp.zeros_like(dqt)

    here = pl.ds(pl.multiple_of(slot_of(j) * SEQ + kb * KB, KB), KB)
    dkv[here, D_S:] += dot(es_ref[0], dmz[...])
    for h in range(HEADS):
        lanes = slice(h * QB, h * QB + QB)
        for c in range(KB // 256):
            part = slice(c * 256, c * 256 + 256)
            d_probs = dot(sv_ref[part, :], dmt[h])
            s_exp, t_exp = es_ref[0, part, lanes].astype(F32), et_ref[0, part, lanes].astype(F32)
            d_scores = (d_probs - rows[h, 0:1, :]) * rows[h, 1:2, :] * s_exp - t_exp * rows[h, 2:3, :]
            ds[part, lanes] = d_scores.astype(BF16)
        own = slice(h * HEAD_S, h * HEAD_S + HEAD_S)
        dqt[own, :] += dot(skt_ref[own, :], ds[:, lanes])
    dkv[here, :D_S] += dot(ds[...], sqd[...])

    @pl.when(kb == pl.num_programs(1) - 1)
    def _():
        dq[pl.ds(pl.multiple_of(j * QB, QB), QB), :] = (dqt[...] * s_scale).T

    @pl.when((j == 2) & (kb == pl.num_programs(1) - 1))
    def _():
        qkv_w = wqkv_ref[...]
        dq_low = dq[...].astype(BF16)
        own = pl.ds(pl.multiple_of(first_block() * QB, QB), OWN)
        q_grad = dot_tn(first_ref[own, :], dq_low)
        own_part = dsum_ref[...] + dot_nt(dq_low, qkv_w[:, :D_S])
        kv_grad = jnp.zeros((D_S, 2 * D_S), F32)
        kv_bias = jnp.zeros((1, 2 * D_S), F32)
        for c in range(8):
            part = pl.ds(c * 512, 512)
            wide = dkv[part, :]
            low = jnp.concatenate([(wide[:, :D_S] * s_scale).astype(BF16), wide[:, D_S:].astype(BF16)], 1)
            kv_grad += dot_tn(first_ref[part, :], low)
            kv_bias += jnp.sum(low.astype(F32), 0, keepdims=True)
            dfirst[part, :] = dot_nt(low, qkv_w[:, D_S:])
        dfirst[own, :] += own_part
        in_grad = jnp.zeros((D_S, D_E), F32)
        in_bias = jnp.zeros((1, D_S), F32)
        two = has_two()
        for c in range(8):
            part = pl.ds(c * 512, 512)
            low = dfirst[part, :].astype(BF16)
            emb = emb_ref[part, :]
            if c >= 4:
                emb = jnp.where(two, emb, jnp.zeros_like(emb))
            in_grad += dot_tn(low, emb)
            in_bias += jnp.sum(low.astype(F32), 0, keepdims=True)
        flat[0:512, :] = in_grad.T
        flat[pl.ds(512, 128, stride=3), :] = q_grad
        flat[pl.ds(513, 128, stride=3), :] = kv_grad[:, :D_S]
        flat[pl.ds(514, 128, stride=3), :] = kv_grad[:, D_S:]
        vecs[...] = vgrad_ref[...]
        vecs[0:1, :] = in_bias
        vecs[1:2, :] = jnp.sum(dq_low.astype(F32), 0, keepdims=True)
        vecs[2:3, :] = kv_bias[:, :D_S]
        vecs[3:4, :] = kv_bias[:, D_S:]
        late.wait()
        lane = lax.broadcasted_iota(jnp.int32, (1, 128), 1)
        rest = jnp.zeros((BLOCK - SHARD - 1, 128), F32)
        for pair in range(64):
            both = flat[88 * pair : 88 * pair + 88, :]
            for i in range(2):
                owner = 2 * pair + i
                row, shift = divmod(47 * owner, 128)
                entries = vecs[row : row + 1, :]
                if shift + 47 > 128:
                    entries = jnp.where(lane >= shift, entries, vecs[row + 1 : row + 2, :])
                if shift:
                    entries = pltpu.roll(entries, 128 - shift, 1)
                entries = jnp.where(lane < 47, entries, 0.0)
                mine = both[SHARD * i : SHARD * (i + 1)]
                block_ref[owner // 32, owner // 16 % 2, owner % 16] = jnp.concatenate([mine, entries, rest], 0).astype(BF16)
        kl = jnp.sum(kls[0:1, :], keepdims=True)
        corner = (lax.broadcasted_iota(jnp.int32, (8, 128), 0) == 0) & (lax.broadcasted_iota(jnp.int32, (8, 128), 1) == 0)
        part_ref[...] = part_in[...] + jnp.where(corner, kl, 0.0)


def back(et, es, stat, smix, dmix, weight, sq, sv, skt, dsum, emb, first, wqkv, vgrad, part, late):
    count = SEQ // KB
    place = lambda j, k: slot_of(j) * count + k
    return pl.pallas_call(
        back_kernel,
        grid=(3, count),
        in_specs=[
            pl.BlockSpec((1, KB, HEADS * QB), lambda j, k: (j, k, 0)),
            pl.BlockSpec((1, KB, HEADS * QB), lambda j, k: (j, k, 0)),
            pl.BlockSpec((1, HEADS, 8, QB), lambda j, k: (j, 0, 0, 0)),
            pl.BlockSpec((1, D_S, QB), lambda j, k: (j, 0, 0)),
            pl.BlockSpec((QB, D_S), lambda j, k: (j, 0)),
            pl.BlockSpec((1, 1, QB), lambda j, k: (j, 0, 0)),
            pl.BlockSpec((QB, D_S), lambda j, k: (first_block() + j, 0)),
            pl.BlockSpec((KB, D_S), lambda j, k: (place(j, k), 0)),
            pl.BlockSpec((D_S, KB), lambda j, k: (0, place(j, k))),
            whole(OWN, D_S),
            whole(SLOTS, D_E),
            whole(SLOTS, D_S),
            whole(D_S, 3 * D_S),
            whole(48, 128),
            whole(8, 128),
            pl.BlockSpec(memory_space=pl.ANY),
        ],
        out_specs=[whole(4, 2, 16, BLOCK, 128), whole(8, 128)],
        out_shape=[
            jax.ShapeDtypeStruct((4, 2, 16, BLOCK, 128), BF16),
            jax.ShapeDtypeStruct((8, 128), F32),
        ],
        scratch_shapes=[
            pltpu.VMEM((SLOTS, 2 * D_S), F32),
            pltpu.VMEM((D_S, QB), F32),
            pltpu.VMEM((KB, HEADS * QB), BF16),
            pltpu.VMEM((OWN, D_S), F32),
            pltpu.VMEM((SLOTS, D_S), F32),
            pltpu.VMEM((HEADS, D_S, QB), BF16),
            pltpu.VMEM((HEADS * QB, D_S), BF16),
            pltpu.VMEM((HEADS * QB, D_S), BF16),
            pltpu.VMEM((HEADS, 8, QB), F32),
            pltpu.VMEM((5632, 128), F32),
            pltpu.VMEM((48, 128), F32),
            pltpu.VMEM((8, QB), F32),
            pltpu.SemaphoreType.DMA,
        ],
        compiler_params=params(),
        name="back",
    )(et, es, stat, smix, dmix, weight, sq, sv, skt, dsum, emb, first, wqkv, vgrad, part, late)


def update_kernel(g_ref, part_ref, master_mat, master_vec, first_mat, first_vec, second_mat, second_vec,
                  new_ref, newf_ref, news_ref, scal_ref, packs, half_in, mine, block_out, blocks_in, tile_out, tiles_f, tiles_d,
                  half_sems, block_send, block_recv, f_send, f_recv, d_send, d_recv):
    dp, fs = lax.axis_index("dp"), lax.axis_index("fsdp")
    x, core = dp // 2, dp % 2
    sibling = (2 * x + 1 - core, fs)
    barrier = pltpu.get_barrier_semaphore()

    def chip(k):
        return (2 * ((x + k // 16) % 4) + core, (fs + k) % 16)

    def greet(k, _):
        pl.semaphore_signal(barrier, inc=1, device_id=chip(k), device_id_type=MESH)
        return 0

    lax.fori_loop(1, 64, greet, 0)
    for k in range(4):
        other = (2 * ((x + k) % 4) + 1 - core, fs)
        pl.semaphore_signal(barrier, inc=1, device_id=other, device_id_type=MESH)

    packs[...] = jnp.zeros_like(packs)
    for i, (mat, vec) in enumerate([(master_mat, master_vec), (first_mat, first_vec), (second_mat, second_vec)]):
        packs[i, 0:SHARD, :] = mat[...]
        packs[i, SHARD : SHARD + 1, 0:47] = vec[...]
    pl.semaphore_wait(barrier, 67)
    swap = pltpu.make_async_remote_copy(
        g_ref.at[:, 1 - core], half_in, half_sems.at[0], half_sems.at[1], device_id=sibling, device_id_type=MESH
    )
    swap.start()
    swap.wait()

    def join(i, _):
        summed = g_ref[i // 16, core, i % 16].astype(F32) + half_in[i // 16, i % 16].astype(F32)
        block_out[i] = summed.astype(BF16)
        return 0

    lax.fori_loop(0, 64, join, 0)
    mine[...] = g_ref[x, core, fs].astype(F32) + half_in[x, fs].astype(F32)

    def block_copy(k):
        xk, fk = (x + k // 16) % 4, (fs + k) % 16
        return pltpu.make_async_remote_copy(
            block_out.at[xk * 16 + fk], blocks_in.at[k], block_send.at[k], block_recv.at[k],
            device_id=(2 * xk + core, fk), device_id_type=MESH,
        )

    def start(k, _):
        block_copy(k).start()
        return 0

    lax.fori_loop(1, 64, start, 0)

    def gather(k, _):
        block_copy(k).wait()
        mine[...] += blocks_in[k].astype(F32)
        return 0

    lax.fori_loop(1, 64, gather, 0)

    row = lax.broadcasted_iota(jnp.int32, (BLOCK, 128), 0)
    lane8 = lax.broadcasted_iota(jnp.int32, (8, 128), 1)
    row8 = lax.broadcasted_iota(jnp.int32, (8, 128), 0)
    place = (dp * 16 + fs) * SHARD + row
    is_matrix = row < SHARD
    bounds = [0]
    for rows in MAT_ROWS:
        bounds.append(bounds[-1] + rows)
    members = [is_matrix & (place >= bounds[i]) & (place < bounds[i + 1]) for i in range(6)]

    def everyone(tile, turn):
        tile_out[turn, 0] = tile
        tiles_f[turn, fs] = tile

        def f_copy(k):
            return pltpu.make_async_remote_copy(
                tile_out.at[turn, 0], tiles_f.at[turn, fs], f_send.at[turn, k], f_recv.at[turn, k],
                device_id=(dp, (fs + k) % 16), device_id_type=MESH,
            )

        def d_copy(k):
            return pltpu.make_async_remote_copy(
                tile_out.at[turn, 1], tiles_d.at[turn, dp], d_send.at[turn, k], d_recv.at[turn, k],
                device_id=((dp + k) % 8, fs), device_id_type=MESH,
            )

        for k in range(1, 16):
            f_copy(k).start()
        for k in range(1, 16):
            f_copy(k).wait()
        total = tiles_f[turn, 0]
        for k in range(1, 16):
            total = total + tiles_f[turn, k]
        tile_out[turn, 1] = total
        tiles_d[turn, dp] = total
        for k in range(1, 8):
            d_copy(k).start()
        for k in range(1, 8):
            d_copy(k).wait()
        total = tiles_d[turn, 0]
        for k in range(1, 8):
            total = total + tiles_d[turn, k]
        return total

    def entry(tile, i):
        return jnp.sum(jnp.where((row8 == 0) & (lane8 == i), tile, 0.0), keepdims=True)

    def tile_of(values):
        tile = jnp.zeros((8, 128), F32)
        for i, value in values:
            tile += jnp.where((row8 == 0) & (lane8 == i), value, 0.0)
        return tile

    grad = mine[...]
    master = packs[0]
    squares = master * master
    tile = part_ref[...] + tile_of(
        [(2, jnp.sum(grad * grad, keepdims=True))]
        + [(3 + i, jnp.sum(jnp.where(members[i], squares, 0.0), keepdims=True)) for i in range(6)]
    )
    tile = everyone(tile, 0)
    loss, count = entry(tile, 0), entry(tile, 1)
    inverse = 1.0 / count
    norm = jnp.sqrt(entry(tile, 2)) * inverse
    factor = CLIP_NORM / jnp.maximum(norm, CLIP_NORM)
    grad = grad * inverse * factor
    first = BETA_ONE * packs[1] + (1.0 - BETA_ONE) * grad
    second = BETA_TWO * packs[2] + (1.0 - BETA_TWO) * grad * grad
    newf_ref[...] = first
    news_ref[...] = second
    ratio = first / (1.0 - BETA_ONE**STEP) / (jnp.sqrt(second / (1.0 - BETA_TWO**STEP)) + ADAM_EPS)
    ratio = ratio + jnp.where(is_matrix, WEIGHT_DECAY * master, 0.0)
    squares = ratio * ratio
    steps = everyone(tile_of([(3 + i, jnp.sum(jnp.where(members[i], squares, 0.0), keepdims=True)) for i in range(6)]), 1)
    trust = jnp.ones((BLOCK, 128), F32)
    for i in range(6):
        trust = jnp.where(members[i], jnp.sqrt(entry(tile, 3 + i)) / jnp.sqrt(entry(steps, 3 + i)), trust)
    new_ref[...] = master - LEARN_RATE * (trust * ratio)
    scal_ref[...] = tile_of([(0, loss), (1, count), (2, norm)])


def update(grads, part, *state):
    vmem = pl.BlockSpec(memory_space=pltpu.VMEM)
    block = jax.ShapeDtypeStruct((BLOCK, 128), F32)
    dma = pltpu.SemaphoreType.DMA
    return pl.pallas_call(
        update_kernel,
        in_specs=[vmem] * 8,
        out_specs=[vmem] * 4,
        out_shape=[block, block, block, jax.ShapeDtypeStruct((8, 128), F32)],
        scratch_shapes=[
            pltpu.VMEM((3, BLOCK, 128), F32),
            pltpu.VMEM((4, 16, BLOCK, 128), BF16),
            pltpu.VMEM((BLOCK, 128), F32),
            pltpu.VMEM((64, BLOCK, 128), BF16),
            pltpu.VMEM((64, BLOCK, 128), BF16),
            pltpu.VMEM((2, 2, 8, 128), F32),
            pltpu.VMEM((2, 16, 8, 128), F32),
            pltpu.VMEM((2, 8, 8, 128), F32),
            dma((2,)),
            dma((64,)),
            dma((64,)),
            dma((2, 16)),
            dma((2, 16)),
            dma((2, 8)),
            dma((2, 8)),
        ],
        compiler_params=params(collective_id=1, has_side_effects=True),
        name="update",
    )(grads, part, *state)


def finish_kernel(new_ref, newf_ref, news_ref, scal_ref, loss, count, norm, m0, m1, m2, v0, v1, v2):
    for source, mat, vec in ((new_ref, m0, v0), (newf_ref, m1, v1), (news_ref, m2, v2)):
        mat[...] = source[0:SHARD, :]
        vec[...] = source[SHARD : SHARD + 1, 0:47]
    for i, out in enumerate((loss, count, norm)):
        out[...] = scal_ref[0:1, i : i + 1]


def finish(*made):
    vmem = pl.BlockSpec(memory_space=pltpu.VMEM)
    shape = lambda *dims: jax.ShapeDtypeStruct(dims, F32)
    return pl.pallas_call(
        finish_kernel,
        in_specs=[vmem] * 4,
        out_specs=[vmem] * 9,
        out_shape=[shape(1, 1)] * 3 + [shape(SHARD, 128)] * 3 + [shape(1, 47)] * 3,
        name="finish",
    )(*made)


def per_device(
    token_ids,
    splits,
    valid_mask,
    embed_table,
    embed_proj,
    embed_bias,
    type_table,
    teach_in,
    teach_qkv,
    teach_att,
    teach_up,
    teach_down,
    teach_out,
    teach_bias,
    teach_gain,
    teach_shift,
    matrices,
    vectors,
    matrix_first,
    matrix_second,
    vector_first,
    vector_second,
):
    mat = lambda v: v.reshape(SHARD, 128)
    vec = lambda v: v.reshape(1, 47)
    rows_128 = lambda v: v.reshape(-1, 128)
    bias = rows_128(teach_bias)
    emb, t_keys, t_values, own_emb, hidden, t_queries, weights, packed = front(
        embed_table[token_ids], valid_mask, splits, mat(matrices), vec(vectors), embed_proj, teach_in, teach_qkv,
        rows_128(embed_bias), type_table, bias,
    )
    first, s_q, s_k, s_v, s_kt, s_vt, in_w, qkv_w, att_w, up_w, down_w, out_w, vecs = student_in(emb, packed)
    et, es, t_mixed, s_mixed, stat = attend(t_queries, t_keys, t_values, s_q, s_k, s_vt)
    target = teacher(
        t_mixed, hidden, own_emb, teach_att, teach_up, teach_down, teach_out, bias, rows_128(teach_gain), rows_128(teach_shift)
    )
    late, vgrads, d_sum, d_mixed, part = student(
        own_emb, s_mixed, target, weights, in_w, att_w, up_w, down_w, out_w, vecs
    )
    blocks, part = back(
        et, es, stat, s_mixed, d_mixed, weights, s_q, s_v, s_kt, d_sum, emb, first, qkv_w, vgrads, part, late
    )
    made = update(
        blocks, part, mat(matrices), vec(vectors), mat(matrix_first), vec(vector_first), mat(matrix_second), vec(vector_second)
    )
    loss, count, norm, m0, m1, m2, v0, v1, v2 = finish(*made)
    flat = lambda v: v.reshape(-1)
    scalar = lambda v: v.reshape(())
    return (
        scalar(loss), scalar(count), scalar(norm), flat(m0), flat(m1), flat(m2), flat(v0), flat(v1), flat(v2),
    )


def solution(mesh):
    both = P(("dp", "fsdp"))
    return jax.shard_map(
        per_device,
        mesh=mesh,
        in_specs=(P("dp", "fsdp"), P("dp"), P("dp", "fsdp")) + (P(),) * 13 + (both,) * 6,
        out_specs=(P(), P(), P(), both, both, both, both, both, both),
        check_vma=False,
    )
```

```python
import functools
import math

import jax
import jax.numpy as jnp
from jax import lax
from jax.experimental import pallas as pl
from jax.experimental.pallas import tpu as pltpu
from jax.sharding import PartitionSpec as P

D_E = 512
D_T = 1024
FF_T = 4096
D_S = 128
FF_S = 512
HEADS = 4
FFN_COUNT = 4
STEP = 5
HEAD_T = 256
HEAD_S = 32
SEQ = 2048
QB = 256
OWN = 3 * QB
SLOTS = 2 * SEQ

CLIP_NORM = 0.05
BETA_ONE = 0.9
BETA_TWO = 0.999
LEARN_RATE = 0.3
WEIGHT_DECAY = 0.01
ADAM_EPS = 1e-06

F32 = jnp.float32
BF16 = jnp.bfloat16
LOG2E = 1.4426950408889634
MESH = pl.DeviceIdType.MESH

MAT_ROWS = (512, 384, 128, 2048, 2048, 512)
SHARD = 44
BLOCK = 48
(V_IN, V_QKV, V_ATT, V_AGAIN, V_ASHIFT, V_UP, V_DOWN, V_FGAIN, V_FSHIFT, V_OUT, V_OGAIN, V_OSHIFT) = (
    0, 1, 4, 5, 6, 7, 23, 27, 31, 35, 39, 43)


def dot(left, right):
    return jnp.dot(left, right, preferred_element_type=F32)


def dot_nt(left, right):
    return lax.dot_general(left, right, (((1,), (1,)), ((), ())), preferred_element_type=F32)


def dot_tn(left, right):
    return lax.dot_general(left, right, (((0,), (0,)), ((), ())), preferred_element_type=F32)


def layer_norm(values, gain, shift):
    center = values - jnp.mean(values, -1, keepdims=True)
    spread = jnp.mean(center * center, -1, keepdims=True)
    return center * lax.rsqrt(spread + 1e-05) * gain + shift


def gelu(values):
    return 0.5 * values * (1.0 + lax.erf(values * 0.7071067811865476))


def params(mib, **more):
    return pltpu.CompilerParams(vmem_limit_bytes=mib * 2**20, **more)


def whole(*shape):
    return pl.BlockSpec(shape, lambda *_: (0,) * len(shape))


def line(ref, row, count=1):
    if count == 1:
        return ref[row : row + 1, :]
    return jnp.concatenate([ref[row + i : row + i + 1, :] for i in range(count)], 1)


def fold(values, op=jnp.sum):
    return op(values.reshape(values.shape[0] // 8, 8, values.shape[1]), 0)


def spots():
    dp, fs = lax.axis_index("dp"), lax.axis_index("fsdp")
    return dp // 2, dp % 2, fs // 4, fs % 4


def place_in_group():
    _, core, _, y = spots()
    return 2 * y + core


def first_block():
    return (3 * place_in_group()) % 8


def slot_of(j):
    return (first_block() + j) // 8


def has_two():
    i = place_in_group()
    return (i == 2) | (i == 5)


PT = 512
TILES = SEQ // PT


CHUNK = 2048
VOCAB = 30522
WHOLE = VOCAB // 16 * 16


def front_kernel(ids_ref, table_hbm, tail_ref, mask_ref, splits_ref, mats_ref, vecs_ref, proj_hbm, win_hbm, wqkv_hbm, ebias_ref,
                 types_ref, bias_ref, emb_hbm, k_hbm, vt_hbm, own_ref, hid_ref, tq_ref, weight_ref, params_ref,
                 table_low, table, picked, e_ref, note, notes, wide, block, e_all, proj_ref, win_ref, wqkv_ref, emb_t, k_t, vt_t,
                 t_sem, load, e_send, e_recv, n_send, n_recv, a_send, a_recv, b_send, b_recv, c_send, c_recv,
                 out, s_send, s_recv, own_sem):
    dp, me = lax.axis_index("dp"), lax.axis_index("fsdp")
    x, core, z, y = spots()
    i = 2 * y + core
    sibling = (2 * x + 1 - core, me)
    source_dp = 2 * x + z // 2
    is_source = z // 2 == core
    loads = [
        pltpu.make_async_copy(hbm, ref, load.at[n])
        for n, (hbm, ref) in enumerate([(proj_hbm, proj_ref), (win_hbm, win_ref), (wqkv_hbm, wqkv_ref)])
    ]
    barrier = pltpu.get_barrier_semaphore()

    def signal(device):
        pl.semaphore_signal(barrier, inc=1, device_id=device, device_id_type=MESH)

    def greet_source(f, _):
        @pl.when(jnp.logical_not(is_source & (f == me)))
        def _():
            signal((source_dp, f))

        return 0

    def greet_plane(k, _):
        signal((dp, (me + k) % 16))
        return 0

    lax.fori_loop(0, 16, greet_source, 0)
    lax.fori_loop(1, 16, greet_plane, 0)
    for k in range(1, 4):
        signal((2 * ((x + k) % 4) + core, me))
    signal(sibling)
    chunks = [(c, min(CHUNK, WHOLE - c)) for c in range(0, WHOLE, CHUNK)]
    table_copies = [
        pltpu.make_async_copy(table_hbm.at[pl.ds(c, size)], table_low.at[pl.ds(c, size)], t_sem.at[n])
        for n, (c, size) in enumerate(chunks)
    ]
    for copy in table_copies:
        copy.start()
    for copy in loads:
        copy.start()

    lane = lax.broadcasted_iota(jnp.int32, (1, 128), 1)
    note[0:6, :] = mask_ref[...]
    line_of_splits = jnp.zeros((1, 128), jnp.int32)
    for r in range(6):
        line_of_splits = jnp.where(lane == r, splits_ref[r], line_of_splits)
    note[6:7, :] = line_of_splits
    note[7:8, :] = jnp.zeros((1, 128), jnp.int32)
    wide[...] = jnp.zeros((BLOCK, 128), F32)
    wide[0:SHARD, :] = mats_ref[...]
    wide[SHARD : SHARD + 1, 0:47] = vecs_ref[...]
    block[...] = wide[...].astype(BF16)
    params_ref[dp * 16 + me] = block[...]
    main = (3 * i + 1) // 8
    table[WHOLE : WHOLE + 16, :] = tail_ref[...].astype(F32)
    for copy, (c, size) in zip(table_copies, chunks):
        copy.wait()
        table[c : c + size, :] = table_low[c : c + size, :].astype(F32)

    def pick(g, _):
        for u in range(16):
            token = ids_ref[g // 8, g % 8 * 16 + u]
            picked[pl.ds(g * 16 + u, 1), :] = table[pl.ds(token, 1), :]
        return 0

    lax.fori_loop(0, 48, pick, 0)
    for r in range(6):
        e_ref[r] = picked[128 * r : 128 * r + 128, :].astype(BF16)

    @pl.when(is_source)
    def _():
        e_all[pl.ds(pl.multiple_of(me * 128, 128), 128), :] = e_ref[3 * (z % 2) + main]
        notes[me] = note[...]

    pl.semaphore_wait(barrier, jnp.where(is_source, 15, 16) + 15 + 3 + 1)

    def e_copy(d, noted):
        zd, yd, cd = 2 * core + d // 8, d // 2 % 4, d % 2
        where = dict(device_id=(2 * x + cd, 4 * zd + yd), device_id_type=MESH)
        if noted:
            return pltpu.make_async_remote_copy(note, notes.at[me], n_send.at[d], n_recv.at[me], **where)
        row = 3 * (d // 8) + (3 * (2 * yd + cd) + 1) // 8
        here = pl.ds(pl.multiple_of(me * 128, 128), 128)
        return pltpu.make_async_remote_copy(e_ref.at[row], e_all.at[here], e_send.at[d], e_recv.at[me], **where)

    def is_other(d):
        return jnp.logical_not((2 * core + d // 8 == z) & (d // 2 % 4 == y) & (d % 2 == core))

    def e_start(d, _):
        @pl.when(is_other(d))
        def _():
            e_copy(d, False).start()
            e_copy(d, True).start()

        return 0

    lax.fori_loop(0, 16, e_start, 0)

    def e_sent(d, _):
        @pl.when(is_other(d))
        def _():
            e_copy(d, False).wait_send()
            e_copy(d, True).wait_send()

        return 0

    def e_arrived(f, _):
        @pl.when(jnp.logical_not(is_source & (f == me)))
        def _():
            where = dict(device_id=(source_dp, f), device_id_type=MESH)
            there = pl.ds(pl.multiple_of(f * 128, 128), 128)
            pltpu.make_async_remote_copy(e_ref.at[0], e_all.at[there], e_send.at[0], e_recv.at[f], **where).wait_recv()
            pltpu.make_async_remote_copy(note, notes.at[f], n_send.at[0], n_recv.at[f], **where).wait_recv()

        return 0

    def a_copy(k):
        return pltpu.make_async_remote_copy(
            block, params_ref.at[dp * 16 + me], a_send.at[k], a_recv.at[k], device_id=(dp, (me + k) % 16), device_id_type=MESH
        )

    def b_copy(k):
        mine = params_ref.at[pl.ds(dp * 16, 16)]
        return pltpu.make_async_remote_copy(
            mine, mine, b_send.at[k], b_recv.at[k], device_id=(2 * ((x + k) % 4) + core, me), device_id_type=MESH
        )

    def c_copy(k):
        mine = params_ref.at[pl.ds((2 * k + core) * 16, 16)]
        return pltpu.make_async_remote_copy(mine, mine, c_send.at[k], c_recv.at[k], device_id=sibling, device_id_type=MESH)

    def a_start(k, _):
        a_copy(k).start()
        return 0

    def a_wait(k, _):
        a_copy(k).wait()
        return 0

    lax.fori_loop(1, 16, a_start, 0)

    gives = ((y == 1) & (core == 1)) | ((y == 2) & (core == 0))
    takes = has_two()
    main_slot = jnp.where(i == 5, 1, 0)
    his_slot = jnp.where(y == 1, 1, 0)

    made = ((emb_t, emb_hbm), (k_t, k_hbm), (vt_t, vt_hbm))

    def target(n, slot, t):
        rows = pl.ds(pl.multiple_of(slot * SEQ + t * PT, PT), PT)
        return made[n][1].at[:, rows] if n == 2 else made[n][1].at[rows]

    def out_copy(n, t):
        return pltpu.make_async_copy(made[n][0].at[t % 2], target(n, main_slot, t), out.at[n, t % 2])

    def give_copy(n, t):
        return pltpu.make_async_remote_copy(
            made[n][0].at[t % 2], target(n, his_slot, t), s_send.at[n, t], s_recv.at[n, t],
            device_id=sibling, device_id_type=MESH,
        )

    def settle(t, parts):
        for n in parts:
            out_copy(n, t).wait()

        @pl.when(gives)
        def _():
            for n in parts:
                give_copy(n, t).wait_send()

    per = SEQ // PT
    row = lax.broadcasted_iota(jnp.int32, (PT, 1), 0)
    for t in range(TILES):
        b = t % 2
        lax.fori_loop(4 * t + (1 if t else 0), min(4 * t + 5, 16), e_arrived, 0)
        if t == 0:
            loads[0].wait()
            split = jnp.sum(jnp.where(lane == 3 * (z % 2) + main, notes[0, 6:7, :], 0), keepdims=True)
        mid = e_all[t * PT : t * PT + PT, :]
        if t:
            before = e_all[t * PT - 16 : t * PT, :].astype(F32)[15:16]
        else:
            before = jnp.zeros((1, 128), F32)
        if t < TILES - 1:
            after = e_all[t * PT + PT : t * PT + PT + 16, :].astype(F32)[0:1]
        else:
            after = jnp.zeros((1, 128), F32)
        broad = mid.astype(F32)
        left = jnp.where(row == 0, before, pltpu.roll(broad, 1, 0)).astype(BF16)
        right = jnp.where(row == PT - 1, after, pltpu.roll(broad, PT - 1, 0)).astype(BF16)
        trigram = jnp.concatenate([left, mid, right], 1)
        typed = jnp.where(row + t * PT >= split, types_ref[1:2, :], types_ref[0:1, :])
        emb = (dot(trigram, proj_ref[...]) + line(ebias_ref, 0, 4) + typed).astype(BF16)
        if t == 0:
            loads[1].wait()
        hidden = (dot(emb, win_ref[...]) + line(bias_ref, 0, 8)).astype(BF16)
        if t == 0:
            loads[2].wait()
        keys = (dot(hidden, wqkv_ref[:, D_T : 2 * D_T]) + line(bias_ref, 16, 8)).astype(BF16)
        values = (dot(hidden, wqkv_ref[:, 2 * D_T :]) + line(bias_ref, 24, 8)).astype(BF16)
        if t >= 2:
            settle(t - 2, range(3))
        emb_t[b] = emb
        k_t[b] = keys
        vt_t[b] = values.T
        for n in range(3):
            out_copy(n, t).start()

        @pl.when(gives)
        def _(t=t):
            for n in range(3):
                give_copy(n, t).start()

        if t == 0:
            lax.fori_loop(1, 16, a_wait, 0)
            for k in range(1, 4):
                b_copy(k).start()
        if t == 2:
            for k in range(1, 4):
                b_copy(k).wait()
            for k in range(4):
                c_copy(k).start()
    for t in range(TILES - 2, TILES):
        settle(t, [0])

    def arrive(n):
        @pl.when(takes)
        def _():
            for t in range(TILES):
                give_copy(n, t).wait_recv()

    arrive(0)
    own = pltpu.make_async_copy(emb_hbm.at[pl.ds(pl.multiple_of(first_block() * QB, QB), OWN)], own_ref, own_sem)
    own.start()
    for j in range(3):
        t = first_block() + j
        local = 3 * (z % 2) + (3 * i + j) // 8
        for half in range(2):
            weight_ref[j, :, half * 128 : half * 128 + 128] = notes[2 * (t % 8) + half, pl.ds(local, 1), :].astype(F32)
    own.wait()
    hidden = dot(own_ref[...], win_ref[...]) + line(bias_ref, 0, 8)
    hid_ref[...] = hidden
    queries = (dot(hidden.astype(BF16), wqkv_ref[:, :D_T]) + line(bias_ref, 8, 8)).astype(BF16)
    tq_ref[...] = queries * jnp.asarray(HEAD_T**-0.5, BF16)
    lax.fori_loop(0, 16, e_sent, 0)
    for t in range(TILES - 2, TILES):
        settle(t, [1, 2])
    arrive(1)
    arrive(2)
    for k in range(4):
        c_copy(k).wait()


def front(ids, table, tail, mask, splits, mats, vecs, proj, win, wqkv, ebias, types, bias):
    vmem = pl.BlockSpec(memory_space=pltpu.VMEM)
    hbm = pl.BlockSpec(memory_space=pl.ANY)
    smem = pl.BlockSpec(memory_space=pltpu.SMEM)
    dma = pltpu.SemaphoreType.DMA
    return pl.pallas_call(
        front_kernel,
        in_specs=[smem, hbm, vmem, vmem, smem, vmem, vmem, hbm, hbm, hbm, vmem, vmem, vmem],
        out_specs=[hbm, hbm, hbm, vmem, vmem, vmem, vmem, vmem],
        out_shape=[
            jax.ShapeDtypeStruct((SLOTS, D_E), BF16),
            jax.ShapeDtypeStruct((SLOTS, D_T), BF16),
            jax.ShapeDtypeStruct((D_T, SLOTS), BF16),
            jax.ShapeDtypeStruct((OWN, D_E), BF16),
            jax.ShapeDtypeStruct((OWN, D_T), F32),
            jax.ShapeDtypeStruct((OWN, D_T), BF16),
            jax.ShapeDtypeStruct((3, 1, QB), F32),
            jax.ShapeDtypeStruct((128, BLOCK, 128), BF16),
        ],
        scratch_shapes=[
            pltpu.VMEM((WHOLE, 128), BF16),
            pltpu.VMEM((WHOLE + 16, 128), F32),
            pltpu.VMEM((OWN, 128), F32),
            pltpu.VMEM((6, 128, 128), BF16),
            pltpu.VMEM((8, 128), jnp.int32),
            pltpu.VMEM((16, 8, 128), jnp.int32),
            pltpu.VMEM((BLOCK, 128), F32),
            pltpu.VMEM((BLOCK, 128), BF16),
            pltpu.VMEM((SEQ, 128), BF16),
            pltpu.VMEM((3 * 128, D_E), BF16),
            pltpu.VMEM((D_E, D_T), BF16),
            pltpu.VMEM((D_T, 3 * D_T), BF16),
            pltpu.VMEM((2, PT, D_E), BF16),
            pltpu.VMEM((2, PT, D_T), BF16),
            pltpu.VMEM((2, D_T, PT), BF16),
            dma((-(-WHOLE // CHUNK),)),
            dma((3,)),
            dma((16,)),
            dma((16,)),
            dma((16,)),
            dma((16,)),
            dma((16,)),
            dma((16,)),
            dma((4,)),
            dma((4,)),
            dma((4,)),
            dma((4,)),
            dma((3, 2)),
            dma((3, TILES)),
            dma((3, TILES)),
            dma,
        ],
        compiler_params=params(56, collective_id=0, has_side_effects=True),
        name="front",
    )(ids, table, tail, mask, splits, mats, vecs, proj, win, wqkv, ebias, types, bias)


def unpack(packed_ref, flat, win_ref, wqkv_ref, watt_ref, wup_ref, wdown_ref, wout_ref, vec_ref):
    lane = lax.broadcasted_iota(jnp.int32, (1, 128), 1)
    vec_ref[...] = jnp.zeros((48, 128), F32)
    for pair in range(64):
        both = [packed_ref[2 * pair + i].astype(F32) for i in range(2)]
        flat[88 * pair : 88 * pair + 88, :] = jnp.concatenate([b[:SHARD] for b in both], 0)
        for i in range(2):
            row, shift = divmod(47 * (2 * pair + i), 128)
            entries = both[i][SHARD : SHARD + 1, :]
            moved = pltpu.roll(entries, shift, 1) if shift else entries
            vec_ref[row : row + 1, :] += jnp.where(lane >= shift, moved, 0.0)
            if shift + 47 > 128:
                vec_ref[row + 1 : row + 2, :] += jnp.where(lane < shift, moved, 0.0)
    win_ref[...] = flat[0:512, :].astype(BF16)
    for n in range(3):
        wqkv_ref[:, n * 128 : n * 128 + 128] = flat[pl.ds(512 + n, 128, stride=3), :].astype(BF16)
    watt_ref[...] = flat[896:1024, :].astype(BF16)
    for i in range(FFN_COUNT):
        for n in range(4):
            wup_ref[i, :, n * 128 : n * 128 + 128] = flat[pl.ds(1024 + 512 * i + n, 128, stride=4), :].astype(BF16)
        wdown_ref[i] = flat[3072 + 512 * i : 3584 + 512 * i, :].astype(BF16)
    for n in range(4):
        wout_ref[:, n * 128 : n * 128 + 128] = flat[pl.ds(5120 + n, 128, stride=4), :].astype(BF16)


ST = 1024


def student_in_kernel(emb_ref, packed_ref, first_ref, sq_ref, sk_ref, sv_ref, skt_ref, svt_ref,
                      win_ref, wqkv_ref, watt_ref, wup_ref, wdown_ref, wout_ref, vec_ref, flat):
    t = pl.program_id(0)

    @pl.when(t == 0)
    def _():
        unpack(packed_ref, flat, win_ref, wqkv_ref, watt_ref, wup_ref, wdown_ref, wout_ref, vec_ref)

    emb = emb_ref[...]
    emb = jnp.where((t < SEQ // ST) | has_two(), emb, jnp.zeros_like(emb))
    first = (dot(emb, win_ref[...]) + line(vec_ref, V_IN)).astype(BF16)
    first_ref[...] = first
    qkv = dot(first, wqkv_ref[...])
    sq_ref[...] = (qkv[:, :D_S] + line(vec_ref, V_QKV)).astype(BF16)
    s_keys = (qkv[:, D_S : 2 * D_S] + line(vec_ref, V_QKV + 1)).astype(BF16)
    s_values = (qkv[:, 2 * D_S :] + line(vec_ref, V_QKV + 2)).astype(BF16)
    sk_ref[...] = s_keys
    sv_ref[...] = s_values
    skt_ref[...] = s_keys.T
    svt_ref[...] = s_values.T


def student_in(emb, packed):
    tall = jax.ShapeDtypeStruct((SLOTS, D_S), BF16)
    flat = jax.ShapeDtypeStruct((D_S, SLOTS), BF16)
    down = pl.BlockSpec((ST, D_S), lambda t: (t, 0))
    across = pl.BlockSpec((D_S, ST), lambda t: (0, t))
    made = [
        ((D_E, D_S), BF16),
        ((D_S, 3 * D_S), BF16),
        ((D_S, D_S), BF16),
        ((FFN_COUNT, D_S, FF_S), BF16),
        ((FFN_COUNT, FF_S, D_S), BF16),
        ((D_S, D_E), BF16),
        ((48, 128), F32),
    ]
    return pl.pallas_call(
        student_in_kernel,
        grid=(SLOTS // ST,),
        in_specs=[pl.BlockSpec((ST, D_E), lambda t: (t, 0)), whole(128, BLOCK, 128)],
        out_specs=[down] * 4 + [across] * 2 + [whole(*shape) for shape, _ in made],
        out_shape=[tall] * 4 + [flat] * 2 + [jax.ShapeDtypeStruct(*entry) for entry in made],
        scratch_shapes=[pltpu.VMEM((5632, 128), F32)],
        compiler_params=params(40),
        name="student_in",
    )(emb, packed)


CB = 256
SUB = 64
STEPS = 3 * HEADS


def head_lanes(values, head):
    lane = lax.broadcasted_iota(jnp.int32, (1, D_S), 1)
    return jnp.where(lane // HEAD_S == head, values, jnp.zeros_like(values))


def attend_kernel(tq_ref, tk_ref, tvt_ref, sq_ref, sk_ref, svt_ref, skt_ref, et_ref, es_ref, tmix_ref, smix_ref, stat_ref,
                  ts0, ts1, ss0, ss1, mx0, mx1, sqt0, sqt1):
    n = pl.program_id(0)
    s_factor = HEAD_S**-0.5 * LOG2E

    def work(ts, ss, mx, sqt, tr, sr, mr, sqr, scores, mixes):
        if scores:
            queries, s_queries = tq_ref[...], head_lanes(sq_ref[...], n % HEADS)
            tall = s_queries.astype(F32).T
            sqt[...] = sum(tall[h * HEAD_S : (h + 1) * HEAD_S] for h in range(HEADS))
            t_max = s_max = jnp.full((8, QB), -jnp.inf, F32)
        if mixes:
            t_top, s_top = jnp.max(mr[0], 0, keepdims=True), jnp.max(mr[1], 0, keepdims=True)
            t_off, s_off = t_top * LOG2E, s_top * s_factor
            entropy = jnp.zeros((8, QB), F32)
            ones = jnp.ones((16, CB), BF16)
            t_mix = jnp.zeros((HEAD_T + HEAD_S + 16, QB), F32)
            s_mix = jnp.zeros((HEAD_S + 16, QB), F32)
        for c in range(SEQ // CB):
            part = slice(c * CB, c * CB + CB)
            if scores:
                t_part = dot_nt(tk_ref[part, :], queries)
                ts[part, :] = t_part
                s_part = dot_nt(sk_ref[part, :], s_queries)
                ss[part, :] = s_part
                t_max = jnp.maximum(t_max, fold(t_part, jnp.max))
                s_max = jnp.maximum(s_max, fold(s_part, jnp.max))
            if mixes:
                for u in range(c * CB, c * CB + CB, SUB):
                    some = slice(u, u + SUB)
                    t_log = tr[some, :] * LOG2E - t_off
                    t_exp = jnp.exp2(t_log)
                    et_ref[0, some, :] = t_exp.astype(BF16)
                    es_ref[0, some, :] = jnp.exp2(sr[some, :] * s_factor - s_off).astype(BF16)
                    entropy = entropy + fold(t_exp * t_log)
                t_mix += dot(jnp.concatenate([tvt_ref[:, part], skt_ref[:, part], ones], 0), et_ref[0, part, :])
                s_mix += dot(jnp.concatenate([svt_ref[:, part], ones], 0), es_ref[0, part, :])
        if scores:
            mx[0], mx[1] = t_max, s_max
        if mixes:
            t_sum, s_sum = t_mix[HEAD_T + HEAD_S : HEAD_T + HEAD_S + 1], s_mix[HEAD_S : HEAD_S + 1]
            t_inv, s_inv = 1.0 / t_sum, 1.0 / s_sum
            cross = jnp.sum(sqr[...] * t_mix[HEAD_T : HEAD_T + HEAD_S], 0, keepdims=True) * s_factor - s_off * t_sum
            kl = (jnp.sum(entropy, 0, keepdims=True) - cross) * t_inv * (1.0 / LOG2E)
            stat_ref[0, 0, 0:1, :] = t_inv
            stat_ref[0, 0, 1:2, :] = s_inv
            stat_ref[0, 0, 2:3, :] = kl - jnp.log(t_sum) + jnp.log(s_sum)
            stat_ref[0, 0, 3:8, :] = jnp.zeros((5, QB), F32)
            tmix_ref[...] = (t_mix[:HEAD_T] * t_inv).T.astype(BF16)
            smix_ref[0] = s_mix[:HEAD_S] * s_inv

    even, odd = (ts0, ss0, mx0, sqt0), (ts1, ss1, mx1, sqt1)
    pl.when(n == 0)(lambda: work(*even, *odd, True, False))
    pl.when((n > 0) & (n < STEPS) & (n % 2 == 0))(lambda: work(*even, *odd, True, True))
    pl.when((n > 0) & (n < STEPS) & (n % 2 == 1))(lambda: work(*odd, *even, True, True))
    pl.when(n == STEPS)(lambda: work(*even, *odd, False, True))


def attend(tq, tk, tvt, sq, sk, svt, skt):
    now = lambda n: jnp.minimum(n, STEPS - 1)
    last = lambda n: jnp.maximum(n - 1, 0)
    block = lambda n: n // HEADS
    head = lambda n: n % HEADS
    return pl.pallas_call(
        attend_kernel,
        grid=(STEPS + 1,),
        in_specs=[
            pl.BlockSpec((QB, HEAD_T), lambda n: (block(now(n)), head(now(n)))),
            pl.BlockSpec((SEQ, HEAD_T), lambda n: (slot_of(block(now(n))), head(now(n)))),
            pl.BlockSpec((HEAD_T, SEQ), lambda n: (head(last(n)), slot_of(block(last(n))))),
            pl.BlockSpec((QB, D_S), lambda n: (first_block() + block(now(n)), 0)),
            pl.BlockSpec((SEQ, D_S), lambda n: (slot_of(block(now(n))), 0)),
            pl.BlockSpec((HEAD_S, SEQ), lambda n: (head(last(n)), slot_of(block(last(n))))),
            pl.BlockSpec((HEAD_S, SEQ), lambda n: (head(last(n)), slot_of(block(last(n))))),
        ],
        out_specs=[
            pl.BlockSpec((1, SEQ, QB), lambda n: (block(last(n)), 0, head(last(n)))),
            pl.BlockSpec((1, SEQ, QB), lambda n: (block(last(n)), 0, head(last(n)))),
            pl.BlockSpec((QB, HEAD_T), lambda n: (block(last(n)), head(last(n)))),
            pl.BlockSpec((1, HEAD_S, QB), lambda n: (block(last(n)), head(last(n)), 0)),
            pl.BlockSpec((1, 1, 8, QB), lambda n: (block(last(n)), head(last(n)), 0, 0)),
        ],
        out_shape=[
            jax.ShapeDtypeStruct((3, SEQ, HEADS * QB), BF16),
            jax.ShapeDtypeStruct((3, SEQ, HEADS * QB), BF16),
            jax.ShapeDtypeStruct((OWN, D_T), BF16),
            jax.ShapeDtypeStruct((3, D_S, QB), F32),
            jax.ShapeDtypeStruct((3, HEADS, 8, QB), F32),
        ],
        scratch_shapes=[pltpu.VMEM((SEQ, QB), F32)] * 4 + [pltpu.VMEM((2, 8, QB), F32)] * 2 + [pltpu.VMEM((HEAD_S, QB), F32)] * 2,
        compiler_params=params(40),
        name="attend",
    )(tq, tk, tvt, sq, sk, svt, skt)


FC = 1024


def teacher_kernel(mix_ref, hid_ref, emb_ref, att_ref, up_ref, down_ref, out_ref, bias_ref, gain_ref, shift_ref, target_ref, norm, low, acc):
    c = pl.program_id(0)

    @pl.when(c == 0)
    def _():
        summed = hid_ref[...] + dot(mix_ref[...], att_ref[...]) + line(bias_ref, 32, 8)
        one = layer_norm(summed, line(gain_ref, 0, 8), line(shift_ref, 0, 8))
        norm[...] = one
        low[...] = one.astype(BF16)

    rows = FC // 128
    up_bias = bias_ref[pl.ds(pl.multiple_of(40 + rows * c, 8), rows), :]
    act = gelu(dot(low[...], up_ref[...]) + line(up_bias, 0, rows)).astype(BF16)
    part = dot(act, down_ref[...])

    @pl.when(c == 0)
    def _():
        acc[...] = part

    @pl.when(c > 0)
    def _():
        acc[...] += part

    @pl.when(c == pl.num_programs(0) - 1)
    def _():
        summed = norm[...] + acc[...] + line(bias_ref, 72, 8)
        two = layer_norm(summed, line(gain_ref, 8, 8), line(shift_ref, 8, 8))
        last = emb_ref[...].astype(F32) + dot(two.astype(BF16), out_ref[...]) + line(bias_ref, 80, 4)
        target_ref[...] = layer_norm(last, line(gain_ref, 16, 4), line(shift_ref, 16, 4))


def teacher(mix, hid, emb, att, up, down, out, bias, gain, shift):
    return pl.pallas_call(
        teacher_kernel,
        grid=(FF_T // FC,),
        in_specs=[
            whole(OWN, D_T),
            whole(OWN, D_T),
            whole(OWN, D_E),
            whole(D_T, D_T),
            pl.BlockSpec((D_T, FC), lambda c: (0, c)),
            pl.BlockSpec((FC, D_T), lambda c: (c, 0)),
            whole(D_T, D_E),
            whole(84, 128),
            whole(20, 128),
            whole(20, 128),
        ],
        out_specs=whole(OWN, D_E),
        out_shape=jax.ShapeDtypeStruct((OWN, D_E), F32),
        scratch_shapes=[pltpu.VMEM((OWN, D_T), F32), pltpu.VMEM((OWN, D_T), BF16), pltpu.VMEM((OWN, D_T), F32)],
        compiler_params=params(40),
        name="teacher",
    )(mix, hid, emb, att, up, down, out, bias, gain, shift)


def student_kernel(emb_ref, smix_ref, target_ref, weight_ref, win_ref, watt_ref, wup_ref, wdown_ref, wout_ref, vec_ref,
                   grad_ref, vgrad_ref, dsum_ref, dmix_ref, part_ref, states, inners, outers):

    def put(r, value):
        for i in range(value.shape[1] // 128):
            vgrad_ref[r + i : r + i + 1, :] = value[:, i * 128 : i * 128 + 128]

    total = lambda v: jnp.sum(v.astype(F32), 0, keepdims=True)
    emb = emb_ref[...]
    source = emb.astype(F32)
    first = dot(emb, win_ref[...]) + line(vec_ref, V_IN)
    mixed = jnp.concatenate([smix_ref[j].T for j in range(3)], 0).astype(BF16)
    branch = dot(mixed, watt_ref[...]) + line(vec_ref, V_ATT)
    state = line(vec_ref, V_AGAIN) * (first + branch) + line(vec_ref, V_ASHIFT)
    for i in range(FFN_COUNT):
        states[i] = state
        inner = dot(state.astype(BF16), wup_ref[i]) + line(vec_ref, V_UP + 4 * i, 4)
        inners[i] = inner
        act = gelu(inner).astype(BF16)
        pre = state + dot(act, wdown_ref[i]) + line(vec_ref, V_DOWN + i)
        outers[i] = pre
        state = line(vec_ref, V_FGAIN + i) * pre + line(vec_ref, V_FSHIFT + i)
    state_low = state.astype(BF16)
    summed = source + dot(state_low, wout_ref[...]) + line(vec_ref, V_OUT, 4)
    diff = line(vec_ref, V_OGAIN, 4) * summed + line(vec_ref, V_OSHIFT, 4) - target_ref[...]
    weight = jnp.concatenate([jnp.broadcast_to(weight_ref[j], (8, QB)).T[:, 0:1] for j in range(3)], 0)
    loss = jnp.sum(weight * jnp.sum(diff * diff, 1, keepdims=True)) * (1.0 / D_E)
    count = jnp.sum(weight)
    d_result = (weight * (2.0 / D_E)) * diff
    put(V_OGAIN, total(d_result * summed))
    put(V_OSHIFT, total(d_result))
    d_output = (d_result * line(vec_ref, V_OGAIN, 4)).astype(BF16)
    out_g = dot_tn(state_low, d_output)
    for n in range(4):
        grad_ref[pl.ds(4224 + n, 128, stride=4), :] = out_g[:, n * 128 : n * 128 + 128]
    put(V_OUT, total(d_output))
    d_state = dot_nt(d_output, wout_ref[...])
    for i in reversed(range(FFN_COUNT)):
        inner = inners[i]
        put(V_FGAIN + i, total(d_state * outers[i]))
        put(V_FSHIFT + i, total(d_state))
        d_sum = d_state * line(vec_ref, V_FGAIN + i)
        d_outer = d_sum.astype(BF16)
        half = 0.5 * (1.0 + lax.erf(inner * 0.7071067811865476))
        act = (inner * half).astype(BF16)
        slope = half + inner * jnp.exp(-0.5 * inner * inner) * 0.3989422804014327
        grad_ref[2176 + 512 * i : 2176 + 512 * (i + 1), :] = dot_tn(act, d_outer)
        d_inner = (dot_nt(d_outer, wdown_ref[i]) * slope).astype(BF16)
        up_g = dot_tn(states[i].astype(BF16), d_inner)
        for n in range(4):
            grad_ref[pl.ds(128 + 512 * i + n, 128, stride=4), :] = up_g[:, n * 128 : n * 128 + 128]
        put(V_UP + 4 * i, total(d_inner))
        put(V_DOWN + i, total(d_outer))
        d_state = d_sum + dot_nt(d_inner, wup_ref[i])
    put(V_AGAIN, total(d_state * (first + branch)))
    put(V_ASHIFT, total(d_state))
    d_sum = d_state * line(vec_ref, V_AGAIN)
    d_branch = d_sum.astype(BF16)
    grad_ref[0:128, :] = dot_tn(mixed, d_branch)
    put(V_ATT, total(d_branch))
    dsum_ref[...] = d_sum
    dmix_ref[...] = dot_nt(d_branch, watt_ref[...]).astype(BF16)
    for r in (0, 1, 2, 3, 47):
        vgrad_ref[r : r + 1, :] = jnp.zeros((1, 128), F32)
    row = lax.broadcasted_iota(jnp.int32, (8, 128), 0)
    lane = lax.broadcasted_iota(jnp.int32, (8, 128), 1)
    part_ref[...] = jnp.where((row == 0) & (lane == 0), loss, 0.0) + jnp.where((row == 0) & (lane == 1), count, 0.0)


def student(emb, smix, target, weight, win, watt, wup, wdown, wout, vecs):
    return pl.pallas_call(
        student_kernel,
        grid=(1,),
        in_specs=[
            whole(OWN, D_E),
            whole(3, D_S, QB),
            whole(OWN, D_E),
            whole(3, 1, QB),
            whole(D_E, D_S),
            whole(D_S, D_S),
            whole(FFN_COUNT, D_S, FF_S),
            whole(FFN_COUNT, FF_S, D_S),
            whole(D_S, D_E),
            whole(48, 128),
        ],
        out_specs=[whole(4736, 128), whole(48, 128), whole(OWN, D_S), whole(OWN, D_S), whole(8, 128)],
        out_shape=[
            jax.ShapeDtypeStruct((4736, 128), F32),
            jax.ShapeDtypeStruct((48, 128), F32),
            jax.ShapeDtypeStruct((OWN, D_S), F32),
            jax.ShapeDtypeStruct((OWN, D_S), BF16),
            jax.ShapeDtypeStruct((8, 128), F32),
        ],
        scratch_shapes=[
            pltpu.VMEM((FFN_COUNT, OWN, D_S), F32),
            pltpu.VMEM((FFN_COUNT, OWN, FF_S), F32),
            pltpu.VMEM((FFN_COUNT, OWN, D_S), F32),
        ],
        compiler_params=params(40),
        name="student",
    )(emb, smix, target, weight, win, watt, wup, wdown, wout, vecs)


KB = 1024


def back_kernel(et_ref, es_ref, stat_ref, smix_ref, dmix_ref, weight_ref, sq_ref, sv_ref, skt_ref, dsum_ref, emb_ref, first_ref,
                wqkv_ref, vgrad_ref, part_in, late_ref, *rest):
    state_refs, rest = rest[:6], rest[6:]
    new_refs, rest = rest[:4], rest[4:]
    (dkv, dqt, ds, dq, dfirst, dmt, dmz, sqd, rows, flat, vecs, kls, block_ref, sem), buffers = rest[:14], rest[14:]
    j, kb = pl.program_id(0), pl.program_id(1)
    s_scale = HEAD_S**-0.5
    late = pltpu.make_async_copy(late_ref, flat.at[896:5632], sem)

    @pl.when((j == 0) & (kb == 0))
    def _():
        greet()
        late.start()
        dkv[...] = jnp.zeros_like(dkv)
        kls[...] = jnp.zeros_like(kls)

    @pl.when(kb == 0)
    def _():
        quarter = weight_ref[0] * (1.0 / HEADS)
        wide = dmix_ref[...].astype(F32)
        tall = wide.T
        place = lax.broadcasted_iota(jnp.int32, (D_S, 1), 0) // HEAD_S
        for h in range(HEADS):
            own = slice(h * HEAD_S, h * HEAD_S + HEAD_S)
            mine = slice(h * QB, h * QB + QB)
            t_inv, s_inv = stat_ref[0, h, 0:1, :], stat_ref[0, h, 1:2, :]
            kls[0:1, :] += quarter * stat_ref[0, h, 2:3, :]
            row_dot = jnp.sum(tall[own] * smix_ref[0, own, :], 0, keepdims=True)
            rows[h, 0:1, :] = row_dot - quarter
            rows[h, 1:2, :] = s_inv
            rows[h, 2:3, :] = quarter * t_inv
            dmt[h] = jnp.where(place == h, tall, 0.0).astype(BF16)
            dmz[mine, :] = head_lanes(wide * stat_ref[0, h].T[:, 1:2], h).astype(BF16)
            sqd[mine, :] = head_lanes(sq_ref[...], h)
        dqt[...] = jnp.zeros_like(dqt)

    here = pl.ds(pl.multiple_of(slot_of(j) * SEQ + kb * KB, KB), KB)
    dkv[here, D_S:] += dot(es_ref[0], dmz[...])
    for h in range(HEADS):
        lanes = slice(h * QB, h * QB + QB)
        for c in range(KB // 256):
            part = slice(c * 256, c * 256 + 256)
            d_probs = dot(sv_ref[part, :], dmt[h])
            s_exp, t_exp = es_ref[0, part, lanes].astype(F32), et_ref[0, part, lanes].astype(F32)
            d_scores = (d_probs - rows[h, 0:1, :]) * rows[h, 1:2, :] * s_exp - t_exp * rows[h, 2:3, :]
            ds[part, lanes] = d_scores.astype(BF16)
        own = slice(h * HEAD_S, h * HEAD_S + HEAD_S)
        dqt[own, :] += dot(skt_ref[own, :], ds[:, lanes])
    dkv[here, :D_S] += dot(ds[...], sqd[...])

    @pl.when(kb == pl.num_programs(1) - 1)
    def _():
        dq[pl.ds(pl.multiple_of(j * QB, QB), QB), :] = (dqt[...] * s_scale).T

    @pl.when((j == 2) & (kb == pl.num_programs(1) - 1))
    def _():
        qkv_w = wqkv_ref[...]
        dq_low = dq[...].astype(BF16)
        own = pl.ds(pl.multiple_of(first_block() * QB, QB), OWN)
        q_grad = dot_tn(first_ref[own, :], dq_low)
        own_part = dsum_ref[...] + dot_nt(dq_low, qkv_w[:, :D_S])
        kv_grad = jnp.zeros((D_S, 2 * D_S), F32)
        kv_bias = jnp.zeros((1, 2 * D_S), F32)
        for c in range(8):
            part = pl.ds(c * 512, 512)
            wide = dkv[part, :]
            low = jnp.concatenate([(wide[:, :D_S] * s_scale).astype(BF16), wide[:, D_S:].astype(BF16)], 1)
            kv_grad += dot_tn(first_ref[part, :], low)
            kv_bias += jnp.sum(low.astype(F32), 0, keepdims=True)
            dfirst[part, :] = dot_nt(low, qkv_w[:, D_S:])
        dfirst[own, :] += own_part
        in_grad = jnp.zeros((D_S, D_E), F32)
        in_bias = jnp.zeros((1, D_S), F32)
        two = has_two()
        for c in range(8):
            part = pl.ds(c * 512, 512)
            low = dfirst[part, :].astype(BF16)
            emb = emb_ref[part, :]
            if c >= 4:
                emb = jnp.where(two, emb, jnp.zeros_like(emb))
            in_grad += dot_tn(low, emb)
            in_bias += jnp.sum(low.astype(F32), 0, keepdims=True)
        flat[0:512, :] = in_grad.T
        flat[pl.ds(512, 128, stride=3), :] = q_grad
        flat[pl.ds(513, 128, stride=3), :] = kv_grad[:, :D_S]
        flat[pl.ds(514, 128, stride=3), :] = kv_grad[:, D_S:]
        vecs[...] = vgrad_ref[...]
        vecs[0:1, :] = in_bias
        vecs[1:2, :] = jnp.sum(dq_low.astype(F32), 0, keepdims=True)
        vecs[2:3, :] = kv_bias[:, :D_S]
        vecs[3:4, :] = kv_bias[:, D_S:]
        late.wait()
        lane = lax.broadcasted_iota(jnp.int32, (1, 128), 1)
        rest = jnp.zeros((BLOCK - SHARD - 1, 128), F32)
        for pair in range(64):
            both = flat[88 * pair : 88 * pair + 88, :]
            for i in range(2):
                owner = 2 * pair + i
                row, shift = divmod(47 * owner, 128)
                entries = vecs[row : row + 1, :]
                if shift + 47 > 128:
                    entries = jnp.where(lane >= shift, entries, vecs[row + 1 : row + 2, :])
                if shift:
                    entries = pltpu.roll(entries, 128 - shift, 1)
                entries = jnp.where(lane < 47, entries, 0.0)
                mine = both[SHARD * i : SHARD * (i + 1)]
                block_ref[owner // 32, owner // 16 % 2, owner % 16] = jnp.concatenate([mine, entries, rest], 0).astype(BF16)
        kl = jnp.sum(kls[0:1, :], keepdims=True)
        corner = (lax.broadcasted_iota(jnp.int32, (8, 128), 0) == 0) & (lax.broadcasted_iota(jnp.int32, (8, 128), 1) == 0)
        update(block_ref, part_in[...] + jnp.where(corner, kl, 0.0), state_refs, new_refs, buffers)


def back(et, es, stat, smix, dmix, weight, sq, sv, skt, dsum, emb, first, wqkv, vgrad, part, late, *state):
    count = SEQ // KB
    place = lambda j, k: slot_of(j) * count + k
    shard = jax.ShapeDtypeStruct((BLOCK, 128), F32)
    dma = pltpu.SemaphoreType.DMA
    return pl.pallas_call(
        back_kernel,
        grid=(3, count),
        in_specs=[
            pl.BlockSpec((1, KB, HEADS * QB), lambda j, k: (j, k, 0)),
            pl.BlockSpec((1, KB, HEADS * QB), lambda j, k: (j, k, 0)),
            pl.BlockSpec((1, HEADS, 8, QB), lambda j, k: (j, 0, 0, 0)),
            pl.BlockSpec((1, D_S, QB), lambda j, k: (j, 0, 0)),
            pl.BlockSpec((QB, D_S), lambda j, k: (j, 0)),
            pl.BlockSpec((1, 1, QB), lambda j, k: (j, 0, 0)),
            pl.BlockSpec((QB, D_S), lambda j, k: (first_block() + j, 0)),
            pl.BlockSpec((KB, D_S), lambda j, k: (place(j, k), 0)),
            pl.BlockSpec((D_S, KB), lambda j, k: (0, place(j, k))),
            whole(OWN, D_S),
            whole(SLOTS, D_E),
            whole(SLOTS, D_S),
            whole(D_S, 3 * D_S),
            whole(48, 128),
            whole(8, 128),
            pl.BlockSpec(memory_space=pl.ANY),
        ]
        + [whole(SHARD, 128), whole(1, 47)] * 3,
        out_specs=[whole(BLOCK, 128)] * 3 + [whole(8, 128)],
        out_shape=[shard, shard, shard, jax.ShapeDtypeStruct((8, 128), F32)],
        scratch_shapes=[
            pltpu.VMEM((SLOTS, 2 * D_S), F32),
            pltpu.VMEM((D_S, QB), F32),
            pltpu.VMEM((KB, HEADS * QB), BF16),
            pltpu.VMEM((OWN, D_S), F32),
            pltpu.VMEM((SLOTS, D_S), F32),
            pltpu.VMEM((HEADS, D_S, QB), BF16),
            pltpu.VMEM((HEADS * QB, D_S), BF16),
            pltpu.VMEM((HEADS * QB, D_S), BF16),
            pltpu.VMEM((HEADS, 8, QB), F32),
            pltpu.VMEM((5632, 128), F32),
            pltpu.VMEM((48, 128), F32),
            pltpu.VMEM((8, QB), F32),
            pltpu.VMEM((4, 2, 16, BLOCK, 128), BF16),
            dma,
            pltpu.VMEM((3, BLOCK, 128), F32),
            pltpu.VMEM((4, 16, BLOCK, 128), BF16),
            pltpu.VMEM((BLOCK, 128), F32),
            pltpu.VMEM((64, BLOCK, 128), BF16),
            pltpu.VMEM((64, BLOCK, 128), BF16),
            pltpu.VMEM((2, 2, 8, 128), F32),
            pltpu.VMEM((2, 16, 8, 128), F32),
            pltpu.VMEM((2, 8, 8, 128), F32),
            dma((2,)),
            dma((64,)),
            dma((64,)),
            dma((2, 16)),
            dma((2, 16)),
            dma((2, 8)),
            dma((2, 8)),
        ],
        compiler_params=params(44, collective_id=1, has_side_effects=True),
        name="back",
    )(et, es, stat, smix, dmix, weight, sq, sv, skt, dsum, emb, first, wqkv, vgrad, part, late, *state)


def chip(k):
    dp, fs = lax.axis_index("dp"), lax.axis_index("fsdp")
    return (2 * ((dp // 2 + k // 16) % 4) + dp % 2, (fs + k) % 16)


def greet():
    dp, fs = lax.axis_index("dp"), lax.axis_index("fsdp")
    barrier = pltpu.get_barrier_semaphore()

    def signal(k, _):
        pl.semaphore_signal(barrier, inc=1, device_id=chip(k), device_id_type=MESH)
        return 0

    lax.fori_loop(1, 64, signal, 0)
    for k in range(4):
        other = (2 * ((dp // 2 + k) % 4) + 1 - dp % 2, fs)
        pl.semaphore_signal(barrier, inc=1, device_id=other, device_id_type=MESH)


def update(g_ref, part, state_refs, new_refs, buffers):
    master_mat, master_vec, first_mat, first_vec, second_mat, second_vec = state_refs
    new_ref, newf_ref, news_ref, scal_ref = new_refs
    (packs, half_in, mine, block_out, blocks_in, tile_out, tiles_f, tiles_d,
     half_sems, block_send, block_recv, f_send, f_recv, d_send, d_recv) = buffers
    dp, fs = lax.axis_index("dp"), lax.axis_index("fsdp")
    x, core = dp // 2, dp % 2
    sibling = (2 * x + 1 - core, fs)
    barrier = pltpu.get_barrier_semaphore()
    packs[...] = jnp.zeros_like(packs)
    for i, (mat, vec) in enumerate([(master_mat, master_vec), (first_mat, first_vec), (second_mat, second_vec)]):
        packs[i, 0:SHARD, :] = mat[...]
        packs[i, SHARD : SHARD + 1, 0:47] = vec[...]
    pl.semaphore_wait(barrier, 67)
    swap = pltpu.make_async_remote_copy(
        g_ref.at[:, 1 - core], half_in, half_sems.at[0], half_sems.at[1], device_id=sibling, device_id_type=MESH
    )
    swap.start()
    swap.wait()

    def join(i, _):
        summed = g_ref[i // 16, core, i % 16].astype(F32) + half_in[i // 16, i % 16].astype(F32)
        block_out[i] = summed.astype(BF16)
        return 0

    lax.fori_loop(0, 64, join, 0)
    mine[...] = g_ref[x, core, fs].astype(F32) + half_in[x, fs].astype(F32)

    def block_copy(k):
        xk, fk = (x + k // 16) % 4, (fs + k) % 16
        return pltpu.make_async_remote_copy(
            block_out.at[xk * 16 + fk], blocks_in.at[k], block_send.at[k], block_recv.at[k],
            device_id=(2 * xk + core, fk), device_id_type=MESH,
        )

    def start(k, _):
        block_copy(k).start()
        return 0

    lax.fori_loop(1, 64, start, 0)

    def gather(k, _):
        block_copy(k).wait()
        mine[...] += blocks_in[k].astype(F32)
        return 0

    lax.fori_loop(1, 64, gather, 0)

    row = lax.broadcasted_iota(jnp.int32, (BLOCK, 128), 0)
    lane8 = lax.broadcasted_iota(jnp.int32, (8, 128), 1)
    row8 = lax.broadcasted_iota(jnp.int32, (8, 128), 0)
    place = (dp * 16 + fs) * SHARD + row
    is_matrix = row < SHARD
    bounds = [0]
    for rows in MAT_ROWS:
        bounds.append(bounds[-1] + rows)
    members = [is_matrix & (place >= bounds[i]) & (place < bounds[i + 1]) for i in range(6)]

    def everyone(tile, turn):
        tile_out[turn, 0] = tile
        tiles_f[turn, fs] = tile

        def f_copy(k):
            return pltpu.make_async_remote_copy(
                tile_out.at[turn, 0], tiles_f.at[turn, fs], f_send.at[turn, k], f_recv.at[turn, k],
                device_id=(dp, (fs + k) % 16), device_id_type=MESH,
            )

        def d_copy(k):
            return pltpu.make_async_remote_copy(
                tile_out.at[turn, 1], tiles_d.at[turn, dp], d_send.at[turn, k], d_recv.at[turn, k],
                device_id=((dp + k) % 8, fs), device_id_type=MESH,
            )

        for k in range(1, 16):
            f_copy(k).start()
        for k in range(1, 16):
            f_copy(k).wait()
        total = tiles_f[turn, 0]
        for k in range(1, 16):
            total = total + tiles_f[turn, k]
        tile_out[turn, 1] = total
        tiles_d[turn, dp] = total
        for k in range(1, 8):
            d_copy(k).start()
        for k in range(1, 8):
            d_copy(k).wait()
        total = tiles_d[turn, 0]
        for k in range(1, 8):
            total = total + tiles_d[turn, k]
        return total

    def entry(tile, i):
        return jnp.sum(jnp.where((row8 == 0) & (lane8 == i), tile, 0.0), keepdims=True)

    def tile_of(values):
        tile = jnp.zeros((8, 128), F32)
        for i, value in values:
            tile += jnp.where((row8 == 0) & (lane8 == i), value, 0.0)
        return tile

    grad = mine[...]
    master = packs[0]
    squares = master * master
    tile = part + tile_of(
        [(2, jnp.sum(grad * grad, keepdims=True))]
        + [(3 + i, jnp.sum(jnp.where(members[i], squares, 0.0), keepdims=True)) for i in range(6)]
    )
    tile = everyone(tile, 0)
    loss, count = entry(tile, 0), entry(tile, 1)
    inverse = 1.0 / count
    norm = jnp.sqrt(entry(tile, 2)) * inverse
    factor = CLIP_NORM / jnp.maximum(norm, CLIP_NORM)
    grad = grad * inverse * factor
    first = BETA_ONE * packs[1] + (1.0 - BETA_ONE) * grad
    second = BETA_TWO * packs[2] + (1.0 - BETA_TWO) * grad * grad
    newf_ref[...] = first
    news_ref[...] = second
    ratio = first / (1.0 - BETA_ONE**STEP) / (jnp.sqrt(second / (1.0 - BETA_TWO**STEP)) + ADAM_EPS)
    ratio = ratio + jnp.where(is_matrix, WEIGHT_DECAY * master, 0.0)
    squares = ratio * ratio
    steps = everyone(tile_of([(3 + i, jnp.sum(jnp.where(members[i], squares, 0.0), keepdims=True)) for i in range(6)]), 1)
    trust = jnp.ones((BLOCK, 128), F32)
    for i in range(6):
        trust = jnp.where(members[i], jnp.sqrt(entry(tile, 3 + i)) / jnp.sqrt(entry(steps, 3 + i)), trust)
    new_ref[...] = master - LEARN_RATE * (trust * ratio)
    scal_ref[...] = tile_of([(0, loss), (1, count), (2, norm)])


def finish_kernel(new_ref, newf_ref, news_ref, scal_ref, loss, count, norm, m0, m1, m2, v0, v1, v2):
    for source, mat, vec in ((new_ref, m0, v0), (newf_ref, m1, v1), (news_ref, m2, v2)):
        mat[...] = source[0:SHARD, :]
        vec[...] = source[SHARD : SHARD + 1, 0:47]
    for i, out in enumerate((loss, count, norm)):
        out[...] = scal_ref[0:1, i : i + 1]


def finish(*made):
    vmem = pl.BlockSpec(memory_space=pltpu.VMEM)
    shape = lambda *dims: jax.ShapeDtypeStruct(dims, F32)
    return pl.pallas_call(
        finish_kernel,
        in_specs=[vmem] * 4,
        out_specs=[vmem] * 9,
        out_shape=[shape(1, 1)] * 3 + [shape(SHARD, 128)] * 3 + [shape(1, 47)] * 3,
        name="finish",
    )(*made)


def per_device(
    token_ids,
    splits,
    valid_mask,
    embed_table,
    embed_proj,
    embed_bias,
    type_table,
    teach_in,
    teach_qkv,
    teach_att,
    teach_up,
    teach_down,
    teach_out,
    teach_bias,
    teach_gain,
    teach_shift,
    matrices,
    vectors,
    matrix_first,
    matrix_second,
    vector_first,
    vector_second,
):
    mat = lambda v: v.reshape(SHARD, 128)
    vec = lambda v: v.reshape(1, 47)
    rows_128 = lambda v: v.reshape(-1, 128)
    bias = rows_128(teach_bias)
    emb, t_keys, t_values, own_emb, hidden, t_queries, weights, packed = front(
        token_ids, embed_table, jnp.pad(embed_table[WHOLE:], ((0, WHOLE + 16 - VOCAB), (0, 0))), valid_mask, splits, mat(matrices), vec(vectors), embed_proj, teach_in, teach_qkv,
        rows_128(embed_bias), type_table, bias,
    )
    first, s_q, s_k, s_v, s_kt, s_vt, in_w, qkv_w, att_w, up_w, down_w, out_w, vecs = student_in(emb, packed)
    et, es, t_mixed, s_mixed, stat = attend(t_queries, t_keys, t_values, s_q, s_k, s_vt, s_kt)
    target = teacher(
        t_mixed, hidden, own_emb, teach_att, teach_up, teach_down, teach_out, bias, rows_128(teach_gain), rows_128(teach_shift)
    )
    late, vgrads, d_sum, d_mixed, part = student(
        own_emb, s_mixed, target, weights, in_w, att_w, up_w, down_w, out_w, vecs
    )
    made = back(
        et, es, stat, s_mixed, d_mixed, weights, s_q, s_v, s_kt, d_sum, emb, first, qkv_w, vgrads, part, late,
        mat(matrices), vec(vectors), mat(matrix_first), vec(vector_first), mat(matrix_second), vec(vector_second),
    )
    loss, count, norm, m0, m1, m2, v0, v1, v2 = finish(*made)
    flat = lambda v: v.reshape(-1)
    scalar = lambda v: v.reshape(())
    return (
        scalar(loss), scalar(count), scalar(norm), flat(m0), flat(m1), flat(m2), flat(v0), flat(v1), flat(v2),
    )


def solution(mesh):
    both = P(("dp", "fsdp"))
    return jax.shard_map(
        per_device,
        mesh=mesh,
        in_specs=(P("dp", "fsdp"), P("dp"), P("dp", "fsdp")) + (P(),) * 13 + (both,) * 6,
        out_specs=(P(), P(), P(), both, both, both, both, both, both),
        check_vma=False,
    )
```

```python
import functools
import math

import jax
import jax.numpy as jnp
from jax import lax
from jax.experimental import pallas as pl
from jax.experimental.pallas import tpu as pltpu
from jax.sharding import PartitionSpec as P

D_E = 512
D_T = 1024
FF_T = 4096
D_S = 128
FF_S = 512
HEADS = 4
FFN_COUNT = 4
STEP = 5
HEAD_T = 256
HEAD_S = 32
SEQ = 2048
QB = 256
OWN = 3 * QB
SLOTS = 2 * SEQ

CLIP_NORM = 0.05
BETA_ONE = 0.9
BETA_TWO = 0.999
LEARN_RATE = 0.3
WEIGHT_DECAY = 0.01
ADAM_EPS = 1e-06

F32 = jnp.float32
BF16 = jnp.bfloat16
LOG2E = 1.4426950408889634
MESH = pl.DeviceIdType.MESH

MAT_ROWS = (512, 384, 128, 2048, 2048, 512)
SHARD = 44
BLOCK = 48
(V_IN, V_QKV, V_ATT, V_AGAIN, V_ASHIFT, V_UP, V_DOWN, V_FGAIN, V_FSHIFT, V_OUT, V_OGAIN, V_OSHIFT) = (
    0, 1, 4, 5, 6, 7, 23, 27, 31, 35, 39, 43)


def dot(left, right):
    return jnp.dot(left, right, preferred_element_type=F32)


def dot_nt(left, right):
    return lax.dot_general(left, right, (((1,), (1,)), ((), ())), preferred_element_type=F32)


def dot_tn(left, right):
    return lax.dot_general(left, right, (((0,), (0,)), ((), ())), preferred_element_type=F32)


def layer_norm(values, gain, shift):
    center = values - jnp.mean(values, -1, keepdims=True)
    spread = jnp.mean(center * center, -1, keepdims=True)
    return center * lax.rsqrt(spread + 1e-05) * gain + shift


def gelu(values):
    return 0.5 * values * (1.0 + lax.erf(values * 0.7071067811865476))


def params(mib, **more):
    return pltpu.CompilerParams(vmem_limit_bytes=mib * 2**20, **more)


def whole(*shape):
    return pl.BlockSpec(shape, lambda *_: (0,) * len(shape))


def line(ref, row, count=1):
    if count == 1:
        return ref[row : row + 1, :]
    return jnp.concatenate([ref[row + i : row + i + 1, :] for i in range(count)], 1)


def fold(values, op=jnp.sum):
    return op(values.reshape(values.shape[0] // 8, 8, values.shape[1]), 0)


def spots():
    dp, fs = lax.axis_index("dp"), lax.axis_index("fsdp")
    return dp // 2, dp % 2, fs // 4, fs % 4


def place_in_group():
    _, core, _, y = spots()
    return 2 * y + core


def first_block():
    return (3 * place_in_group()) % 8


def slot_of(j):
    return (first_block() + j) // 8


def has_two():
    i = place_in_group()
    return (i == 2) | (i == 5)


PT = 512
TILES = SEQ // PT


CHUNK = 2048
VOCAB = 30522
WHOLE = VOCAB // 16 * 16


def front_kernel(ids_ref, table_hbm, tail_ref, mask_ref, splits_ref, mats_ref, vecs_ref, proj_hbm, win_hbm, wqkv_hbm, ebias_ref,
                 types_ref, bias_ref, emb_hbm, k_hbm, vt_hbm, own_hbm, hid_hbm, tq_ref, weight_ref, params_hbm,
                 own_ref, hid_ref, params_ref, table_low, table, picked, e_ref, note, notes, wide, block, e_all, proj_ref, win_ref, wqkv_ref, emb_t, k_t, vt_t,
                 t_sem, load, e_send, e_recv, n_send, n_recv, a_send, a_recv, b_send, b_recv, c_send, c_recv,
                 out, s_send, s_recv, own_sem, last_sem):
    dp, me = lax.axis_index("dp"), lax.axis_index("fsdp")
    x, core, z, y = spots()
    i = 2 * y + core
    sibling = (2 * x + 1 - core, me)
    source_dp = 2 * x + z // 2
    is_source = z // 2 == core
    loads = [
        pltpu.make_async_copy(hbm, ref, load.at[n])
        for n, (hbm, ref) in enumerate([(proj_hbm, proj_ref), (win_hbm, win_ref), (wqkv_hbm, wqkv_ref)])
    ]
    barrier = pltpu.get_barrier_semaphore()

    def signal(device):
        pl.semaphore_signal(barrier, inc=1, device_id=device, device_id_type=MESH)

    def greet_source(f, _):
        @pl.when(jnp.logical_not(is_source & (f == me)))
        def _():
            signal((source_dp, f))

        return 0

    def greet_plane(k, _):
        signal((dp, (me + k) % 16))
        return 0

    lax.fori_loop(0, 16, greet_source, 0)
    lax.fori_loop(1, 16, greet_plane, 0)
    for k in range(1, 4):
        signal((2 * ((x + k) % 4) + core, me))
    signal(sibling)
    chunks = [(c, min(CHUNK, WHOLE - c)) for c in range(0, WHOLE, CHUNK)]
    table_copies = [
        pltpu.make_async_copy(table_hbm.at[pl.ds(c, size)], table_low.at[pl.ds(c, size)], t_sem.at[n])
        for n, (c, size) in enumerate(chunks)
    ]
    for copy in table_copies:
        copy.start()

    lane = lax.broadcasted_iota(jnp.int32, (1, 128), 1)
    note[0:6, :] = mask_ref[...]
    line_of_splits = jnp.zeros((1, 128), jnp.int32)
    for r in range(6):
        line_of_splits = jnp.where(lane == r, splits_ref[r], line_of_splits)
    note[6:7, :] = line_of_splits
    note[7:8, :] = jnp.zeros((1, 128), jnp.int32)
    wide[...] = jnp.zeros((BLOCK, 128), F32)
    wide[0:SHARD, :] = mats_ref[...]
    wide[SHARD : SHARD + 1, 0:47] = vecs_ref[...]
    block[...] = wide[...].astype(BF16)
    params_ref[dp * 16 + me] = block[...]
    main = (3 * i + 1) // 8
    for copy, (c, size) in zip(table_copies, chunks):
        copy.wait()
        table[c : c + size, :] = table_low[c : c + size, :].astype(F32)
    for copy in loads:
        copy.start()
    table[WHOLE:VOCAB, :] = tail_ref[...].astype(F32)

    def pick(g, _):
        for u in range(16):
            token = ids_ref[g // 8, g % 8 * 16 + u]
            picked[pl.ds(g * 16 + u, 1), :] = table[pl.ds(token, 1), :]
        return 0

    lax.fori_loop(0, 48, pick, 0)
    for r in range(6):
        e_ref[r] = picked[128 * r : 128 * r + 128, :].astype(BF16)

    @pl.when(is_source)
    def _():
        e_all[pl.ds(pl.multiple_of(me * 128, 128), 128), :] = e_ref[3 * (z % 2) + main]
        notes[me] = note[...]

    pl.semaphore_wait(barrier, jnp.where(is_source, 15, 16) + 15 + 3 + 1)

    def a_copy(k):
        return pltpu.make_async_remote_copy(
            block, params_ref.at[dp * 16 + me], a_send.at[k], a_recv.at[k], device_id=(dp, (me + k) % 16), device_id_type=MESH
        )

    def b_copy(k):
        mine = params_ref.at[pl.ds(dp * 16, 16)]
        return pltpu.make_async_remote_copy(
            mine, mine, b_send.at[k], b_recv.at[k], device_id=(2 * ((x + k) % 4) + core, me), device_id_type=MESH
        )

    def c_copy(k):
        mine = params_ref.at[pl.ds((2 * k + core) * 16, 16)]
        return pltpu.make_async_remote_copy(mine, mine, c_send.at[k], c_recv.at[k], device_id=sibling, device_id_type=MESH)

    def a_start(k, _):
        a_copy(k).start()
        return 0

    def a_wait(k, _):
        a_copy(k).wait()
        return 0

    def e_copy(d, noted):
        zd, yd, cd = 2 * core + d // 8, d // 2 % 4, d % 2
        where = dict(device_id=(2 * x + cd, 4 * zd + yd), device_id_type=MESH)
        if noted:
            return pltpu.make_async_remote_copy(note, notes.at[me], n_send.at[d], n_recv.at[me], **where)
        row = 3 * (d // 8) + (3 * (2 * yd + cd) + 1) // 8
        here = pl.ds(pl.multiple_of(me * 128, 128), 128)
        return pltpu.make_async_remote_copy(e_ref.at[row], e_all.at[here], e_send.at[d], e_recv.at[me], **where)

    def is_other(d):
        return jnp.logical_not((2 * core + d // 8 == z) & (d // 2 % 4 == y) & (d % 2 == core))

    def e_start(n, _):
        d = (n + me) % 16

        @pl.when(is_other(d))
        def _():
            e_copy(d, False).start()
            e_copy(d, True).start()

        return 0

    lax.fori_loop(1, 16, a_start, 0)
    lax.fori_loop(0, 16, e_start, 0)

    def e_sent(d, _):
        @pl.when(is_other(d))
        def _():
            e_copy(d, False).wait_send()
            e_copy(d, True).wait_send()

        return 0

    def e_arrived(f, _):
        @pl.when(jnp.logical_not(is_source & (f == me)))
        def _():
            where = dict(device_id=(source_dp, f), device_id_type=MESH)
            there = pl.ds(pl.multiple_of(f * 128, 128), 128)
            pltpu.make_async_remote_copy(e_ref.at[0], e_all.at[there], e_send.at[0], e_recv.at[f], **where).wait_recv()
            pltpu.make_async_remote_copy(note, notes.at[f], n_send.at[0], n_recv.at[f], **where).wait_recv()

        return 0

    gives = ((y == 1) & (core == 1)) | ((y == 2) & (core == 0))
    takes = has_two()
    main_slot = jnp.where(i == 5, 1, 0)
    his_slot = jnp.where(y == 1, 1, 0)

    made = ((emb_t, emb_hbm), (k_t, k_hbm), (vt_t, vt_hbm))

    def target(n, slot, t):
        rows = pl.ds(pl.multiple_of(slot * SEQ + t * PT, PT), PT)
        return made[n][1].at[:, rows] if n == 2 else made[n][1].at[rows]

    def out_copy(n, t):
        return pltpu.make_async_copy(made[n][0].at[t % 2], target(n, main_slot, t), out.at[n, t % 2])

    def give_copy(n, t):
        return pltpu.make_async_remote_copy(
            made[n][0].at[t % 2], target(n, his_slot, t), s_send.at[n, t], s_recv.at[n, t],
            device_id=sibling, device_id_type=MESH,
        )

    def settle(t, parts):
        for n in parts:
            out_copy(n, t).wait()

        @pl.when(gives)
        def _():
            for n in parts:
                give_copy(n, t).wait_send()

    per = SEQ // PT
    row = lax.broadcasted_iota(jnp.int32, (PT, 1), 0)
    lax.fori_loop(1, 16, a_wait, 0)
    for k in range(1, 4):
        b_copy(k).start()
    for t in range(TILES):
        b = t % 2
        lax.fori_loop(4 * t + (1 if t else 0), min(4 * t + 5, 16), e_arrived, 0)
        if t == 0:
            loads[0].wait()
            split = jnp.sum(jnp.where(lane == 3 * (z % 2) + main, notes[0, 6:7, :], 0), keepdims=True)
        mid = e_all[t * PT : t * PT + PT, :]
        if t:
            before = e_all[t * PT - 16 : t * PT, :].astype(F32)[15:16]
        else:
            before = jnp.zeros((1, 128), F32)
        if t < TILES - 1:
            after = e_all[t * PT + PT : t * PT + PT + 16, :].astype(F32)[0:1]
        else:
            after = jnp.zeros((1, 128), F32)
        broad = mid.astype(F32)
        left = jnp.where(row == 0, before, pltpu.roll(broad, 1, 0)).astype(BF16)
        right = jnp.where(row == PT - 1, after, pltpu.roll(broad, PT - 1, 0)).astype(BF16)
        trigram = jnp.concatenate([left, mid, right], 1)
        typed = jnp.where(row + t * PT >= split, types_ref[1:2, :], types_ref[0:1, :])
        emb = (dot(trigram, proj_ref[...]) + line(ebias_ref, 0, 4) + typed).astype(BF16)
        if t == 0:
            loads[1].wait()
        hidden = (dot(emb, win_ref[...]) + line(bias_ref, 0, 8)).astype(BF16)
        if t == 0:
            loads[2].wait()
        keys = (dot(hidden, wqkv_ref[:, D_T : 2 * D_T]) + line(bias_ref, 16, 8)).astype(BF16)
        values = (dot(hidden, wqkv_ref[:, 2 * D_T :]) + line(bias_ref, 24, 8)).astype(BF16)
        if t >= 2:
            settle(t - 2, range(3))
        emb_t[b] = emb
        k_t[b] = keys
        vt_t[b] = values.T
        for n in range(3):
            out_copy(n, t).start()

        @pl.when(gives)
        def _(t=t):
            for n in range(3):
                give_copy(n, t).start()

        if t == TILES - 1:
            for k in range(1, 4):
                b_copy(k).wait()
            for k in range(4):
                c_copy(k).start()
    for t in range(TILES - 2, TILES):
        settle(t, [0])

    def arrive(n):
        @pl.when(takes)
        def _():
            for t in range(TILES):
                give_copy(n, t).wait_recv()

    arrive(0)
    own = pltpu.make_async_copy(emb_hbm.at[pl.ds(pl.multiple_of(first_block() * QB, QB), OWN)], own_ref, own_sem)
    own.start()
    for j in range(3):
        t = first_block() + j
        local = 3 * (z % 2) + (3 * i + j) // 8
        for half in range(2):
            weight_ref[j, :, half * 128 : half * 128 + 128] = notes[2 * (t % 8) + half, pl.ds(local, 1), :].astype(F32)
    own.wait()
    finals = [
        pltpu.make_async_copy(ref, hbm, last_sem.at[n])
        for n, (ref, hbm) in enumerate([(own_ref, own_hbm), (hid_ref, hid_hbm), (params_ref, params_hbm)])
    ]
    finals[0].start()
    hidden = dot(own_ref[...], win_ref[...]) + line(bias_ref, 0, 8)
    hid_ref[...] = hidden
    finals[1].start()
    for k in range(4):
        c_copy(k).wait()
    finals[2].start()
    queries = (dot(hidden.astype(BF16), wqkv_ref[:, :D_T]) + line(bias_ref, 8, 8)).astype(BF16)
    tq_ref[...] = queries * jnp.asarray(HEAD_T**-0.5, BF16)
    lax.fori_loop(0, 16, e_sent, 0)
    for t in range(TILES - 2, TILES):
        settle(t, [1, 2])
    arrive(1)
    arrive(2)
    for copy in finals:
        copy.wait()


def front(ids, table, tail, mask, splits, mats, vecs, proj, win, wqkv, ebias, types, bias):
    vmem = pl.BlockSpec(memory_space=pltpu.VMEM)
    hbm = pl.BlockSpec(memory_space=pl.ANY)
    smem = pl.BlockSpec(memory_space=pltpu.SMEM)
    dma = pltpu.SemaphoreType.DMA
    return pl.pallas_call(
        front_kernel,
        in_specs=[smem, hbm, vmem, vmem, smem, vmem, vmem, hbm, hbm, hbm, vmem, vmem, vmem],
        out_specs=[hbm, hbm, hbm, hbm, hbm, vmem, vmem, hbm],
        out_shape=[
            jax.ShapeDtypeStruct((SLOTS, D_E), BF16),
            jax.ShapeDtypeStruct((SLOTS, D_T), BF16),
            jax.ShapeDtypeStruct((D_T, SLOTS), BF16),
            jax.ShapeDtypeStruct((OWN, D_E), BF16),
            jax.ShapeDtypeStruct((OWN, D_T), F32),
            jax.ShapeDtypeStruct((OWN, D_T), BF16),
            jax.ShapeDtypeStruct((3, 1, QB), F32),
            jax.ShapeDtypeStruct((128, BLOCK, 128), BF16),
        ],
        scratch_shapes=[
            pltpu.VMEM((OWN, D_E), BF16),
            pltpu.VMEM((OWN, D_T), F32),
            pltpu.VMEM((128, BLOCK, 128), BF16),
            pltpu.VMEM((WHOLE, 128), BF16),
            pltpu.VMEM((WHOLE + 16, 128), F32),
            pltpu.VMEM((OWN, 128), F32),
            pltpu.VMEM((6, 128, 128), BF16),
            pltpu.VMEM((8, 128), jnp.int32),
            pltpu.VMEM((16, 8, 128), jnp.int32),
            pltpu.VMEM((BLOCK, 128), F32),
            pltpu.VMEM((BLOCK, 128), BF16),
            pltpu.VMEM((SEQ, 128), BF16),
            pltpu.VMEM((3 * 128, D_E), BF16),
            pltpu.VMEM((D_E, D_T), BF16),
            pltpu.VMEM((D_T, 3 * D_T), BF16),
            pltpu.VMEM((2, PT, D_E), BF16),
            pltpu.VMEM((2, PT, D_T), BF16),
            pltpu.VMEM((2, D_T, PT), BF16),
            dma((-(-WHOLE // CHUNK),)),
            dma((3,)),
            dma((16,)),
            dma((16,)),
            dma((16,)),
            dma((16,)),
            dma((16,)),
            dma((16,)),
            dma((4,)),
            dma((4,)),
            dma((4,)),
            dma((4,)),
            dma((3, 2)),
            dma((3, TILES)),
            dma((3, TILES)),
            dma,
            dma((3,)),
        ],
        compiler_params=params(56, collective_id=0, has_side_effects=True),
        name="front",
    )(ids, table, tail, mask, splits, mats, vecs, proj, win, wqkv, ebias, types, bias)


def unpack_rows(pairs, packed_ref, flat):
    for pair in pairs:
        both = [packed_ref[2 * pair + i].astype(F32)[:SHARD] for i in range(2)]
        flat[88 * pair : 88 * pair + 88, :] = jnp.concatenate(both, 0)


def unpack_vectors(packed_ref, vec_ref):
    lane = lax.broadcasted_iota(jnp.int32, (1, 128), 1)
    rows = [jnp.zeros((1, 128), F32)] * 48
    for owner in range(128):
        row, shift = divmod(47 * owner, 128)
        entries = packed_ref[owner].astype(F32)[SHARD : SHARD + 1, :]
        moved = pltpu.roll(entries, shift, 1) if shift else entries
        if shift + 47 > 128:
            rows[row] = jnp.where(lane >= shift, moved, rows[row])
            rows[row + 1] = jnp.where(lane < shift + 47 - 128, moved, rows[row + 1])
        else:
            rows[row] = jnp.where((lane >= shift) & (lane < shift + 47), moved, rows[row])
    for row in range(48):
        vec_ref[row : row + 1, :] = rows[row]


ST = 1024


def student_in_kernel(emb_ref, packed_ref, first_ref, sq_ref, sk_ref, sv_ref, skt_ref, svt_ref,
                      win_ref, wqkv_ref, watt_ref, wup_ref, wdown_ref, wout_ref, vec_ref, flat):
    t = pl.program_id(0)

    @pl.when(t == 0)
    def _():
        unpack_vectors(packed_ref, vec_ref)
        unpack_rows(range(12), packed_ref, flat)
        win_ref[...] = flat[0:512, :].astype(BF16)
        for n in range(3):
            wqkv_ref[:, n * 128 : n * 128 + 128] = flat[pl.ds(512 + n, 128, stride=3), :].astype(BF16)
        watt_ref[...] = flat[896:1024, :].astype(BF16)

    for step in range(SLOTS // ST):

        @pl.when(t == step)
        def _(step=step):
            student_tile(t, emb_ref, win_ref, wqkv_ref, vec_ref, first_ref, sq_ref, sk_ref, sv_ref, skt_ref, svt_ref)
            unpack_rows(range(12 + 13 * step, 12 + 13 * (step + 1)), packed_ref, flat)
            if step == 1:
                for i in range(FFN_COUNT):
                    for n in range(4):
                        part = flat[pl.ds(1024 + 512 * i + n, 128, stride=4), :]
                        wup_ref[i, :, n * 128 : n * 128 + 128] = part.astype(BF16)
            if step == 3:
                for i in range(FFN_COUNT):
                    wdown_ref[i] = flat[3072 + 512 * i : 3584 + 512 * i, :].astype(BF16)
                for n in range(4):
                    wout_ref[:, n * 128 : n * 128 + 128] = flat[pl.ds(5120 + n, 128, stride=4), :].astype(BF16)


def student_tile(t, emb_ref, win_ref, wqkv_ref, vec_ref, first_ref, sq_ref, sk_ref, sv_ref, skt_ref, svt_ref):
    emb = emb_ref[...]
    emb = jnp.where((t < SEQ // ST) | has_two(), emb, jnp.zeros_like(emb))
    first = (dot(emb, win_ref[...]) + line(vec_ref, V_IN)).astype(BF16)
    first_ref[...] = first
    qkv = dot(first, wqkv_ref[...])
    sq_ref[...] = (qkv[:, :D_S] + line(vec_ref, V_QKV)).astype(BF16)
    s_keys = (qkv[:, D_S : 2 * D_S] + line(vec_ref, V_QKV + 1)).astype(BF16)
    s_values = (qkv[:, 2 * D_S :] + line(vec_ref, V_QKV + 2)).astype(BF16)
    sk_ref[...] = s_keys
    sv_ref[...] = s_values
    skt_ref[...] = s_keys.T
    svt_ref[...] = s_values.T


def student_in(emb, packed):
    tall = jax.ShapeDtypeStruct((SLOTS, D_S), BF16)
    flat = jax.ShapeDtypeStruct((D_S, SLOTS), BF16)
    down = pl.BlockSpec((ST, D_S), lambda t: (t, 0))
    across = pl.BlockSpec((D_S, ST), lambda t: (0, t))
    made = [
        ((D_E, D_S), BF16),
        ((D_S, 3 * D_S), BF16),
        ((D_S, D_S), BF16),
        ((FFN_COUNT, D_S, FF_S), BF16),
        ((FFN_COUNT, FF_S, D_S), BF16),
        ((D_S, D_E), BF16),
        ((48, 128), F32),
    ]
    return pl.pallas_call(
        student_in_kernel,
        grid=(SLOTS // ST,),
        in_specs=[pl.BlockSpec((ST, D_E), lambda t: (t, 0)), whole(128, BLOCK, 128)],
        out_specs=[down] * 4 + [across] * 2 + [whole(*shape) for shape, _ in made],
        out_shape=[tall] * 4 + [flat] * 2 + [jax.ShapeDtypeStruct(*entry) for entry in made],
        scratch_shapes=[pltpu.VMEM((5632, 128), F32)],
        compiler_params=params(40),
        name="student_in",
    )(emb, packed)


CB = 256
SUB = 64
STEPS = 3 * HEADS


def head_lanes(values, head):
    lane = lax.broadcasted_iota(jnp.int32, (1, D_S), 1)
    return jnp.where(lane // HEAD_S == head, values, jnp.zeros_like(values))


def attend_kernel(tq_ref, tk_ref, tvt_ref, sq_ref, sk_ref, svt_ref, skt_ref, et_ref, es_ref, tmix_ref, smix_ref, stat_ref,
                  ts0, ts1, ss0, ss1, mx0, mx1, sqt0, sqt1):
    n = pl.program_id(0)
    s_factor = HEAD_S**-0.5 * LOG2E

    def work(ts, ss, mx, sqt, tr, sr, mr, sqr, scores, mixes):
        if scores:
            queries, s_queries = tq_ref[...], head_lanes(sq_ref[...], n % HEADS)
            tall = s_queries.astype(F32).T
            sqt[...] = sum(tall[h * HEAD_S : (h + 1) * HEAD_S] for h in range(HEADS))
            t_max = s_max = jnp.full((8, QB), -jnp.inf, F32)
        if mixes:
            t_top, s_top = jnp.max(mr[0], 0, keepdims=True), jnp.max(mr[1], 0, keepdims=True)
            t_off, s_off = t_top * LOG2E, s_top * s_factor
            entropy = jnp.zeros((8, QB), F32)
            ones = jnp.ones((16, CB), BF16)
            t_mix = jnp.zeros((HEAD_T + HEAD_S + 16, QB), F32)
            s_mix = jnp.zeros((HEAD_S + 16, QB), F32)
        for c in range(SEQ // CB):
            part = slice(c * CB, c * CB + CB)
            if scores:
                t_part = dot_nt(tk_ref[part, :], queries)
                ts[part, :] = t_part
                s_part = dot_nt(sk_ref[part, :], s_queries)
                ss[part, :] = s_part
                t_max = jnp.maximum(t_max, fold(t_part, jnp.max))
                s_max = jnp.maximum(s_max, fold(s_part, jnp.max))
            if mixes:
                for u in range(c * CB, c * CB + CB, SUB):
                    some = slice(u, u + SUB)
                    t_log = tr[some, :] * LOG2E - t_off
                    t_exp = jnp.exp2(t_log)
                    et_ref[0, some, :] = t_exp.astype(BF16)
                    es_ref[0, some, :] = jnp.exp2(sr[some, :] * s_factor - s_off).astype(BF16)
                    entropy = entropy + fold(t_exp * t_log)
                t_mix += dot(jnp.concatenate([tvt_ref[:, part], skt_ref[:, part], ones], 0), et_ref[0, part, :])
                s_mix += dot(jnp.concatenate([svt_ref[:, part], ones], 0), es_ref[0, part, :])
        if scores:
            mx[0], mx[1] = t_max, s_max
        if mixes:
            t_sum, s_sum = t_mix[HEAD_T + HEAD_S : HEAD_T + HEAD_S + 1], s_mix[HEAD_S : HEAD_S + 1]
            t_inv, s_inv = 1.0 / t_sum, 1.0 / s_sum
            cross = jnp.sum(sqr[...] * t_mix[HEAD_T : HEAD_T + HEAD_S], 0, keepdims=True) * s_factor - s_off * t_sum
            kl = (jnp.sum(entropy, 0, keepdims=True) - cross) * t_inv * (1.0 / LOG2E)
            stat_ref[0, 0, 0:1, :] = t_inv
            stat_ref[0, 0, 1:2, :] = s_inv
            stat_ref[0, 0, 2:3, :] = kl - jnp.log(t_sum) + jnp.log(s_sum)
            stat_ref[0, 0, 3:8, :] = jnp.zeros((5, QB), F32)
            tmix_ref[...] = (t_mix[:HEAD_T] * t_inv).T.astype(BF16)
            smix_ref[0] = s_mix[:HEAD_S] * s_inv

    even, odd = (ts0, ss0, mx0, sqt0), (ts1, ss1, mx1, sqt1)
    pl.when(n == 0)(lambda: work(*even, *odd, True, False))
    pl.when((n > 0) & (n < STEPS) & (n % 2 == 0))(lambda: work(*even, *odd, True, True))
    pl.when((n > 0) & (n < STEPS) & (n % 2 == 1))(lambda: work(*odd, *even, True, True))
    pl.when(n == STEPS)(lambda: work(*even, *odd, False, True))


def attend(tq, tk, tvt, sq, sk, svt, skt):
    now = lambda n: jnp.minimum(n, STEPS - 1)
    last = lambda n: jnp.maximum(n - 1, 0)
    block = lambda n: n // HEADS
    head = lambda n: n % HEADS
    return pl.pallas_call(
        attend_kernel,
        grid=(STEPS + 1,),
        in_specs=[
            pl.BlockSpec((QB, HEAD_T), lambda n: (block(now(n)), head(now(n)))),
            pl.BlockSpec((SEQ, HEAD_T), lambda n: (slot_of(block(now(n))), head(now(n)))),
            pl.BlockSpec((HEAD_T, SEQ), lambda n: (head(last(n)), slot_of(block(last(n))))),
            pl.BlockSpec((QB, D_S), lambda n: (first_block() + block(now(n)), 0)),
            pl.BlockSpec((SEQ, D_S), lambda n: (slot_of(block(now(n))), 0)),
            pl.BlockSpec((HEAD_S, SEQ), lambda n: (head(last(n)), slot_of(block(last(n))))),
            pl.BlockSpec((HEAD_S, SEQ), lambda n: (head(last(n)), slot_of(block(last(n))))),
        ],
        out_specs=[
            pl.BlockSpec((1, SEQ, QB), lambda n: (block(last(n)), 0, head(last(n)))),
            pl.BlockSpec((1, SEQ, QB), lambda n: (block(last(n)), 0, head(last(n)))),
            pl.BlockSpec((QB, HEAD_T), lambda n: (block(last(n)), head(last(n)))),
            pl.BlockSpec((1, HEAD_S, QB), lambda n: (block(last(n)), head(last(n)), 0)),
            pl.BlockSpec((1, 1, 8, QB), lambda n: (block(last(n)), head(last(n)), 0, 0)),
        ],
        out_shape=[
            jax.ShapeDtypeStruct((3, SEQ, HEADS * QB), BF16),
            jax.ShapeDtypeStruct((3, SEQ, HEADS * QB), BF16),
            jax.ShapeDtypeStruct((OWN, D_T), BF16),
            jax.ShapeDtypeStruct((3, D_S, QB), F32),
            jax.ShapeDtypeStruct((3, HEADS, 8, QB), F32),
        ],
        scratch_shapes=[pltpu.VMEM((SEQ, QB), F32)] * 4 + [pltpu.VMEM((2, 8, QB), F32)] * 2 + [pltpu.VMEM((HEAD_S, QB), F32)] * 2,
        compiler_params=params(40),
        name="attend",
    )(tq, tk, tvt, sq, sk, svt, skt)


FC = 1024


def teacher_kernel(mix_ref, hid_ref, emb_ref, att_ref, up_ref, down_ref, out_ref, bias_ref, gain_ref, shift_ref, target_ref, norm, low, acc):
    c = pl.program_id(0)

    @pl.when(c == 0)
    def _():
        summed = hid_ref[...] + dot(mix_ref[...], att_ref[...]) + line(bias_ref, 32, 8)
        one = layer_norm(summed, line(gain_ref, 0, 8), line(shift_ref, 0, 8))
        norm[...] = one
        low[...] = one.astype(BF16)

    rows = FC // 128
    up_bias = bias_ref[pl.ds(pl.multiple_of(40 + rows * c, 8), rows), :]
    act = gelu(dot(low[...], up_ref[...]) + line(up_bias, 0, rows)).astype(BF16)
    part = dot(act, down_ref[...])

    @pl.when(c == 0)
    def _():
        acc[...] = part

    @pl.when(c > 0)
    def _():
        acc[...] += part

    @pl.when(c == pl.num_programs(0) - 1)
    def _():
        summed = norm[...] + acc[...] + line(bias_ref, 72, 8)
        two = layer_norm(summed, line(gain_ref, 8, 8), line(shift_ref, 8, 8))
        last = emb_ref[...].astype(F32) + dot(two.astype(BF16), out_ref[...]) + line(bias_ref, 80, 4)
        target_ref[...] = layer_norm(last, line(gain_ref, 16, 4), line(shift_ref, 16, 4))


def teacher(mix, hid, emb, att, up, down, out, bias, gain, shift):
    return pl.pallas_call(
        teacher_kernel,
        grid=(FF_T // FC,),
        in_specs=[
            whole(OWN, D_T),
            whole(OWN, D_T),
            whole(OWN, D_E),
            whole(D_T, D_T),
            pl.BlockSpec((D_T, FC), lambda c: (0, c)),
            pl.BlockSpec((FC, D_T), lambda c: (c, 0)),
            whole(D_T, D_E),
            whole(84, 128),
            whole(20, 128),
            whole(20, 128),
        ],
        out_specs=whole(OWN, D_E),
        out_shape=jax.ShapeDtypeStruct((OWN, D_E), F32),
        scratch_shapes=[pltpu.VMEM((OWN, D_T), F32), pltpu.VMEM((OWN, D_T), BF16), pltpu.VMEM((OWN, D_T), F32)],
        compiler_params=params(40),
        name="teacher",
    )(mix, hid, emb, att, up, down, out, bias, gain, shift)


def student_kernel(emb_ref, smix_ref, target_ref, weight_ref, win_ref, watt_ref, wup_ref, wdown_ref, wout_ref, vec_ref,
                   grad_ref, vgrad_ref, dsum_ref, dmix_ref, part_ref, states, slopes, outers, acts):

    def put(r, value):
        for i in range(value.shape[1] // 128):
            vgrad_ref[r + i : r + i + 1, :] = value[:, i * 128 : i * 128 + 128]

    total = lambda v: jnp.sum(v.astype(F32), 0, keepdims=True)
    emb = emb_ref[...]
    source = emb.astype(F32)
    first = dot(emb, win_ref[...]) + line(vec_ref, V_IN)
    mixed = jnp.concatenate([smix_ref[j].T for j in range(3)], 0).astype(BF16)
    branch = dot(mixed, watt_ref[...]) + line(vec_ref, V_ATT)
    state = line(vec_ref, V_AGAIN) * (first + branch) + line(vec_ref, V_ASHIFT)
    for i in range(FFN_COUNT):
        states[i] = state
        inner = dot(state.astype(BF16), wup_ref[i]) + line(vec_ref, V_UP + 4 * i, 4)
        half = 0.5 * (1.0 + lax.erf(inner * 0.7071067811865476))
        slopes[i] = half + inner * jnp.exp(-0.5 * inner * inner) * 0.3989422804014327
        act = (inner * half).astype(BF16)
        acts[i] = act
        pre = state + dot(act, wdown_ref[i]) + line(vec_ref, V_DOWN + i)
        outers[i] = pre
        state = line(vec_ref, V_FGAIN + i) * pre + line(vec_ref, V_FSHIFT + i)
    state_low = state.astype(BF16)
    summed = source + dot(state_low, wout_ref[...]) + line(vec_ref, V_OUT, 4)
    diff = line(vec_ref, V_OGAIN, 4) * summed + line(vec_ref, V_OSHIFT, 4) - target_ref[...]
    weight = jnp.concatenate([jnp.broadcast_to(weight_ref[j], (8, QB)).T[:, 0:1] for j in range(3)], 0)
    loss = jnp.sum(weight * jnp.sum(diff * diff, 1, keepdims=True)) * (1.0 / D_E)
    count = jnp.sum(weight)
    d_result = (weight * (2.0 / D_E)) * diff
    put(V_OGAIN, total(d_result * summed))
    put(V_OSHIFT, total(d_result))
    d_output = (d_result * line(vec_ref, V_OGAIN, 4)).astype(BF16)
    out_g = dot_tn(state_low, d_output)
    for n in range(4):
        grad_ref[pl.ds(4224 + n, 128, stride=4), :] = out_g[:, n * 128 : n * 128 + 128]
    put(V_OUT, total(d_output))
    d_state = dot_nt(d_output, wout_ref[...])
    for i in reversed(range(FFN_COUNT)):
        put(V_FGAIN + i, total(d_state * outers[i]))
        put(V_FSHIFT + i, total(d_state))
        d_sum = d_state * line(vec_ref, V_FGAIN + i)
        d_outer = d_sum.astype(BF16)
        grad_ref[2176 + 512 * i : 2176 + 512 * (i + 1), :] = dot_tn(acts[i], d_outer)
        d_inner = (dot_nt(d_outer, wdown_ref[i]) * slopes[i]).astype(BF16)
        up_g = dot_tn(states[i].astype(BF16), d_inner)
        for n in range(4):
            grad_ref[pl.ds(128 + 512 * i + n, 128, stride=4), :] = up_g[:, n * 128 : n * 128 + 128]
        put(V_UP + 4 * i, total(d_inner))
        put(V_DOWN + i, total(d_outer))
        d_state = d_sum + dot_nt(d_inner, wup_ref[i])
    put(V_AGAIN, total(d_state * (first + branch)))
    put(V_ASHIFT, total(d_state))
    d_sum = d_state * line(vec_ref, V_AGAIN)
    d_branch = d_sum.astype(BF16)
    grad_ref[0:128, :] = dot_tn(mixed, d_branch)
    put(V_ATT, total(d_branch))
    dsum_ref[...] = d_sum
    dmix_ref[...] = dot_nt(d_branch, watt_ref[...]).astype(BF16)
    for r in (0, 1, 2, 3, 47):
        vgrad_ref[r : r + 1, :] = jnp.zeros((1, 128), F32)
    row = lax.broadcasted_iota(jnp.int32, (8, 128), 0)
    lane = lax.broadcasted_iota(jnp.int32, (8, 128), 1)
    part_ref[...] = jnp.where((row == 0) & (lane == 0), loss, 0.0) + jnp.where((row == 0) & (lane == 1), count, 0.0)


def student(emb, smix, target, weight, win, watt, wup, wdown, wout, vecs):
    return pl.pallas_call(
        student_kernel,
        grid=(1,),
        in_specs=[
            whole(OWN, D_E),
            whole(3, D_S, QB),
            whole(OWN, D_E),
            whole(3, 1, QB),
            whole(D_E, D_S),
            whole(D_S, D_S),
            whole(FFN_COUNT, D_S, FF_S),
            whole(FFN_COUNT, FF_S, D_S),
            whole(D_S, D_E),
            whole(48, 128),
        ],
        out_specs=[whole(4736, 128), whole(48, 128), whole(OWN, D_S), whole(OWN, D_S), whole(8, 128)],
        out_shape=[
            jax.ShapeDtypeStruct((4736, 128), F32),
            jax.ShapeDtypeStruct((48, 128), F32),
            jax.ShapeDtypeStruct((OWN, D_S), F32),
            jax.ShapeDtypeStruct((OWN, D_S), BF16),
            jax.ShapeDtypeStruct((8, 128), F32),
        ],
        scratch_shapes=[
            pltpu.VMEM((FFN_COUNT, OWN, D_S), F32),
            pltpu.VMEM((FFN_COUNT, OWN, FF_S), F32),
            pltpu.VMEM((FFN_COUNT, OWN, D_S), F32),
            pltpu.VMEM((FFN_COUNT, OWN, FF_S), BF16),
        ],
        compiler_params=params(40),
        name="student",
    )(emb, smix, target, weight, win, watt, wup, wdown, wout, vecs)


KB = 1024


def back_kernel(et_ref, es_ref, stat_ref, smix_ref, dmix_ref, weight_ref, sq_ref, sv_ref, skt_ref, dsum_ref, emb_ref, first_ref,
                wqkv_ref, vgrad_ref, part_in, late_ref, *rest):
    state_refs, rest = rest[:6], rest[6:]
    made_ref, rest = rest[0], rest[1:]
    (dkv, dqt, ds, dq, dfirst, dmt, dmz, sqd, rows, flat, vecs, kls, block_ref, sem), buffers = rest[:14], rest[14:]
    j, kb = pl.program_id(0), pl.program_id(1)
    s_scale = HEAD_S**-0.5
    late = pltpu.make_async_copy(late_ref, flat.at[896:5632], sem)

    @pl.when((j == 0) & (kb == 0))
    def _():
        greet()
        late.start()
        vecs[...] = vgrad_ref[...]
        dkv[...] = jnp.zeros_like(dkv)
        kls[...] = jnp.zeros_like(kls)

    @pl.when((j == 0) & (kb == 1))
    def _():
        late.wait()
        pack_blocks(range(FIRST_EARLY // 2, 64), flat, vecs, block_ref)
        swap_early(block_ref, buffers)

    @pl.when((j == 1) & (kb == 0))
    def _():
        send_early(block_ref, buffers)

    @pl.when(kb == 0)
    def _():
        quarter = weight_ref[0] * (1.0 / HEADS)
        wide = dmix_ref[...].astype(F32)
        tall = wide.T
        place = lax.broadcasted_iota(jnp.int32, (D_S, 1), 0) // HEAD_S
        for h in range(HEADS):
            own = slice(h * HEAD_S, h * HEAD_S + HEAD_S)
            mine = slice(h * QB, h * QB + QB)
            t_inv, s_inv = stat_ref[0, h, 0:1, :], stat_ref[0, h, 1:2, :]
            kls[0:1, :] += quarter * stat_ref[0, h, 2:3, :]
            row_dot = jnp.sum(tall[own] * smix_ref[0, own, :], 0, keepdims=True)
            rows[h, 0:1, :] = row_dot - quarter
            rows[h, 1:2, :] = s_inv
            rows[h, 2:3, :] = quarter * t_inv
            dmt[h] = jnp.where(place == h, tall, 0.0).astype(BF16)
            dmz[mine, :] = head_lanes(wide * stat_ref[0, h].T[:, 1:2], h).astype(BF16)
            sqd[mine, :] = head_lanes(sq_ref[...], h)
        dqt[...] = jnp.zeros_like(dqt)

    here = pl.ds(pl.multiple_of(slot_of(j) * SEQ + kb * KB, KB), KB)
    dkv[here, D_S:] += dot(es_ref[0], dmz[...])
    for h in range(HEADS):
        lanes = slice(h * QB, h * QB + QB)
        for c in range(KB // 256):
            part = slice(c * 256, c * 256 + 256)
            d_probs = dot(sv_ref[part, :], dmt[h])
            s_exp, t_exp = es_ref[0, part, lanes].astype(F32), et_ref[0, part, lanes].astype(F32)
            d_scores = (d_probs - rows[h, 0:1, :]) * rows[h, 1:2, :] * s_exp - t_exp * rows[h, 2:3, :]
            ds[part, lanes] = d_scores.astype(BF16)
        own = slice(h * HEAD_S, h * HEAD_S + HEAD_S)
        dqt[own, :] += dot(skt_ref[own, :], ds[:, lanes])
    dkv[here, :D_S] += dot(ds[...], sqd[...])

    @pl.when(kb == pl.num_programs(1) - 1)
    def _():
        dq[pl.ds(pl.multiple_of(j * QB, QB), QB), :] = (dqt[...] * s_scale).T

    @pl.when((j == 2) & (kb == pl.num_programs(1) - 1))
    def _():
        qkv_w = wqkv_ref[...]
        dq_low = dq[...].astype(BF16)
        own = pl.ds(pl.multiple_of(first_block() * QB, QB), OWN)
        q_grad = dot_tn(first_ref[own, :], dq_low)
        own_part = dsum_ref[...] + dot_nt(dq_low, qkv_w[:, :D_S])
        kv_grad = jnp.zeros((D_S, 2 * D_S), F32)
        kv_bias = jnp.zeros((1, 2 * D_S), F32)
        for c in range(8):
            part = pl.ds(c * 512, 512)
            wide = dkv[part, :]
            low = jnp.concatenate([(wide[:, :D_S] * s_scale).astype(BF16), wide[:, D_S:].astype(BF16)], 1)
            kv_grad += dot_tn(first_ref[part, :], low)
            kv_bias += jnp.sum(low.astype(F32), 0, keepdims=True)
            dfirst[part, :] = dot_nt(low, qkv_w[:, D_S:])
        dfirst[own, :] += own_part
        in_grad = jnp.zeros((D_S, D_E), F32)
        in_bias = jnp.zeros((1, D_S), F32)
        two = has_two()
        for c in range(8):
            part = pl.ds(c * 512, 512)
            low = dfirst[part, :].astype(BF16)
            emb = emb_ref[part, :]
            if c >= 4:
                emb = jnp.where(two, emb, jnp.zeros_like(emb))
            in_grad += dot_tn(low, emb)
            in_bias += jnp.sum(low.astype(F32), 0, keepdims=True)
        flat[0:512, :] = in_grad.T
        flat[pl.ds(512, 128, stride=3), :] = q_grad
        flat[pl.ds(513, 128, stride=3), :] = kv_grad[:, :D_S]
        flat[pl.ds(514, 128, stride=3), :] = kv_grad[:, D_S:]
        vecs[0:1, :] = in_bias
        vecs[1:2, :] = jnp.sum(dq_low.astype(F32), 0, keepdims=True)
        vecs[2:3, :] = kv_bias[:, :D_S]
        vecs[3:4, :] = kv_bias[:, D_S:]
        pack_blocks(range(FIRST_EARLY // 2), flat, vecs, block_ref)
        kl = jnp.sum(kls[0:1, :], keepdims=True)
        corner = lax.broadcasted_iota(jnp.int32, (1, 128), 1) == 0
        send_rest(block_ref, buffers)
        update(block_ref, part_in[0:1, :] + jnp.where(corner, kl, 0.0), state_refs, made_ref, buffers)


def back(et, es, stat, smix, dmix, weight, sq, sv, skt, dsum, emb, first, wqkv, vgrad, part, late, *state):
    count = SEQ // KB
    place = lambda j, k: slot_of(j) * count + k
    dma = pltpu.SemaphoreType.DMA
    return pl.pallas_call(
        back_kernel,
        grid=(3, count),
        in_specs=[
            pl.BlockSpec((1, KB, HEADS * QB), lambda j, k: (j, k, 0)),
            pl.BlockSpec((1, KB, HEADS * QB), lambda j, k: (j, k, 0)),
            pl.BlockSpec((1, HEADS, 8, QB), lambda j, k: (j, 0, 0, 0)),
            pl.BlockSpec((1, D_S, QB), lambda j, k: (j, 0, 0)),
            pl.BlockSpec((QB, D_S), lambda j, k: (j, 0)),
            pl.BlockSpec((1, 1, QB), lambda j, k: (j, 0, 0)),
            pl.BlockSpec((QB, D_S), lambda j, k: (first_block() + j, 0)),
            pl.BlockSpec((KB, D_S), lambda j, k: (place(j, k), 0)),
            pl.BlockSpec((D_S, KB), lambda j, k: (0, place(j, k))),
            whole(OWN, D_S),
            whole(SLOTS, D_E),
            whole(SLOTS, D_S),
            whole(D_S, 3 * D_S),
            whole(48, 128),
            whole(8, 128),
            pl.BlockSpec(memory_space=pl.ANY),
        ]
        + [whole(SHARD, 128), whole(1, 47)] * 3,
        out_specs=whole(3 * BLOCK + 8, 128),
        out_shape=jax.ShapeDtypeStruct((3 * BLOCK + 8, 128), F32),
        scratch_shapes=[
            pltpu.VMEM((SLOTS, 2 * D_S), F32),
            pltpu.VMEM((D_S, QB), F32),
            pltpu.VMEM((KB, HEADS * QB), BF16),
            pltpu.VMEM((OWN, D_S), F32),
            pltpu.VMEM((SLOTS, D_S), F32),
            pltpu.VMEM((HEADS, D_S, QB), BF16),
            pltpu.VMEM((HEADS * QB, D_S), BF16),
            pltpu.VMEM((HEADS * QB, D_S), BF16),
            pltpu.VMEM((HEADS, 8, QB), F32),
            pltpu.VMEM((5632, 128), F32),
            pltpu.VMEM((48, 128), F32),
            pltpu.VMEM((8, QB), F32),
            pltpu.VMEM((4, 2, 16, BLOCK, 128), BF16),
            dma,
            pltpu.VMEM((3, BLOCK, 128), F32),
            pltpu.VMEM((4, 16, BLOCK, 128), BF16),
            pltpu.VMEM((BLOCK, 128), F32),
            pltpu.VMEM((64, BLOCK, 128), BF16),
            pltpu.VMEM((64, BLOCK, 128), BF16),
            pltpu.VMEM((2, 2, 8, 128), F32),
            pltpu.VMEM((2, 16, 8, 128), F32),
            pltpu.VMEM((2, 8, 8, 128), F32),
            dma((2, 6)),
            dma((64,)),
            dma((64,)),
            dma((2, 16)),
            dma((2, 16)),
            dma((2, 8)),
            dma((2, 8)),
        ],
        compiler_params=params(44, collective_id=1, has_side_effects=True),
        name="back",
    )(et, es, stat, smix, dmix, weight, sq, sv, skt, dsum, emb, first, wqkv, vgrad, part, late, *state)


def chip(k):
    dp, fs = lax.axis_index("dp"), lax.axis_index("fsdp")
    return (2 * ((dp // 2 + k // 16) % 4) + dp % 2, (fs + k) % 16)


def greet():
    dp, fs = lax.axis_index("dp"), lax.axis_index("fsdp")
    barrier = pltpu.get_barrier_semaphore()

    def signal(k, _):
        pl.semaphore_signal(barrier, inc=1, device_id=chip(k), device_id_type=MESH)
        return 0

    lax.fori_loop(1, 64, signal, 0)
    for k in range(4):
        other = (2 * ((dp // 2 + k) % 4) + 1 - dp % 2, fs)
        pl.semaphore_signal(barrier, inc=1, device_id=other, device_id_type=MESH)


FIRST_EARLY = 22


def pack_blocks(pairs, flat, vecs, block_ref):
    lane = lax.broadcasted_iota(jnp.int32, (1, 128), 1)
    rest = jnp.zeros((BLOCK - SHARD - 1, 128), F32)
    for pair in pairs:
        both = flat[88 * pair : 88 * pair + 88, :]
        for i in range(2):
            owner = 2 * pair + i
            row, shift = divmod(47 * owner, 128)
            entries = vecs[row : row + 1, :]
            if shift + 47 > 128:
                entries = jnp.where(lane >= shift, entries, vecs[row + 1 : row + 2, :])
            if shift:
                entries = pltpu.roll(entries, 128 - shift, 1)
            entries = jnp.where(lane < 47, entries, 0.0)
            mine = both[SHARD * i : SHARD * (i + 1)]
            block_ref[owner // 32, owner // 16 % 2, owner % 16] = jnp.concatenate([mine, entries, rest], 0).astype(BF16)


SPLIT = FIRST_EARLY - 16


def swap_copy(n, g_ref, half_in, half_sems):
    dp, fs = lax.axis_index("dp"), lax.axis_index("fsdp")
    core = dp % 2
    if n in (1, 2, 3):
        source, goal = g_ref.at[n, 1 - core], half_in.at[n]
    elif n == 0:
        source, goal = g_ref.at[0, 1, 0:SPLIT], half_in.at[0, 0:SPLIT]
    elif n == 4:
        source, goal = g_ref.at[0, 1, SPLIT:16], half_in.at[0, SPLIT:16]
    else:
        source, goal = g_ref.at[0, 0], half_in.at[0]
    return pltpu.make_async_remote_copy(
        source, goal, half_sems.at[0, n], half_sems.at[1, n], device_id=(dp + 1 - 2 * core, fs), device_id_type=MESH
    )


def swap_early(g_ref, buffers):
    half_in, half_sems = buffers[1], buffers[8]
    pl.semaphore_wait(pltpu.get_barrier_semaphore(), 67)
    for n in (1, 2, 3):
        swap_copy(n, g_ref, half_in, half_sems).start()

    @pl.when(lax.axis_index("dp") % 2 == 0)
    def _():
        swap_copy(4, g_ref, half_in, half_sems).start()


def block_copy(k, buffers):
    block_out, blocks_in, block_send, block_recv = buffers[3], buffers[4], buffers[9], buffers[10]
    dp, fs = lax.axis_index("dp"), lax.axis_index("fsdp")
    place = (dp // 2 + k // 16) % 4 * 16 + (fs + k) % 16
    return pltpu.make_async_remote_copy(
        block_out.at[place], blocks_in.at[k], block_send.at[k], block_recv.at[k], device_id=chip(k), device_id_type=MESH
    )


def is_early(place):
    return (place >= 16) | ((lax.axis_index("dp") % 2 == 1) & (place >= SPLIT))


def join_and_send(early, g_ref, buffers):
    half_in, block_out = buffers[1], buffers[3]
    dp, fs = lax.axis_index("dp"), lax.axis_index("fsdp")
    core = dp % 2

    def join(i, _):
        @pl.when(is_early(i) == early)
        def _():
            summed = g_ref[i // 16, core, i % 16].astype(F32) + half_in[i // 16, i % 16].astype(F32)
            block_out[i] = summed.astype(BF16)

        return 0

    lax.fori_loop(0, 64 if early else 16, join, 0)

    def start(k, _):
        place = (dp // 2 + k // 16) % 4 * 16 + (fs + k) % 16

        @pl.when(is_early(place) == early)
        def _():
            block_copy(k, buffers).start()

        return 0

    lax.fori_loop(1, 64, start, 0)


def send_early(g_ref, buffers):
    half_in, half_sems = buffers[1], buffers[8]
    core = lax.axis_index("dp") % 2
    for n in (1, 2, 3):
        swap_copy(n, g_ref, half_in, half_sems).wait()

    @pl.when(core == 0)
    def _():
        swap_copy(4, g_ref, half_in, half_sems).wait_send()

    @pl.when(core == 1)
    def _():
        swap_copy(4, g_ref, half_in, half_sems).wait_recv()

    join_and_send(True, g_ref, buffers)


def send_rest(g_ref, buffers):
    half_in, half_sems = buffers[1], buffers[8]
    core = lax.axis_index("dp") % 2

    @pl.when(core == 0)
    def _():
        swap_copy(0, g_ref, half_in, half_sems).start()
        swap_copy(5, g_ref, half_in, half_sems).wait_recv()
        swap_copy(0, g_ref, half_in, half_sems).wait_send()

    @pl.when(core == 1)
    def _():
        swap_copy(5, g_ref, half_in, half_sems).start()
        swap_copy(0, g_ref, half_in, half_sems).wait_recv()
        swap_copy(5, g_ref, half_in, half_sems).wait_send()

    join_and_send(False, g_ref, buffers)


def update(g_ref, part, state_refs, made_ref, buffers):
    master_mat, master_vec, first_mat, first_vec, second_mat, second_vec = state_refs
    (packs, half_in, mine, block_out, blocks_in, tile_out, tiles_f, tiles_d,
     half_sems, block_send, block_recv, f_send, f_recv, d_send, d_recv) = buffers
    dp, fs = lax.axis_index("dp"), lax.axis_index("fsdp")
    x, core = dp // 2, dp % 2
    packs[...] = jnp.zeros_like(packs)
    for i, (mat, vec) in enumerate([(master_mat, master_vec), (first_mat, first_vec), (second_mat, second_vec)]):
        packs[i, 0:SHARD, :] = mat[...]
        packs[i, SHARD : SHARD + 1, 0:47] = vec[...]
    mine[...] = g_ref[x, core, fs].astype(F32) + half_in[x, fs].astype(F32)

    def gather(k, _):
        block_copy(k, buffers).wait()
        mine[...] += blocks_in[k].astype(F32)
        return 0

    lax.fori_loop(1, 64, gather, 0)

    row = lax.broadcasted_iota(jnp.int32, (BLOCK, 1), 0)
    place = (dp * 16 + fs) * SHARD + row
    is_matrix = row < SHARD
    bounds = [0]
    for rows in MAT_ROWS:
        bounds.append(bounds[-1] + rows)
    members = [is_matrix & (place >= bounds[i]) & (place < bounds[i + 1]) for i in range(6)]

    def everyone(tile, turn):
        tile_out[turn, 0] = tile
        tiles_d[turn, dp] = tile

        def f_copy(k):
            return pltpu.make_async_remote_copy(
                tile_out.at[turn, 1], tiles_f.at[turn, fs], f_send.at[turn, k], f_recv.at[turn, k],
                device_id=(dp, (fs + k) % 16), device_id_type=MESH,
            )

        def d_copy(k):
            return pltpu.make_async_remote_copy(
                tile_out.at[turn, 0], tiles_d.at[turn, dp], d_send.at[turn, k], d_recv.at[turn, k],
                device_id=((dp + k) % 8, fs), device_id_type=MESH,
            )

        for k in range(1, 8):
            d_copy(k).start()
        for k in range(1, 8):
            d_copy(k).wait()
        total = tiles_d[turn, 0]
        for k in range(1, 8):
            total = total + tiles_d[turn, k]
        tile_out[turn, 1] = total
        tiles_f[turn, fs] = total
        for k in range(1, 16):
            f_copy(k).start()
        for k in range(1, 16):
            f_copy(k).wait()
        total = tiles_f[turn, 0]
        for k in range(1, 16):
            total = total + tiles_f[turn, k]
        return total

    column = lambda v: jnp.sum(v, 0, keepdims=True)

    def tile_of(rows):
        return jnp.concatenate(rows + [jnp.zeros((8 - len(rows), 128), F32)] * (len(rows) < 8), 0)

    grad = mine[...]
    master = packs[0]
    squares = master * master
    tile = everyone(
        tile_of([part, column(grad * grad)] + [column(jnp.where(members[i], squares, 0.0)) for i in range(6)]), 0
    )
    loss, count = tile[0:1, 0:1], tile[0:1, 1:2]
    sums = jnp.sum(tile, 1, keepdims=True)
    inverse = 1.0 / count
    norm = jnp.sqrt(sums[1:2]) * inverse
    factor = CLIP_NORM / jnp.maximum(norm, CLIP_NORM)
    grad = grad * inverse * factor
    first = BETA_ONE * packs[1] + (1.0 - BETA_ONE) * grad
    second = BETA_TWO * packs[2] + (1.0 - BETA_TWO) * grad * grad
    ratio = first / (1.0 - BETA_ONE**STEP) / (jnp.sqrt(second / (1.0 - BETA_TWO**STEP)) + ADAM_EPS)
    ratio = ratio + jnp.where(is_matrix, WEIGHT_DECAY * master, 0.0)
    squares = ratio * ratio
    steps = everyone(tile_of([column(jnp.where(members[i], squares, 0.0)) for i in range(6)]), 1)
    made_ref[BLOCK : 2 * BLOCK, :] = first
    made_ref[2 * BLOCK : 3 * BLOCK, :] = second
    trusts = jnp.sqrt(sums[2:8]) / jnp.sqrt(jnp.sum(steps, 1, keepdims=True)[0:6])
    trust = jnp.ones((BLOCK, 1), F32)
    for i in range(6):
        trust = jnp.where(members[i], trusts[i : i + 1], trust)
    made_ref[0:BLOCK, :] = master - LEARN_RATE * (trust * ratio)
    lane = lax.broadcasted_iota(jnp.int32, (8, 128), 1)
    made_ref[3 * BLOCK :, :] = jnp.where(lane == 0, loss, jnp.where(lane == 1, count, norm))


def finish_kernel(made, loss, count, norm, m0, m1, m2, v0, v1, v2):
    for i, (mat, vec) in enumerate(((m0, v0), (m1, v1), (m2, v2))):
        mat[...] = made[BLOCK * i : BLOCK * i + SHARD, :]
        vec[...] = made[BLOCK * i + SHARD : BLOCK * i + SHARD + 1, 0:47]
    for i, out in enumerate((loss, count, norm)):
        out[...] = made[3 * BLOCK : 3 * BLOCK + 1, i : i + 1]


def finish(made):
    vmem = pl.BlockSpec(memory_space=pltpu.VMEM)
    shape = lambda *dims: jax.ShapeDtypeStruct(dims, F32)
    return pl.pallas_call(
        finish_kernel,
        in_specs=[vmem],
        out_specs=[vmem] * 9,
        out_shape=[shape(1, 1)] * 3 + [shape(SHARD, 128)] * 3 + [shape(1, 47)] * 3,
        compiler_params=params(60),
        name="finish",
    )(made)


def per_device(
    token_ids,
    splits,
    valid_mask,
    embed_table,
    embed_proj,
    embed_bias,
    type_table,
    teach_in,
    teach_qkv,
    teach_att,
    teach_up,
    teach_down,
    teach_out,
    teach_bias,
    teach_gain,
    teach_shift,
    matrices,
    vectors,
    matrix_first,
    matrix_second,
    vector_first,
    vector_second,
):
    mat = lambda v: v.reshape(SHARD, 128)
    vec = lambda v: v.reshape(1, 47)
    rows_128 = lambda v: v.reshape(-1, 128)
    bias = rows_128(teach_bias)
    emb, t_keys, t_values, own_emb, hidden, t_queries, weights, packed = front(
        token_ids, embed_table, embed_table[WHOLE:], valid_mask, splits, mat(matrices), vec(vectors), embed_proj, teach_in, teach_qkv,
        rows_128(embed_bias), type_table, bias,
    )
    first, s_q, s_k, s_v, s_kt, s_vt, in_w, qkv_w, att_w, up_w, down_w, out_w, vecs = student_in(emb, packed)
    et, es, t_mixed, s_mixed, stat = attend(t_queries, t_keys, t_values, s_q, s_k, s_vt, s_kt)
    target = teacher(
        t_mixed, hidden, own_emb, teach_att, teach_up, teach_down, teach_out, bias, rows_128(teach_gain), rows_128(teach_shift)
    )
    late, vgrads, d_sum, d_mixed, part = student(
        own_emb, s_mixed, target, weights, in_w, att_w, up_w, down_w, out_w, vecs
    )
    made = back(
        et, es, stat, s_mixed, d_mixed, weights, s_q, s_v, s_kt, d_sum, emb, first, qkv_w, vgrads, part, late,
        mat(matrices), vec(vectors), mat(matrix_first), vec(vector_first), mat(matrix_second), vec(vector_second),
    )
    loss, count, norm, m0, m1, m2, v0, v1, v2 = finish(made)
    flat = lambda v: v.reshape(-1)
    scalar = lambda v: v.reshape(())
    return (
        scalar(loss), scalar(count), scalar(norm), flat(m0), flat(m1), flat(m2), flat(v0), flat(v1), flat(v2),
    )


def solution(mesh):
    both = P(("dp", "fsdp"))
    return jax.shard_map(
        per_device,
        mesh=mesh,
        in_specs=(P("dp", "fsdp"), P("dp"), P("dp", "fsdp")) + (P(),) * 13 + (both,) * 6,
        out_specs=(P(), P(), P(), both, both, both, both, both, both),
        check_vma=False,
    )
```

```python
import functools
import math

import jax
import jax.numpy as jnp
from jax import lax
from jax.experimental import pallas as pl
from jax.experimental.pallas import tpu as pltpu
from jax.sharding import PartitionSpec as P

D_E = 512
D_T = 1024
FF_T = 4096
D_S = 128
FF_S = 512
HEADS = 4
FFN_COUNT = 4
STEP = 5
HEAD_T = 256
HEAD_S = 32
SEQ = 2048
QB = 256
OWN = 3 * QB
SLOTS = 2 * SEQ

CLIP_NORM = 0.05
BETA_ONE = 0.9
BETA_TWO = 0.999
LEARN_RATE = 0.3
WEIGHT_DECAY = 0.01
ADAM_EPS = 1e-06

F32 = jnp.float32
BF16 = jnp.bfloat16
LOG2E = 1.4426950408889634
MESH = pl.DeviceIdType.MESH

MAT_ROWS = (512, 384, 128, 2048, 2048, 512)
SHARD = 44
BLOCK = 48
(V_IN, V_QKV, V_ATT, V_AGAIN, V_ASHIFT, V_UP, V_DOWN, V_FGAIN, V_FSHIFT, V_OUT, V_OGAIN, V_OSHIFT) = (
    0, 1, 4, 5, 6, 7, 23, 27, 31, 35, 39, 43)


def dot(left, right):
    return jnp.dot(left, right, preferred_element_type=F32)


def dot_nt(left, right):
    return lax.dot_general(left, right, (((1,), (1,)), ((), ())), preferred_element_type=F32)


def dot_tn(left, right):
    return lax.dot_general(left, right, (((0,), (0,)), ((), ())), preferred_element_type=F32)


def layer_norm(values, gain, shift):
    center = values - jnp.mean(values, -1, keepdims=True)
    spread = jnp.mean(center * center, -1, keepdims=True)
    return center * lax.rsqrt(spread + 1e-05) * gain + shift


def gelu(values):
    return 0.5 * values * (1.0 + lax.erf(values * 0.7071067811865476))


def params(mib, **more):
    return pltpu.CompilerParams(vmem_limit_bytes=mib * 2**20, **more)


def whole(*shape):
    return pl.BlockSpec(shape, lambda *_: (0,) * len(shape))


def line(ref, row, count=1):
    if count == 1:
        return ref[row : row + 1, :]
    return jnp.concatenate([ref[row + i : row + i + 1, :] for i in range(count)], 1)


def fold(values, op=jnp.sum):
    return op(values.reshape(values.shape[0] // 8, 8, values.shape[1]), 0)


def spots():
    dp, fs = lax.axis_index("dp"), lax.axis_index("fsdp")
    return dp // 2, dp % 2, fs // 4, fs % 4


def place_in_group():
    _, core, _, y = spots()
    return 2 * y + core


def first_block():
    return (3 * place_in_group()) % 8


def slot_of(j):
    return (first_block() + j) // 8


def has_two():
    i = place_in_group()
    return (i == 2) | (i == 5)


PT = 512
TILES = SEQ // PT


CHUNK = 2048
VOCAB = 30522
WHOLE = VOCAB // 16 * 16


def front_kernel(ids_ref, table_hbm, tail_ref, mask_ref, splits_ref, mats_ref, vecs_ref, proj_hbm, win_hbm, wqkv_hbm, ebias_ref,
                 types_ref, bias_ref, emb_hbm, k_hbm, vt_hbm, own_hbm, hid_hbm, tq_ref, weight_ref, params_hbm,
                 own_ref, hid_ref, params_ref, table_low, table, picked, e_ref, note, notes, wide, block, e_all, proj_ref, win_ref, wqkv_ref, emb_t, k_t, vt_t,
                 t_sem, load, e_send, e_recv, n_send, n_recv, a_send, a_recv, b_send, b_recv, c_send, c_recv,
                 out, s_send, s_recv, own_sem, last_sem):
    dp, me = lax.axis_index("dp"), lax.axis_index("fsdp")
    x, core, z, y = spots()
    i = 2 * y + core
    sibling = (2 * x + 1 - core, me)
    source_dp = 2 * x + z // 2
    is_source = z // 2 == core
    loads = [
        pltpu.make_async_copy(hbm, ref, load.at[n])
        for n, (hbm, ref) in enumerate([(proj_hbm, proj_ref), (win_hbm, win_ref), (wqkv_hbm, wqkv_ref)])
    ]
    barrier = pltpu.get_barrier_semaphore()

    def signal(device):
        pl.semaphore_signal(barrier, inc=1, device_id=device, device_id_type=MESH)

    def greet_source(f, _):
        @pl.when(jnp.logical_not(is_source & (f == me)))
        def _():
            signal((source_dp, f))

        return 0

    def greet_plane(k, _):
        signal((dp, (me + k) % 16))
        return 0

    lax.fori_loop(0, 16, greet_source, 0)
    lax.fori_loop(1, 16, greet_plane, 0)
    for k in range(1, 4):
        signal((2 * ((x + k) % 4) + core, me))
    signal(sibling)
    chunks = [(c, min(CHUNK, WHOLE - c)) for c in range(0, WHOLE, CHUNK)]
    table_copies = [
        pltpu.make_async_copy(table_hbm.at[pl.ds(c, size)], table_low.at[pl.ds(c, size)], t_sem.at[n])
        for n, (c, size) in enumerate(chunks)
    ]
    for copy in table_copies:
        copy.start()

    lane = lax.broadcasted_iota(jnp.int32, (1, 128), 1)
    note[0:6, :] = mask_ref[...]
    line_of_splits = jnp.zeros((1, 128), jnp.int32)
    for r in range(6):
        line_of_splits = jnp.where(lane == r, splits_ref[r], line_of_splits)
    note[6:7, :] = line_of_splits
    note[7:8, :] = jnp.zeros((1, 128), jnp.int32)
    wide[...] = jnp.zeros((BLOCK, 128), F32)
    wide[0:SHARD, :] = mats_ref[...]
    wide[SHARD : SHARD + 1, 0:47] = vecs_ref[...]
    block[...] = wide[...].astype(BF16)
    params_ref[dp * 16 + me] = block[...]
    main = (3 * i + 1) // 8
    for copy, (c, size) in zip(table_copies, chunks):
        copy.wait()
        table[c : c + size, :] = table_low[c : c + size, :].astype(F32)
    for copy in loads:
        copy.start()
    table[WHOLE:VOCAB, :] = tail_ref[...].astype(F32)[0 : VOCAB - WHOLE]

    def pick(g, _):
        for u in range(16):
            token = ids_ref[g // 8, g % 8 * 16 + u]
            picked[pl.ds(g * 16 + u, 1), :] = table[pl.ds(token, 1), :]
        return 0

    lax.fori_loop(0, 48, pick, 0)
    for r in range(6):
        e_ref[r] = picked[128 * r : 128 * r + 128, :].astype(BF16)

    @pl.when(is_source)
    def _():
        e_all[pl.ds(pl.multiple_of(me * 128, 128), 128), :] = e_ref[3 * (z % 2) + main]
        notes[me] = note[...]

    pl.semaphore_wait(barrier, jnp.where(is_source, 15, 16) + 15 + 3 + 1)

    def a_copy(k):
        return pltpu.make_async_remote_copy(
            block, params_ref.at[dp * 16 + me], a_send.at[k], a_recv.at[k], device_id=(dp, (me + k) % 16), device_id_type=MESH
        )

    def b_copy(k):
        mine = params_ref.at[pl.ds(dp * 16, 16)]
        return pltpu.make_async_remote_copy(
            mine, mine, b_send.at[k], b_recv.at[k], device_id=(2 * ((x + k) % 4) + core, me), device_id_type=MESH
        )

    def c_copy(k):
        mine = params_ref.at[pl.ds((2 * k + core) * 16, 16)]
        return pltpu.make_async_remote_copy(mine, mine, c_send.at[k], c_recv.at[k], device_id=sibling, device_id_type=MESH)

    def a_start(k, _):
        a_copy(k).start()
        return 0

    def a_wait(k, _):
        a_copy(k).wait()
        return 0

    def e_copy(d, noted):
        zd, yd, cd = 2 * core + d // 8, d // 2 % 4, d % 2
        where = dict(device_id=(2 * x + cd, 4 * zd + yd), device_id_type=MESH)
        if noted:
            return pltpu.make_async_remote_copy(note, notes.at[me], n_send.at[d], n_recv.at[me], **where)
        row = 3 * (d // 8) + (3 * (2 * yd + cd) + 1) // 8
        here = pl.ds(pl.multiple_of(me * 128, 128), 128)
        return pltpu.make_async_remote_copy(e_ref.at[row], e_all.at[here], e_send.at[d], e_recv.at[me], **where)

    def is_other(d):
        return jnp.logical_not((2 * core + d // 8 == z) & (d // 2 % 4 == y) & (d % 2 == core))

    def e_start(n, _):
        d = (n + me) % 16

        @pl.when(is_other(d))
        def _():
            e_copy(d, False).start()
            e_copy(d, True).start()

        return 0

    lax.fori_loop(1, 16, a_start, 0)
    lax.fori_loop(0, 16, e_start, 0)

    def e_sent(d, _):
        @pl.when(is_other(d))
        def _():
            e_copy(d, False).wait_send()
            e_copy(d, True).wait_send()

        return 0

    def e_arrived(f, _):
        @pl.when(jnp.logical_not(is_source & (f == me)))
        def _():
            where = dict(device_id=(source_dp, f), device_id_type=MESH)
            there = pl.ds(pl.multiple_of(f * 128, 128), 128)
            pltpu.make_async_remote_copy(e_ref.at[0], e_all.at[there], e_send.at[0], e_recv.at[f], **where).wait_recv()
            pltpu.make_async_remote_copy(note, notes.at[f], n_send.at[0], n_recv.at[f], **where).wait_recv()

        return 0

    gives = ((y == 1) & (core == 1)) | ((y == 2) & (core == 0))
    takes = has_two()
    main_slot = jnp.where(i == 5, 1, 0)
    his_slot = jnp.where(y == 1, 1, 0)

    made = ((emb_t, emb_hbm), (k_t, k_hbm), (vt_t, vt_hbm))

    def target(n, slot, t):
        rows = pl.ds(pl.multiple_of(slot * SEQ + t * PT, PT), PT)
        return made[n][1].at[:, rows] if n == 2 else made[n][1].at[rows]

    def out_copy(n, t):
        return pltpu.make_async_copy(made[n][0].at[t % 2], target(n, main_slot, t), out.at[n, t % 2])

    def give_copy(n, t):
        return pltpu.make_async_remote_copy(
            made[n][0].at[t % 2], target(n, his_slot, t), s_send.at[n, t], s_recv.at[n, t],
            device_id=sibling, device_id_type=MESH,
        )

    def settle(t, parts):
        for n in parts:
            out_copy(n, t).wait()

        @pl.when(gives)
        def _():
            for n in parts:
                give_copy(n, t).wait_send()

    per = SEQ // PT
    row = lax.broadcasted_iota(jnp.int32, (PT, 1), 0)
    lax.fori_loop(1, 16, a_wait, 0)
    for k in range(1, 4):
        b_copy(k).start()
    for t in range(TILES):
        b = t % 2
        lax.fori_loop(4 * t + (1 if t else 0), min(4 * t + 5, 16), e_arrived, 0)
        if t == 0:
            loads[0].wait()
            split = jnp.sum(jnp.where(lane == 3 * (z % 2) + main, notes[0, 6:7, :], 0), keepdims=True)
        mid = e_all[t * PT : t * PT + PT, :]
        if t:
            before = e_all[t * PT - 16 : t * PT, :].astype(F32)[15:16]
        else:
            before = jnp.zeros((1, 128), F32)
        if t < TILES - 1:
            after = e_all[t * PT + PT : t * PT + PT + 16, :].astype(F32)[0:1]
        else:
            after = jnp.zeros((1, 128), F32)
        broad = mid.astype(F32)
        left = jnp.where(row == 0, before, pltpu.roll(broad, 1, 0)).astype(BF16)
        right = jnp.where(row == PT - 1, after, pltpu.roll(broad, PT - 1, 0)).astype(BF16)
        trigram = jnp.concatenate([left, mid, right], 1)
        typed = jnp.where(row + t * PT >= split, types_ref[1:2, :], types_ref[0:1, :])
        emb = (dot(trigram, proj_ref[...]) + line(ebias_ref, 0, 4) + typed).astype(BF16)
        if t == 0:
            loads[1].wait()
        hidden = (dot(emb, win_ref[...]) + line(bias_ref, 0, 8)).astype(BF16)
        if t == 0:
            loads[2].wait()
        keys = (dot(hidden, wqkv_ref[:, D_T : 2 * D_T]) + line(bias_ref, 16, 8)).astype(BF16)
        values = (dot(hidden, wqkv_ref[:, 2 * D_T :]) + line(bias_ref, 24, 8)).astype(BF16)
        if t >= 2:
            settle(t - 2, range(3))
        emb_t[b] = emb
        k_t[b] = keys
        vt_t[b] = values.T
        for n in range(3):
            out_copy(n, t).start()

        @pl.when(gives)
        def _(t=t):
            for n in range(3):
                give_copy(n, t).start()

        if t == TILES - 1:
            for k in range(1, 4):
                b_copy(k).wait()
            for k in range(4):
                c_copy(k).start()
    for t in range(TILES - 2, TILES):
        settle(t, [0])

    def arrive(n):
        @pl.when(takes)
        def _():
            for t in range(TILES):
                give_copy(n, t).wait_recv()

    arrive(0)
    own = pltpu.make_async_copy(emb_hbm.at[pl.ds(pl.multiple_of(first_block() * QB, QB), OWN)], own_ref, own_sem)
    own.start()
    for j in range(3):
        t = first_block() + j
        local = 3 * (z % 2) + (3 * i + j) // 8
        for half in range(2):
            weight_ref[j, :, half * 128 : half * 128 + 128] = notes[2 * (t % 8) + half, pl.ds(local, 1), :].astype(F32)
    own.wait()
    finals = [
        pltpu.make_async_copy(ref, hbm, last_sem.at[n])
        for n, (ref, hbm) in enumerate([(own_ref, own_hbm), (hid_ref, hid_hbm), (params_ref, params_hbm)])
    ]
    finals[0].start()
    hidden = dot(own_ref[...], win_ref[...]) + line(bias_ref, 0, 8)
    hid_ref[...] = hidden
    finals[1].start()
    for k in range(4):
        c_copy(k).wait()
    finals[2].start()
    queries = (dot(hidden.astype(BF16), wqkv_ref[:, :D_T]) + line(bias_ref, 8, 8)).astype(BF16)
    tq_ref[...] = queries * jnp.asarray(HEAD_T**-0.5, BF16)
    lax.fori_loop(0, 16, e_sent, 0)
    for t in range(TILES - 2, TILES):
        settle(t, [1, 2])
    arrive(1)
    arrive(2)
    for copy in finals:
        copy.wait()


def front(ids, table, table_end, mask, splits, mats, vecs, proj, win, wqkv, ebias, types, bias):
    vmem = pl.BlockSpec(memory_space=pltpu.VMEM)
    hbm = pl.BlockSpec(memory_space=pl.ANY)
    smem = pl.BlockSpec(memory_space=pltpu.SMEM)
    tail = pl.BlockSpec((16, 128), lambda _: (WHOLE // 16, 0))
    dma = pltpu.SemaphoreType.DMA
    return pl.pallas_call(
        front_kernel,
        grid=(1,),
        in_specs=[smem, hbm, tail, vmem, smem, vmem, vmem, hbm, hbm, hbm, vmem, vmem, vmem],
        out_specs=[hbm, hbm, hbm, hbm, hbm, vmem, vmem, hbm],
        out_shape=[
            jax.ShapeDtypeStruct((SLOTS, D_E), BF16),
            jax.ShapeDtypeStruct((SLOTS, D_T), BF16),
            jax.ShapeDtypeStruct((D_T, SLOTS), BF16),
            jax.ShapeDtypeStruct((OWN, D_E), BF16),
            jax.ShapeDtypeStruct((OWN, D_T), F32),
            jax.ShapeDtypeStruct((OWN, D_T), BF16),
            jax.ShapeDtypeStruct((3, 1, QB), F32),
            jax.ShapeDtypeStruct((128, BLOCK, 128), BF16),
        ],
        scratch_shapes=[
            pltpu.VMEM((OWN, D_E), BF16),
            pltpu.VMEM((OWN, D_T), F32),
            pltpu.VMEM((128, BLOCK, 128), BF16),
            pltpu.VMEM((WHOLE, 128), BF16),
            pltpu.VMEM((WHOLE + 16, 128), F32),
            pltpu.VMEM((OWN, 128), F32),
            pltpu.VMEM((6, 128, 128), BF16),
            pltpu.VMEM((8, 128), jnp.int32),
            pltpu.VMEM((16, 8, 128), jnp.int32),
            pltpu.VMEM((BLOCK, 128), F32),
            pltpu.VMEM((BLOCK, 128), BF16),
            pltpu.VMEM((SEQ, 128), BF16),
            pltpu.VMEM((3 * 128, D_E), BF16),
            pltpu.VMEM((D_E, D_T), BF16),
            pltpu.VMEM((D_T, 3 * D_T), BF16),
            pltpu.VMEM((2, PT, D_E), BF16),
            pltpu.VMEM((2, PT, D_T), BF16),
            pltpu.VMEM((2, D_T, PT), BF16),
            dma((-(-WHOLE // CHUNK),)),
            dma((3,)),
            dma((16,)),
            dma((16,)),
            dma((16,)),
            dma((16,)),
            dma((16,)),
            dma((16,)),
            dma((4,)),
            dma((4,)),
            dma((4,)),
            dma((4,)),
            dma((3, 2)),
            dma((3, TILES)),
            dma((3, TILES)),
            dma,
            dma((3,)),
        ],
        compiler_params=params(58, collective_id=0, has_side_effects=True),
        name="front",
    )(ids, table, table_end, mask, splits, mats, vecs, proj, win, wqkv, ebias, types, bias)


def unpack_rows(pairs, packed_ref, flat):
    for pair in pairs:
        both = [packed_ref[2 * pair + i].astype(F32)[:SHARD] for i in range(2)]
        flat[88 * pair : 88 * pair + 88, :] = jnp.concatenate(both, 0)


def unpack_vectors(packed_ref, vec_ref):
    lane = lax.broadcasted_iota(jnp.int32, (1, 128), 1)
    rows = [jnp.zeros((1, 128), F32)] * 48
    for owner in range(128):
        row, shift = divmod(47 * owner, 128)
        entries = packed_ref[owner].astype(F32)[SHARD : SHARD + 1, :]
        moved = pltpu.roll(entries, shift, 1) if shift else entries
        if shift + 47 > 128:
            rows[row] = jnp.where(lane >= shift, moved, rows[row])
            rows[row + 1] = jnp.where(lane < shift + 47 - 128, moved, rows[row + 1])
        else:
            rows[row] = jnp.where((lane >= shift) & (lane < shift + 47), moved, rows[row])
    for row in range(48):
        vec_ref[row : row + 1, :] = rows[row]


ST = 1024


def student_in_kernel(emb_ref, packed_ref, first_ref, sq_ref, sk_ref, sv_ref, skt_ref, svt_ref,
                      win_ref, wqkv_ref, watt_ref, wup_ref, wdown_ref, wout_ref, vec_ref, flat):
    t = pl.program_id(0)

    @pl.when(t == 0)
    def _():
        unpack_vectors(packed_ref, vec_ref)
        unpack_rows(range(12), packed_ref, flat)
        win_ref[...] = flat[0:512, :].astype(BF16)
        for n in range(3):
            wqkv_ref[:, n * 128 : n * 128 + 128] = flat[pl.ds(512 + n, 128, stride=3), :].astype(BF16)
        watt_ref[...] = flat[896:1024, :].astype(BF16)

    for step in range(SLOTS // ST):

        @pl.when(t == step)
        def _(step=step):
            student_tile(t, emb_ref, win_ref, wqkv_ref, vec_ref, first_ref, sq_ref, sk_ref, sv_ref, skt_ref, svt_ref)
            unpack_rows(range(12 + 13 * step, 12 + 13 * (step + 1)), packed_ref, flat)
            if step == 1:
                for i in range(FFN_COUNT):
                    for n in range(4):
                        part = flat[pl.ds(1024 + 512 * i + n, 128, stride=4), :]
                        wup_ref[i, :, n * 128 : n * 128 + 128] = part.astype(BF16)
            if step == 3:
                for i in range(FFN_COUNT):
                    wdown_ref[i] = flat[3072 + 512 * i : 3584 + 512 * i, :].astype(BF16)
                for n in range(4):
                    wout_ref[:, n * 128 : n * 128 + 128] = flat[pl.ds(5120 + n, 128, stride=4), :].astype(BF16)


def student_tile(t, emb_ref, win_ref, wqkv_ref, vec_ref, first_ref, sq_ref, sk_ref, sv_ref, skt_ref, svt_ref):
    emb = emb_ref[...]
    emb = jnp.where((t < SEQ // ST) | has_two(), emb, jnp.zeros_like(emb))
    first = (dot(emb, win_ref[...]) + line(vec_ref, V_IN)).astype(BF16)
    first_ref[...] = first
    qkv = dot(first, wqkv_ref[...])
    sq_ref[...] = (qkv[:, :D_S] + line(vec_ref, V_QKV)).astype(BF16)
    s_keys = (qkv[:, D_S : 2 * D_S] + line(vec_ref, V_QKV + 1)).astype(BF16)
    s_values = (qkv[:, 2 * D_S :] + line(vec_ref, V_QKV + 2)).astype(BF16)
    sk_ref[...] = s_keys
    sv_ref[...] = s_values
    skt_ref[...] = s_keys.T
    svt_ref[...] = s_values.T


def student_in(emb, packed):
    tall = jax.ShapeDtypeStruct((SLOTS, D_S), BF16)
    flat = jax.ShapeDtypeStruct((D_S, SLOTS), BF16)
    down = pl.BlockSpec((ST, D_S), lambda t: (t, 0))
    across = pl.BlockSpec((D_S, ST), lambda t: (0, t))
    made = [
        ((D_E, D_S), BF16),
        ((D_S, 3 * D_S), BF16),
        ((D_S, D_S), BF16),
        ((FFN_COUNT, D_S, FF_S), BF16),
        ((FFN_COUNT, FF_S, D_S), BF16),
        ((D_S, D_E), BF16),
        ((48, 128), F32),
    ]
    return pl.pallas_call(
        student_in_kernel,
        grid=(SLOTS // ST,),
        in_specs=[pl.BlockSpec((ST, D_E), lambda t: (t, 0)), whole(128, BLOCK, 128)],
        out_specs=[down] * 4 + [across] * 2 + [whole(*shape) for shape, _ in made],
        out_shape=[tall] * 4 + [flat] * 2 + [jax.ShapeDtypeStruct(*entry) for entry in made],
        scratch_shapes=[pltpu.VMEM((5632, 128), F32)],
        compiler_params=params(40),
        name="student_in",
    )(emb, packed)


CB = 256
SUB = 64
STEPS = 3 * HEADS


def head_lanes(values, head):
    lane = lax.broadcasted_iota(jnp.int32, (1, D_S), 1)
    return jnp.where(lane // HEAD_S == head, values, jnp.zeros_like(values))


def attend_kernel(tq_ref, tk_ref, tvt_ref, sq_ref, sk_ref, svt_ref, skt_ref, et_ref, es_ref, tmix_ref, smix_ref, stat_ref,
                  ts0, ts1, ss0, ss1, mx0, mx1, sqt0, sqt1):
    n = pl.program_id(0)
    s_factor = HEAD_S**-0.5 * LOG2E

    def work(ts, ss, mx, sqt, tr, sr, mr, sqr, scores, mixes):
        if scores:
            queries, s_queries = tq_ref[...], head_lanes(sq_ref[...], n // 3)
            tall = s_queries.astype(F32).T
            sqt[...] = sum(tall[h * HEAD_S : (h + 1) * HEAD_S] for h in range(HEADS))
            t_max = s_max = jnp.full((8, QB), -jnp.inf, F32)
        if mixes:
            t_top, s_top = jnp.max(mr[0], 0, keepdims=True), jnp.max(mr[1], 0, keepdims=True)
            t_off, s_off = t_top * LOG2E, s_top * s_factor
            entropy = jnp.zeros((8, QB), F32)
            ones = jnp.ones((16, CB), BF16)
            t_mix = jnp.zeros((HEAD_T + HEAD_S + 16, QB), F32)
            s_mix = jnp.zeros((HEAD_S + 16, QB), F32)
        for c in range(SEQ // CB):
            part = slice(c * CB, c * CB + CB)
            if scores:
                t_part = dot_nt(tk_ref[part, :], queries)
                ts[part, :] = t_part
                s_part = dot_nt(sk_ref[part, :], s_queries)
                ss[part, :] = s_part
                t_max = jnp.maximum(t_max, fold(t_part, jnp.max))
                s_max = jnp.maximum(s_max, fold(s_part, jnp.max))
            if mixes:
                for u in range(c * CB, c * CB + CB, SUB):
                    some = slice(u, u + SUB)
                    t_log = tr[some, :] * LOG2E - t_off
                    t_exp = jnp.exp2(t_log)
                    et_ref[0, some, :] = t_exp.astype(BF16)
                    es_ref[0, some, :] = jnp.exp2(sr[some, :] * s_factor - s_off).astype(BF16)
                    entropy = entropy + fold(t_exp * t_log)
                t_mix += dot(jnp.concatenate([tvt_ref[:, part], skt_ref[:, part], ones], 0), et_ref[0, part, :])
                s_mix += dot(jnp.concatenate([svt_ref[:, part], ones], 0), es_ref[0, part, :])
        if scores:
            mx[0], mx[1] = t_max, s_max
        if mixes:
            t_sum, s_sum = t_mix[HEAD_T + HEAD_S : HEAD_T + HEAD_S + 1], s_mix[HEAD_S : HEAD_S + 1]
            t_inv, s_inv = 1.0 / t_sum, 1.0 / s_sum
            cross = jnp.sum(sqr[...] * t_mix[HEAD_T : HEAD_T + HEAD_S], 0, keepdims=True) * s_factor - s_off * t_sum
            kl = (jnp.sum(entropy, 0, keepdims=True) - cross) * t_inv * (1.0 / LOG2E)
            stat_ref[0, 0, 0:1, :] = t_inv
            stat_ref[0, 0, 1:2, :] = s_inv
            stat_ref[0, 0, 2:3, :] = kl - jnp.log(t_sum) + jnp.log(s_sum)
            stat_ref[0, 0, 3:8, :] = jnp.zeros((5, QB), F32)
            tmix_ref[...] = (t_mix[:HEAD_T] * t_inv).T.astype(BF16)
            smix_ref[0] = s_mix[:HEAD_S] * s_inv

    even, odd = (ts0, ss0, mx0, sqt0), (ts1, ss1, mx1, sqt1)
    pl.when(n == 0)(lambda: work(*even, *odd, True, False))
    pl.when((n > 0) & (n < STEPS) & (n % 2 == 0))(lambda: work(*even, *odd, True, True))
    pl.when((n > 0) & (n < STEPS) & (n % 2 == 1))(lambda: work(*odd, *even, True, True))
    pl.when(n == STEPS)(lambda: work(*even, *odd, False, True))


def attend(tq, tk, tvt, sq, sk, svt, skt):
    now = lambda n: jnp.minimum(n, STEPS - 1)
    last = lambda n: jnp.maximum(n - 1, 0)
    block = lambda n: n % 3
    head = lambda n: n // 3
    return pl.pallas_call(
        attend_kernel,
        grid=(STEPS + 1,),
        in_specs=[
            pl.BlockSpec((QB, HEAD_T), lambda n: (block(now(n)), head(now(n)))),
            pl.BlockSpec((SEQ, HEAD_T), lambda n: (slot_of(block(now(n))), head(now(n)))),
            pl.BlockSpec((HEAD_T, SEQ), lambda n: (head(last(n)), slot_of(block(last(n))))),
            pl.BlockSpec((QB, D_S), lambda n: (first_block() + block(now(n)), 0)),
            pl.BlockSpec((SEQ, D_S), lambda n: (slot_of(block(now(n))), 0)),
            pl.BlockSpec((HEAD_S, SEQ), lambda n: (head(last(n)), slot_of(block(last(n))))),
            pl.BlockSpec((HEAD_S, SEQ), lambda n: (head(last(n)), slot_of(block(last(n))))),
        ],
        out_specs=[
            pl.BlockSpec((1, SEQ, QB), lambda n: (block(last(n)), 0, head(last(n)))),
            pl.BlockSpec((1, SEQ, QB), lambda n: (block(last(n)), 0, head(last(n)))),
            pl.BlockSpec((QB, HEAD_T), lambda n: (block(last(n)), head(last(n)))),
            pl.BlockSpec((1, HEAD_S, QB), lambda n: (block(last(n)), head(last(n)), 0)),
            pl.BlockSpec((1, 1, 8, QB), lambda n: (block(last(n)), head(last(n)), 0, 0)),
        ],
        out_shape=[
            jax.ShapeDtypeStruct((3, SEQ, HEADS * QB), BF16),
            jax.ShapeDtypeStruct((3, SEQ, HEADS * QB), BF16),
            jax.ShapeDtypeStruct((OWN, D_T), BF16),
            jax.ShapeDtypeStruct((3, D_S, QB), F32),
            jax.ShapeDtypeStruct((3, HEADS, 8, QB), F32),
        ],
        scratch_shapes=[pltpu.VMEM((SEQ, QB), F32)] * 4 + [pltpu.VMEM((2, 8, QB), F32)] * 2 + [pltpu.VMEM((HEAD_S, QB), F32)] * 2,
        compiler_params=params(40),
        name="attend",
    )(tq, tk, tvt, sq, sk, svt, skt)


FC = 1024


def teacher_kernel(mix_ref, hid_ref, emb_ref, att_ref, up_ref, down_ref, out_ref, bias_ref, gain_ref, shift_ref, target_ref, norm, low, acc):
    c = pl.program_id(0)

    @pl.when(c == 0)
    def _():
        summed = hid_ref[...] + dot(mix_ref[...], att_ref[...]) + line(bias_ref, 32, 8)
        one = layer_norm(summed, line(gain_ref, 0, 8), line(shift_ref, 0, 8))
        norm[...] = one
        low[...] = one.astype(BF16)

    rows = FC // 128
    up_bias = bias_ref[pl.ds(pl.multiple_of(40 + rows * c, 8), rows), :]
    act = gelu(dot(low[...], up_ref[...]) + line(up_bias, 0, rows)).astype(BF16)
    part = dot(act, down_ref[...])

    @pl.when(c == 0)
    def _():
        acc[...] = part

    @pl.when(c > 0)
    def _():
        acc[...] += part

    @pl.when(c == pl.num_programs(0) - 1)
    def _():
        summed = norm[...] + acc[...] + line(bias_ref, 72, 8)
        two = layer_norm(summed, line(gain_ref, 8, 8), line(shift_ref, 8, 8))
        last = emb_ref[...].astype(F32) + dot(two.astype(BF16), out_ref[...]) + line(bias_ref, 80, 4)
        target_ref[...] = layer_norm(last, line(gain_ref, 16, 4), line(shift_ref, 16, 4))


def teacher(mix, hid, emb, att, up, down, out, bias, gain, shift):
    return pl.pallas_call(
        teacher_kernel,
        grid=(FF_T // FC,),
        in_specs=[
            whole(OWN, D_T),
            whole(OWN, D_T),
            whole(OWN, D_E),
            whole(D_T, D_T),
            pl.BlockSpec((D_T, FC), lambda c: (0, c)),
            pl.BlockSpec((FC, D_T), lambda c: (c, 0)),
            whole(D_T, D_E),
            whole(84, 128),
            whole(20, 128),
            whole(20, 128),
        ],
        out_specs=whole(OWN, D_E),
        out_shape=jax.ShapeDtypeStruct((OWN, D_E), F32),
        scratch_shapes=[pltpu.VMEM((OWN, D_T), F32), pltpu.VMEM((OWN, D_T), BF16), pltpu.VMEM((OWN, D_T), F32)],
        compiler_params=params(40),
        name="teacher",
    )(mix, hid, emb, att, up, down, out, bias, gain, shift)


def student_kernel(emb_ref, smix_ref, target_ref, weight_ref, win_ref, watt_ref, wup_ref, wdown_ref, wout_ref, vec_ref,
                   grad_ref, vgrad_ref, dsum_ref, dmix_ref, part_ref, states, slopes, outers, acts):

    def put(r, value):
        for i in range(value.shape[1] // 128):
            vgrad_ref[r + i : r + i + 1, :] = value[:, i * 128 : i * 128 + 128]

    total = lambda v: jnp.sum(v.astype(F32), 0, keepdims=True)
    emb = emb_ref[...]
    source = emb.astype(F32)
    first = dot(emb, win_ref[...]) + line(vec_ref, V_IN)
    mixed = jnp.concatenate([smix_ref[j].T for j in range(3)], 0).astype(BF16)
    branch = dot(mixed, watt_ref[...]) + line(vec_ref, V_ATT)
    state = line(vec_ref, V_AGAIN) * (first + branch) + line(vec_ref, V_ASHIFT)
    for i in range(FFN_COUNT):
        states[i] = state
        inner = dot(state.astype(BF16), wup_ref[i]) + line(vec_ref, V_UP + 4 * i, 4)
        half = 0.5 * (1.0 + lax.erf(inner * 0.7071067811865476))
        slopes[i] = half + inner * jnp.exp(-0.5 * inner * inner) * 0.3989422804014327
        act = (inner * half).astype(BF16)
        acts[i] = act
        pre = state + dot(act, wdown_ref[i]) + line(vec_ref, V_DOWN + i)
        outers[i] = pre
        state = line(vec_ref, V_FGAIN + i) * pre + line(vec_ref, V_FSHIFT + i)
    state_low = state.astype(BF16)
    summed = source + dot(state_low, wout_ref[...]) + line(vec_ref, V_OUT, 4)
    diff = line(vec_ref, V_OGAIN, 4) * summed + line(vec_ref, V_OSHIFT, 4) - target_ref[...]
    weight = jnp.concatenate([jnp.broadcast_to(weight_ref[j], (8, QB)).T[:, 0:1] for j in range(3)], 0)
    loss = jnp.sum(weight * jnp.sum(diff * diff, 1, keepdims=True)) * (1.0 / D_E)
    count = jnp.sum(weight)
    d_result = (weight * (2.0 / D_E)) * diff
    put(V_OGAIN, total(d_result * summed))
    put(V_OSHIFT, total(d_result))
    d_output = (d_result * line(vec_ref, V_OGAIN, 4)).astype(BF16)
    out_g = dot_tn(state_low, d_output)
    for n in range(4):
        grad_ref[pl.ds(4224 + n, 128, stride=4), :] = out_g[:, n * 128 : n * 128 + 128]
    put(V_OUT, total(d_output))
    d_state = dot_nt(d_output, wout_ref[...])
    for i in reversed(range(FFN_COUNT)):
        put(V_FGAIN + i, total(d_state * outers[i]))
        put(V_FSHIFT + i, total(d_state))
        d_sum = d_state * line(vec_ref, V_FGAIN + i)
        d_outer = d_sum.astype(BF16)
        grad_ref[2176 + 512 * i : 2176 + 512 * (i + 1), :] = dot_tn(acts[i], d_outer)
        d_inner = (dot_nt(d_outer, wdown_ref[i]) * slopes[i]).astype(BF16)
        up_g = dot_tn(states[i].astype(BF16), d_inner)
        for n in range(4):
            grad_ref[pl.ds(128 + 512 * i + n, 128, stride=4), :] = up_g[:, n * 128 : n * 128 + 128]
        put(V_UP + 4 * i, total(d_inner))
        put(V_DOWN + i, total(d_outer))
        d_state = d_sum + dot_nt(d_inner, wup_ref[i])
    put(V_AGAIN, total(d_state * (first + branch)))
    put(V_ASHIFT, total(d_state))
    d_sum = d_state * line(vec_ref, V_AGAIN)
    d_branch = d_sum.astype(BF16)
    grad_ref[0:128, :] = dot_tn(mixed, d_branch)
    put(V_ATT, total(d_branch))
    dsum_ref[...] = d_sum
    dmix_ref[...] = dot_nt(d_branch, watt_ref[...]).astype(BF16)
    for r in (0, 1, 2, 3, 47):
        vgrad_ref[r : r + 1, :] = jnp.zeros((1, 128), F32)
    row = lax.broadcasted_iota(jnp.int32, (8, 128), 0)
    lane = lax.broadcasted_iota(jnp.int32, (8, 128), 1)
    part_ref[...] = jnp.where((row == 0) & (lane == 0), loss, 0.0) + jnp.where((row == 0) & (lane == 1), count, 0.0)


def student(emb, smix, target, weight, win, watt, wup, wdown, wout, vecs):
    return pl.pallas_call(
        student_kernel,
        grid=(1,),
        in_specs=[
            whole(OWN, D_E),
            whole(3, D_S, QB),
            whole(OWN, D_E),
            whole(3, 1, QB),
            whole(D_E, D_S),
            whole(D_S, D_S),
            whole(FFN_COUNT, D_S, FF_S),
            whole(FFN_COUNT, FF_S, D_S),
            whole(D_S, D_E),
            whole(48, 128),
        ],
        out_specs=[whole(4736, 128), whole(48, 128), whole(OWN, D_S), whole(OWN, D_S), whole(8, 128)],
        out_shape=[
            jax.ShapeDtypeStruct((4736, 128), F32),
            jax.ShapeDtypeStruct((48, 128), F32),
            jax.ShapeDtypeStruct((OWN, D_S), F32),
            jax.ShapeDtypeStruct((OWN, D_S), BF16),
            jax.ShapeDtypeStruct((8, 128), F32),
        ],
        scratch_shapes=[
            pltpu.VMEM((FFN_COUNT, OWN, D_S), F32),
            pltpu.VMEM((FFN_COUNT, OWN, FF_S), F32),
            pltpu.VMEM((FFN_COUNT, OWN, D_S), F32),
            pltpu.VMEM((FFN_COUNT, OWN, FF_S), BF16),
        ],
        compiler_params=params(40),
        name="student",
    )(emb, smix, target, weight, win, watt, wup, wdown, wout, vecs)


KB = 1024


def back_kernel(et_ref, es_ref, stat_ref, smix_ref, dmix_ref, weight_ref, sq_ref, sv_ref, skt_ref, dsum_ref, emb_ref, first_ref,
                wqkv_ref, vgrad_ref, part_in, late_ref, *rest):
    state_refs, rest = rest[:6], rest[6:]
    made_ref, rest = rest[0], rest[1:]
    (dkv, dqt, ds, dq, dfirst, dmt, dmz, sqd, rows, flat, vecs, kls, block_ref, sem), buffers = rest[:14], rest[14:]
    j, kb = pl.program_id(0), pl.program_id(1)
    s_scale = HEAD_S**-0.5
    late = pltpu.make_async_copy(late_ref, flat.at[896:5632], sem)

    @pl.when((j == 0) & (kb == 0))
    def _():
        greet()
        late.start()
        vecs[...] = vgrad_ref[...]
        dkv[...] = jnp.zeros_like(dkv)
        kls[...] = jnp.zeros_like(kls)

    @pl.when((j == 0) & (kb == 1))
    def _():
        late.wait()
        pack_blocks(range(FIRST_EARLY // 2, 64), flat, vecs, block_ref)
        swap_early(block_ref, buffers)

    @pl.when((j == 1) & (kb == 0))
    def _():
        send_early(block_ref, buffers)

    @pl.when(kb == 0)
    def _():
        quarter = weight_ref[0] * (1.0 / HEADS)
        wide = dmix_ref[...].astype(F32)
        tall = wide.T
        place = lax.broadcasted_iota(jnp.int32, (D_S, 1), 0) // HEAD_S
        for h in range(HEADS):
            own = slice(h * HEAD_S, h * HEAD_S + HEAD_S)
            mine = slice(h * QB, h * QB + QB)
            t_inv, s_inv = stat_ref[0, h, 0:1, :], stat_ref[0, h, 1:2, :]
            kls[0:1, :] += quarter * stat_ref[0, h, 2:3, :]
            row_dot = jnp.sum(tall[own] * smix_ref[0, own, :], 0, keepdims=True)
            rows[h, 0:1, :] = row_dot - quarter
            rows[h, 1:2, :] = s_inv
            rows[h, 2:3, :] = quarter * t_inv
            dmt[h] = jnp.where(place == h, tall, 0.0).astype(BF16)
            dmz[mine, :] = head_lanes(wide * stat_ref[0, h].T[:, 1:2], h).astype(BF16)
            sqd[mine, :] = head_lanes(sq_ref[...], h)
        dqt[...] = jnp.zeros_like(dqt)

    here = pl.ds(pl.multiple_of(slot_of(j) * SEQ + kb * KB, KB), KB)
    dkv[here, D_S:] += dot(es_ref[0], dmz[...])
    for h in range(HEADS):
        lanes = slice(h * QB, h * QB + QB)
        for c in range(KB // 256):
            part = slice(c * 256, c * 256 + 256)
            d_probs = dot(sv_ref[part, :], dmt[h])
            s_exp, t_exp = es_ref[0, part, lanes].astype(F32), et_ref[0, part, lanes].astype(F32)
            d_scores = (d_probs - rows[h, 0:1, :]) * rows[h, 1:2, :] * s_exp - t_exp * rows[h, 2:3, :]
            ds[part, lanes] = d_scores.astype(BF16)
        own = slice(h * HEAD_S, h * HEAD_S + HEAD_S)
        dqt[own, :] += dot(skt_ref[own, :], ds[:, lanes])
    dkv[here, :D_S] += dot(ds[...], sqd[...])

    @pl.when(kb == pl.num_programs(1) - 1)
    def _():
        dq[pl.ds(pl.multiple_of(j * QB, QB), QB), :] = (dqt[...] * s_scale).T

    @pl.when((j == 2) & (kb == pl.num_programs(1) - 1))
    def _():
        qkv_w = wqkv_ref[...]
        dq_low = dq[...].astype(BF16)
        own = pl.ds(pl.multiple_of(first_block() * QB, QB), OWN)
        q_grad = dot_tn(first_ref[own, :], dq_low)
        own_part = dsum_ref[...] + dot_nt(dq_low, qkv_w[:, :D_S])
        kv_grad = jnp.zeros((D_S, 2 * D_S), F32)
        kv_bias = jnp.zeros((1, 2 * D_S), F32)
        for c in range(8):
            part = pl.ds(c * 512, 512)
            wide = dkv[part, :]
            low = jnp.concatenate([(wide[:, :D_S] * s_scale).astype(BF16), wide[:, D_S:].astype(BF16)], 1)
            kv_grad += dot_tn(first_ref[part, :], low)
            kv_bias += jnp.sum(low.astype(F32), 0, keepdims=True)
            dfirst[part, :] = dot_nt(low, qkv_w[:, D_S:])
        dfirst[own, :] += own_part
        in_grad = jnp.zeros((D_S, D_E), F32)
        in_bias = jnp.zeros((1, D_S), F32)
        two = has_two()
        for c in range(8):
            part = pl.ds(c * 512, 512)
            low = dfirst[part, :].astype(BF16)
            emb = emb_ref[part, :]
            if c >= 4:
                emb = jnp.where(two, emb, jnp.zeros_like(emb))
            in_grad += dot_tn(low, emb)
            in_bias += jnp.sum(low.astype(F32), 0, keepdims=True)
        flat[0:512, :] = in_grad.T
        flat[pl.ds(512, 128, stride=3), :] = q_grad
        flat[pl.ds(513, 128, stride=3), :] = kv_grad[:, :D_S]
        flat[pl.ds(514, 128, stride=3), :] = kv_grad[:, D_S:]
        vecs[0:1, :] = in_bias
        vecs[1:2, :] = jnp.sum(dq_low.astype(F32), 0, keepdims=True)
        vecs[2:3, :] = kv_bias[:, :D_S]
        vecs[3:4, :] = kv_bias[:, D_S:]
        pack_blocks(range(FIRST_EARLY // 2), flat, vecs, block_ref)
        kl = jnp.sum(kls[0:1, :], keepdims=True)
        corner = lax.broadcasted_iota(jnp.int32, (1, 128), 1) == 0
        send_rest(block_ref, buffers)
        update(block_ref, part_in[0:1, :] + jnp.where(corner, kl, 0.0), state_refs, made_ref, buffers)


def back(et, es, stat, smix, dmix, weight, sq, sv, skt, dsum, emb, first, wqkv, vgrad, part, late, *state):
    count = SEQ // KB
    place = lambda j, k: slot_of(j) * count + k
    dma = pltpu.SemaphoreType.DMA
    return pl.pallas_call(
        back_kernel,
        grid=(3, count),
        in_specs=[
            pl.BlockSpec((1, KB, HEADS * QB), lambda j, k: (j, k, 0)),
            pl.BlockSpec((1, KB, HEADS * QB), lambda j, k: (j, k, 0)),
            pl.BlockSpec((1, HEADS, 8, QB), lambda j, k: (j, 0, 0, 0)),
            pl.BlockSpec((1, D_S, QB), lambda j, k: (j, 0, 0)),
            pl.BlockSpec((QB, D_S), lambda j, k: (j, 0)),
            pl.BlockSpec((1, 1, QB), lambda j, k: (j, 0, 0)),
            pl.BlockSpec((QB, D_S), lambda j, k: (first_block() + j, 0)),
            pl.BlockSpec((KB, D_S), lambda j, k: (place(j, k), 0)),
            pl.BlockSpec((D_S, KB), lambda j, k: (0, place(j, k))),
            whole(OWN, D_S),
            whole(SLOTS, D_E),
            whole(SLOTS, D_S),
            whole(D_S, 3 * D_S),
            whole(48, 128),
            whole(8, 128),
            pl.BlockSpec(memory_space=pl.ANY),
        ]
        + [whole(SHARD, 128), whole(1, 47)] * 3,
        out_specs=whole(3 * BLOCK + 8, 128),
        out_shape=jax.ShapeDtypeStruct((3 * BLOCK + 8, 128), F32),
        scratch_shapes=[
            pltpu.VMEM((SLOTS, 2 * D_S), F32),
            pltpu.VMEM((D_S, QB), F32),
            pltpu.VMEM((KB, HEADS * QB), BF16),
            pltpu.VMEM((OWN, D_S), F32),
            pltpu.VMEM((SLOTS, D_S), F32),
            pltpu.VMEM((HEADS, D_S, QB), BF16),
            pltpu.VMEM((HEADS * QB, D_S), BF16),
            pltpu.VMEM((HEADS * QB, D_S), BF16),
            pltpu.VMEM((HEADS, 8, QB), F32),
            pltpu.VMEM((5632, 128), F32),
            pltpu.VMEM((48, 128), F32),
            pltpu.VMEM((8, QB), F32),
            pltpu.VMEM((4, 2, 16, BLOCK, 128), BF16),
            dma,
            pltpu.VMEM((3, BLOCK, 128), F32),
            pltpu.VMEM((4, 16, BLOCK, 128), BF16),
            pltpu.VMEM((BLOCK, 128), F32),
            pltpu.VMEM((64, BLOCK, 128), BF16),
            pltpu.VMEM((64, BLOCK, 128), BF16),
            pltpu.VMEM((2, 2, 8, 128), F32),
            pltpu.VMEM((2, 16, 8, 128), F32),
            pltpu.VMEM((2, 8, 8, 128), F32),
            dma((2, 6)),
            dma((64,)),
            dma((64,)),
            dma((2, 16)),
            dma((2, 16)),
            dma((2, 8)),
            dma((2, 8)),
        ],
        compiler_params=params(44, collective_id=1, has_side_effects=True),
        name="back",
    )(et, es, stat, smix, dmix, weight, sq, sv, skt, dsum, emb, first, wqkv, vgrad, part, late, *state)


def chip(k):
    dp, fs = lax.axis_index("dp"), lax.axis_index("fsdp")
    return (2 * ((dp // 2 + k // 16) % 4) + dp % 2, (fs + k) % 16)


def greet():
    dp, fs = lax.axis_index("dp"), lax.axis_index("fsdp")
    barrier = pltpu.get_barrier_semaphore()

    def signal(k, _):
        pl.semaphore_signal(barrier, inc=1, device_id=chip(k), device_id_type=MESH)
        return 0

    lax.fori_loop(1, 64, signal, 0)
    for k in range(4):
        other = (2 * ((dp // 2 + k) % 4) + 1 - dp % 2, fs)
        pl.semaphore_signal(barrier, inc=1, device_id=other, device_id_type=MESH)


FIRST_EARLY = 22


def pack_blocks(pairs, flat, vecs, block_ref):
    lane = lax.broadcasted_iota(jnp.int32, (1, 128), 1)
    rest = jnp.zeros((BLOCK - SHARD - 1, 128), F32)
    for pair in pairs:
        both = flat[88 * pair : 88 * pair + 88, :]
        for i in range(2):
            owner = 2 * pair + i
            row, shift = divmod(47 * owner, 128)
            entries = vecs[row : row + 1, :]
            if shift + 47 > 128:
                entries = jnp.where(lane >= shift, entries, vecs[row + 1 : row + 2, :])
            if shift:
                entries = pltpu.roll(entries, 128 - shift, 1)
            entries = jnp.where(lane < 47, entries, 0.0)
            mine = both[SHARD * i : SHARD * (i + 1)]
            block_ref[owner // 32, owner // 16 % 2, owner % 16] = jnp.concatenate([mine, entries, rest], 0).astype(BF16)


SPLIT = FIRST_EARLY - 16


def swap_copy(n, g_ref, half_in, half_sems):
    dp, fs = lax.axis_index("dp"), lax.axis_index("fsdp")
    core = dp % 2
    if n in (1, 2, 3):
        source, goal = g_ref.at[n, 1 - core], half_in.at[n]
    elif n == 0:
        source, goal = g_ref.at[0, 1, 0:SPLIT], half_in.at[0, 0:SPLIT]
    elif n == 4:
        source, goal = g_ref.at[0, 1, SPLIT:16], half_in.at[0, SPLIT:16]
    else:
        source, goal = g_ref.at[0, 0], half_in.at[0]
    return pltpu.make_async_remote_copy(
        source, goal, half_sems.at[0, n], half_sems.at[1, n], device_id=(dp + 1 - 2 * core, fs), device_id_type=MESH
    )


def swap_early(g_ref, buffers):
    half_in, half_sems = buffers[1], buffers[8]
    pl.semaphore_wait(pltpu.get_barrier_semaphore(), 67)
    for n in (1, 2, 3):
        swap_copy(n, g_ref, half_in, half_sems).start()

    @pl.when(lax.axis_index("dp") % 2 == 0)
    def _():
        swap_copy(4, g_ref, half_in, half_sems).start()


def block_copy(k, buffers):
    block_out, blocks_in, block_send, block_recv = buffers[3], buffers[4], buffers[9], buffers[10]
    dp, fs = lax.axis_index("dp"), lax.axis_index("fsdp")
    place = (dp // 2 + k // 16) % 4 * 16 + (fs + k) % 16
    return pltpu.make_async_remote_copy(
        block_out.at[place], blocks_in.at[k], block_send.at[k], block_recv.at[k], device_id=chip(k), device_id_type=MESH
    )


def is_early(place):
    return (place >= 16) | ((lax.axis_index("dp") % 2 == 1) & (place >= SPLIT))


def join_and_send(early, g_ref, buffers):
    half_in, block_out = buffers[1], buffers[3]
    dp, fs = lax.axis_index("dp"), lax.axis_index("fsdp")
    core = dp % 2

    def join(i, _):
        @pl.when(is_early(i) == early)
        def _():
            summed = g_ref[i // 16, core, i % 16].astype(F32) + half_in[i // 16, i % 16].astype(F32)
            block_out[i] = summed.astype(BF16)

        return 0

    lax.fori_loop(0, 64 if early else 16, join, 0)

    def start(k, _):
        place = (dp // 2 + k // 16) % 4 * 16 + (fs + k) % 16

        @pl.when(is_early(place) == early)
        def _():
            block_copy(k, buffers).start()

        return 0

    lax.fori_loop(1, 64, start, 0)


def send_early(g_ref, buffers):
    half_in, half_sems = buffers[1], buffers[8]
    core = lax.axis_index("dp") % 2
    for n in (1, 2, 3):
        swap_copy(n, g_ref, half_in, half_sems).wait()

    @pl.when(core == 0)
    def _():
        swap_copy(4, g_ref, half_in, half_sems).wait_send()

    @pl.when(core == 1)
    def _():
        swap_copy(4, g_ref, half_in, half_sems).wait_recv()

    join_and_send(True, g_ref, buffers)


def send_rest(g_ref, buffers):
    half_in, half_sems = buffers[1], buffers[8]
    core = lax.axis_index("dp") % 2

    @pl.when(core == 0)
    def _():
        swap_copy(0, g_ref, half_in, half_sems).start()
        swap_copy(5, g_ref, half_in, half_sems).wait_recv()
        swap_copy(0, g_ref, half_in, half_sems).wait_send()

    @pl.when(core == 1)
    def _():
        swap_copy(5, g_ref, half_in, half_sems).start()
        swap_copy(0, g_ref, half_in, half_sems).wait_recv()
        swap_copy(5, g_ref, half_in, half_sems).wait_send()

    join_and_send(False, g_ref, buffers)


def update(g_ref, part, state_refs, made_ref, buffers):
    master_mat, master_vec, first_mat, first_vec, second_mat, second_vec = state_refs
    (packs, half_in, mine, block_out, blocks_in, tile_out, tiles_f, tiles_d,
     half_sems, block_send, block_recv, f_send, f_recv, d_send, d_recv) = buffers
    dp, fs = lax.axis_index("dp"), lax.axis_index("fsdp")
    x, core = dp // 2, dp % 2
    packs[...] = jnp.zeros_like(packs)
    for i, (mat, vec) in enumerate([(master_mat, master_vec), (first_mat, first_vec), (second_mat, second_vec)]):
        packs[i, 0:SHARD, :] = mat[...]
        packs[i, SHARD : SHARD + 1, 0:47] = vec[...]
    mine[...] = g_ref[x, core, fs].astype(F32) + half_in[x, fs].astype(F32)

    def gather(k, _):
        block_copy(k, buffers).wait()
        mine[...] += blocks_in[k].astype(F32)
        return 0

    lax.fori_loop(1, 64, gather, 0)

    row = lax.broadcasted_iota(jnp.int32, (BLOCK, 1), 0)
    place = (dp * 16 + fs) * SHARD + row
    is_matrix = row < SHARD
    bounds = [0]
    for rows in MAT_ROWS:
        bounds.append(bounds[-1] + rows)
    members = [is_matrix & (place >= bounds[i]) & (place < bounds[i + 1]) for i in range(6)]

    def everyone(tile, turn):
        tile_out[turn, 0] = tile
        tiles_d[turn, dp] = tile

        def f_copy(k):
            return pltpu.make_async_remote_copy(
                tile_out.at[turn, 1], tiles_f.at[turn, fs], f_send.at[turn, k], f_recv.at[turn, k],
                device_id=(dp, (fs + k) % 16), device_id_type=MESH,
            )

        def d_copy(k):
            return pltpu.make_async_remote_copy(
                tile_out.at[turn, 0], tiles_d.at[turn, dp], d_send.at[turn, k], d_recv.at[turn, k],
                device_id=((dp + k) % 8, fs), device_id_type=MESH,
            )

        for k in range(1, 8):
            d_copy(k).start()
        for k in range(1, 8):
            d_copy(k).wait()
        total = tiles_d[turn, 0]
        for k in range(1, 8):
            total = total + tiles_d[turn, k]
        tile_out[turn, 1] = total
        tiles_f[turn, fs] = total
        for k in range(1, 16):
            f_copy(k).start()
        for k in range(1, 16):
            f_copy(k).wait()
        total = tiles_f[turn, 0]
        for k in range(1, 16):
            total = total + tiles_f[turn, k]
        return total

    column = lambda v: jnp.sum(v, 0, keepdims=True)

    def tile_of(rows):
        return jnp.concatenate(rows + [jnp.zeros((8 - len(rows), 128), F32)] * (len(rows) < 8), 0)

    grad = mine[...]
    master = packs[0]
    squares = master * master
    tile = everyone(
        tile_of([part, column(grad * grad)] + [column(jnp.where(members[i], squares, 0.0)) for i in range(6)]), 0
    )
    loss, count = tile[0:1, 0:1], tile[0:1, 1:2]
    sums = jnp.sum(tile, 1, keepdims=True)
    inverse = 1.0 / count
    norm = jnp.sqrt(sums[1:2]) * inverse
    factor = CLIP_NORM / jnp.maximum(norm, CLIP_NORM)
    grad = grad * inverse * factor
    first = BETA_ONE * packs[1] + (1.0 - BETA_ONE) * grad
    second = BETA_TWO * packs[2] + (1.0 - BETA_TWO) * grad * grad
    ratio = first / (1.0 - BETA_ONE**STEP) / (jnp.sqrt(second / (1.0 - BETA_TWO**STEP)) + ADAM_EPS)
    ratio = ratio + jnp.where(is_matrix, WEIGHT_DECAY * master, 0.0)
    squares = ratio * ratio
    steps = everyone(tile_of([column(jnp.where(members[i], squares, 0.0)) for i in range(6)]), 1)
    made_ref[BLOCK : 2 * BLOCK, :] = first
    made_ref[2 * BLOCK : 3 * BLOCK, :] = second
    trusts = jnp.sqrt(sums[2:8]) / jnp.sqrt(jnp.sum(steps, 1, keepdims=True)[0:6])
    trust = jnp.ones((BLOCK, 1), F32)
    for i in range(6):
        trust = jnp.where(members[i], trusts[i : i + 1], trust)
    made_ref[0:BLOCK, :] = master - LEARN_RATE * (trust * ratio)
    lane = lax.broadcasted_iota(jnp.int32, (8, 128), 1)
    made_ref[3 * BLOCK :, :] = jnp.where(lane == 0, loss, jnp.where(lane == 1, count, norm))


def finish_kernel(made, loss, count, norm, m0, m1, m2, v0, v1, v2):
    for i, (mat, vec) in enumerate(((m0, v0), (m1, v1), (m2, v2))):
        mat[...] = made[BLOCK * i : BLOCK * i + SHARD, :]
        vec[...] = made[BLOCK * i + SHARD : BLOCK * i + SHARD + 1, 0:47]
    for i, out in enumerate((loss, count, norm)):
        out[...] = made[3 * BLOCK : 3 * BLOCK + 1, i : i + 1]


def finish(made):
    vmem = pl.BlockSpec(memory_space=pltpu.VMEM)
    shape = lambda *dims: jax.ShapeDtypeStruct(dims, F32)
    return pl.pallas_call(
        finish_kernel,
        in_specs=[vmem],
        out_specs=[vmem] * 9,
        out_shape=[shape(1, 1)] * 3 + [shape(SHARD, 128)] * 3 + [shape(1, 47)] * 3,
        compiler_params=params(63),
        name="finish",
    )(made)


def per_device(
    token_ids,
    splits,
    valid_mask,
    embed_table,
    embed_proj,
    embed_bias,
    type_table,
    teach_in,
    teach_qkv,
    teach_att,
    teach_up,
    teach_down,
    teach_out,
    teach_bias,
    teach_gain,
    teach_shift,
    matrices,
    vectors,
    matrix_first,
    matrix_second,
    vector_first,
    vector_second,
):
    mat = lambda v: v.reshape(SHARD, 128)
    vec = lambda v: v.reshape(1, 47)
    rows_128 = lambda v: v.reshape(-1, 128)
    bias = rows_128(teach_bias)
    emb, t_keys, t_values, own_emb, hidden, t_queries, weights, packed = front(
        token_ids, embed_table, embed_table, valid_mask, splits, mat(matrices), vec(vectors), embed_proj, teach_in, teach_qkv,
        rows_128(embed_bias), type_table, bias,
    )
    first, s_q, s_k, s_v, s_kt, s_vt, in_w, qkv_w, att_w, up_w, down_w, out_w, vecs = student_in(emb, packed)
    et, es, t_mixed, s_mixed, stat = attend(t_queries, t_keys, t_values, s_q, s_k, s_vt, s_kt)
    target = teacher(
        t_mixed, hidden, own_emb, teach_att, teach_up, teach_down, teach_out, bias, rows_128(teach_gain), rows_128(teach_shift)
    )
    late, vgrads, d_sum, d_mixed, part = student(
        own_emb, s_mixed, target, weights, in_w, att_w, up_w, down_w, out_w, vecs
    )
    made = back(
        et, es, stat, s_mixed, d_mixed, weights, s_q, s_v, s_kt, d_sum, emb, first, qkv_w, vgrads, part, late,
        mat(matrices), vec(vectors), mat(matrix_first), vec(vector_first), mat(matrix_second), vec(vector_second),
    )
    loss, count, norm, m0, m1, m2, v0, v1, v2 = finish(made)
    flat = lambda v: v.reshape(-1)
    scalar = lambda v: v.reshape(())
    return (
        scalar(loss), scalar(count), scalar(norm), flat(m0), flat(m1), flat(m2), flat(v0), flat(v1), flat(v2),
    )


def solution(mesh):
    both = P(("dp", "fsdp"))
    return jax.shard_map(
        per_device,
        mesh=mesh,
        in_specs=(P("dp", "fsdp"), P("dp"), P("dp", "fsdp")) + (P(),) * 13 + (both,) * 6,
        out_specs=(P(), P(), P(), both, both, both, both, both, both),
        check_vma=False,
    )
```

```python
import functools
import math

import jax
import jax.numpy as jnp
from jax import lax
from jax.experimental import pallas as pl
from jax.experimental.pallas import tpu as pltpu
from jax.sharding import PartitionSpec as P

D_E = 512
D_T = 1024
FF_T = 4096
D_S = 128
FF_S = 512
HEADS = 4
FFN_COUNT = 4
STEP = 5
HEAD_T = 256
HEAD_S = 32
SEQ = 2048
QB = 256
OWN = 3 * QB
SLOTS = 2 * SEQ

CLIP_NORM = 0.05
BETA_ONE = 0.9
BETA_TWO = 0.999
LEARN_RATE = 0.3
WEIGHT_DECAY = 0.01
ADAM_EPS = 1e-06

F32 = jnp.float32
BF16 = jnp.bfloat16
LOG2E = 1.4426950408889634
MESH = pl.DeviceIdType.MESH

MAT_ROWS = (512, 384, 128, 2048, 2048, 512)
SHARD = 44
BLOCK = 48
(V_IN, V_QKV, V_ATT, V_AGAIN, V_ASHIFT, V_UP, V_DOWN, V_FGAIN, V_FSHIFT, V_OUT, V_OGAIN, V_OSHIFT) = (
    0, 1, 4, 5, 6, 7, 23, 27, 31, 35, 39, 43)


def dot(left, right):
    return jnp.dot(left, right, preferred_element_type=F32)


def dot_nt(left, right):
    return lax.dot_general(left, right, (((1,), (1,)), ((), ())), preferred_element_type=F32)


def dot_tn(left, right):
    return lax.dot_general(left, right, (((0,), (0,)), ((), ())), preferred_element_type=F32)


def layer_norm(values, gain, shift):
    center = values - jnp.mean(values, -1, keepdims=True)
    spread = jnp.mean(center * center, -1, keepdims=True)
    return center * lax.rsqrt(spread + 1e-05) * gain + shift


def gelu(values):
    return 0.5 * values * (1.0 + lax.erf(values * 0.7071067811865476))


def params(mib, **more):
    return pltpu.CompilerParams(vmem_limit_bytes=mib * 2**20, **more)


def whole(*shape):
    return pl.BlockSpec(shape, lambda *_: (0,) * len(shape))


def line(ref, row, count=1):
    if count == 1:
        return ref[row : row + 1, :]
    return jnp.concatenate([ref[row + i : row + i + 1, :] for i in range(count)], 1)


def fold(values, op=jnp.sum):
    return op(values.reshape(values.shape[0] // 8, 8, values.shape[1]), 0)


def spots():
    dp, fs = lax.axis_index("dp"), lax.axis_index("fsdp")
    return dp // 2, dp % 2, fs // 4, fs % 4


def place_in_group():
    _, core, _, y = spots()
    return 2 * y + core


def first_block():
    return (3 * place_in_group()) % 8


def slot_of(j):
    return (first_block() + j) // 8


def has_two():
    i = place_in_group()
    return (i == 2) | (i == 5)


PT = 512
TILES = SEQ // PT
C_TILE = 2


CHUNK = 2048
VOCAB = 30522
WHOLE = VOCAB // 16 * 16


def front_kernel(ids_ref, table_hbm, tail_ref, mask_ref, splits_ref, mats_ref, vecs_ref, proj_hbm, win_hbm, wqkv_hbm, ebias_ref,
                 types_ref, bias_ref, emb_hbm, k_hbm, vt_hbm, own_hbm, hid_hbm, tq_ref, weight_ref, params_hbm,
                 own_ref, hid_ref, params_ref, table_low, table, picked, e_ref, note, notes, wide, block, e_all, proj_ref, win_ref, wqkv_ref, emb_t, k_t, vt_t,
                 t_sem, load, e_send, e_recv, n_send, n_recv, a_send, a_recv, b_send, b_recv, c_send, c_recv,
                 out, s_send, s_recv, own_sem, last_sem):
    dp, me = lax.axis_index("dp"), lax.axis_index("fsdp")
    x, core, z, y = spots()
    i = 2 * y + core
    sibling = (2 * x + 1 - core, me)
    source_dp = 2 * x + z // 2
    is_source = z // 2 == core
    loads = [
        pltpu.make_async_copy(hbm, ref, load.at[n])
        for n, (hbm, ref) in enumerate([(proj_hbm, proj_ref), (win_hbm, win_ref), (wqkv_hbm, wqkv_ref)])
    ]
    barrier = pltpu.get_barrier_semaphore()

    def signal(device):
        pl.semaphore_signal(barrier, inc=1, device_id=device, device_id_type=MESH)

    def greet_source(f, _):
        @pl.when(jnp.logical_not(is_source & (f == me)))
        def _():
            signal((source_dp, f))

        return 0

    def greet_plane(k, _):
        signal((dp, (me + k) % 16))
        return 0

    lax.fori_loop(0, 16, greet_source, 0)
    lax.fori_loop(1, 16, greet_plane, 0)
    for k in range(1, 4):
        signal((2 * ((x + k) % 4) + core, me))
    signal(sibling)
    chunks = [(c, min(CHUNK, WHOLE - c)) for c in range(0, WHOLE, CHUNK)]
    table_copies = [
        pltpu.make_async_copy(table_hbm.at[pl.ds(c, size)], table_low.at[pl.ds(c, size)], t_sem.at[n])
        for n, (c, size) in enumerate(chunks)
    ]
    for copy in table_copies:
        copy.start()

    lane = lax.broadcasted_iota(jnp.int32, (1, 128), 1)
    note[0:6, :] = mask_ref[...]
    line_of_splits = jnp.zeros((1, 128), jnp.int32)
    for r in range(6):
        line_of_splits = jnp.where(lane == r, splits_ref[r], line_of_splits)
    note[6:7, :] = line_of_splits
    note[7:8, :] = jnp.zeros((1, 128), jnp.int32)
    wide[...] = jnp.zeros((BLOCK, 128), F32)
    wide[0:SHARD, :] = mats_ref[...]
    wide[SHARD : SHARD + 1, 0:47] = vecs_ref[...]
    block[...] = wide[...].astype(BF16)
    params_ref[dp * 16 + me] = block[...]
    main = (3 * i + 1) // 8
    for copy, (c, size) in zip(table_copies, chunks):
        copy.wait()
        table[c : c + size, :] = table_low[c : c + size, :].astype(F32)
    for copy in loads:
        copy.start()
    table[WHOLE:VOCAB, :] = tail_ref[...].astype(F32)[0 : VOCAB - WHOLE]

    def pick(g, _):
        for u in range(16):
            token = ids_ref[g // 8, g % 8 * 16 + u]
            picked[pl.ds(g * 16 + u, 1), :] = table[pl.ds(token, 1), :]
        return 0

    lax.fori_loop(0, 48, pick, 0)
    for r in range(6):
        e_ref[r] = picked[128 * r : 128 * r + 128, :].astype(BF16)

    @pl.when(is_source)
    def _():
        e_all[pl.ds(pl.multiple_of(me * 128, 128), 128), :] = e_ref[3 * (z % 2) + main]
        notes[me] = note[...]

    pl.semaphore_wait(barrier, jnp.where(is_source, 15, 16) + 15 + 3 + 1)

    def a_copy(k):
        return pltpu.make_async_remote_copy(
            block, params_ref.at[dp * 16 + me], a_send.at[k], a_recv.at[k], device_id=(dp, (me + k) % 16), device_id_type=MESH
        )

    def b_copy(k):
        mine = params_ref.at[pl.ds(dp * 16, 16)]
        return pltpu.make_async_remote_copy(
            mine, mine, b_send.at[k], b_recv.at[k], device_id=(2 * ((x + k) % 4) + core, me), device_id_type=MESH
        )

    def c_copy(k):
        mine = params_ref.at[pl.ds((2 * ((x + k) % 4) + core) * 16, 16)]
        return pltpu.make_async_remote_copy(mine, mine, c_send.at[k], c_recv.at[k], device_id=sibling, device_id_type=MESH)

    def a_start(k, _):
        a_copy(k).start()
        return 0

    def a_wait(k, _):
        a_copy(k).wait()
        return 0

    def e_copy(d, noted):
        zd, yd, cd = 2 * core + d // 8, d // 2 % 4, d % 2
        where = dict(device_id=(2 * x + cd, 4 * zd + yd), device_id_type=MESH)
        if noted:
            return pltpu.make_async_remote_copy(note, notes.at[me], n_send.at[d], n_recv.at[me], **where)
        row = 3 * (d // 8) + (3 * (2 * yd + cd) + 1) // 8
        here = pl.ds(pl.multiple_of(me * 128, 128), 128)
        return pltpu.make_async_remote_copy(e_ref.at[row], e_all.at[here], e_send.at[d], e_recv.at[me], **where)

    def is_other(d):
        return jnp.logical_not((2 * core + d // 8 == z) & (d // 2 % 4 == y) & (d % 2 == core))

    def e_start(n, _):
        d = (n + me) % 16

        @pl.when(is_other(d))
        def _():
            e_copy(d, False).start()

        return 0

    def n_start(n, _):
        d = (n + me) % 16

        @pl.when(is_other(d))
        def _():
            e_copy(d, True).start()

        return 0

    lax.fori_loop(1, 16, a_start, 0)
    lax.fori_loop(0, 16, e_start, 0)
    lax.fori_loop(0, 16, n_start, 0)

    def e_sent(d, _):
        @pl.when(is_other(d))
        def _():
            e_copy(d, False).wait_send()
            e_copy(d, True).wait_send()

        return 0

    def e_arrived(f, _):
        @pl.when(jnp.logical_not(is_source & (f == me)))
        def _():
            where = dict(device_id=(source_dp, f), device_id_type=MESH)
            there = pl.ds(pl.multiple_of(f * 128, 128), 128)
            pltpu.make_async_remote_copy(e_ref.at[0], e_all.at[there], e_send.at[0], e_recv.at[f], **where).wait_recv()

        return 0

    def n_arrived(f, _):
        @pl.when(jnp.logical_not(is_source & (f == me)))
        def _():
            where = dict(device_id=(source_dp, f), device_id_type=MESH)
            pltpu.make_async_remote_copy(note, notes.at[f], n_send.at[0], n_recv.at[f], **where).wait_recv()

        return 0

    gives = ((y == 1) & (core == 1)) | ((y == 2) & (core == 0))
    takes = has_two()
    main_slot = jnp.where(i == 5, 1, 0)
    his_slot = jnp.where(y == 1, 1, 0)

    made = ((emb_t, emb_hbm), (k_t, k_hbm), (vt_t, vt_hbm))

    def target(n, slot, t):
        rows = pl.ds(pl.multiple_of(slot * SEQ + t * PT, PT), PT)
        return made[n][1].at[:, rows] if n == 2 else made[n][1].at[rows]

    def out_copy(n, t):
        return pltpu.make_async_copy(made[n][0].at[t % 2], target(n, main_slot, t), out.at[n, t % 2])

    def give_copy(n, t):
        return pltpu.make_async_remote_copy(
            made[n][0].at[t % 2], target(n, his_slot, t), s_send.at[n, t], s_recv.at[n, t],
            device_id=sibling, device_id_type=MESH,
        )

    def settle(t, parts):
        for n in parts:
            out_copy(n, t).wait()

        @pl.when(gives)
        def _():
            for n in parts:
                give_copy(n, t).wait_send()

    per = SEQ // PT
    row = lax.broadcasted_iota(jnp.int32, (PT, 1), 0)
    lax.fori_loop(1, 16, a_wait, 0)
    for k in range(1, 4):
        b_copy(k).start()
    c_copy(0).start()
    for t in range(TILES):
        b = t % 2
        lax.fori_loop(4 * t + (1 if t else 0), min(4 * t + 5, 16), e_arrived, 0)
        if t == 0:
            n_arrived(0, 0)
            loads[0].wait()
            split = jnp.sum(jnp.where(lane == 3 * (z % 2) + main, notes[0, 6:7, :], 0), keepdims=True)
        mid = e_all[t * PT : t * PT + PT, :]
        if t:
            before = e_all[t * PT - 16 : t * PT, :].astype(F32)[15:16]
        else:
            before = jnp.zeros((1, 128), F32)
        if t < TILES - 1:
            after = e_all[t * PT + PT : t * PT + PT + 16, :].astype(F32)[0:1]
        else:
            after = jnp.zeros((1, 128), F32)
        broad = mid.astype(F32)
        left = jnp.where(row == 0, before, pltpu.roll(broad, 1, 0)).astype(BF16)
        right = jnp.where(row == PT - 1, after, pltpu.roll(broad, PT - 1, 0)).astype(BF16)
        trigram = jnp.concatenate([left, mid, right], 1)
        typed = jnp.where(row + t * PT >= split, types_ref[1:2, :], types_ref[0:1, :])
        emb = (dot(trigram, proj_ref[...]) + line(ebias_ref, 0, 4) + typed).astype(BF16)
        if t == 0:
            loads[1].wait()
        hidden = (dot(emb, win_ref[...]) + line(bias_ref, 0, 8)).astype(BF16)
        if t == 0:
            loads[2].wait()
        keys = (dot(hidden, wqkv_ref[:, D_T : 2 * D_T]) + line(bias_ref, 16, 8)).astype(BF16)
        values = (dot(hidden, wqkv_ref[:, 2 * D_T :]) + line(bias_ref, 24, 8)).astype(BF16)
        if t >= 2:
            settle(t - 2, range(3))
        emb_t[b] = emb
        k_t[b] = keys
        vt_t[b] = values.T
        for n in range(3):
            out_copy(n, t).start()

        @pl.when(gives)
        def _(t=t):
            for n in range(3):
                give_copy(n, t).start()


        if t == C_TILE:
            for k in range(1, 4):
                b_copy(k).wait()
                c_copy(4 - k).start()
    for t in range(TILES - 2, TILES):
        settle(t, [0])

    def arrive(n):
        @pl.when(takes)
        def _():
            for t in range(TILES):
                give_copy(n, t).wait_recv()

    arrive(0)
    own = pltpu.make_async_copy(emb_hbm.at[pl.ds(pl.multiple_of(first_block() * QB, QB), OWN)], own_ref, own_sem)
    own.start()
    lax.fori_loop(1, 16, n_arrived, 0)
    for j in range(3):
        t = first_block() + j
        local = 3 * (z % 2) + (3 * i + j) // 8
        for half in range(2):
            weight_ref[j, :, half * 128 : half * 128 + 128] = notes[2 * (t % 8) + half, pl.ds(local, 1), :].astype(F32)
    own.wait()
    finals = [
        pltpu.make_async_copy(ref, hbm, last_sem.at[n])
        for n, (ref, hbm) in enumerate([(own_ref, own_hbm), (hid_ref, hid_hbm), (params_ref, params_hbm)])
    ]
    finals[0].start()
    hidden = dot(own_ref[...], win_ref[...]) + line(bias_ref, 0, 8)
    hid_ref[...] = hidden
    finals[1].start()
    for k in range(4):
        c_copy(k).wait()
    finals[2].start()
    queries = (dot(hidden.astype(BF16), wqkv_ref[:, :D_T]) + line(bias_ref, 8, 8)).astype(BF16)
    tq_ref[...] = queries * jnp.asarray(HEAD_T**-0.5, BF16)
    lax.fori_loop(0, 16, e_sent, 0)
    for t in range(TILES - 2, TILES):
        settle(t, [1, 2])
    arrive(1)
    arrive(2)
    for copy in finals:
        copy.wait()


def front(ids, table, table_end, mask, splits, mats, vecs, proj, win, wqkv, ebias, types, bias):
    vmem = pl.BlockSpec(memory_space=pltpu.VMEM)
    hbm = pl.BlockSpec(memory_space=pl.ANY)
    smem = pl.BlockSpec(memory_space=pltpu.SMEM)
    tail = pl.BlockSpec((16, 128), lambda _: (WHOLE // 16, 0))
    dma = pltpu.SemaphoreType.DMA
    return pl.pallas_call(
        front_kernel,
        grid=(1,),
        in_specs=[smem, hbm, tail, vmem, smem, vmem, vmem, hbm, hbm, hbm, vmem, vmem, vmem],
        out_specs=[hbm, hbm, hbm, hbm, hbm, vmem, vmem, hbm],
        out_shape=[
            jax.ShapeDtypeStruct((SLOTS, D_E), BF16),
            jax.ShapeDtypeStruct((SLOTS, D_T), BF16),
            jax.ShapeDtypeStruct((D_T, SLOTS), BF16),
            jax.ShapeDtypeStruct((OWN, D_E), BF16),
            jax.ShapeDtypeStruct((OWN, D_T), F32),
            jax.ShapeDtypeStruct((OWN, D_T), BF16),
            jax.ShapeDtypeStruct((3, 1, QB), F32),
            jax.ShapeDtypeStruct((128, BLOCK, 128), BF16),
        ],
        scratch_shapes=[
            pltpu.VMEM((OWN, D_E), BF16),
            pltpu.VMEM((OWN, D_T), F32),
            pltpu.VMEM((128, BLOCK, 128), BF16),
            pltpu.VMEM((WHOLE, 128), BF16),
            pltpu.VMEM((WHOLE + 16, 128), F32),
            pltpu.VMEM((OWN, 128), F32),
            pltpu.VMEM((6, 128, 128), BF16),
            pltpu.VMEM((8, 128), jnp.int32),
            pltpu.VMEM((16, 8, 128), jnp.int32),
            pltpu.VMEM((BLOCK, 128), F32),
            pltpu.VMEM((BLOCK, 128), BF16),
            pltpu.VMEM((SEQ, 128), BF16),
            pltpu.VMEM((3 * 128, D_E), BF16),
            pltpu.VMEM((D_E, D_T), BF16),
            pltpu.VMEM((D_T, 3 * D_T), BF16),
            pltpu.VMEM((2, PT, D_E), BF16),
            pltpu.VMEM((2, PT, D_T), BF16),
            pltpu.VMEM((2, D_T, PT), BF16),
            dma((-(-WHOLE // CHUNK),)),
            dma((3,)),
            dma((16,)),
            dma((16,)),
            dma((16,)),
            dma((16,)),
            dma((16,)),
            dma((16,)),
            dma((4,)),
            dma((4,)),
            dma((4,)),
            dma((4,)),
            dma((3, 2)),
            dma((3, TILES)),
            dma((3, TILES)),
            dma,
            dma((3,)),
        ],
        compiler_params=params(58, collective_id=0, has_side_effects=True),
        name="front",
    )(ids, table, table_end, mask, splits, mats, vecs, proj, win, wqkv, ebias, types, bias)


def unpack_rows(pairs, packed_ref, flat):
    for pair in pairs:
        both = [packed_ref[2 * pair + i].astype(F32)[:SHARD] for i in range(2)]
        flat[88 * pair : 88 * pair + 88, :] = jnp.concatenate(both, 0)


def unpack_vectors(packed_ref, vec_ref):
    lane = lax.broadcasted_iota(jnp.int32, (1, 128), 1)
    rows = [jnp.zeros((1, 128), F32)] * 48
    for owner in range(128):
        row, shift = divmod(47 * owner, 128)
        entries = packed_ref[owner].astype(F32)[SHARD : SHARD + 1, :]
        moved = pltpu.roll(entries, shift, 1) if shift else entries
        if shift + 47 > 128:
            rows[row] = jnp.where(lane >= shift, moved, rows[row])
            rows[row + 1] = jnp.where(lane < shift + 47 - 128, moved, rows[row + 1])
        else:
            rows[row] = jnp.where((lane >= shift) & (lane < shift + 47), moved, rows[row])
    for row in range(48):
        vec_ref[row : row + 1, :] = rows[row]


ST = 1024


def student_in_kernel(emb_ref, packed_ref, first_ref, sq_ref, sk_ref, sv_ref, skt_ref, svt_ref,
                      win_ref, wqkv_ref, watt_ref, wup_ref, wdown_ref, wout_ref, vec_ref, flat):
    t = pl.program_id(0)

    @pl.when(t == 0)
    def _():
        unpack_vectors(packed_ref, vec_ref)
        unpack_rows(range(12), packed_ref, flat)
        win_ref[...] = flat[0:512, :].astype(BF16)
        for n in range(3):
            wqkv_ref[:, n * 128 : n * 128 + 128] = flat[pl.ds(512 + n, 128, stride=3), :].astype(BF16)
        watt_ref[...] = flat[896:1024, :].astype(BF16)

    for step in range(SLOTS // ST):

        @pl.when(t == step)
        def _(step=step):
            student_tile(t, emb_ref, win_ref, wqkv_ref, vec_ref, first_ref, sq_ref, sk_ref, sv_ref, skt_ref, svt_ref)
            unpack_rows(range(12 + 13 * step, 12 + 13 * (step + 1)), packed_ref, flat)
            if step == 1:
                for i in range(FFN_COUNT):
                    for n in range(4):
                        part = flat[pl.ds(1024 + 512 * i + n, 128, stride=4), :]
                        wup_ref[i, :, n * 128 : n * 128 + 128] = part.astype(BF16)
            if step == 3:
                for i in range(FFN_COUNT):
                    wdown_ref[i] = flat[3072 + 512 * i : 3584 + 512 * i, :].astype(BF16)
                for n in range(4):
                    wout_ref[:, n * 128 : n * 128 + 128] = flat[pl.ds(5120 + n, 128, stride=4), :].astype(BF16)


def student_tile(t, emb_ref, win_ref, wqkv_ref, vec_ref, first_ref, sq_ref, sk_ref, sv_ref, skt_ref, svt_ref):
    emb = emb_ref[...]
    emb = jnp.where((t < SEQ // ST) | has_two(), emb, jnp.zeros_like(emb))
    first = (dot(emb, win_ref[...]) + line(vec_ref, V_IN)).astype(BF16)
    first_ref[...] = first
    qkv = dot(first, wqkv_ref[...])
    sq_ref[...] = (qkv[:, :D_S] + line(vec_ref, V_QKV)).astype(BF16)
    s_keys = (qkv[:, D_S : 2 * D_S] + line(vec_ref, V_QKV + 1)).astype(BF16)
    s_values = (qkv[:, 2 * D_S :] + line(vec_ref, V_QKV + 2)).astype(BF16)
    sk_ref[...] = s_keys
    sv_ref[...] = s_values
    skt_ref[...] = s_keys.T
    svt_ref[...] = s_values.T


def student_in(emb, packed):
    tall = jax.ShapeDtypeStruct((SLOTS, D_S), BF16)
    flat = jax.ShapeDtypeStruct((D_S, SLOTS), BF16)
    down = pl.BlockSpec((ST, D_S), lambda t: (t, 0))
    across = pl.BlockSpec((D_S, ST), lambda t: (0, t))
    made = [
        ((D_E, D_S), BF16),
        ((D_S, 3 * D_S), BF16),
        ((D_S, D_S), BF16),
        ((FFN_COUNT, D_S, FF_S), BF16),
        ((FFN_COUNT, FF_S, D_S), BF16),
        ((D_S, D_E), BF16),
        ((48, 128), F32),
    ]
    return pl.pallas_call(
        student_in_kernel,
        grid=(SLOTS // ST,),
        in_specs=[pl.BlockSpec((ST, D_E), lambda t: (t, 0)), whole(128, BLOCK, 128)],
        out_specs=[down] * 4 + [across] * 2 + [whole(*shape) for shape, _ in made],
        out_shape=[tall] * 4 + [flat] * 2 + [jax.ShapeDtypeStruct(*entry) for entry in made],
        scratch_shapes=[pltpu.VMEM((5632, 128), F32)],
        compiler_params=params(40),
        name="student_in",
    )(emb, packed)


CB = 256
SUB = 64
STEPS = 3 * HEADS


def head_lanes(values, head):
    lane = lax.broadcasted_iota(jnp.int32, (1, D_S), 1)
    return jnp.where(lane // HEAD_S == head, values, jnp.zeros_like(values))


def attend_kernel(tq_ref, tk_ref, tvt_ref, sq_ref, sk_ref, svt_ref, skt_ref, et_ref, es_ref, tmix_ref, smix_ref, stat_ref,
                  ts0, ts1, ss0, ss1, mx0, mx1, sqt0, sqt1):
    n = pl.program_id(0)
    s_factor = HEAD_S**-0.5 * LOG2E

    def work(ts, ss, mx, sqt, tr, sr, mr, sqr, scores, mixes):
        if scores:
            queries, s_queries = tq_ref[...], head_lanes(sq_ref[...], n // 3)
            tall = s_queries.astype(F32).T
            sqt[...] = sum(tall[h * HEAD_S : (h + 1) * HEAD_S] for h in range(HEADS))
            t_max = s_max = jnp.full((8, QB), -jnp.inf, F32)
        if mixes:
            t_top, s_top = jnp.max(mr[0], 0, keepdims=True), jnp.max(mr[1], 0, keepdims=True)
            t_off, s_off = t_top * LOG2E, s_top * s_factor
            entropy = jnp.zeros((8, QB), F32)
            ones = jnp.ones((16, CB), BF16)
            t_mix = jnp.zeros((HEAD_T + HEAD_S + 16, QB), F32)
            s_mix = jnp.zeros((HEAD_S + 16, QB), F32)
        for c in range(SEQ // CB):
            part = slice(c * CB, c * CB + CB)
            if scores:
                t_part = dot_nt(tk_ref[part, :], queries)
                ts[part, :] = t_part
                s_part = dot_nt(sk_ref[part, :], s_queries)
                ss[part, :] = s_part
                t_max = jnp.maximum(t_max, fold(t_part, jnp.max))
                s_max = jnp.maximum(s_max, fold(s_part, jnp.max))
            if mixes:
                for u in range(c * CB, c * CB + CB, SUB):
                    some = slice(u, u + SUB)
                    t_log = tr[some, :] * LOG2E - t_off
                    t_exp = jnp.exp2(t_log)
                    et_ref[0, some, :] = t_exp.astype(BF16)
                    es_ref[0, some, :] = jnp.exp2(sr[some, :] * s_factor - s_off).astype(BF16)
                    entropy = entropy + fold(t_exp * t_log)
                t_mix += dot(jnp.concatenate([tvt_ref[:, part], skt_ref[:, part], ones], 0), et_ref[0, part, :])
                s_mix += dot(jnp.concatenate([svt_ref[:, part], ones], 0), es_ref[0, part, :])
        if scores:
            mx[0], mx[1] = t_max, s_max
        if mixes:
            t_sum, s_sum = t_mix[HEAD_T + HEAD_S : HEAD_T + HEAD_S + 1], s_mix[HEAD_S : HEAD_S + 1]
            t_inv, s_inv = 1.0 / t_sum, 1.0 / s_sum
            cross = jnp.sum(sqr[...] * t_mix[HEAD_T : HEAD_T + HEAD_S], 0, keepdims=True) * s_factor - s_off * t_sum
            kl = (jnp.sum(entropy, 0, keepdims=True) - cross) * t_inv * (1.0 / LOG2E)
            stat_ref[0, 0, 0:1, :] = t_inv
            stat_ref[0, 0, 1:2, :] = s_inv
            stat_ref[0, 0, 2:3, :] = kl - jnp.log(t_sum) + jnp.log(s_sum)
            stat_ref[0, 0, 3:8, :] = jnp.zeros((5, QB), F32)
            tmix_ref[...] = (t_mix[:HEAD_T] * t_inv).T.astype(BF16)
            smix_ref[0] = s_mix[:HEAD_S] * s_inv

    even, odd = (ts0, ss0, mx0, sqt0), (ts1, ss1, mx1, sqt1)
    pl.when(n == 0)(lambda: work(*even, *odd, True, False))
    pl.when((n > 0) & (n < STEPS) & (n % 2 == 0))(lambda: work(*even, *odd, True, True))
    pl.when((n > 0) & (n < STEPS) & (n % 2 == 1))(lambda: work(*odd, *even, True, True))
    pl.when(n == STEPS)(lambda: work(*even, *odd, False, True))


def attend(tq, tk, tvt, sq, sk, svt, skt):
    now = lambda n: jnp.minimum(n, STEPS - 1)
    last = lambda n: jnp.maximum(n - 1, 0)
    block = lambda n: n % 3
    head = lambda n: n // 3
    return pl.pallas_call(
        attend_kernel,
        grid=(STEPS + 1,),
        in_specs=[
            pl.BlockSpec((QB, HEAD_T), lambda n: (block(now(n)), head(now(n)))),
            pl.BlockSpec((SEQ, HEAD_T), lambda n: (slot_of(block(now(n))), head(now(n)))),
            pl.BlockSpec((HEAD_T, SEQ), lambda n: (head(last(n)), slot_of(block(last(n))))),
            pl.BlockSpec((QB, D_S), lambda n: (first_block() + block(now(n)), 0)),
            pl.BlockSpec((SEQ, D_S), lambda n: (slot_of(block(now(n))), 0)),
            pl.BlockSpec((HEAD_S, SEQ), lambda n: (head(last(n)), slot_of(block(last(n))))),
            pl.BlockSpec((HEAD_S, SEQ), lambda n: (head(last(n)), slot_of(block(last(n))))),
        ],
        out_specs=[
            pl.BlockSpec((1, SEQ, QB), lambda n: (block(last(n)), 0, head(last(n)))),
            pl.BlockSpec((1, SEQ, QB), lambda n: (block(last(n)), 0, head(last(n)))),
            pl.BlockSpec((QB, HEAD_T), lambda n: (block(last(n)), head(last(n)))),
            pl.BlockSpec((1, HEAD_S, QB), lambda n: (block(last(n)), head(last(n)), 0)),
            pl.BlockSpec((1, 1, 8, QB), lambda n: (block(last(n)), head(last(n)), 0, 0)),
        ],
        out_shape=[
            jax.ShapeDtypeStruct((3, SEQ, HEADS * QB), BF16),
            jax.ShapeDtypeStruct((3, SEQ, HEADS * QB), BF16),
            jax.ShapeDtypeStruct((OWN, D_T), BF16),
            jax.ShapeDtypeStruct((3, D_S, QB), F32),
            jax.ShapeDtypeStruct((3, HEADS, 8, QB), F32),
        ],
        scratch_shapes=[pltpu.VMEM((SEQ, QB), F32)] * 4 + [pltpu.VMEM((2, 8, QB), F32)] * 2 + [pltpu.VMEM((HEAD_S, QB), F32)] * 2,
        compiler_params=params(40),
        name="attend",
    )(tq, tk, tvt, sq, sk, svt, skt)


FC = 1024


def teacher_kernel(mix_ref, hid_ref, emb_ref, att_ref, up_hbm, down_hbm, out_ref, bias_ref, gain_ref, shift_ref, target_ref,
                   norm, low, acc, up_parts, down_parts, sems):
    c = pl.program_id(0)

    def loads(part):
        here = pl.ds(pl.multiple_of(part * FC, FC), FC)
        slot = part % 2
        return (
            pltpu.make_async_copy(up_hbm.at[:, here], up_parts.at[slot], sems.at[0, slot]),
            pltpu.make_async_copy(down_hbm.at[here], down_parts.at[slot], sems.at[1, slot]),
        )

    @pl.when(c == 0)
    def _():
        for copy in loads(0):
            copy.start()

    @pl.when(c < pl.num_programs(0) - 1)
    def _():
        for copy in loads(c + 1):
            copy.start()


    @pl.when(c == 0)
    def _():
        summed = hid_ref[...] + dot(mix_ref[...], att_ref[...]) + line(bias_ref, 32, 8)
        one = layer_norm(summed, line(gain_ref, 0, 8), line(shift_ref, 0, 8))
        norm[...] = one
        low[...] = one.astype(BF16)

    up_load, down_load = loads(c)
    up_load.wait()
    rows = FC // 128
    up_bias = bias_ref[pl.ds(pl.multiple_of(40 + rows * c, 8), rows), :]
    act = gelu(dot(low[...], up_parts[c % 2]) + line(up_bias, 0, rows)).astype(BF16)
    down_load.wait()
    part = dot(act, down_parts[c % 2])

    @pl.when(c == 0)
    def _():
        acc[...] = part

    @pl.when(c > 0)
    def _():
        acc[...] += part

    @pl.when(c == pl.num_programs(0) - 1)
    def _():
        summed = norm[...] + acc[...] + line(bias_ref, 72, 8)
        two = layer_norm(summed, line(gain_ref, 8, 8), line(shift_ref, 8, 8))
        last = emb_ref[...].astype(F32) + dot(two.astype(BF16), out_ref[...]) + line(bias_ref, 80, 4)
        target_ref[...] = layer_norm(last, line(gain_ref, 16, 4), line(shift_ref, 16, 4))


def teacher(mix, hid, emb, att, up, down, out, bias, gain, shift):
    return pl.pallas_call(
        teacher_kernel,
        grid=(FF_T // FC,),
        in_specs=[
            whole(OWN, D_T),
            whole(OWN, D_T),
            whole(OWN, D_E),
            whole(D_T, D_T),
            pl.BlockSpec(memory_space=pl.ANY),
            pl.BlockSpec(memory_space=pl.ANY),
            whole(D_T, D_E),
            whole(84, 128),
            whole(20, 128),
            whole(20, 128),
        ],
        out_specs=whole(OWN, D_E),
        out_shape=jax.ShapeDtypeStruct((OWN, D_E), F32),
        scratch_shapes=[
            pltpu.VMEM((OWN, D_T), F32),
            pltpu.VMEM((OWN, D_T), BF16),
            pltpu.VMEM((OWN, D_T), F32),
            pltpu.VMEM((2, D_T, FC), BF16),
            pltpu.VMEM((2, FC, D_T), BF16),
            pltpu.SemaphoreType.DMA((2, 2)),
        ],
        compiler_params=params(40),
        name="teacher",
    )(mix, hid, emb, att, up, down, out, bias, gain, shift)


def student_kernel(emb_ref, smix_ref, target_ref, weight_ref, win_ref, watt_ref, wup_ref, wdown_ref, wout_ref, vec_ref,
                   grad_ref, vgrad_ref, dsum_ref, dmix_ref, part_ref, states, slopes, outers, acts):

    def put(r, value):
        for i in range(value.shape[1] // 128):
            vgrad_ref[r + i : r + i + 1, :] = value[:, i * 128 : i * 128 + 128]

    total = lambda v: jnp.sum(v.astype(F32), 0, keepdims=True)
    emb = emb_ref[...]
    source = emb.astype(F32)
    first = dot(emb, win_ref[...]) + line(vec_ref, V_IN)
    mixed = jnp.concatenate([smix_ref[j].T for j in range(3)], 0).astype(BF16)
    branch = dot(mixed, watt_ref[...]) + line(vec_ref, V_ATT)
    state = line(vec_ref, V_AGAIN) * (first + branch) + line(vec_ref, V_ASHIFT)
    for i in range(FFN_COUNT):
        states[i] = state
        inner = dot(state.astype(BF16), wup_ref[i]) + line(vec_ref, V_UP + 4 * i, 4)
        half = 0.5 * (1.0 + lax.erf(inner * 0.7071067811865476))
        slopes[i] = half + inner * jnp.exp(-0.5 * inner * inner) * 0.3989422804014327
        act = (inner * half).astype(BF16)
        acts[i] = act
        pre = state + dot(act, wdown_ref[i]) + line(vec_ref, V_DOWN + i)
        outers[i] = pre
        state = line(vec_ref, V_FGAIN + i) * pre + line(vec_ref, V_FSHIFT + i)
    state_low = state.astype(BF16)
    summed = source + dot(state_low, wout_ref[...]) + line(vec_ref, V_OUT, 4)
    diff = line(vec_ref, V_OGAIN, 4) * summed + line(vec_ref, V_OSHIFT, 4) - target_ref[...]
    weight = jnp.concatenate([jnp.broadcast_to(weight_ref[j], (8, QB)).T[:, 0:1] for j in range(3)], 0)
    loss = jnp.sum(weight * jnp.sum(diff * diff, 1, keepdims=True)) * (1.0 / D_E)
    count = jnp.sum(weight)
    d_result = (weight * (2.0 / D_E)) * diff
    put(V_OGAIN, total(d_result * summed))
    put(V_OSHIFT, total(d_result))
    d_output = (d_result * line(vec_ref, V_OGAIN, 4)).astype(BF16)
    out_g = dot_tn(state_low, d_output)
    for n in range(4):
        grad_ref[pl.ds(4224 + n, 128, stride=4), :] = out_g[:, n * 128 : n * 128 + 128]
    put(V_OUT, total(d_output))
    d_state = dot_nt(d_output, wout_ref[...])
    for i in reversed(range(FFN_COUNT)):
        put(V_FGAIN + i, total(d_state * outers[i]))
        put(V_FSHIFT + i, total(d_state))
        d_sum = d_state * line(vec_ref, V_FGAIN + i)
        d_outer = d_sum.astype(BF16)
        grad_ref[2176 + 512 * i : 2176 + 512 * (i + 1), :] = dot_tn(acts[i], d_outer)
        d_inner = (dot_nt(d_outer, wdown_ref[i]) * slopes[i]).astype(BF16)
        up_g = dot_tn(states[i].astype(BF16), d_inner)
        for n in range(4):
            grad_ref[pl.ds(128 + 512 * i + n, 128, stride=4), :] = up_g[:, n * 128 : n * 128 + 128]
        put(V_UP + 4 * i, total(d_inner))
        put(V_DOWN + i, total(d_outer))
        d_state = d_sum + dot_nt(d_inner, wup_ref[i])
    put(V_AGAIN, total(d_state * (first + branch)))
    put(V_ASHIFT, total(d_state))
    d_sum = d_state * line(vec_ref, V_AGAIN)
    d_branch = d_sum.astype(BF16)
    grad_ref[0:128, :] = dot_tn(mixed, d_branch)
    put(V_ATT, total(d_branch))
    dsum_ref[...] = d_sum
    dmix_ref[...] = dot_nt(d_branch, watt_ref[...]).astype(BF16)
    for r in (0, 1, 2, 3, 47):
        vgrad_ref[r : r + 1, :] = jnp.zeros((1, 128), F32)
    row = lax.broadcasted_iota(jnp.int32, (8, 128), 0)
    lane = lax.broadcasted_iota(jnp.int32, (8, 128), 1)
    part_ref[...] = jnp.where((row == 0) & (lane == 0), loss, 0.0) + jnp.where((row == 0) & (lane == 1), count, 0.0)


def student(emb, smix, target, weight, win, watt, wup, wdown, wout, vecs):
    return pl.pallas_call(
        student_kernel,
        grid=(1,),
        in_specs=[
            whole(OWN, D_E),
            whole(3, D_S, QB),
            whole(OWN, D_E),
            whole(3, 1, QB),
            whole(D_E, D_S),
            whole(D_S, D_S),
            whole(FFN_COUNT, D_S, FF_S),
            whole(FFN_COUNT, FF_S, D_S),
            whole(D_S, D_E),
            whole(48, 128),
        ],
        out_specs=[whole(4736, 128), whole(48, 128), whole(OWN, D_S), whole(OWN, D_S), whole(8, 128)],
        out_shape=[
            jax.ShapeDtypeStruct((4736, 128), F32),
            jax.ShapeDtypeStruct((48, 128), F32),
            jax.ShapeDtypeStruct((OWN, D_S), F32),
            jax.ShapeDtypeStruct((OWN, D_S), BF16),
            jax.ShapeDtypeStruct((8, 128), F32),
        ],
        scratch_shapes=[
            pltpu.VMEM((FFN_COUNT, OWN, D_S), F32),
            pltpu.VMEM((FFN_COUNT, OWN, FF_S), F32),
            pltpu.VMEM((FFN_COUNT, OWN, D_S), F32),
            pltpu.VMEM((FFN_COUNT, OWN, FF_S), BF16),
        ],
        compiler_params=params(40),
        name="student",
    )(emb, smix, target, weight, win, watt, wup, wdown, wout, vecs)


KB = 1024


def back_kernel(et_ref, es_ref, stat_ref, smix_ref, dmix_ref, weight_ref, sq_ref, sv_ref, skt_ref, dsum_ref, emb_hbm, first_ref,
                wqkv_ref, vgrad_ref, part_in, late_ref, *rest):
    state_refs, rest = rest[:6], rest[6:]
    made_ref, rest = rest[0], rest[1:]
    (dkv, dqt, ds, dq, dfirst, dmt, dmz, sqd, rows, flat, vecs, kls, block_ref, emb_ref, sem, emb_sem), buffers = rest[:16], rest[16:]
    j, kb = pl.program_id(0), pl.program_id(1)
    s_scale = HEAD_S**-0.5
    late = pltpu.make_async_copy(late_ref, flat.at[896:5632], sem)
    emb_load = pltpu.make_async_copy(emb_hbm, emb_ref, emb_sem)

    @pl.when((j == 0) & (kb == 0))
    def _():
        greet()
        late.start()
        emb_load.start()
        vecs[...] = vgrad_ref[...]
        dkv[...] = jnp.zeros_like(dkv)
        kls[...] = jnp.zeros_like(kls)

    @pl.when((j == 0) & (kb == 1))
    def _():
        late.wait()
        pack_blocks(range(FIRST_EARLY // 2, 64), flat, vecs, block_ref)
        swap_early(block_ref, buffers)

    @pl.when((j == 1) & (kb == 0))
    def _():
        send_early(block_ref, buffers)

    @pl.when(kb == 0)
    def _():
        quarter = weight_ref[0] * (1.0 / HEADS)
        wide = dmix_ref[...].astype(F32)
        tall = wide.T
        place = lax.broadcasted_iota(jnp.int32, (D_S, 1), 0) // HEAD_S
        for h in range(HEADS):
            own = slice(h * HEAD_S, h * HEAD_S + HEAD_S)
            mine = slice(h * QB, h * QB + QB)
            t_inv, s_inv = stat_ref[0, h, 0:1, :], stat_ref[0, h, 1:2, :]
            kls[0:1, :] += quarter * stat_ref[0, h, 2:3, :]
            row_dot = jnp.sum(tall[own] * smix_ref[0, own, :], 0, keepdims=True)
            rows[h, 0:1, :] = row_dot - quarter
            rows[h, 1:2, :] = s_inv
            rows[h, 2:3, :] = quarter * t_inv
            dmt[h] = jnp.where(place == h, tall, 0.0).astype(BF16)
            dmz[mine, :] = head_lanes(wide * stat_ref[0, h].T[:, 1:2], h).astype(BF16)
            sqd[mine, :] = head_lanes(sq_ref[...], h)
        dqt[...] = jnp.zeros_like(dqt)

    here = pl.ds(pl.multiple_of(slot_of(j) * SEQ + kb * KB, KB), KB)
    dkv[here, D_S:] += dot(es_ref[0], dmz[...])
    for h in range(HEADS):
        lanes = slice(h * QB, h * QB + QB)
        for c in range(KB // 256):
            part = slice(c * 256, c * 256 + 256)
            d_probs = dot(sv_ref[part, :], dmt[h])
            s_exp, t_exp = es_ref[0, part, lanes].astype(F32), et_ref[0, part, lanes].astype(F32)
            d_scores = (d_probs - rows[h, 0:1, :]) * rows[h, 1:2, :] * s_exp - t_exp * rows[h, 2:3, :]
            ds[part, lanes] = d_scores.astype(BF16)
        own = slice(h * HEAD_S, h * HEAD_S + HEAD_S)
        dqt[own, :] += dot(skt_ref[own, :], ds[:, lanes])
    dkv[here, :D_S] += dot(ds[...], sqd[...])

    @pl.when(kb == pl.num_programs(1) - 1)
    def _():
        dq[pl.ds(pl.multiple_of(j * QB, QB), QB), :] = (dqt[...] * s_scale).T

    @pl.when((j == 2) & (kb == pl.num_programs(1) - 1))
    def _():
        qkv_w = wqkv_ref[...]
        dq_low = dq[...].astype(BF16)
        own = pl.ds(pl.multiple_of(first_block() * QB, QB), OWN)
        q_grad = dot_tn(first_ref[own, :], dq_low)
        own_part = dsum_ref[...] + dot_nt(dq_low, qkv_w[:, :D_S])
        kv_grad = jnp.zeros((D_S, 2 * D_S), F32)
        kv_bias = jnp.zeros((1, 2 * D_S), F32)
        for c in range(8):
            part = pl.ds(c * 512, 512)
            wide = dkv[part, :]
            low = jnp.concatenate([(wide[:, :D_S] * s_scale).astype(BF16), wide[:, D_S:].astype(BF16)], 1)
            kv_grad += dot_tn(first_ref[part, :], low)
            kv_bias += jnp.sum(low.astype(F32), 0, keepdims=True)
            dfirst[part, :] = dot_nt(low, qkv_w[:, D_S:])
        dfirst[own, :] += own_part
        in_grad = jnp.zeros((D_S, D_E), F32)
        in_bias = jnp.zeros((1, D_S), F32)
        two = has_two()
        emb_load.wait()
        for c in range(8):
            part = pl.ds(c * 512, 512)
            low = dfirst[part, :].astype(BF16)
            emb = emb_ref[part, :]
            if c >= 4:
                emb = jnp.where(two, emb, jnp.zeros_like(emb))
            in_grad += dot_tn(low, emb)
            in_bias += jnp.sum(low.astype(F32), 0, keepdims=True)
        flat[0:512, :] = in_grad.T
        flat[pl.ds(512, 128, stride=3), :] = q_grad
        flat[pl.ds(513, 128, stride=3), :] = kv_grad[:, :D_S]
        flat[pl.ds(514, 128, stride=3), :] = kv_grad[:, D_S:]
        vecs[0:1, :] = in_bias
        vecs[1:2, :] = jnp.sum(dq_low.astype(F32), 0, keepdims=True)
        vecs[2:3, :] = kv_bias[:, :D_S]
        vecs[3:4, :] = kv_bias[:, D_S:]
        pack_blocks(range(FIRST_EARLY // 2), flat, vecs, block_ref)
        kl = jnp.sum(kls[0:1, :], keepdims=True)
        corner = lax.broadcasted_iota(jnp.int32, (1, 128), 1) == 0
        send_rest(block_ref, buffers)
        update(block_ref, part_in[0:1, :] + jnp.where(corner, kl, 0.0), state_refs, made_ref, buffers)


def back(et, es, stat, smix, dmix, weight, sq, sv, skt, dsum, emb, first, wqkv, vgrad, part, late, *state):
    count = SEQ // KB
    place = lambda j, k: slot_of(j) * count + k
    dma = pltpu.SemaphoreType.DMA
    return pl.pallas_call(
        back_kernel,
        grid=(3, count),
        in_specs=[
            pl.BlockSpec((1, KB, HEADS * QB), lambda j, k: (j, k, 0)),
            pl.BlockSpec((1, KB, HEADS * QB), lambda j, k: (j, k, 0)),
            pl.BlockSpec((1, HEADS, 8, QB), lambda j, k: (j, 0, 0, 0)),
            pl.BlockSpec((1, D_S, QB), lambda j, k: (j, 0, 0)),
            pl.BlockSpec((QB, D_S), lambda j, k: (j, 0)),
            pl.BlockSpec((1, 1, QB), lambda j, k: (j, 0, 0)),
            pl.BlockSpec((QB, D_S), lambda j, k: (first_block() + j, 0)),
            pl.BlockSpec((KB, D_S), lambda j, k: (place(j, k), 0)),
            pl.BlockSpec((D_S, KB), lambda j, k: (0, place(j, k))),
            whole(OWN, D_S),
            pl.BlockSpec(memory_space=pl.ANY),
            whole(SLOTS, D_S),
            whole(D_S, 3 * D_S),
            whole(48, 128),
            whole(8, 128),
            pl.BlockSpec(memory_space=pl.ANY),
        ]
        + [whole(SHARD, 128), whole(1, 47)] * 3,
        out_specs=whole(3 * BLOCK + 8, 128),
        out_shape=jax.ShapeDtypeStruct((3 * BLOCK + 8, 128), F32),
        scratch_shapes=[
            pltpu.VMEM((SLOTS, 2 * D_S), F32),
            pltpu.VMEM((D_S, QB), F32),
            pltpu.VMEM((KB, HEADS * QB), BF16),
            pltpu.VMEM((OWN, D_S), F32),
            pltpu.VMEM((SLOTS, D_S), F32),
            pltpu.VMEM((HEADS, D_S, QB), BF16),
            pltpu.VMEM((HEADS * QB, D_S), BF16),
            pltpu.VMEM((HEADS * QB, D_S), BF16),
            pltpu.VMEM((HEADS, 8, QB), F32),
            pltpu.VMEM((5632, 128), F32),
            pltpu.VMEM((48, 128), F32),
            pltpu.VMEM((8, QB), F32),
            pltpu.VMEM((4, 2, 16, BLOCK, 128), BF16),
            pltpu.VMEM((SLOTS, D_E), BF16),
            dma,
            dma,
            pltpu.VMEM((3, BLOCK, 128), F32),
            pltpu.VMEM((4, 16, BLOCK, 128), BF16),
            pltpu.VMEM((BLOCK, 128), F32),
            pltpu.VMEM((64, BLOCK, 128), BF16),
            pltpu.VMEM((64, BLOCK, 128), BF16),
            pltpu.VMEM((2, 2, 8, 128), F32),
            pltpu.VMEM((2, 16, 8, 128), F32),
            pltpu.VMEM((2, 8, 8, 128), F32),
            dma((2, 6)),
            dma((64,)),
            dma((64,)),
            dma((2, 16)),
            dma((2, 16)),
            dma((2, 8)),
            dma((2, 8)),
        ],
        compiler_params=params(44, collective_id=1, has_side_effects=True),
        name="back",
    )(et, es, stat, smix, dmix, weight, sq, sv, skt, dsum, emb, first, wqkv, vgrad, part, late, *state)


def chip(k):
    dp, fs = lax.axis_index("dp"), lax.axis_index("fsdp")
    return (2 * ((dp // 2 + k // 16) % 4) + dp % 2, (fs + k) % 16)


def greet():
    dp, fs = lax.axis_index("dp"), lax.axis_index("fsdp")
    barrier = pltpu.get_barrier_semaphore()

    def signal(k, _):
        pl.semaphore_signal(barrier, inc=1, device_id=chip(k), device_id_type=MESH)
        return 0

    lax.fori_loop(1, 64, signal, 0)
    for k in range(4):
        other = (2 * ((dp // 2 + k) % 4) + 1 - dp % 2, fs)
        pl.semaphore_signal(barrier, inc=1, device_id=other, device_id_type=MESH)


FIRST_EARLY = 22


def pack_blocks(pairs, flat, vecs, block_ref):
    lane = lax.broadcasted_iota(jnp.int32, (1, 128), 1)
    rest = jnp.zeros((BLOCK - SHARD - 1, 128), F32)
    for pair in pairs:
        both = flat[88 * pair : 88 * pair + 88, :]
        for i in range(2):
            owner = 2 * pair + i
            row, shift = divmod(47 * owner, 128)
            entries = vecs[row : row + 1, :]
            if shift + 47 > 128:
                entries = jnp.where(lane >= shift, entries, vecs[row + 1 : row + 2, :])
            if shift:
                entries = pltpu.roll(entries, 128 - shift, 1)
            entries = jnp.where(lane < 47, entries, 0.0)
            mine = both[SHARD * i : SHARD * (i + 1)]
            block_ref[owner // 32, owner // 16 % 2, owner % 16] = jnp.concatenate([mine, entries, rest], 0).astype(BF16)


SPLIT = FIRST_EARLY - 16


def swap_copy(n, g_ref, half_in, half_sems):
    dp, fs = lax.axis_index("dp"), lax.axis_index("fsdp")
    core = dp % 2
    if n in (1, 2, 3):
        source, goal = g_ref.at[n, 1 - core], half_in.at[n]
    elif n == 0:
        source, goal = g_ref.at[0, 1, 0:SPLIT], half_in.at[0, 0:SPLIT]
    elif n == 4:
        source, goal = g_ref.at[0, 1, SPLIT:16], half_in.at[0, SPLIT:16]
    else:
        source, goal = g_ref.at[0, 0], half_in.at[0]
    return pltpu.make_async_remote_copy(
        source, goal, half_sems.at[0, n], half_sems.at[1, n], device_id=(dp + 1 - 2 * core, fs), device_id_type=MESH
    )


def swap_early(g_ref, buffers):
    half_in, half_sems = buffers[1], buffers[8]
    pl.semaphore_wait(pltpu.get_barrier_semaphore(), 67)
    for n in (1, 2, 3):
        swap_copy(n, g_ref, half_in, half_sems).start()

    @pl.when(lax.axis_index("dp") % 2 == 0)
    def _():
        swap_copy(4, g_ref, half_in, half_sems).start()


def block_copy(k, buffers):
    block_out, blocks_in, block_send, block_recv = buffers[3], buffers[4], buffers[9], buffers[10]
    dp, fs = lax.axis_index("dp"), lax.axis_index("fsdp")
    place = (dp // 2 + k // 16) % 4 * 16 + (fs + k) % 16
    return pltpu.make_async_remote_copy(
        block_out.at[place], blocks_in.at[k], block_send.at[k], block_recv.at[k], device_id=chip(k), device_id_type=MESH
    )


def is_early(place):
    return (place >= 16) | ((lax.axis_index("dp") % 2 == 1) & (place >= SPLIT))


def join_and_send(early, g_ref, buffers):
    half_in, block_out = buffers[1], buffers[3]
    dp, fs = lax.axis_index("dp"), lax.axis_index("fsdp")
    core = dp % 2

    def join(i, _):
        @pl.when(is_early(i) == early)
        def _():
            summed = g_ref[i // 16, core, i % 16].astype(F32) + half_in[i // 16, i % 16].astype(F32)
            block_out[i] = summed.astype(BF16)

        return 0

    lax.fori_loop(0, 64 if early else 16, join, 0)

    def start(k, _):
        place = (dp // 2 + k // 16) % 4 * 16 + (fs + k) % 16

        @pl.when(is_early(place) == early)
        def _():
            block_copy(k, buffers).start()

        return 0

    lax.fori_loop(1, 64, start, 0)


def send_early(g_ref, buffers):
    half_in, half_sems = buffers[1], buffers[8]
    core = lax.axis_index("dp") % 2
    for n in (1, 2, 3):
        swap_copy(n, g_ref, half_in, half_sems).wait()

    @pl.when(core == 0)
    def _():
        swap_copy(4, g_ref, half_in, half_sems).wait_send()

    @pl.when(core == 1)
    def _():
        swap_copy(4, g_ref, half_in, half_sems).wait_recv()

    join_and_send(True, g_ref, buffers)


def send_rest(g_ref, buffers):
    half_in, half_sems = buffers[1], buffers[8]
    core = lax.axis_index("dp") % 2

    @pl.when(core == 0)
    def _():
        swap_copy(0, g_ref, half_in, half_sems).start()
        swap_copy(5, g_ref, half_in, half_sems).wait_recv()
        swap_copy(0, g_ref, half_in, half_sems).wait_send()

    @pl.when(core == 1)
    def _():
        swap_copy(5, g_ref, half_in, half_sems).start()
        swap_copy(0, g_ref, half_in, half_sems).wait_recv()
        swap_copy(5, g_ref, half_in, half_sems).wait_send()

    join_and_send(False, g_ref, buffers)


def update(g_ref, part, state_refs, made_ref, buffers):
    master_mat, master_vec, first_mat, first_vec, second_mat, second_vec = state_refs
    (packs, half_in, mine, block_out, blocks_in, tile_out, tiles_f, tiles_d,
     half_sems, block_send, block_recv, f_send, f_recv, d_send, d_recv) = buffers
    dp, fs = lax.axis_index("dp"), lax.axis_index("fsdp")
    x, core = dp // 2, dp % 2
    packs[...] = jnp.zeros_like(packs)
    for i, (mat, vec) in enumerate([(master_mat, master_vec), (first_mat, first_vec), (second_mat, second_vec)]):
        packs[i, 0:SHARD, :] = mat[...]
        packs[i, SHARD : SHARD + 1, 0:47] = vec[...]
    mine[...] = g_ref[x, core, fs].astype(F32) + half_in[x, fs].astype(F32)

    def gather(k, _):
        block_copy(k, buffers).wait()
        mine[...] += blocks_in[k].astype(F32)
        return 0

    lax.fori_loop(1, 64, gather, 0)

    row = lax.broadcasted_iota(jnp.int32, (BLOCK, 1), 0)
    place = (dp * 16 + fs) * SHARD + row
    is_matrix = row < SHARD
    bounds = [0]
    for rows in MAT_ROWS:
        bounds.append(bounds[-1] + rows)
    members = [is_matrix & (place >= bounds[i]) & (place < bounds[i + 1]) for i in range(6)]

    hops = lambda k: min(k, 4 - k)
    in_plane = sorted(range(1, 16), key=lambda k: -hops(k // 4) - hops(k % 4))
    along_x = sorted(range(1, 8), key=lambda k: -hops(k // 2) - k % 2)

    def everyone(tile, turn):
        tile_out[turn, 0] = tile
        tiles_d[turn, dp] = tile

        def f_copy(k):
            return pltpu.make_async_remote_copy(
                tile_out.at[turn, 1], tiles_f.at[turn, fs], f_send.at[turn, k], f_recv.at[turn, k],
                device_id=(dp, (fs // 4 + k // 4) % 4 * 4 + (fs + k) % 4), device_id_type=MESH,
            )

        def d_copy(k):
            return pltpu.make_async_remote_copy(
                tile_out.at[turn, 0], tiles_d.at[turn, dp], d_send.at[turn, k], d_recv.at[turn, k],
                device_id=((x + k // 2) % 4 * 2 + (core + k) % 2, fs), device_id_type=MESH,
            )

        for k in along_x:
            d_copy(k).start()
        for k in along_x:
            d_copy(k).wait()
        total = tiles_d[turn, 0]
        for k in range(1, 8):
            total = total + tiles_d[turn, k]
        tile_out[turn, 1] = total
        tiles_f[turn, fs] = total
        for k in in_plane:
            f_copy(k).start()
        for k in in_plane:
            f_copy(k).wait()
        total = tiles_f[turn, 0]
        for k in range(1, 16):
            total = total + tiles_f[turn, k]
        return total

    column = lambda v: jnp.sum(v, 0, keepdims=True)

    def tile_of(rows):
        return jnp.concatenate(rows + [jnp.zeros((8 - len(rows), 128), F32)] * (len(rows) < 8), 0)

    grad = mine[...]
    master = packs[0]
    squares = master * master
    tile = everyone(
        tile_of([part, column(grad * grad)] + [column(jnp.where(members[i], squares, 0.0)) for i in range(6)]), 0
    )
    loss, count = tile[0:1, 0:1], tile[0:1, 1:2]
    sums = jnp.sum(tile, 1, keepdims=True)
    inverse = 1.0 / count
    norm = jnp.sqrt(sums[1:2]) * inverse
    factor = CLIP_NORM / jnp.maximum(norm, CLIP_NORM)
    grad = grad * inverse * factor
    first = BETA_ONE * packs[1] + (1.0 - BETA_ONE) * grad
    second = BETA_TWO * packs[2] + (1.0 - BETA_TWO) * grad * grad
    ratio = first / (1.0 - BETA_ONE**STEP) / (jnp.sqrt(second / (1.0 - BETA_TWO**STEP)) + ADAM_EPS)
    ratio = ratio + jnp.where(is_matrix, WEIGHT_DECAY * master, 0.0)
    squares = ratio * ratio
    steps = everyone(tile_of([column(jnp.where(members[i], squares, 0.0)) for i in range(6)]), 1)
    made_ref[BLOCK : 2 * BLOCK, :] = first
    made_ref[2 * BLOCK : 3 * BLOCK, :] = second
    trusts = jnp.sqrt(sums[2:8]) / jnp.sqrt(jnp.sum(steps, 1, keepdims=True)[0:6])
    trust = jnp.ones((BLOCK, 1), F32)
    for i in range(6):
        trust = jnp.where(members[i], trusts[i : i + 1], trust)
    made_ref[0:BLOCK, :] = master - LEARN_RATE * (trust * ratio)
    lane = lax.broadcasted_iota(jnp.int32, (8, 128), 1)
    made_ref[3 * BLOCK :, :] = jnp.where(lane == 0, loss, jnp.where(lane == 1, count, norm))


def finish_kernel(made, loss, count, norm, m0, m1, m2, v0, v1, v2):
    for i, (mat, vec) in enumerate(((m0, v0), (m1, v1), (m2, v2))):
        mat[...] = made[BLOCK * i : BLOCK * i + SHARD, :]
        vec[...] = made[BLOCK * i + SHARD : BLOCK * i + SHARD + 1, 0:47]
    for i, out in enumerate((loss, count, norm)):
        out[...] = made[3 * BLOCK : 3 * BLOCK + 1, i : i + 1]


def finish(made):
    vmem = pl.BlockSpec(memory_space=pltpu.VMEM)
    shape = lambda *dims: jax.ShapeDtypeStruct(dims, F32)
    return pl.pallas_call(
        finish_kernel,
        in_specs=[vmem],
        out_specs=[vmem] * 9,
        out_shape=[shape(1, 1)] * 3 + [shape(SHARD, 128)] * 3 + [shape(1, 47)] * 3,
        compiler_params=params(63),
        name="finish",
    )(made)


def per_device(
    token_ids,
    splits,
    valid_mask,
    embed_table,
    embed_proj,
    embed_bias,
    type_table,
    teach_in,
    teach_qkv,
    teach_att,
    teach_up,
    teach_down,
    teach_out,
    teach_bias,
    teach_gain,
    teach_shift,
    matrices,
    vectors,
    matrix_first,
    matrix_second,
    vector_first,
    vector_second,
):
    mat = lambda v: v.reshape(SHARD, 128)
    vec = lambda v: v.reshape(1, 47)
    rows_128 = lambda v: v.reshape(-1, 128)
    bias = rows_128(teach_bias)
    emb, t_keys, t_values, own_emb, hidden, t_queries, weights, packed = front(
        token_ids, embed_table, embed_table, valid_mask, splits, mat(matrices), vec(vectors), embed_proj, teach_in, teach_qkv,
        rows_128(embed_bias), type_table, bias,
    )
    first, s_q, s_k, s_v, s_kt, s_vt, in_w, qkv_w, att_w, up_w, down_w, out_w, vecs = student_in(emb, packed)
    et, es, t_mixed, s_mixed, stat = attend(t_queries, t_keys, t_values, s_q, s_k, s_vt, s_kt)
    target = teacher(
        t_mixed, hidden, own_emb, teach_att, teach_up, teach_down, teach_out, bias, rows_128(teach_gain), rows_128(teach_shift)
    )
    late, vgrads, d_sum, d_mixed, part = student(
        own_emb, s_mixed, target, weights, in_w, att_w, up_w, down_w, out_w, vecs
    )
    made = back(
        et, es, stat, s_mixed, d_mixed, weights, s_q, s_v, s_kt, d_sum, emb, first, qkv_w, vgrads, part, late,
        mat(matrices), vec(vectors), mat(matrix_first), vec(vector_first), mat(matrix_second), vec(vector_second),
    )
    loss, count, norm, m0, m1, m2, v0, v1, v2 = finish(made)
    flat = lambda v: v.reshape(-1)
    scalar = lambda v: v.reshape(())
    return (
        scalar(loss), scalar(count), scalar(norm), flat(m0), flat(m1), flat(m2), flat(v0), flat(v1), flat(v2),
    )


def solution(mesh):
    both = P(("dp", "fsdp"))
    return jax.shard_map(
        per_device,
        mesh=mesh,
        in_specs=(P("dp", "fsdp"), P("dp"), P("dp", "fsdp")) + (P(),) * 13 + (both,) * 6,
        out_specs=(P(), P(), P(), both, both, both, both, both, both),
        check_vma=False,
    )
```

```python
import functools
import math

import jax
import jax.numpy as jnp
from jax import lax
from jax.experimental import pallas as pl
from jax.experimental.pallas import tpu as pltpu
from jax.sharding import PartitionSpec as P

D_E = 512
D_T = 1024
FF_T = 4096
D_S = 128
FF_S = 512
HEADS = 4
FFN_COUNT = 4
STEP = 5
HEAD_T = 256
HEAD_S = 32
SEQ = 2048
QB = 256
OWN = 3 * QB
SLOTS = 2 * SEQ

CLIP_NORM = 0.05
BETA_ONE = 0.9
BETA_TWO = 0.999
LEARN_RATE = 0.3
WEIGHT_DECAY = 0.01
ADAM_EPS = 1e-06

F32 = jnp.float32
BF16 = jnp.bfloat16
LOG2E = 1.4426950408889634
MESH = pl.DeviceIdType.MESH

MAT_ROWS = (512, 384, 128, 2048, 2048, 512)
SHARD = 44
BLOCK = 48
(V_IN, V_QKV, V_ATT, V_AGAIN, V_ASHIFT, V_UP, V_DOWN, V_FGAIN, V_FSHIFT, V_OUT, V_OGAIN, V_OSHIFT) = (
    0, 1, 4, 5, 6, 7, 23, 27, 31, 35, 39, 43)


def dot(left, right):
    return jnp.dot(left, right, preferred_element_type=F32)


def dot_nt(left, right):
    return lax.dot_general(left, right, (((1,), (1,)), ((), ())), preferred_element_type=F32)


def dot_tn(left, right):
    return lax.dot_general(left, right, (((0,), (0,)), ((), ())), preferred_element_type=F32)


def layer_norm(values, gain, shift):
    center = values - jnp.mean(values, -1, keepdims=True)
    spread = jnp.mean(center * center, -1, keepdims=True)
    return center * lax.rsqrt(spread + 1e-05) * gain + shift


def gelu(values):
    return 0.5 * values * (1.0 + lax.erf(values * 0.7071067811865476))


def params(mib, **more):
    return pltpu.CompilerParams(vmem_limit_bytes=mib * 2**20, **more)


def whole(*shape):
    return pl.BlockSpec(shape, lambda *_: (0,) * len(shape))


def line(ref, row, count=1):
    if count == 1:
        return ref[row : row + 1, :]
    return jnp.concatenate([ref[row + i : row + i + 1, :] for i in range(count)], 1)


def fold(values, op=jnp.sum):
    return op(values.reshape(values.shape[0] // 8, 8, values.shape[1]), 0)


def spots():
    dp, fs = lax.axis_index("dp"), lax.axis_index("fsdp")
    return dp // 2, dp % 2, fs // 4, fs % 4


def place_in_group():
    _, core, _, y = spots()
    return 2 * y + core


def first_block():
    return (3 * place_in_group()) % 8


def slot_of(j):
    return (first_block() + j) // 8


def has_two():
    i = place_in_group()
    return (i == 2) | (i == 5)


PT = 512
TILES = SEQ // PT
C_TILE = 2


CHUNK = 2048
VOCAB = 30522
WHOLE = VOCAB // 16 * 16


def front_kernel(ids_ref, table_hbm, tail_ref, mask_ref, splits_ref, mats_ref, vecs_ref, proj_hbm, win_hbm, wqkv_hbm, ebias_ref,
                 types_ref, bias_ref, emb_hbm, k_hbm, vt_hbm, own_hbm, hid_hbm, tq_ref, weight_ref, params_hbm,
                 own_ref, hid_ref, params_ref, table_low, table, picked, e_ref, note, notes, wide, block, e_all, proj_ref, win_ref, wqkv_ref, emb_t, k_t, vt_t,
                 t_sem, load, e_send, e_recv, n_send, n_recv, a_send, a_recv, b_send, b_recv, c_send, c_recv,
                 out, s_send, s_recv, own_sem, last_sem):
    dp, me = lax.axis_index("dp"), lax.axis_index("fsdp")
    x, core, z, y = spots()
    i = 2 * y + core
    sibling = (2 * x + 1 - core, me)
    source_dp = 2 * x + z // 2
    is_source = z // 2 == core
    loads = [
        pltpu.make_async_copy(hbm, ref, load.at[n])
        for n, (hbm, ref) in enumerate([(proj_hbm, proj_ref), (win_hbm, win_ref), (wqkv_hbm, wqkv_ref)])
    ]
    barrier = pltpu.get_barrier_semaphore()

    def signal(device):
        pl.semaphore_signal(barrier, inc=1, device_id=device, device_id_type=MESH)

    def greet_source(f, _):
        @pl.when(jnp.logical_not(is_source & (f == me)))
        def _():
            signal((source_dp, f))

        return 0

    def greet_plane(k, _):
        signal((dp, (me + k) % 16))
        return 0

    lax.fori_loop(0, 16, greet_source, 0)
    lax.fori_loop(1, 16, greet_plane, 0)
    for k in range(1, 4):
        signal((2 * ((x + k) % 4) + core, me))
    signal(sibling)
    chunks = [(c, min(CHUNK, WHOLE - c)) for c in range(0, WHOLE, CHUNK)]
    table_copies = [
        pltpu.make_async_copy(table_hbm.at[pl.ds(c, size)], table_low.at[pl.ds(c, size)], t_sem.at[n])
        for n, (c, size) in enumerate(chunks)
    ]
    for copy in table_copies:
        copy.start()

    lane = lax.broadcasted_iota(jnp.int32, (1, 128), 1)
    note[0:6, :] = mask_ref[...]
    line_of_splits = jnp.zeros((1, 128), jnp.int32)
    for r in range(6):
        line_of_splits = jnp.where(lane == r, splits_ref[r], line_of_splits)
    note[6:7, :] = line_of_splits
    note[7:8, :] = jnp.zeros((1, 128), jnp.int32)
    wide[...] = jnp.zeros((BLOCK, 128), F32)
    wide[0:SHARD, :] = mats_ref[...]
    wide[SHARD : SHARD + 1, 0:47] = vecs_ref[...]
    block[...] = wide[...].astype(BF16)
    params_ref[dp * 16 + me] = block[...]
    main = (3 * i + 1) // 8
    for copy, (c, size) in zip(table_copies, chunks):
        copy.wait()
        table[c : c + size, :] = table_low[c : c + size, :].astype(F32)
    for copy in loads:
        copy.start()
    table[WHOLE:VOCAB, :] = tail_ref[...].astype(F32)[0 : VOCAB - WHOLE]

    def pick(g, _):
        for u in range(16):
            token = ids_ref[g // 8, g % 8 * 16 + u]
            picked[pl.ds(g * 16 + u, 1), :] = table[pl.ds(token, 1), :]
        return 0

    lax.fori_loop(0, 48, pick, 0)
    for r in range(6):
        e_ref[r] = picked[128 * r : 128 * r + 128, :].astype(BF16)

    @pl.when(is_source)
    def _():
        e_all[pl.ds(pl.multiple_of(me * 128, 128), 128), :] = e_ref[3 * (z % 2) + main]
        notes[me] = note[...]

    pl.semaphore_wait(barrier, jnp.where(is_source, 15, 16) + 15 + 3 + 1)

    def a_copy(k):
        return pltpu.make_async_remote_copy(
            block, params_ref.at[dp * 16 + me], a_send.at[k], a_recv.at[k], device_id=(dp, (me + k) % 16), device_id_type=MESH
        )

    def b_copy(k):
        mine = params_ref.at[pl.ds(dp * 16, 16)]
        return pltpu.make_async_remote_copy(
            mine, mine, b_send.at[k], b_recv.at[k], device_id=(2 * ((x + k) % 4) + core, me), device_id_type=MESH
        )

    def c_copy(k):
        mine = params_ref.at[pl.ds((2 * ((x + k) % 4) + core) * 16, 16)]
        return pltpu.make_async_remote_copy(mine, mine, c_send.at[k], c_recv.at[k], device_id=sibling, device_id_type=MESH)

    def a_start(k, _):
        a_copy(k).start()
        return 0

    def a_wait(k, _):
        a_copy(k).wait()
        return 0

    def e_copy(d, noted):
        zd, yd, cd = 2 * core + d // 8, d // 2 % 4, d % 2
        where = dict(device_id=(2 * x + cd, 4 * zd + yd), device_id_type=MESH)
        if noted:
            return pltpu.make_async_remote_copy(note, notes.at[me], n_send.at[d], n_recv.at[me], **where)
        row = 3 * (d // 8) + (3 * (2 * yd + cd) + 1) // 8
        here = pl.ds(pl.multiple_of(me * 128, 128), 128)
        return pltpu.make_async_remote_copy(e_ref.at[row], e_all.at[here], e_send.at[d], e_recv.at[me], **where)

    def is_other(d):
        return jnp.logical_not((2 * core + d // 8 == z) & (d // 2 % 4 == y) & (d % 2 == core))

    def e_start(n, _):
        d = (n + me) % 16

        @pl.when(is_other(d))
        def _():
            e_copy(d, False).start()

        return 0

    def n_start(n, _):
        d = (n + me) % 16

        @pl.when(is_other(d))
        def _():
            e_copy(d, True).start()

        return 0

    lax.fori_loop(1, 16, a_start, 0)
    lax.fori_loop(0, 16, e_start, 0)
    lax.fori_loop(0, 16, n_start, 0)

    def e_sent(d, _):
        @pl.when(is_other(d))
        def _():
            e_copy(d, False).wait_send()
            e_copy(d, True).wait_send()

        return 0

    def e_arrived(f, _):
        @pl.when(jnp.logical_not(is_source & (f == me)))
        def _():
            where = dict(device_id=(source_dp, f), device_id_type=MESH)
            there = pl.ds(pl.multiple_of(f * 128, 128), 128)
            pltpu.make_async_remote_copy(e_ref.at[0], e_all.at[there], e_send.at[0], e_recv.at[f], **where).wait_recv()

        return 0

    def n_arrived(f, _):
        @pl.when(jnp.logical_not(is_source & (f == me)))
        def _():
            where = dict(device_id=(source_dp, f), device_id_type=MESH)
            pltpu.make_async_remote_copy(note, notes.at[f], n_send.at[0], n_recv.at[f], **where).wait_recv()

        return 0

    gives = ((y == 1) & (core == 1)) | ((y == 2) & (core == 0))
    takes = has_two()
    main_slot = jnp.where(i == 5, 1, 0)
    his_slot = jnp.where(y == 1, 1, 0)

    made = ((emb_t, emb_hbm), (k_t, k_hbm), (vt_t, vt_hbm))

    def target(n, slot, t):
        rows = pl.ds(pl.multiple_of(slot * SEQ + t * PT, PT), PT)
        return made[n][1].at[:, rows] if n == 2 else made[n][1].at[rows]

    def out_copy(n, t):
        return pltpu.make_async_copy(made[n][0].at[t % 2], target(n, main_slot, t), out.at[n, t % 2])

    def give_copy(n, t):
        return pltpu.make_async_remote_copy(
            made[n][0].at[t % 2], target(n, his_slot, t), s_send.at[n, t], s_recv.at[n, t],
            device_id=sibling, device_id_type=MESH,
        )

    def settle(t, parts):
        for n in parts:
            out_copy(n, t).wait()

        @pl.when(gives)
        def _():
            for n in parts:
                give_copy(n, t).wait_send()

    per = SEQ // PT
    row = lax.broadcasted_iota(jnp.int32, (PT, 1), 0)
    lax.fori_loop(1, 16, a_wait, 0)
    for k in range(1, 4):
        b_copy(k).start()
    c_copy(0).start()
    for t in range(TILES):
        b = t % 2
        lax.fori_loop(4 * t + (1 if t else 0), min(4 * t + 5, 16), e_arrived, 0)
        if t == 0:
            n_arrived(0, 0)
            loads[0].wait()
            split = jnp.sum(jnp.where(lane == 3 * (z % 2) + main, notes[0, 6:7, :], 0), keepdims=True)
        mid = e_all[t * PT : t * PT + PT, :]
        if t:
            before = e_all[t * PT - 16 : t * PT, :].astype(F32)[15:16]
        else:
            before = jnp.zeros((1, 128), F32)
        if t < TILES - 1:
            after = e_all[t * PT + PT : t * PT + PT + 16, :].astype(F32)[0:1]
        else:
            after = jnp.zeros((1, 128), F32)
        broad = mid.astype(F32)
        left = jnp.where(row == 0, before, pltpu.roll(broad, 1, 0)).astype(BF16)
        right = jnp.where(row == PT - 1, after, pltpu.roll(broad, PT - 1, 0)).astype(BF16)
        trigram = jnp.concatenate([left, mid, right], 1)
        typed = jnp.where(row + t * PT >= split, types_ref[1:2, :], types_ref[0:1, :])
        emb = (dot(trigram, proj_ref[...]) + line(ebias_ref, 0, 4) + typed).astype(BF16)
        if t == 0:
            loads[1].wait()
        hidden = (dot(emb, win_ref[...]) + line(bias_ref, 0, 8)).astype(BF16)
        if t == 0:
            loads[2].wait()
        keys = (dot(hidden, wqkv_ref[:, D_T : 2 * D_T]) + line(bias_ref, 16, 8)).astype(BF16)
        values = (dot(hidden, wqkv_ref[:, 2 * D_T :]) + line(bias_ref, 24, 8)).astype(BF16)
        if t >= 2:
            settle(t - 2, range(3))
        emb_t[b] = emb
        k_t[b] = keys
        vt_t[b] = values.T
        for n in range(3):
            out_copy(n, t).start()

        @pl.when(gives)
        def _(t=t):
            for n in range(3):
                give_copy(n, t).start()


        if t == C_TILE:
            for k in range(1, 4):
                b_copy(k).wait()
                c_copy(4 - k).start()
    for t in range(TILES - 2, TILES):
        settle(t, [0])

    def arrive(n):
        @pl.when(takes)
        def _():
            for t in range(TILES):
                give_copy(n, t).wait_recv()

    arrive(0)
    own = pltpu.make_async_copy(emb_hbm.at[pl.ds(pl.multiple_of(first_block() * QB, QB), OWN)], own_ref, own_sem)
    own.start()
    lax.fori_loop(1, 16, n_arrived, 0)
    for j in range(3):
        t = first_block() + j
        local = 3 * (z % 2) + (3 * i + j) // 8
        for half in range(2):
            weight_ref[j, :, half * 128 : half * 128 + 128] = notes[2 * (t % 8) + half, pl.ds(local, 1), :].astype(F32)
    own.wait()
    finals = [
        pltpu.make_async_copy(ref, hbm, last_sem.at[n])
        for n, (ref, hbm) in enumerate([(own_ref, own_hbm), (hid_ref, hid_hbm), (params_ref, params_hbm)])
    ]
    finals[0].start()
    hidden = dot(own_ref[...], win_ref[...]) + line(bias_ref, 0, 8)
    hid_ref[...] = hidden
    finals[1].start()
    for k in range(4):
        c_copy(k).wait()
    finals[2].start()
    queries = (dot(hidden.astype(BF16), wqkv_ref[:, :D_T]) + line(bias_ref, 8, 8)).astype(BF16)
    tq_ref[...] = queries * jnp.asarray(HEAD_T**-0.5, BF16)
    lax.fori_loop(0, 16, e_sent, 0)
    for t in range(TILES - 2, TILES):
        settle(t, [1, 2])
    arrive(1)
    arrive(2)
    for copy in finals:
        copy.wait()


def front(ids, table, table_end, mask, splits, mats, vecs, proj, win, wqkv, ebias, types, bias):
    vmem = pl.BlockSpec(memory_space=pltpu.VMEM)
    hbm = pl.BlockSpec(memory_space=pl.ANY)
    smem = pl.BlockSpec(memory_space=pltpu.SMEM)
    tail = pl.BlockSpec((16, 128), lambda _: (WHOLE // 16, 0))
    dma = pltpu.SemaphoreType.DMA
    return pl.pallas_call(
        front_kernel,
        grid=(1,),
        in_specs=[smem, hbm, tail, vmem, smem, vmem, vmem, hbm, hbm, hbm, vmem, vmem, vmem],
        out_specs=[hbm, hbm, hbm, hbm, hbm, vmem, vmem, hbm],
        out_shape=[
            jax.ShapeDtypeStruct((SLOTS, D_E), BF16),
            jax.ShapeDtypeStruct((SLOTS, D_T), BF16),
            jax.ShapeDtypeStruct((D_T, SLOTS), BF16),
            jax.ShapeDtypeStruct((OWN, D_E), BF16),
            jax.ShapeDtypeStruct((OWN, D_T), F32),
            jax.ShapeDtypeStruct((OWN, D_T), BF16),
            jax.ShapeDtypeStruct((3, 1, QB), F32),
            jax.ShapeDtypeStruct((128, BLOCK, 128), BF16),
        ],
        scratch_shapes=[
            pltpu.VMEM((OWN, D_E), BF16),
            pltpu.VMEM((OWN, D_T), F32),
            pltpu.VMEM((128, BLOCK, 128), BF16),
            pltpu.VMEM((WHOLE, 128), BF16),
            pltpu.VMEM((WHOLE + 16, 128), F32),
            pltpu.VMEM((OWN, 128), F32),
            pltpu.VMEM((6, 128, 128), BF16),
            pltpu.VMEM((8, 128), jnp.int32),
            pltpu.VMEM((16, 8, 128), jnp.int32),
            pltpu.VMEM((BLOCK, 128), F32),
            pltpu.VMEM((BLOCK, 128), BF16),
            pltpu.VMEM((SEQ, 128), BF16),
            pltpu.VMEM((3 * 128, D_E), BF16),
            pltpu.VMEM((D_E, D_T), BF16),
            pltpu.VMEM((D_T, 3 * D_T), BF16),
            pltpu.VMEM((2, PT, D_E), BF16),
            pltpu.VMEM((2, PT, D_T), BF16),
            pltpu.VMEM((2, D_T, PT), BF16),
            dma((-(-WHOLE // CHUNK),)),
            dma((3,)),
            dma((16,)),
            dma((16,)),
            dma((16,)),
            dma((16,)),
            dma((16,)),
            dma((16,)),
            dma((4,)),
            dma((4,)),
            dma((4,)),
            dma((4,)),
            dma((3, 2)),
            dma((3, TILES)),
            dma((3, TILES)),
            dma,
            dma((3,)),
        ],
        compiler_params=params(58, collective_id=0, has_side_effects=True),
        name="front",
    )(ids, table, table_end, mask, splits, mats, vecs, proj, win, wqkv, ebias, types, bias)


def unpack_rows(pairs, packed_ref, flat):
    for pair in pairs:
        both = [packed_ref[2 * pair + i].astype(F32)[:SHARD] for i in range(2)]
        flat[88 * pair : 88 * pair + 88, :] = jnp.concatenate(both, 0)


def unpack_vectors(packed_ref, vec_ref):
    lane = lax.broadcasted_iota(jnp.int32, (1, 128), 1)
    rows = [jnp.zeros((1, 128), F32)] * 48
    for owner in range(128):
        row, shift = divmod(47 * owner, 128)
        entries = packed_ref[owner].astype(F32)[SHARD : SHARD + 1, :]
        moved = pltpu.roll(entries, shift, 1) if shift else entries
        if shift + 47 > 128:
            rows[row] = jnp.where(lane >= shift, moved, rows[row])
            rows[row + 1] = jnp.where(lane < shift + 47 - 128, moved, rows[row + 1])
        else:
            rows[row] = jnp.where((lane >= shift) & (lane < shift + 47), moved, rows[row])
    for row in range(48):
        vec_ref[row : row + 1, :] = rows[row]


ST = 1024


def student_in_kernel(emb_hbm, packed_hbm, first_ref, sq_ref, sk_ref, sv_ref, skt_ref, svt_ref,
                      win_ref, wqkv_ref, watt_ref, wup_ref, wdown_ref, wout_ref, vec_ref, flat, emb_parts, packed_ref, sems):
    t = pl.program_id(0)
    packed_load = pltpu.make_async_copy(packed_hbm, packed_ref, sems.at[SLOTS // ST])

    def emb_load(n):
        return pltpu.make_async_copy(emb_hbm.at[n * ST : n * ST + ST], emb_parts.at[n], sems.at[n])

    @pl.when(t == 0)
    def _():
        packed_load.start()
        for n in range(SLOTS // ST):
            emb_load(n).start()
        packed_load.wait()
        unpack_vectors(packed_ref, vec_ref)
        unpack_rows(range(12), packed_ref, flat)
        win_ref[...] = flat[0:512, :].astype(BF16)
        for n in range(3):
            wqkv_ref[:, n * 128 : n * 128 + 128] = flat[pl.ds(512 + n, 128, stride=3), :].astype(BF16)
        watt_ref[...] = flat[896:1024, :].astype(BF16)

    for step in range(SLOTS // ST):

        @pl.when(t == step)
        def _(step=step):
            emb_load(step).wait()
            student_tile(t, emb_parts.at[step], win_ref, wqkv_ref, vec_ref, first_ref, sq_ref, sk_ref, sv_ref, skt_ref, svt_ref)
            unpack_rows(range(12 + 13 * step, 12 + 13 * (step + 1)), packed_ref, flat)
            if step == 1:
                for i in range(FFN_COUNT):
                    for n in range(4):
                        part = flat[pl.ds(1024 + 512 * i + n, 128, stride=4), :]
                        wup_ref[i, :, n * 128 : n * 128 + 128] = part.astype(BF16)
            if step == 3:
                for i in range(FFN_COUNT):
                    wdown_ref[i] = flat[3072 + 512 * i : 3584 + 512 * i, :].astype(BF16)
                for n in range(4):
                    wout_ref[:, n * 128 : n * 128 + 128] = flat[pl.ds(5120 + n, 128, stride=4), :].astype(BF16)


def student_tile(t, emb_ref, win_ref, wqkv_ref, vec_ref, first_ref, sq_ref, sk_ref, sv_ref, skt_ref, svt_ref):
    emb = emb_ref[...]
    emb = jnp.where((t < SEQ // ST) | has_two(), emb, jnp.zeros_like(emb))
    first = (dot(emb, win_ref[...]) + line(vec_ref, V_IN)).astype(BF16)
    first_ref[...] = first
    qkv = dot(first, wqkv_ref[...])
    sq_ref[...] = (qkv[:, :D_S] + line(vec_ref, V_QKV)).astype(BF16)
    s_keys = (qkv[:, D_S : 2 * D_S] + line(vec_ref, V_QKV + 1)).astype(BF16)
    s_values = (qkv[:, 2 * D_S :] + line(vec_ref, V_QKV + 2)).astype(BF16)
    sk_ref[...] = s_keys
    sv_ref[...] = s_values
    skt_ref[...] = s_keys.T
    svt_ref[...] = s_values.T


def student_in(emb, packed):
    tall = jax.ShapeDtypeStruct((SLOTS, D_S), BF16)
    flat = jax.ShapeDtypeStruct((D_S, SLOTS), BF16)
    down = pl.BlockSpec((ST, D_S), lambda t: (t, 0))
    across = pl.BlockSpec((D_S, ST), lambda t: (0, t))
    made = [
        ((D_E, D_S), BF16),
        ((D_S, 3 * D_S), BF16),
        ((D_S, D_S), BF16),
        ((FFN_COUNT, D_S, FF_S), BF16),
        ((FFN_COUNT, FF_S, D_S), BF16),
        ((D_S, D_E), BF16),
        ((48, 128), F32),
    ]
    return pl.pallas_call(
        student_in_kernel,
        grid=(SLOTS // ST,),
        in_specs=[pl.BlockSpec(memory_space=pl.ANY)] * 2,
        out_specs=[down] * 4 + [across] * 2 + [whole(*shape) for shape, _ in made],
        out_shape=[tall] * 4 + [flat] * 2 + [jax.ShapeDtypeStruct(*entry) for entry in made],
        scratch_shapes=[
            pltpu.VMEM((5632, 128), F32),
            pltpu.VMEM((SLOTS // ST, ST, D_E), BF16),
            pltpu.VMEM((128, BLOCK, 128), BF16),
            pltpu.SemaphoreType.DMA((SLOTS // ST + 1,)),
        ],
        compiler_params=params(46),
        name="student_in",
    )(emb, packed)


CB = 256
SUB = 64
STEPS = 3 * HEADS


def head_lanes(values, head):
    lane = lax.broadcasted_iota(jnp.int32, (1, D_S), 1)
    return jnp.where(lane // HEAD_S == head, values, jnp.zeros_like(values))


def attend_kernel(tq_ref, tk_ref, tvt_ref, sq_ref, sk_ref, svt_ref, skt_ref, et_ref, es_ref, tmix_ref, smix_ref, stat_ref,
                  ts0, ts1, ss0, ss1, mx0, mx1, sqt0, sqt1):
    n = pl.program_id(0)
    s_factor = HEAD_S**-0.5 * LOG2E

    def work(ts, ss, mx, sqt, tr, sr, mr, sqr, scores, mixes):
        if scores:
            queries, s_queries = tq_ref[...], head_lanes(sq_ref[...], n // 3)
            tall = s_queries.astype(F32).T
            sqt[...] = sum(tall[h * HEAD_S : (h + 1) * HEAD_S] for h in range(HEADS))
            t_max = s_max = jnp.full((8, QB), -jnp.inf, F32)
        if mixes:
            t_top, s_top = jnp.max(mr[0], 0, keepdims=True), jnp.max(mr[1], 0, keepdims=True)
            t_off, s_off = t_top * LOG2E, s_top * s_factor
            entropy = jnp.zeros((8, QB), F32)
            ones = jnp.ones((16, CB), BF16)
            t_mix = jnp.zeros((HEAD_T + HEAD_S + 16, QB), F32)
            s_mix = jnp.zeros((HEAD_S + 16, QB), F32)
        for c in range(SEQ // CB):
            part = slice(c * CB, c * CB + CB)
            if scores:
                t_part = dot_nt(tk_ref[part, :], queries)
                ts[part, :] = t_part
                s_part = dot_nt(sk_ref[part, :], s_queries)
                ss[part, :] = s_part
                t_max = jnp.maximum(t_max, fold(t_part, jnp.max))
                s_max = jnp.maximum(s_max, fold(s_part, jnp.max))
            if mixes:
                for u in range(c * CB, c * CB + CB, SUB):
                    some = slice(u, u + SUB)
                    t_log = tr[some, :] * LOG2E - t_off
                    t_exp = jnp.exp2(t_log)
                    et_ref[0, some, :] = t_exp.astype(BF16)
                    es_ref[0, some, :] = jnp.exp2(sr[some, :] * s_factor - s_off).astype(BF16)
                    entropy = entropy + fold(t_exp * t_log)
                t_mix += dot(jnp.concatenate([tvt_ref[:, part], skt_ref[:, part], ones], 0), et_ref[0, part, :])
                s_mix += dot(jnp.concatenate([svt_ref[:, part], ones], 0), es_ref[0, part, :])
        if scores:
            mx[0], mx[1] = t_max, s_max
        if mixes:
            t_sum, s_sum = t_mix[HEAD_T + HEAD_S : HEAD_T + HEAD_S + 1], s_mix[HEAD_S : HEAD_S + 1]
            t_inv, s_inv = 1.0 / t_sum, 1.0 / s_sum
            cross = jnp.sum(sqr[...] * t_mix[HEAD_T : HEAD_T + HEAD_S], 0, keepdims=True) * s_factor - s_off * t_sum
            kl = (jnp.sum(entropy, 0, keepdims=True) - cross) * t_inv * (1.0 / LOG2E)
            stat_ref[0, 0, 0:1, :] = t_inv
            stat_ref[0, 0, 1:2, :] = s_inv
            stat_ref[0, 0, 2:3, :] = kl - jnp.log(t_sum) + jnp.log(s_sum)
            stat_ref[0, 0, 3:8, :] = jnp.zeros((5, QB), F32)
            tmix_ref[...] = (t_mix[:HEAD_T] * t_inv).T.astype(BF16)
            smix_ref[0] = s_mix[:HEAD_S] * s_inv

    even, odd = (ts0, ss0, mx0, sqt0), (ts1, ss1, mx1, sqt1)
    pl.when(n == 0)(lambda: work(*even, *odd, True, False))
    pl.when((n > 0) & (n < STEPS) & (n % 2 == 0))(lambda: work(*even, *odd, True, True))
    pl.when((n > 0) & (n < STEPS) & (n % 2 == 1))(lambda: work(*odd, *even, True, True))
    pl.when(n == STEPS)(lambda: work(*even, *odd, False, True))


def attend(tq, tk, tvt, sq, sk, svt, skt):
    now = lambda n: jnp.minimum(n, STEPS - 1)
    last = lambda n: jnp.maximum(n - 1, 0)
    block = lambda n: n % 3
    head = lambda n: n // 3
    return pl.pallas_call(
        attend_kernel,
        grid=(STEPS + 1,),
        in_specs=[
            pl.BlockSpec((QB, HEAD_T), lambda n: (block(now(n)), head(now(n)))),
            pl.BlockSpec((SEQ, HEAD_T), lambda n: (slot_of(block(now(n))), head(now(n)))),
            pl.BlockSpec((HEAD_T, SEQ), lambda n: (head(last(n)), slot_of(block(last(n))))),
            pl.BlockSpec((QB, D_S), lambda n: (first_block() + block(now(n)), 0)),
            pl.BlockSpec((SEQ, D_S), lambda n: (slot_of(block(now(n))), 0)),
            pl.BlockSpec((HEAD_S, SEQ), lambda n: (head(last(n)), slot_of(block(last(n))))),
            pl.BlockSpec((HEAD_S, SEQ), lambda n: (head(last(n)), slot_of(block(last(n))))),
        ],
        out_specs=[
            pl.BlockSpec((1, SEQ, QB), lambda n: (block(last(n)), 0, head(last(n)))),
            pl.BlockSpec((1, SEQ, QB), lambda n: (block(last(n)), 0, head(last(n)))),
            pl.BlockSpec((QB, HEAD_T), lambda n: (block(last(n)), head(last(n)))),
            pl.BlockSpec((1, HEAD_S, QB), lambda n: (block(last(n)), head(last(n)), 0)),
            pl.BlockSpec((1, 1, 8, QB), lambda n: (block(last(n)), head(last(n)), 0, 0)),
        ],
        out_shape=[
            jax.ShapeDtypeStruct((3, SEQ, HEADS * QB), BF16),
            jax.ShapeDtypeStruct((3, SEQ, HEADS * QB), BF16),
            jax.ShapeDtypeStruct((OWN, D_T), BF16),
            jax.ShapeDtypeStruct((3, D_S, QB), F32),
            jax.ShapeDtypeStruct((3, HEADS, 8, QB), F32),
        ],
        scratch_shapes=[pltpu.VMEM((SEQ, QB), F32)] * 4 + [pltpu.VMEM((2, 8, QB), F32)] * 2 + [pltpu.VMEM((HEAD_S, QB), F32)] * 2,
        compiler_params=params(40),
        name="attend",
    )(tq, tk, tvt, sq, sk, svt, skt)


FC = 1024


def teacher_kernel(mix_ref, hid_ref, emb_ref, att_ref, up_hbm, down_hbm, out_ref, bias_ref, gain_ref, shift_ref, target_ref,
                   norm, low, acc, up_parts, down_parts, sems):
    c = pl.program_id(0)

    def loads(part):
        here = pl.ds(pl.multiple_of(part * FC, FC), FC)
        slot = part % 2
        return (
            pltpu.make_async_copy(up_hbm.at[:, here], up_parts.at[slot], sems.at[0, slot]),
            pltpu.make_async_copy(down_hbm.at[here], down_parts.at[slot], sems.at[1, slot]),
        )

    @pl.when(c == 0)
    def _():
        for copy in loads(0):
            copy.start()

    @pl.when(c < pl.num_programs(0) - 1)
    def _():
        for copy in loads(c + 1):
            copy.start()


    @pl.when(c == 0)
    def _():
        summed = hid_ref[...] + dot(mix_ref[...], att_ref[...]) + line(bias_ref, 32, 8)
        one = layer_norm(summed, line(gain_ref, 0, 8), line(shift_ref, 0, 8))
        norm[...] = one
        low[...] = one.astype(BF16)

    up_load, down_load = loads(c)
    up_load.wait()
    rows = FC // 128
    up_bias = bias_ref[pl.ds(pl.multiple_of(40 + rows * c, 8), rows), :]
    act = gelu(dot(low[...], up_parts[c % 2]) + line(up_bias, 0, rows)).astype(BF16)
    down_load.wait()
    part = dot(act, down_parts[c % 2])

    @pl.when(c == 0)
    def _():
        acc[...] = part

    @pl.when(c > 0)
    def _():
        acc[...] += part

    @pl.when(c == pl.num_programs(0) - 1)
    def _():
        summed = norm[...] + acc[...] + line(bias_ref, 72, 8)
        two = layer_norm(summed, line(gain_ref, 8, 8), line(shift_ref, 8, 8))
        last = emb_ref[...].astype(F32) + dot(two.astype(BF16), out_ref[...]) + line(bias_ref, 80, 4)
        target_ref[...] = layer_norm(last, line(gain_ref, 16, 4), line(shift_ref, 16, 4))


def teacher(mix, hid, emb, att, up, down, out, bias, gain, shift):
    return pl.pallas_call(
        teacher_kernel,
        grid=(FF_T // FC,),
        in_specs=[
            whole(OWN, D_T),
            whole(OWN, D_T),
            whole(OWN, D_E),
            whole(D_T, D_T),
            pl.BlockSpec(memory_space=pl.ANY),
            pl.BlockSpec(memory_space=pl.ANY),
            whole(D_T, D_E),
            whole(84, 128),
            whole(20, 128),
            whole(20, 128),
        ],
        out_specs=whole(OWN, D_E),
        out_shape=jax.ShapeDtypeStruct((OWN, D_E), F32),
        scratch_shapes=[
            pltpu.VMEM((OWN, D_T), F32),
            pltpu.VMEM((OWN, D_T), BF16),
            pltpu.VMEM((OWN, D_T), F32),
            pltpu.VMEM((2, D_T, FC), BF16),
            pltpu.VMEM((2, FC, D_T), BF16),
            pltpu.SemaphoreType.DMA((2, 2)),
        ],
        compiler_params=params(40),
        name="teacher",
    )(mix, hid, emb, att, up, down, out, bias, gain, shift)


def student_kernel(emb_ref, smix_ref, target_ref, weight_ref, win_ref, watt_ref, wup_ref, wdown_ref, wout_ref, vec_ref,
                   grad_ref, vgrad_ref, dsum_ref, dmix_ref, part_ref, states, slopes, outers, acts):

    def put(r, value):
        for i in range(value.shape[1] // 128):
            vgrad_ref[r + i : r + i + 1, :] = value[:, i * 128 : i * 128 + 128]

    total = lambda v: jnp.sum(v.astype(F32), 0, keepdims=True)
    emb = emb_ref[...]
    source = emb.astype(F32)
    first = dot(emb, win_ref[...]) + line(vec_ref, V_IN)
    mixed = jnp.concatenate([smix_ref[j].T for j in range(3)], 0).astype(BF16)
    branch = dot(mixed, watt_ref[...]) + line(vec_ref, V_ATT)
    state = line(vec_ref, V_AGAIN) * (first + branch) + line(vec_ref, V_ASHIFT)
    for i in range(FFN_COUNT):
        states[i] = state
        inner = dot(state.astype(BF16), wup_ref[i]) + line(vec_ref, V_UP + 4 * i, 4)
        half = 0.5 * (1.0 + lax.erf(inner * 0.7071067811865476))
        slopes[i] = half + inner * jnp.exp(-0.5 * inner * inner) * 0.3989422804014327
        act = (inner * half).astype(BF16)
        acts[i] = act
        pre = state + dot(act, wdown_ref[i]) + line(vec_ref, V_DOWN + i)
        outers[i] = pre
        state = line(vec_ref, V_FGAIN + i) * pre + line(vec_ref, V_FSHIFT + i)
    state_low = state.astype(BF16)
    summed = source + dot(state_low, wout_ref[...]) + line(vec_ref, V_OUT, 4)
    diff = line(vec_ref, V_OGAIN, 4) * summed + line(vec_ref, V_OSHIFT, 4) - target_ref[...]
    weight = jnp.concatenate([jnp.broadcast_to(weight_ref[j], (8, QB)).T[:, 0:1] for j in range(3)], 0)
    loss = jnp.sum(weight * jnp.sum(diff * diff, 1, keepdims=True)) * (1.0 / D_E)
    count = jnp.sum(weight)
    d_result = (weight * (2.0 / D_E)) * diff
    put(V_OGAIN, total(d_result * summed))
    put(V_OSHIFT, total(d_result))
    d_output = (d_result * line(vec_ref, V_OGAIN, 4)).astype(BF16)
    out_g = dot_tn(state_low, d_output)
    for n in range(4):
        grad_ref[pl.ds(4224 + n, 128, stride=4), :] = out_g[:, n * 128 : n * 128 + 128]
    put(V_OUT, total(d_output))
    d_state = dot_nt(d_output, wout_ref[...])
    for i in reversed(range(FFN_COUNT)):
        put(V_FGAIN + i, total(d_state * outers[i]))
        put(V_FSHIFT + i, total(d_state))
        d_sum = d_state * line(vec_ref, V_FGAIN + i)
        d_outer = d_sum.astype(BF16)
        grad_ref[2176 + 512 * i : 2176 + 512 * (i + 1), :] = dot_tn(acts[i], d_outer)
        d_inner = (dot_nt(d_outer, wdown_ref[i]) * slopes[i]).astype(BF16)
        up_g = dot_tn(states[i].astype(BF16), d_inner)
        for n in range(4):
            grad_ref[pl.ds(128 + 512 * i + n, 128, stride=4), :] = up_g[:, n * 128 : n * 128 + 128]
        put(V_UP + 4 * i, total(d_inner))
        put(V_DOWN + i, total(d_outer))
        d_state = d_sum + dot_nt(d_inner, wup_ref[i])
    put(V_AGAIN, total(d_state * (first + branch)))
    put(V_ASHIFT, total(d_state))
    d_sum = d_state * line(vec_ref, V_AGAIN)
    d_branch = d_sum.astype(BF16)
    grad_ref[0:128, :] = dot_tn(mixed, d_branch)
    put(V_ATT, total(d_branch))
    dsum_ref[...] = d_sum
    dmix_ref[...] = dot_nt(d_branch, watt_ref[...]).astype(BF16)
    for r in (0, 1, 2, 3, 47):
        vgrad_ref[r : r + 1, :] = jnp.zeros((1, 128), F32)
    row = lax.broadcasted_iota(jnp.int32, (8, 128), 0)
    lane = lax.broadcasted_iota(jnp.int32, (8, 128), 1)
    part_ref[...] = jnp.where((row == 0) & (lane == 0), loss, 0.0) + jnp.where((row == 0) & (lane == 1), count, 0.0)


def student(emb, smix, target, weight, win, watt, wup, wdown, wout, vecs):
    return pl.pallas_call(
        student_kernel,
        grid=(1,),
        in_specs=[
            whole(OWN, D_E),
            whole(3, D_S, QB),
            whole(OWN, D_E),
            whole(3, 1, QB),
            whole(D_E, D_S),
            whole(D_S, D_S),
            whole(FFN_COUNT, D_S, FF_S),
            whole(FFN_COUNT, FF_S, D_S),
            whole(D_S, D_E),
            whole(48, 128),
        ],
        out_specs=[whole(4736, 128), whole(48, 128), whole(OWN, D_S), whole(OWN, D_S), whole(8, 128)],
        out_shape=[
            jax.ShapeDtypeStruct((4736, 128), F32),
            jax.ShapeDtypeStruct((48, 128), F32),
            jax.ShapeDtypeStruct((OWN, D_S), F32),
            jax.ShapeDtypeStruct((OWN, D_S), BF16),
            jax.ShapeDtypeStruct((8, 128), F32),
        ],
        scratch_shapes=[
            pltpu.VMEM((FFN_COUNT, OWN, D_S), F32),
            pltpu.VMEM((FFN_COUNT, OWN, FF_S), F32),
            pltpu.VMEM((FFN_COUNT, OWN, D_S), F32),
            pltpu.VMEM((FFN_COUNT, OWN, FF_S), BF16),
        ],
        compiler_params=params(40),
        name="student",
    )(emb, smix, target, weight, win, watt, wup, wdown, wout, vecs)


KB = 1024


def back_kernel(et_ref, es_ref, stat_ref, smix_ref, dmix_ref, weight_ref, sq_ref, sv_ref, skt_ref, dsum_ref, emb_hbm, first_ref,
                wqkv_ref, vgrad_ref, part_in, late_ref, *rest):
    state_refs, rest = rest[:6], rest[6:]
    made_ref, rest = rest[0], rest[1:]
    (dkv, dqt, ds, dq, dfirst, dmt, dmz, sqd, rows, flat, vecs, kls, block_ref, emb_ref, sem, emb_sem), buffers = rest[:16], rest[16:]
    j, kb = pl.program_id(0), pl.program_id(1)
    s_scale = HEAD_S**-0.5
    late = pltpu.make_async_copy(late_ref, flat.at[896:5632], sem)
    emb_load = pltpu.make_async_copy(emb_hbm, emb_ref, emb_sem)

    @pl.when((j == 0) & (kb == 0))
    def _():
        greet()
        late.start()
        emb_load.start()
        vecs[...] = vgrad_ref[...]
        dkv[...] = jnp.zeros_like(dkv)
        kls[...] = jnp.zeros_like(kls)

    @pl.when((j == 0) & (kb == 1))
    def _():
        late.wait()
        pack_blocks(range(FIRST_EARLY // 2, 64), flat, vecs, block_ref)
        swap_early(block_ref, buffers)

    @pl.when((j == 1) & (kb == 0))
    def _():
        send_early(block_ref, buffers)

    @pl.when(kb == 0)
    def _():
        quarter = weight_ref[0] * (1.0 / HEADS)
        wide = dmix_ref[...].astype(F32)
        tall = wide.T
        place = lax.broadcasted_iota(jnp.int32, (D_S, 1), 0) // HEAD_S
        for h in range(HEADS):
            own = slice(h * HEAD_S, h * HEAD_S + HEAD_S)
            mine = slice(h * QB, h * QB + QB)
            t_inv, s_inv = stat_ref[0, h, 0:1, :], stat_ref[0, h, 1:2, :]
            kls[0:1, :] += quarter * stat_ref[0, h, 2:3, :]
            row_dot = jnp.sum(tall[own] * smix_ref[0, own, :], 0, keepdims=True)
            rows[h, 0:1, :] = row_dot - quarter
            rows[h, 1:2, :] = s_inv
            rows[h, 2:3, :] = quarter * t_inv
            dmt[h] = jnp.where(place == h, tall, 0.0).astype(BF16)
            dmz[mine, :] = head_lanes(wide * stat_ref[0, h].T[:, 1:2], h).astype(BF16)
            sqd[mine, :] = head_lanes(sq_ref[...], h)
        dqt[...] = jnp.zeros_like(dqt)

    here = pl.ds(pl.multiple_of(slot_of(j) * SEQ + kb * KB, KB), KB)
    dkv[here, D_S:] += dot(es_ref[0], dmz[...])
    for h in range(HEADS):
        lanes = slice(h * QB, h * QB + QB)
        for c in range(KB // 256):
            part = slice(c * 256, c * 256 + 256)
            d_probs = dot(sv_ref[part, :], dmt[h])
            s_exp, t_exp = es_ref[0, part, lanes].astype(F32), et_ref[0, part, lanes].astype(F32)
            d_scores = (d_probs - rows[h, 0:1, :]) * rows[h, 1:2, :] * s_exp - t_exp * rows[h, 2:3, :]
            ds[part, lanes] = d_scores.astype(BF16)
        own = slice(h * HEAD_S, h * HEAD_S + HEAD_S)
        dqt[own, :] += dot(skt_ref[own, :], ds[:, lanes])
    dkv[here, :D_S] += dot(ds[...], sqd[...])

    @pl.when(kb == pl.num_programs(1) - 1)
    def _():
        dq[pl.ds(pl.multiple_of(j * QB, QB), QB), :] = (dqt[...] * s_scale).T

    @pl.when((j == 2) & (kb == pl.num_programs(1) - 1))
    def _():
        qkv_w = wqkv_ref[...]
        dq_low = dq[...].astype(BF16)
        own = pl.ds(pl.multiple_of(first_block() * QB, QB), OWN)
        q_grad = dot_tn(first_ref[own, :], dq_low)
        own_part = dsum_ref[...] + dot_nt(dq_low, qkv_w[:, :D_S])
        kv_grad = jnp.zeros((D_S, 2 * D_S), F32)
        kv_bias = jnp.zeros((1, 2 * D_S), F32)
        for c in range(8):
            part = pl.ds(c * 512, 512)
            wide = dkv[part, :]
            low = jnp.concatenate([(wide[:, :D_S] * s_scale).astype(BF16), wide[:, D_S:].astype(BF16)], 1)
            kv_grad += dot_tn(first_ref[part, :], low)
            kv_bias += jnp.sum(low.astype(F32), 0, keepdims=True)
            dfirst[part, :] = dot_nt(low, qkv_w[:, D_S:])
        dfirst[own, :] += own_part
        in_grad = jnp.zeros((D_S, D_E), F32)
        in_bias = jnp.zeros((1, D_S), F32)
        two = has_two()
        emb_load.wait()
        for c in range(8):
            part = pl.ds(c * 512, 512)
            low = dfirst[part, :].astype(BF16)
            emb = emb_ref[part, :]
            if c >= 4:
                emb = jnp.where(two, emb, jnp.zeros_like(emb))
            in_grad += dot_tn(low, emb)
            in_bias += jnp.sum(low.astype(F32), 0, keepdims=True)
        flat[0:512, :] = in_grad.T
        flat[pl.ds(512, 128, stride=3), :] = q_grad
        flat[pl.ds(513, 128, stride=3), :] = kv_grad[:, :D_S]
        flat[pl.ds(514, 128, stride=3), :] = kv_grad[:, D_S:]
        vecs[0:1, :] = in_bias
        vecs[1:2, :] = jnp.sum(dq_low.astype(F32), 0, keepdims=True)
        vecs[2:3, :] = kv_bias[:, :D_S]
        vecs[3:4, :] = kv_bias[:, D_S:]
        pack_blocks(range(FIRST_EARLY // 2), flat, vecs, block_ref)
        kl = jnp.sum(kls[0:1, :], keepdims=True)
        corner = lax.broadcasted_iota(jnp.int32, (1, 128), 1) == 0
        send_rest(block_ref, buffers)
        update(block_ref, part_in[0:1, :] + jnp.where(corner, kl, 0.0), state_refs, made_ref, buffers)


def back(et, es, stat, smix, dmix, weight, sq, sv, skt, dsum, emb, first, wqkv, vgrad, part, late, *state):
    count = SEQ // KB
    place = lambda j, k: slot_of(j) * count + k
    dma = pltpu.SemaphoreType.DMA
    return pl.pallas_call(
        back_kernel,
        grid=(3, count),
        in_specs=[
            pl.BlockSpec((1, KB, HEADS * QB), lambda j, k: (j, k, 0)),
            pl.BlockSpec((1, KB, HEADS * QB), lambda j, k: (j, k, 0)),
            pl.BlockSpec((1, HEADS, 8, QB), lambda j, k: (j, 0, 0, 0)),
            pl.BlockSpec((1, D_S, QB), lambda j, k: (j, 0, 0)),
            pl.BlockSpec((QB, D_S), lambda j, k: (j, 0)),
            pl.BlockSpec((1, 1, QB), lambda j, k: (j, 0, 0)),
            pl.BlockSpec((QB, D_S), lambda j, k: (first_block() + j, 0)),
            pl.BlockSpec((KB, D_S), lambda j, k: (place(j, k), 0)),
            pl.BlockSpec((D_S, KB), lambda j, k: (0, place(j, k))),
            whole(OWN, D_S),
            pl.BlockSpec(memory_space=pl.ANY),
            whole(SLOTS, D_S),
            whole(D_S, 3 * D_S),
            whole(48, 128),
            whole(8, 128),
            pl.BlockSpec(memory_space=pl.ANY),
        ]
        + [whole(SHARD, 128), whole(1, 47)] * 3,
        out_specs=whole(3 * BLOCK + 8, 128),
        out_shape=jax.ShapeDtypeStruct((3 * BLOCK + 8, 128), F32),
        scratch_shapes=[
            pltpu.VMEM((SLOTS, 2 * D_S), F32),
            pltpu.VMEM((D_S, QB), F32),
            pltpu.VMEM((KB, HEADS * QB), BF16),
            pltpu.VMEM((OWN, D_S), F32),
            pltpu.VMEM((SLOTS, D_S), F32),
            pltpu.VMEM((HEADS, D_S, QB), BF16),
            pltpu.VMEM((HEADS * QB, D_S), BF16),
            pltpu.VMEM((HEADS * QB, D_S), BF16),
            pltpu.VMEM((HEADS, 8, QB), F32),
            pltpu.VMEM((5632, 128), F32),
            pltpu.VMEM((48, 128), F32),
            pltpu.VMEM((8, QB), F32),
            pltpu.VMEM((4, 2, 16, BLOCK, 128), BF16),
            pltpu.VMEM((SLOTS, D_E), BF16),
            dma,
            dma,
            pltpu.VMEM((3, BLOCK, 128), F32),
            pltpu.VMEM((4, 16, BLOCK, 128), BF16),
            pltpu.VMEM((BLOCK, 128), F32),
            pltpu.VMEM((64, BLOCK, 128), BF16),
            pltpu.VMEM((64, BLOCK, 128), BF16),
            pltpu.VMEM((2, 2, 8, 128), F32),
            pltpu.VMEM((2, 16, 8, 128), F32),
            pltpu.VMEM((2, 8, 8, 128), F32),
            dma((2, 6)),
            dma((64,)),
            dma((64,)),
            dma((2, 16)),
            dma((2, 16)),
            dma((2, 8)),
            dma((2, 8)),
        ],
        compiler_params=params(44, collective_id=1, has_side_effects=True),
        name="back",
    )(et, es, stat, smix, dmix, weight, sq, sv, skt, dsum, emb, first, wqkv, vgrad, part, late, *state)


def chip(k):
    dp, fs = lax.axis_index("dp"), lax.axis_index("fsdp")
    return (2 * ((dp // 2 + k // 16) % 4) + dp % 2, (fs + k) % 16)


def greet():
    dp, fs = lax.axis_index("dp"), lax.axis_index("fsdp")
    barrier = pltpu.get_barrier_semaphore()

    def signal(k, _):
        pl.semaphore_signal(barrier, inc=1, device_id=chip(k), device_id_type=MESH)
        return 0

    lax.fori_loop(1, 64, signal, 0)
    for k in range(4):
        other = (2 * ((dp // 2 + k) % 4) + 1 - dp % 2, fs)
        pl.semaphore_signal(barrier, inc=1, device_id=other, device_id_type=MESH)


FIRST_EARLY = 22


def pack_blocks(pairs, flat, vecs, block_ref):
    lane = lax.broadcasted_iota(jnp.int32, (1, 128), 1)
    rest = jnp.zeros((BLOCK - SHARD - 1, 128), F32)
    for pair in pairs:
        both = flat[88 * pair : 88 * pair + 88, :]
        for i in range(2):
            owner = 2 * pair + i
            row, shift = divmod(47 * owner, 128)
            entries = vecs[row : row + 1, :]
            if shift + 47 > 128:
                entries = jnp.where(lane >= shift, entries, vecs[row + 1 : row + 2, :])
            if shift:
                entries = pltpu.roll(entries, 128 - shift, 1)
            entries = jnp.where(lane < 47, entries, 0.0)
            mine = both[SHARD * i : SHARD * (i + 1)]
            block_ref[owner // 32, owner // 16 % 2, owner % 16] = jnp.concatenate([mine, entries, rest], 0).astype(BF16)


SPLIT = FIRST_EARLY - 16


def swap_copy(n, g_ref, half_in, half_sems):
    dp, fs = lax.axis_index("dp"), lax.axis_index("fsdp")
    core = dp % 2
    if n in (1, 2, 3):
        source, goal = g_ref.at[n, 1 - core], half_in.at[n]
    elif n == 0:
        source, goal = g_ref.at[0, 1, 0:SPLIT], half_in.at[0, 0:SPLIT]
    elif n == 4:
        source, goal = g_ref.at[0, 1, SPLIT:16], half_in.at[0, SPLIT:16]
    else:
        source, goal = g_ref.at[0, 0], half_in.at[0]
    return pltpu.make_async_remote_copy(
        source, goal, half_sems.at[0, n], half_sems.at[1, n], device_id=(dp + 1 - 2 * core, fs), device_id_type=MESH
    )


def swap_early(g_ref, buffers):
    half_in, half_sems = buffers[1], buffers[8]
    pl.semaphore_wait(pltpu.get_barrier_semaphore(), 67)
    for n in (1, 2, 3):
        swap_copy(n, g_ref, half_in, half_sems).start()

    @pl.when(lax.axis_index("dp") % 2 == 0)
    def _():
        swap_copy(4, g_ref, half_in, half_sems).start()


def block_copy(k, buffers):
    block_out, blocks_in, block_send, block_recv = buffers[3], buffers[4], buffers[9], buffers[10]
    dp, fs = lax.axis_index("dp"), lax.axis_index("fsdp")
    place = (dp // 2 + k // 16) % 4 * 16 + (fs + k) % 16
    return pltpu.make_async_remote_copy(
        block_out.at[place], blocks_in.at[k], block_send.at[k], block_recv.at[k], device_id=chip(k), device_id_type=MESH
    )


def is_early(place):
    return (place >= 16) | ((lax.axis_index("dp") % 2 == 1) & (place >= SPLIT))


def join_and_send(early, g_ref, buffers):
    half_in, block_out = buffers[1], buffers[3]
    dp, fs = lax.axis_index("dp"), lax.axis_index("fsdp")
    core = dp % 2

    def join(i, _):
        @pl.when(is_early(i) == early)
        def _():
            summed = g_ref[i // 16, core, i % 16].astype(F32) + half_in[i // 16, i % 16].astype(F32)
            block_out[i] = summed.astype(BF16)

        return 0

    lax.fori_loop(0, 64 if early else 16, join, 0)

    def start(k, _):
        place = (dp // 2 + k // 16) % 4 * 16 + (fs + k) % 16

        @pl.when(is_early(place) == early)
        def _():
            block_copy(k, buffers).start()

        return 0

    lax.fori_loop(1, 64, start, 0)


def send_early(g_ref, buffers):
    half_in, half_sems = buffers[1], buffers[8]
    core = lax.axis_index("dp") % 2
    for n in (1, 2, 3):
        swap_copy(n, g_ref, half_in, half_sems).wait()

    @pl.when(core == 0)
    def _():
        swap_copy(4, g_ref, half_in, half_sems).wait_send()

    @pl.when(core == 1)
    def _():
        swap_copy(4, g_ref, half_in, half_sems).wait_recv()

    join_and_send(True, g_ref, buffers)


def send_rest(g_ref, buffers):
    half_in, half_sems = buffers[1], buffers[8]
    core = lax.axis_index("dp") % 2

    @pl.when(core == 0)
    def _():
        swap_copy(0, g_ref, half_in, half_sems).start()
        swap_copy(5, g_ref, half_in, half_sems).wait_recv()
        swap_copy(0, g_ref, half_in, half_sems).wait_send()

    @pl.when(core == 1)
    def _():
        swap_copy(5, g_ref, half_in, half_sems).start()
        swap_copy(0, g_ref, half_in, half_sems).wait_recv()
        swap_copy(5, g_ref, half_in, half_sems).wait_send()

    join_and_send(False, g_ref, buffers)


def update(g_ref, part, state_refs, made_ref, buffers):
    master_mat, master_vec, first_mat, first_vec, second_mat, second_vec = state_refs
    (packs, half_in, mine, block_out, blocks_in, tile_out, tiles_f, tiles_d,
     half_sems, block_send, block_recv, f_send, f_recv, d_send, d_recv) = buffers
    dp, fs = lax.axis_index("dp"), lax.axis_index("fsdp")
    x, core = dp // 2, dp % 2
    packs[...] = jnp.zeros_like(packs)
    for i, (mat, vec) in enumerate([(master_mat, master_vec), (first_mat, first_vec), (second_mat, second_vec)]):
        packs[i, 0:SHARD, :] = mat[...]
        packs[i, SHARD : SHARD + 1, 0:47] = vec[...]
    mine[...] = g_ref[x, core, fs].astype(F32) + half_in[x, fs].astype(F32)

    def gather(k, _):
        block_copy(k, buffers).wait()
        mine[...] += blocks_in[k].astype(F32)
        return 0

    lax.fori_loop(1, 64, gather, 0)

    row = lax.broadcasted_iota(jnp.int32, (BLOCK, 1), 0)
    place = (dp * 16 + fs) * SHARD + row
    is_matrix = row < SHARD
    bounds = [0]
    for rows in MAT_ROWS:
        bounds.append(bounds[-1] + rows)
    members = [is_matrix & (place >= bounds[i]) & (place < bounds[i + 1]) for i in range(6)]

    hops = lambda k: min(k, 4 - k)
    in_plane = sorted(range(1, 16), key=lambda k: -hops(k // 4) - hops(k % 4))
    along_x = sorted(range(1, 8), key=lambda k: -hops(k // 2) - k % 2)

    def everyone(tile, turn):
        tile_out[turn, 0] = tile
        tiles_d[turn, dp] = tile

        def f_copy(k):
            return pltpu.make_async_remote_copy(
                tile_out.at[turn, 1], tiles_f.at[turn, fs], f_send.at[turn, k], f_recv.at[turn, k],
                device_id=(dp, (fs // 4 + k // 4) % 4 * 4 + (fs + k) % 4), device_id_type=MESH,
            )

        def d_copy(k):
            return pltpu.make_async_remote_copy(
                tile_out.at[turn, 0], tiles_d.at[turn, dp], d_send.at[turn, k], d_recv.at[turn, k],
                device_id=((x + k // 2) % 4 * 2 + (core + k) % 2, fs), device_id_type=MESH,
            )

        for k in along_x:
            d_copy(k).start()
        for k in along_x:
            d_copy(k).wait()
        total = tiles_d[turn, 0]
        for k in range(1, 8):
            total = total + tiles_d[turn, k]
        tile_out[turn, 1] = total
        tiles_f[turn, fs] = total
        for k in in_plane:
            f_copy(k).start()
        for k in in_plane:
            f_copy(k).wait()
        total = tiles_f[turn, 0]
        for k in range(1, 16):
            total = total + tiles_f[turn, k]
        return total

    column = lambda v: jnp.sum(v, 0, keepdims=True)

    def tile_of(rows):
        return jnp.concatenate(rows + [jnp.zeros((8 - len(rows), 128), F32)] * (len(rows) < 8), 0)

    grad = mine[...]
    master = packs[0]
    squares = master * master
    tile = everyone(
        tile_of([part, column(grad * grad)] + [column(jnp.where(members[i], squares, 0.0)) for i in range(6)]), 0
    )
    loss, count = tile[0:1, 0:1], tile[0:1, 1:2]
    sums = jnp.sum(tile, 1, keepdims=True)
    inverse = 1.0 / count
    norm = jnp.sqrt(sums[1:2]) * inverse
    factor = CLIP_NORM / jnp.maximum(norm, CLIP_NORM)
    grad = grad * inverse * factor
    first = BETA_ONE * packs[1] + (1.0 - BETA_ONE) * grad
    second = BETA_TWO * packs[2] + (1.0 - BETA_TWO) * grad * grad
    ratio = first / (1.0 - BETA_ONE**STEP) / (jnp.sqrt(second / (1.0 - BETA_TWO**STEP)) + ADAM_EPS)
    ratio = ratio + jnp.where(is_matrix, WEIGHT_DECAY * master, 0.0)
    squares = ratio * ratio
    steps = everyone(tile_of([column(jnp.where(members[i], squares, 0.0)) for i in range(6)]), 1)
    made_ref[BLOCK : 2 * BLOCK, :] = first
    made_ref[2 * BLOCK : 3 * BLOCK, :] = second
    trusts = jnp.sqrt(sums[2:8]) / jnp.sqrt(jnp.sum(steps, 1, keepdims=True)[0:6])
    trust = jnp.ones((BLOCK, 1), F32)
    for i in range(6):
        trust = jnp.where(members[i], trusts[i : i + 1], trust)
    made_ref[0:BLOCK, :] = master - LEARN_RATE * (trust * ratio)
    lane = lax.broadcasted_iota(jnp.int32, (8, 128), 1)
    made_ref[3 * BLOCK :, :] = jnp.where(lane == 0, loss, jnp.where(lane == 1, count, norm))


def finish_kernel(made, loss, count, norm, m0, m1, m2, v0, v1, v2):
    for i, (mat, vec) in enumerate(((m0, v0), (m1, v1), (m2, v2))):
        mat[...] = made[BLOCK * i : BLOCK * i + SHARD, :]
        vec[...] = made[BLOCK * i + SHARD : BLOCK * i + SHARD + 1, 0:47]
    for i, out in enumerate((loss, count, norm)):
        out[...] = made[3 * BLOCK : 3 * BLOCK + 1, i : i + 1]


def finish(made):
    vmem = pl.BlockSpec(memory_space=pltpu.VMEM)
    shape = lambda *dims: jax.ShapeDtypeStruct(dims, F32)
    return pl.pallas_call(
        finish_kernel,
        in_specs=[vmem],
        out_specs=[vmem] * 9,
        out_shape=[shape(1, 1)] * 3 + [shape(SHARD, 128)] * 3 + [shape(1, 47)] * 3,
        compiler_params=params(63),
        name="finish",
    )(made)


def per_device(
    token_ids,
    splits,
    valid_mask,
    embed_table,
    embed_proj,
    embed_bias,
    type_table,
    teach_in,
    teach_qkv,
    teach_att,
    teach_up,
    teach_down,
    teach_out,
    teach_bias,
    teach_gain,
    teach_shift,
    matrices,
    vectors,
    matrix_first,
    matrix_second,
    vector_first,
    vector_second,
):
    mat = lambda v: v.reshape(SHARD, 128)
    vec = lambda v: v.reshape(1, 47)
    rows_128 = lambda v: v.reshape(-1, 128)
    bias = rows_128(teach_bias)
    emb, t_keys, t_values, own_emb, hidden, t_queries, weights, packed = front(
        token_ids, embed_table, embed_table, valid_mask, splits, mat(matrices), vec(vectors), embed_proj, teach_in, teach_qkv,
        rows_128(embed_bias), type_table, bias,
    )
    first, s_q, s_k, s_v, s_kt, s_vt, in_w, qkv_w, att_w, up_w, down_w, out_w, vecs = student_in(emb, packed)
    et, es, t_mixed, s_mixed, stat = attend(t_queries, t_keys, t_values, s_q, s_k, s_vt, s_kt)
    target = teacher(
        t_mixed, hidden, own_emb, teach_att, teach_up, teach_down, teach_out, bias, rows_128(teach_gain), rows_128(teach_shift)
    )
    late, vgrads, d_sum, d_mixed, part = student(
        own_emb, s_mixed, target, weights, in_w, att_w, up_w, down_w, out_w, vecs
    )
    made = back(
        et, es, stat, s_mixed, d_mixed, weights, s_q, s_v, s_kt, d_sum, emb, first, qkv_w, vgrads, part, late,
        mat(matrices), vec(vectors), mat(matrix_first), vec(vector_first), mat(matrix_second), vec(vector_second),
    )
    loss, count, norm, m0, m1, m2, v0, v1, v2 = finish(made)
    flat = lambda v: v.reshape(-1)
    scalar = lambda v: v.reshape(())
    return (
        scalar(loss), scalar(count), scalar(norm), flat(m0), flat(m1), flat(m2), flat(v0), flat(v1), flat(v2),
    )


def solution(mesh):
    both = P(("dp", "fsdp"))
    return jax.shard_map(
        per_device,
        mesh=mesh,
        in_specs=(P("dp", "fsdp"), P("dp"), P("dp", "fsdp")) + (P(),) * 13 + (both,) * 6,
        out_specs=(P(), P(), P(), both, both, both, both, both, both),
        check_vma=False,
    )
```

```python
import functools
import math

import jax
import jax.numpy as jnp
from jax import lax
from jax.experimental import pallas as pl
from jax.experimental.pallas import tpu as pltpu
from jax.sharding import PartitionSpec as P

D_E = 512
D_T = 1024
FF_T = 4096
D_S = 128
FF_S = 512
HEADS = 4
FFN_COUNT = 4
STEP = 5
HEAD_T = 256
HEAD_S = 32
SEQ = 2048
QB = 256
OWN = 3 * QB
SLOTS = 2 * SEQ

CLIP_NORM = 0.05
BETA_ONE = 0.9
BETA_TWO = 0.999
LEARN_RATE = 0.3
WEIGHT_DECAY = 0.01
ADAM_EPS = 1e-06

F32 = jnp.float32
BF16 = jnp.bfloat16
LOG2E = 1.4426950408889634
MESH = pl.DeviceIdType.MESH

MAT_ROWS = (512, 384, 128, 2048, 2048, 512)
SHARD = 44
BLOCK = 48
(V_IN, V_QKV, V_ATT, V_AGAIN, V_ASHIFT, V_UP, V_DOWN, V_FGAIN, V_FSHIFT, V_OUT, V_OGAIN, V_OSHIFT) = (
    0, 1, 4, 5, 6, 7, 23, 27, 31, 35, 39, 43)


def dot(left, right):
    return jnp.dot(left, right, preferred_element_type=F32)


def dot_nt(left, right):
    return lax.dot_general(left, right, (((1,), (1,)), ((), ())), preferred_element_type=F32)


def dot_tn(left, right):
    return lax.dot_general(left, right, (((0,), (0,)), ((), ())), preferred_element_type=F32)


def layer_norm(values, gain, shift):
    center = values - jnp.mean(values, -1, keepdims=True)
    spread = jnp.mean(center * center, -1, keepdims=True)
    return center * lax.rsqrt(spread + 1e-05) * gain + shift


def gelu(values):
    return 0.5 * values * (1.0 + lax.erf(values * 0.7071067811865476))


def params(mib, **more):
    return pltpu.CompilerParams(vmem_limit_bytes=mib * 2**20, **more)


def whole(*shape):
    return pl.BlockSpec(shape, lambda *_: (0,) * len(shape))


def line(ref, row, count=1):
    if count == 1:
        return ref[row : row + 1, :]
    return jnp.concatenate([ref[row + i : row + i + 1, :] for i in range(count)], 1)


def fold(values, op=jnp.sum):
    return op(values.reshape(values.shape[0] // 8, 8, values.shape[1]), 0)


def spots():
    dp, fs = lax.axis_index("dp"), lax.axis_index("fsdp")
    return dp // 2, dp % 2, fs // 4, fs % 4


def place_in_group():
    _, core, _, y = spots()
    return 2 * y + core


def first_block():
    return (3 * place_in_group()) % 8


def slot_of(j):
    return (first_block() + j) // 8


def has_two():
    i = place_in_group()
    return (i == 2) | (i == 5)


PT = 512
TILES = SEQ // PT
C_TILE = 2


CHUNK = 2048
VOCAB = 30522
WHOLE = VOCAB // 16 * 16


def front_kernel(ids_ref, table_hbm, tail_ref, mask_ref, splits_ref, mats_ref, vecs_ref, proj_hbm, win_hbm, wqkv_hbm, ebias_ref,
                 types_ref, bias_ref, emb_hbm, k_hbm, vt_hbm, own_hbm, hid_hbm, tq_ref, weight_ref, params_hbm,
                 own_ref, hid_ref, params_ref, table_low, table, picked, e_ref, note, notes, wide, block, e_all, proj_ref, win_ref, wqkv_ref, emb_t, k_t, vt_t,
                 t_sem, load, e_send, e_recv, n_send, n_recv, a_send, a_recv, b_send, b_recv, c_send, c_recv,
                 out, s_send, s_recv, own_sem, last_sem):
    dp, me = lax.axis_index("dp"), lax.axis_index("fsdp")
    x, core, z, y = spots()
    i = 2 * y + core
    sibling = (2 * x + 1 - core, me)
    source_dp = 2 * x + z // 2
    is_source = z // 2 == core
    loads = [
        pltpu.make_async_copy(hbm, ref, load.at[n])
        for n, (hbm, ref) in enumerate([(proj_hbm, proj_ref), (win_hbm, win_ref), (wqkv_hbm, wqkv_ref)])
    ]
    barrier = pltpu.get_barrier_semaphore()

    def signal(device):
        pl.semaphore_signal(barrier, inc=1, device_id=device, device_id_type=MESH)

    def greet_source(f, _):
        @pl.when(jnp.logical_not(is_source & (f == me)))
        def _():
            signal((source_dp, f))

        return 0

    def greet_plane(k, _):
        signal((dp, (me + k) % 16))
        return 0

    lax.fori_loop(0, 16, greet_source, 0)
    lax.fori_loop(1, 16, greet_plane, 0)
    for k in range(1, 4):
        signal((2 * ((x + k) % 4) + core, me))
    signal(sibling)
    chunks = [(c, min(CHUNK, WHOLE - c)) for c in range(0, WHOLE, CHUNK)]
    table_copies = [
        pltpu.make_async_copy(table_hbm.at[pl.ds(c, size)], table_low.at[pl.ds(c, size)], t_sem.at[n])
        for n, (c, size) in enumerate(chunks)
    ]
    for copy in table_copies:
        copy.start()

    lane = lax.broadcasted_iota(jnp.int32, (1, 128), 1)
    note[0:6, :] = mask_ref[...]
    line_of_splits = jnp.zeros((1, 128), jnp.int32)
    for r in range(6):
        line_of_splits = jnp.where(lane == r, splits_ref[r], line_of_splits)
    note[6:7, :] = line_of_splits
    note[7:8, :] = jnp.zeros((1, 128), jnp.int32)
    wide[...] = jnp.zeros((BLOCK, 128), F32)
    wide[0:SHARD, :] = mats_ref[...]
    wide[SHARD : SHARD + 1, 0:47] = vecs_ref[...]
    block[...] = wide[...].astype(BF16)
    params_ref[dp * 16 + me] = block[...]
    main = (3 * i + 1) // 8
    for copy, (c, size) in zip(table_copies, chunks):
        copy.wait()
        table[c : c + size, :] = table_low[c : c + size, :].astype(F32)
    for copy in loads:
        copy.start()
    table[WHOLE:VOCAB, :] = tail_ref[...].astype(F32)[0 : VOCAB - WHOLE]

    def pick(g, _):
        for u in range(16):
            token = ids_ref[g // 8, g % 8 * 16 + u]
            picked[pl.ds(g * 16 + u, 1), :] = table[pl.ds(token, 1), :]
        return 0

    lax.fori_loop(0, 48, pick, 0)
    for r in range(6):
        e_ref[r] = picked[128 * r : 128 * r + 128, :].astype(BF16)

    @pl.when(is_source)
    def _():
        e_all[pl.ds(pl.multiple_of(me * 128, 128), 128), :] = e_ref[3 * (z % 2) + main]
        notes[me] = note[...]

    pl.semaphore_wait(barrier, jnp.where(is_source, 15, 16) + 15 + 3 + 1)

    def a_copy(k):
        return pltpu.make_async_remote_copy(
            block, params_ref.at[dp * 16 + me], a_send.at[k], a_recv.at[k], device_id=(dp, (me + k) % 16), device_id_type=MESH
        )

    def b_copy(k):
        mine = params_ref.at[pl.ds(dp * 16, 16)]
        return pltpu.make_async_remote_copy(
            mine, mine, b_send.at[k], b_recv.at[k], device_id=(2 * ((x + k) % 4) + core, me), device_id_type=MESH
        )

    def c_copy(k):
        mine = params_ref.at[pl.ds((2 * ((x + k) % 4) + core) * 16, 16)]
        return pltpu.make_async_remote_copy(mine, mine, c_send.at[k], c_recv.at[k], device_id=sibling, device_id_type=MESH)

    def a_start(k, _):
        a_copy(k).start()
        return 0

    def a_wait(k, _):
        a_copy(k).wait()
        return 0

    def e_copy(d, noted):
        zd, yd, cd = 2 * core + d // 8, d // 2 % 4, d % 2
        where = dict(device_id=(2 * x + cd, 4 * zd + yd), device_id_type=MESH)
        if noted:
            return pltpu.make_async_remote_copy(note, notes.at[me], n_send.at[d], n_recv.at[me], **where)
        row = 3 * (d // 8) + (3 * (2 * yd + cd) + 1) // 8
        here = pl.ds(pl.multiple_of(me * 128, 128), 128)
        return pltpu.make_async_remote_copy(e_ref.at[row], e_all.at[here], e_send.at[d], e_recv.at[me], **where)

    def is_other(d):
        return jnp.logical_not((2 * core + d // 8 == z) & (d // 2 % 4 == y) & (d % 2 == core))

    def e_start(n, _):
        d = (n + me) % 16

        @pl.when(is_other(d))
        def _():
            e_copy(d, False).start()

        return 0

    def n_start(n, _):
        d = (n + me) % 16

        @pl.when(is_other(d))
        def _():
            e_copy(d, True).start()

        return 0

    lax.fori_loop(1, 16, a_start, 0)
    lax.fori_loop(0, 16, e_start, 0)
    lax.fori_loop(0, 16, n_start, 0)

    def e_sent(d, _):
        @pl.when(is_other(d))
        def _():
            e_copy(d, False).wait_send()
            e_copy(d, True).wait_send()

        return 0

    def e_arrived(f, _):
        @pl.when(jnp.logical_not(is_source & (f == me)))
        def _():
            where = dict(device_id=(source_dp, f), device_id_type=MESH)
            there = pl.ds(pl.multiple_of(f * 128, 128), 128)
            pltpu.make_async_remote_copy(e_ref.at[0], e_all.at[there], e_send.at[0], e_recv.at[f], **where).wait_recv()

        return 0

    def n_arrived(f, _):
        @pl.when(jnp.logical_not(is_source & (f == me)))
        def _():
            where = dict(device_id=(source_dp, f), device_id_type=MESH)
            pltpu.make_async_remote_copy(note, notes.at[f], n_send.at[0], n_recv.at[f], **where).wait_recv()

        return 0

    gives = ((y == 1) & (core == 1)) | ((y == 2) & (core == 0))
    takes = has_two()
    main_slot = jnp.where(i == 5, 1, 0)
    his_slot = jnp.where(y == 1, 1, 0)

    made = ((emb_t, emb_hbm), (k_t, k_hbm), (vt_t, vt_hbm))

    def target(n, slot, t):
        rows = pl.ds(pl.multiple_of(slot * SEQ + t * PT, PT), PT)
        return made[n][1].at[:, rows] if n == 2 else made[n][1].at[rows]

    def out_copy(n, t):
        return pltpu.make_async_copy(made[n][0].at[t % 2], target(n, main_slot, t), out.at[n, t % 2])

    def give_copy(n, t):
        return pltpu.make_async_remote_copy(
            made[n][0].at[t % 2], target(n, his_slot, t), s_send.at[n, t], s_recv.at[n, t],
            device_id=sibling, device_id_type=MESH,
        )

    def settle(t, parts):
        for n in parts:
            out_copy(n, t).wait()

        @pl.when(gives)
        def _():
            for n in parts:
                give_copy(n, t).wait_send()

    per = SEQ // PT
    row = lax.broadcasted_iota(jnp.int32, (PT, 1), 0)
    lax.fori_loop(1, 16, a_wait, 0)
    for k in range(1, 4):
        b_copy(k).start()
    c_copy(0).start()
    for t in range(TILES):
        b = t % 2
        lax.fori_loop(4 * t + (1 if t else 0), min(4 * t + 5, 16), e_arrived, 0)
        if t == 0:
            n_arrived(0, 0)
            loads[0].wait()
            split = jnp.sum(jnp.where(lane == 3 * (z % 2) + main, notes[0, 6:7, :], 0), keepdims=True)
        mid = e_all[t * PT : t * PT + PT, :]
        if t:
            before = e_all[t * PT - 16 : t * PT, :].astype(F32)[15:16]
        else:
            before = jnp.zeros((1, 128), F32)
        if t < TILES - 1:
            after = e_all[t * PT + PT : t * PT + PT + 16, :].astype(F32)[0:1]
        else:
            after = jnp.zeros((1, 128), F32)
        broad = mid.astype(F32)
        left = jnp.where(row == 0, before, pltpu.roll(broad, 1, 0)).astype(BF16)
        right = jnp.where(row == PT - 1, after, pltpu.roll(broad, PT - 1, 0)).astype(BF16)
        trigram = jnp.concatenate([left, mid, right], 1)
        typed = jnp.where(row + t * PT >= split, types_ref[1:2, :], types_ref[0:1, :])
        emb = (dot(trigram, proj_ref[...]) + line(ebias_ref, 0, 4) + typed).astype(BF16)
        if t == 0:
            loads[1].wait()
        hidden = (dot(emb, win_ref[...]) + line(bias_ref, 0, 8)).astype(BF16)
        if t == 0:
            loads[2].wait()
        keys = (dot(hidden, wqkv_ref[:, D_T : 2 * D_T]) + line(bias_ref, 16, 8)).astype(BF16)
        values = (dot(hidden, wqkv_ref[:, 2 * D_T :]) + line(bias_ref, 24, 8)).astype(BF16)
        if t >= 2:
            settle(t - 2, range(3))
        emb_t[b] = emb
        k_t[b] = keys
        vt_t[b] = values.T
        for n in range(3):
            out_copy(n, t).start()

        @pl.when(gives)
        def _(t=t):
            for n in range(3):
                give_copy(n, t).start()


        if t == C_TILE:
            for k in range(1, 4):
                b_copy(k).wait()
                c_copy(4 - k).start()
    for t in range(TILES - 2, TILES):
        settle(t, [0])

    def arrive(n):
        @pl.when(takes)
        def _():
            for t in range(TILES):
                give_copy(n, t).wait_recv()

    arrive(0)
    own = pltpu.make_async_copy(emb_hbm.at[pl.ds(pl.multiple_of(first_block() * QB, QB), OWN)], own_ref, own_sem)
    own.start()
    lax.fori_loop(1, 16, n_arrived, 0)
    for j in range(3):
        t = first_block() + j
        local = 3 * (z % 2) + (3 * i + j) // 8
        for half in range(2):
            weight_ref[j, :, half * 128 : half * 128 + 128] = notes[2 * (t % 8) + half, pl.ds(local, 1), :].astype(F32)
    own.wait()
    finals = [
        pltpu.make_async_copy(ref, hbm, last_sem.at[n])
        for n, (ref, hbm) in enumerate([(own_ref, own_hbm), (hid_ref, hid_hbm), (params_ref, params_hbm)])
    ]
    finals[0].start()
    hidden = dot(own_ref[...], win_ref[...]) + line(bias_ref, 0, 8)
    hid_ref[...] = hidden
    finals[1].start()
    for k in range(4):
        c_copy(k).wait()
    finals[2].start()
    queries = (dot(hidden.astype(BF16), wqkv_ref[:, :D_T]) + line(bias_ref, 8, 8)).astype(BF16)
    tq_ref[...] = queries * jnp.asarray(HEAD_T**-0.5, BF16)
    lax.fori_loop(0, 16, e_sent, 0)
    for t in range(TILES - 2, TILES):
        settle(t, [1, 2])
    arrive(1)
    arrive(2)
    for copy in finals:
        copy.wait()


def front(ids, table, table_end, mask, splits, mats, vecs, proj, win, wqkv, ebias, types, bias):
    vmem = pl.BlockSpec(memory_space=pltpu.VMEM)
    hbm = pl.BlockSpec(memory_space=pl.ANY)
    smem = pl.BlockSpec(memory_space=pltpu.SMEM)
    tail = pl.BlockSpec((16, 128), lambda _: (WHOLE // 16, 0))
    dma = pltpu.SemaphoreType.DMA
    return pl.pallas_call(
        front_kernel,
        grid=(1,),
        in_specs=[smem, hbm, tail, vmem, smem, vmem, vmem, hbm, hbm, hbm, vmem, vmem, vmem],
        out_specs=[hbm, hbm, hbm, hbm, hbm, vmem, vmem, hbm],
        out_shape=[
            jax.ShapeDtypeStruct((SLOTS, D_E), BF16),
            jax.ShapeDtypeStruct((SLOTS, D_T), BF16),
            jax.ShapeDtypeStruct((D_T, SLOTS), BF16),
            jax.ShapeDtypeStruct((OWN, D_E), BF16),
            jax.ShapeDtypeStruct((OWN, D_T), F32),
            jax.ShapeDtypeStruct((OWN, D_T), BF16),
            jax.ShapeDtypeStruct((3, 1, QB), F32),
            jax.ShapeDtypeStruct((128, BLOCK, 128), BF16),
        ],
        scratch_shapes=[
            pltpu.VMEM((OWN, D_E), BF16),
            pltpu.VMEM((OWN, D_T), F32),
            pltpu.VMEM((128, BLOCK, 128), BF16),
            pltpu.VMEM((WHOLE, 128), BF16),
            pltpu.VMEM((WHOLE + 16, 128), F32),
            pltpu.VMEM((OWN, 128), F32),
            pltpu.VMEM((6, 128, 128), BF16),
            pltpu.VMEM((8, 128), jnp.int32),
            pltpu.VMEM((16, 8, 128), jnp.int32),
            pltpu.VMEM((BLOCK, 128), F32),
            pltpu.VMEM((BLOCK, 128), BF16),
            pltpu.VMEM((SEQ, 128), BF16),
            pltpu.VMEM((3 * 128, D_E), BF16),
            pltpu.VMEM((D_E, D_T), BF16),
            pltpu.VMEM((D_T, 3 * D_T), BF16),
            pltpu.VMEM((2, PT, D_E), BF16),
            pltpu.VMEM((2, PT, D_T), BF16),
            pltpu.VMEM((2, D_T, PT), BF16),
            dma((-(-WHOLE // CHUNK),)),
            dma((3,)),
            dma((16,)),
            dma((16,)),
            dma((16,)),
            dma((16,)),
            dma((16,)),
            dma((16,)),
            dma((4,)),
            dma((4,)),
            dma((4,)),
            dma((4,)),
            dma((3, 2)),
            dma((3, TILES)),
            dma((3, TILES)),
            dma,
            dma((3,)),
        ],
        compiler_params=params(58, collective_id=0, has_side_effects=True),
        name="front",
    )(ids, table, table_end, mask, splits, mats, vecs, proj, win, wqkv, ebias, types, bias)


def unpack_rows(pairs, packed_ref, flat):
    for pair in pairs:
        both = [packed_ref[2 * pair + i].astype(F32)[:SHARD] for i in range(2)]
        flat[88 * pair : 88 * pair + 88, :] = jnp.concatenate(both, 0)


def unpack_vectors(packed_ref, vec_ref):
    lane = lax.broadcasted_iota(jnp.int32, (1, 128), 1)
    rows = [jnp.zeros((1, 128), F32)] * 48
    for owner in range(128):
        row, shift = divmod(47 * owner, 128)
        entries = packed_ref[owner].astype(F32)[SHARD : SHARD + 1, :]
        moved = pltpu.roll(entries, shift, 1) if shift else entries
        if shift + 47 > 128:
            rows[row] = jnp.where(lane >= shift, moved, rows[row])
            rows[row + 1] = jnp.where(lane < shift + 47 - 128, moved, rows[row + 1])
        else:
            rows[row] = jnp.where((lane >= shift) & (lane < shift + 47), moved, rows[row])
    for row in range(48):
        vec_ref[row : row + 1, :] = rows[row]


ST = 1024


def student_in_kernel(emb_hbm, packed_hbm, first_ref, sq_ref, sk_ref, sv_ref, skt_ref, svt_ref,
                      win_ref, wqkv_ref, watt_ref, wup_ref, wdown_ref, wout_ref, vec_ref, flat, emb_parts, packed_ref, sems):
    t = pl.program_id(0)
    packed_load = pltpu.make_async_copy(packed_hbm, packed_ref, sems.at[SLOTS // ST])

    def emb_load(n):
        return pltpu.make_async_copy(emb_hbm.at[n * ST : n * ST + ST], emb_parts.at[n], sems.at[n])

    @pl.when(t == 0)
    def _():
        packed_load.start()
        for n in range(SLOTS // ST):
            emb_load(n).start()
        packed_load.wait()
        unpack_vectors(packed_ref, vec_ref)
        unpack_rows(range(12), packed_ref, flat)
        win_ref[...] = flat[0:512, :].astype(BF16)
        for n in range(3):
            wqkv_ref[:, n * 128 : n * 128 + 128] = flat[pl.ds(512 + n, 128, stride=3), :].astype(BF16)
        watt_ref[...] = flat[896:1024, :].astype(BF16)

    for step in range(SLOTS // ST):

        @pl.when(t == step)
        def _(step=step):
            emb_load(step).wait()
            student_tile(t, emb_parts.at[step], win_ref, wqkv_ref, vec_ref, first_ref, sq_ref, sk_ref, sv_ref, skt_ref, svt_ref)
            unpack_rows(range(12 + 13 * step, 12 + 13 * (step + 1)), packed_ref, flat)
            if step == 1:
                for i in range(FFN_COUNT):
                    for n in range(4):
                        part = flat[pl.ds(1024 + 512 * i + n, 128, stride=4), :]
                        wup_ref[i, :, n * 128 : n * 128 + 128] = part.astype(BF16)
            if step == 3:
                for i in range(FFN_COUNT):
                    wdown_ref[i] = flat[3072 + 512 * i : 3584 + 512 * i, :].astype(BF16)
                for n in range(4):
                    wout_ref[:, n * 128 : n * 128 + 128] = flat[pl.ds(5120 + n, 128, stride=4), :].astype(BF16)


def student_tile(t, emb_ref, win_ref, wqkv_ref, vec_ref, first_ref, sq_ref, sk_ref, sv_ref, skt_ref, svt_ref):
    emb = emb_ref[...]
    emb = jnp.where((t < SEQ // ST) | has_two(), emb, jnp.zeros_like(emb))
    first = (dot(emb, win_ref[...]) + line(vec_ref, V_IN)).astype(BF16)
    first_ref[...] = first
    qkv = dot(first, wqkv_ref[...])
    sq_ref[...] = (qkv[:, :D_S] + line(vec_ref, V_QKV)).astype(BF16)
    s_keys = (qkv[:, D_S : 2 * D_S] + line(vec_ref, V_QKV + 1)).astype(BF16)
    s_values = (qkv[:, 2 * D_S :] + line(vec_ref, V_QKV + 2)).astype(BF16)
    sk_ref[...] = s_keys
    sv_ref[...] = s_values
    skt_ref[...] = s_keys.T
    svt_ref[...] = s_values.T


def student_in(emb, packed):
    tall = jax.ShapeDtypeStruct((SLOTS, D_S), BF16)
    flat = jax.ShapeDtypeStruct((D_S, SLOTS), BF16)
    down = pl.BlockSpec((ST, D_S), lambda t: (t, 0))
    across = pl.BlockSpec((D_S, ST), lambda t: (0, t))
    made = [
        ((D_E, D_S), BF16),
        ((D_S, 3 * D_S), BF16),
        ((D_S, D_S), BF16),
        ((FFN_COUNT, D_S, FF_S), BF16),
        ((FFN_COUNT, FF_S, D_S), BF16),
        ((D_S, D_E), BF16),
        ((48, 128), F32),
    ]
    return pl.pallas_call(
        student_in_kernel,
        grid=(SLOTS // ST,),
        in_specs=[pl.BlockSpec(memory_space=pl.ANY)] * 2,
        out_specs=[down] * 4 + [across] * 2 + [whole(*shape) for shape, _ in made],
        out_shape=[tall] * 4 + [flat] * 2 + [jax.ShapeDtypeStruct(*entry) for entry in made],
        scratch_shapes=[
            pltpu.VMEM((5632, 128), F32),
            pltpu.VMEM((SLOTS // ST, ST, D_E), BF16),
            pltpu.VMEM((128, BLOCK, 128), BF16),
            pltpu.SemaphoreType.DMA((SLOTS // ST + 1,)),
        ],
        compiler_params=params(46),
        name="student_in",
    )(emb, packed)


CB = 256
SUB = 64
STEPS = 3 * HEADS


def head_lanes(values, head):
    lane = lax.broadcasted_iota(jnp.int32, (1, D_S), 1)
    return jnp.where(lane // HEAD_S == head, values, jnp.zeros_like(values))


def attend_kernel(tq_ref, tk_ref, tvt_ref, sq_ref, sk_ref, svt_ref, skt_ref, et_ref, es_ref, tmix_ref, smix_ref, stat_ref,
                  ts0, ts1, ss0, ss1, mx0, mx1, sqt0, sqt1):
    n = pl.program_id(0)
    s_factor = HEAD_S**-0.5 * LOG2E

    def work(ts, ss, mx, sqt, tr, sr, mr, sqr, scores, mixes):
        if scores:
            queries, s_queries = tq_ref[...], head_lanes(sq_ref[...], n // 3)
            tall = s_queries.astype(F32).T
            sqt[...] = sum(tall[h * HEAD_S : (h + 1) * HEAD_S] for h in range(HEADS))
            t_max = s_max = jnp.full((8, QB), -jnp.inf, F32)
        if mixes:
            t_top, s_top = jnp.max(mr[0], 0, keepdims=True), jnp.max(mr[1], 0, keepdims=True)
            t_off, s_off = t_top * LOG2E, s_top * s_factor
            entropy = jnp.zeros((8, QB), F32)
            ones = jnp.ones((16, CB), BF16)
            t_mix = jnp.zeros((HEAD_T + HEAD_S + 16, QB), F32)
            s_mix = jnp.zeros((HEAD_S + 16, QB), F32)
        for c in range(SEQ // CB):
            part = slice(c * CB, c * CB + CB)
            if scores:
                t_part = dot_nt(tk_ref[part, :], queries)
                ts[part, :] = t_part
                s_part = dot_nt(sk_ref[part, :], s_queries)
                ss[part, :] = s_part
                t_max = jnp.maximum(t_max, fold(t_part, jnp.max))
                s_max = jnp.maximum(s_max, fold(s_part, jnp.max))
            if mixes:
                for u in range(c * CB, c * CB + CB, SUB):
                    some = slice(u, u + SUB)
                    t_log = tr[some, :] * LOG2E - t_off
                    t_exp = jnp.exp2(t_log)
                    et_ref[0, some, :] = t_exp.astype(BF16)
                    es_ref[0, some, :] = jnp.exp2(sr[some, :] * s_factor - s_off).astype(BF16)
                    entropy = entropy + fold(t_exp * t_log)
                t_mix += dot(jnp.concatenate([tvt_ref[:, part], skt_ref[:, part], ones], 0), et_ref[0, part, :])
                s_mix += dot(jnp.concatenate([svt_ref[:, part], ones], 0), es_ref[0, part, :])
        if scores:
            mx[0], mx[1] = t_max, s_max
        if mixes:
            t_sum, s_sum = t_mix[HEAD_T + HEAD_S : HEAD_T + HEAD_S + 1], s_mix[HEAD_S : HEAD_S + 1]
            t_inv, s_inv = 1.0 / t_sum, 1.0 / s_sum
            cross = jnp.sum(sqr[...] * t_mix[HEAD_T : HEAD_T + HEAD_S], 0, keepdims=True) * s_factor - s_off * t_sum
            kl = (jnp.sum(entropy, 0, keepdims=True) - cross) * t_inv * (1.0 / LOG2E)
            stat_ref[0, 0, 0:1, :] = t_inv
            stat_ref[0, 0, 1:2, :] = s_inv
            stat_ref[0, 0, 2:3, :] = kl - jnp.log(t_sum) + jnp.log(s_sum)
            stat_ref[0, 0, 3:8, :] = jnp.zeros((5, QB), F32)
            tmix_ref[...] = (t_mix[:HEAD_T] * t_inv).T.astype(BF16)
            smix_ref[0] = s_mix[:HEAD_S] * s_inv

    even, odd = (ts0, ss0, mx0, sqt0), (ts1, ss1, mx1, sqt1)
    pl.when(n == 0)(lambda: work(*even, *odd, True, False))
    pl.when((n > 0) & (n < STEPS) & (n % 2 == 0))(lambda: work(*even, *odd, True, True))
    pl.when((n > 0) & (n < STEPS) & (n % 2 == 1))(lambda: work(*odd, *even, True, True))
    pl.when(n == STEPS)(lambda: work(*even, *odd, False, True))


def attend(tq, tk, tvt, sq, sk, svt, skt):
    now = lambda n: jnp.minimum(n, STEPS - 1)
    last = lambda n: jnp.maximum(n - 1, 0)
    block = lambda n: n % 3
    head = lambda n: n // 3
    return pl.pallas_call(
        attend_kernel,
        grid=(STEPS + 1,),
        in_specs=[
            pl.BlockSpec((QB, HEAD_T), lambda n: (block(now(n)), head(now(n)))),
            pl.BlockSpec((SEQ, HEAD_T), lambda n: (slot_of(block(now(n))), head(now(n)))),
            pl.BlockSpec((HEAD_T, SEQ), lambda n: (head(last(n)), slot_of(block(last(n))))),
            pl.BlockSpec((QB, D_S), lambda n: (first_block() + block(now(n)), 0)),
            pl.BlockSpec((SEQ, D_S), lambda n: (slot_of(block(now(n))), 0)),
            pl.BlockSpec((HEAD_S, SEQ), lambda n: (head(last(n)), slot_of(block(last(n))))),
            pl.BlockSpec((HEAD_S, SEQ), lambda n: (head(last(n)), slot_of(block(last(n))))),
        ],
        out_specs=[
            pl.BlockSpec((1, SEQ, QB), lambda n: (block(last(n)), 0, head(last(n)))),
            pl.BlockSpec((1, SEQ, QB), lambda n: (block(last(n)), 0, head(last(n)))),
            pl.BlockSpec((QB, HEAD_T), lambda n: (block(last(n)), head(last(n)))),
            pl.BlockSpec((1, HEAD_S, QB), lambda n: (block(last(n)), head(last(n)), 0)),
            pl.BlockSpec((1, 1, 8, QB), lambda n: (block(last(n)), head(last(n)), 0, 0)),
        ],
        out_shape=[
            jax.ShapeDtypeStruct((3, SEQ, HEADS * QB), BF16),
            jax.ShapeDtypeStruct((3, SEQ, HEADS * QB), BF16),
            jax.ShapeDtypeStruct((OWN, D_T), BF16),
            jax.ShapeDtypeStruct((3, D_S, QB), F32),
            jax.ShapeDtypeStruct((3, HEADS, 8, QB), F32),
        ],
        scratch_shapes=[pltpu.VMEM((SEQ, QB), F32)] * 4 + [pltpu.VMEM((2, 8, QB), F32)] * 2 + [pltpu.VMEM((HEAD_S, QB), F32)] * 2,
        compiler_params=params(40),
        name="attend",
    )(tq, tk, tvt, sq, sk, svt, skt)


FC = 1024


def teacher_kernel(mix_ref, hid_ref, emb_ref, att_ref, up_hbm, down_hbm, out_ref, bias_ref, gain_ref, shift_ref, target_ref,
                   norm, low, acc, up_parts, down_parts, sems):
    c = pl.program_id(0)

    def loads(part):
        here = pl.ds(pl.multiple_of(part * FC, FC), FC)
        slot = part % 2
        return (
            pltpu.make_async_copy(up_hbm.at[:, here], up_parts.at[slot], sems.at[0, slot]),
            pltpu.make_async_copy(down_hbm.at[here], down_parts.at[slot], sems.at[1, slot]),
        )

    @pl.when(c == 0)
    def _():
        for copy in loads(0):
            copy.start()

    @pl.when(c < pl.num_programs(0) - 1)
    def _():
        for copy in loads(c + 1):
            copy.start()


    @pl.when(c == 0)
    def _():
        summed = hid_ref[...] + dot(mix_ref[...], att_ref[...]) + line(bias_ref, 32, 8)
        one = layer_norm(summed, line(gain_ref, 0, 8), line(shift_ref, 0, 8))
        norm[...] = one
        low[...] = one.astype(BF16)

    up_load, down_load = loads(c)
    up_load.wait()
    rows = FC // 128
    up_bias = bias_ref[pl.ds(pl.multiple_of(40 + rows * c, 8), rows), :]
    act = gelu(dot(low[...], up_parts[c % 2]) + line(up_bias, 0, rows)).astype(BF16)
    down_load.wait()
    part = dot(act, down_parts[c % 2])

    @pl.when(c == 0)
    def _():
        acc[...] = part

    @pl.when(c > 0)
    def _():
        acc[...] += part

    @pl.when(c == pl.num_programs(0) - 1)
    def _():
        summed = norm[...] + acc[...] + line(bias_ref, 72, 8)
        two = layer_norm(summed, line(gain_ref, 8, 8), line(shift_ref, 8, 8))
        last = emb_ref[...].astype(F32) + dot(two.astype(BF16), out_ref[...]) + line(bias_ref, 80, 4)
        target_ref[...] = layer_norm(last, line(gain_ref, 16, 4), line(shift_ref, 16, 4))


def teacher(mix, hid, emb, att, up, down, out, bias, gain, shift):
    return pl.pallas_call(
        teacher_kernel,
        grid=(FF_T // FC,),
        in_specs=[
            whole(OWN, D_T),
            whole(OWN, D_T),
            whole(OWN, D_E),
            whole(D_T, D_T),
            pl.BlockSpec(memory_space=pl.ANY),
            pl.BlockSpec(memory_space=pl.ANY),
            whole(D_T, D_E),
            whole(84, 128),
            whole(20, 128),
            whole(20, 128),
        ],
        out_specs=whole(OWN, D_E),
        out_shape=jax.ShapeDtypeStruct((OWN, D_E), F32),
        scratch_shapes=[
            pltpu.VMEM((OWN, D_T), F32),
            pltpu.VMEM((OWN, D_T), BF16),
            pltpu.VMEM((OWN, D_T), F32),
            pltpu.VMEM((2, D_T, FC), BF16),
            pltpu.VMEM((2, FC, D_T), BF16),
            pltpu.SemaphoreType.DMA((2, 2)),
        ],
        compiler_params=params(40),
        name="teacher",
    )(mix, hid, emb, att, up, down, out, bias, gain, shift)


def student_kernel(emb_ref, smix_ref, target_ref, weight_ref, win_ref, watt_ref, wup_ref, wdown_ref, wout_ref, vec_ref,
                   grad_ref, vgrad_ref, dsum_ref, dmix_ref, part_ref, states, slopes, outers, acts):

    def put(r, value):
        for i in range(value.shape[1] // 128):
            vgrad_ref[r + i : r + i + 1, :] = value[:, i * 128 : i * 128 + 128]

    total = lambda v: jnp.sum(v.astype(F32), 0, keepdims=True)
    emb = emb_ref[...]
    source = emb.astype(F32)
    first = dot(emb, win_ref[...]) + line(vec_ref, V_IN)
    mixed = jnp.concatenate([smix_ref[j].T for j in range(3)], 0).astype(BF16)
    branch = dot(mixed, watt_ref[...]) + line(vec_ref, V_ATT)
    state = line(vec_ref, V_AGAIN) * (first + branch) + line(vec_ref, V_ASHIFT)
    for i in range(FFN_COUNT):
        states[i] = state
        inner = dot(state.astype(BF16), wup_ref[i]) + line(vec_ref, V_UP + 4 * i, 4)
        half = 0.5 * (1.0 + lax.erf(inner * 0.7071067811865476))
        slopes[i] = half + inner * jnp.exp(-0.5 * inner * inner) * 0.3989422804014327
        act = (inner * half).astype(BF16)
        acts[i] = act
        pre = state + dot(act, wdown_ref[i]) + line(vec_ref, V_DOWN + i)
        outers[i] = pre
        state = line(vec_ref, V_FGAIN + i) * pre + line(vec_ref, V_FSHIFT + i)
    state_low = state.astype(BF16)
    summed = source + dot(state_low, wout_ref[...]) + line(vec_ref, V_OUT, 4)
    diff = line(vec_ref, V_OGAIN, 4) * summed + line(vec_ref, V_OSHIFT, 4) - target_ref[...]
    weight = jnp.concatenate([jnp.broadcast_to(weight_ref[j], (8, QB)).T[:, 0:1] for j in range(3)], 0)
    loss = jnp.sum(weight * jnp.sum(diff * diff, 1, keepdims=True)) * (1.0 / D_E)
    count = jnp.sum(weight)
    d_result = (weight * (2.0 / D_E)) * diff
    put(V_OGAIN, total(d_result * summed))
    put(V_OSHIFT, total(d_result))
    d_output = (d_result * line(vec_ref, V_OGAIN, 4)).astype(BF16)
    out_g = dot_tn(state_low, d_output)
    for n in range(4):
        grad_ref[pl.ds(4224 + n, 128, stride=4), :] = out_g[:, n * 128 : n * 128 + 128]
    put(V_OUT, total(d_output))
    d_state = dot_nt(d_output, wout_ref[...])
    for i in reversed(range(FFN_COUNT)):
        put(V_FGAIN + i, total(d_state * outers[i]))
        put(V_FSHIFT + i, total(d_state))
        d_sum = d_state * line(vec_ref, V_FGAIN + i)
        d_outer = d_sum.astype(BF16)
        grad_ref[2176 + 512 * i : 2176 + 512 * (i + 1), :] = dot_tn(acts[i], d_outer)
        d_inner = (dot_nt(d_outer, wdown_ref[i]) * slopes[i]).astype(BF16)
        up_g = dot_tn(states[i].astype(BF16), d_inner)
        for n in range(4):
            grad_ref[pl.ds(128 + 512 * i + n, 128, stride=4), :] = up_g[:, n * 128 : n * 128 + 128]
        put(V_UP + 4 * i, total(d_inner))
        put(V_DOWN + i, total(d_outer))
        d_state = d_sum + dot_nt(d_inner, wup_ref[i])
    put(V_AGAIN, total(d_state * (first + branch)))
    put(V_ASHIFT, total(d_state))
    d_sum = d_state * line(vec_ref, V_AGAIN)
    d_branch = d_sum.astype(BF16)
    grad_ref[0:128, :] = dot_tn(mixed, d_branch)
    put(V_ATT, total(d_branch))
    dsum_ref[...] = d_sum
    dmix_ref[...] = dot_nt(d_branch, watt_ref[...]).astype(BF16)
    for r in (0, 1, 2, 3, 47):
        vgrad_ref[r : r + 1, :] = jnp.zeros((1, 128), F32)
    row = lax.broadcasted_iota(jnp.int32, (8, 128), 0)
    lane = lax.broadcasted_iota(jnp.int32, (8, 128), 1)
    part_ref[...] = jnp.where((row == 0) & (lane == 0), loss, 0.0) + jnp.where((row == 0) & (lane == 1), count, 0.0)


def student(emb, smix, target, weight, win, watt, wup, wdown, wout, vecs):
    return pl.pallas_call(
        student_kernel,
        grid=(1,),
        in_specs=[
            whole(OWN, D_E),
            whole(3, D_S, QB),
            whole(OWN, D_E),
            whole(3, 1, QB),
            whole(D_E, D_S),
            whole(D_S, D_S),
            whole(FFN_COUNT, D_S, FF_S),
            whole(FFN_COUNT, FF_S, D_S),
            whole(D_S, D_E),
            whole(48, 128),
        ],
        out_specs=[whole(4736, 128), whole(48, 128), whole(OWN, D_S), whole(OWN, D_S), whole(8, 128)],
        out_shape=[
            jax.ShapeDtypeStruct((4736, 128), F32),
            jax.ShapeDtypeStruct((48, 128), F32),
            jax.ShapeDtypeStruct((OWN, D_S), F32),
            jax.ShapeDtypeStruct((OWN, D_S), BF16),
            jax.ShapeDtypeStruct((8, 128), F32),
        ],
        scratch_shapes=[
            pltpu.VMEM((FFN_COUNT, OWN, D_S), F32),
            pltpu.VMEM((FFN_COUNT, OWN, FF_S), F32),
            pltpu.VMEM((FFN_COUNT, OWN, D_S), F32),
            pltpu.VMEM((FFN_COUNT, OWN, FF_S), BF16),
        ],
        compiler_params=params(40),
        name="student",
    )(emb, smix, target, weight, win, watt, wup, wdown, wout, vecs)


KB = 1024


def back_kernel(et_ref, es_ref, stat_ref, smix_ref, dmix_ref, weight_ref, sq_ref, sv_ref, skt_ref, dsum_ref, emb_hbm, first_ref,
                wqkv_ref, vgrad_ref, part_in, late_ref, *rest):
    state_refs, rest = rest[:6], rest[6:]
    made_ref, rest = rest[0], rest[1:]
    (dkv, dqt, ds, dq, dfirst, dmt, dmz, sqd, rows, flat, vecs, kls, block_ref, emb_ref, sem, emb_sem), buffers = rest[:16], rest[16:]
    j, kb = pl.program_id(0), pl.program_id(1)
    s_scale = HEAD_S**-0.5
    late = pltpu.make_async_copy(late_ref, flat.at[896:5632], sem)
    emb_load = pltpu.make_async_copy(emb_hbm, emb_ref, emb_sem)

    @pl.when((j == 0) & (kb == 0))
    def _():
        greet()
        late.start()
        emb_load.start()
        vecs[...] = vgrad_ref[...]
        dkv[...] = jnp.zeros_like(dkv)
        kls[...] = jnp.zeros_like(kls)

    @pl.when((j == 0) & (kb == 1))
    def _():
        late.wait()
        pack_blocks(range(FIRST_EARLY // 2, 64), flat, vecs, block_ref)
        swap_early(block_ref, buffers)

    @pl.when((j == 1) & (kb == 0))
    def _():
        send_early(block_ref, buffers)

    @pl.when(kb == 0)
    def _():
        quarter = weight_ref[0] * (1.0 / HEADS)
        wide = dmix_ref[...].astype(F32)
        tall = wide.T
        place = lax.broadcasted_iota(jnp.int32, (D_S, 1), 0) // HEAD_S
        for h in range(HEADS):
            own = slice(h * HEAD_S, h * HEAD_S + HEAD_S)
            mine = slice(h * QB, h * QB + QB)
            t_inv, s_inv = stat_ref[0, h, 0:1, :], stat_ref[0, h, 1:2, :]
            kls[0:1, :] += quarter * stat_ref[0, h, 2:3, :]
            row_dot = jnp.sum(tall[own] * smix_ref[0, own, :], 0, keepdims=True)
            rows[h, 0:1, :] = row_dot - quarter
            rows[h, 1:2, :] = s_inv
            rows[h, 2:3, :] = quarter * t_inv
            dmt[h] = jnp.where(place == h, tall, 0.0).astype(BF16)
            dmz[mine, :] = head_lanes(wide * stat_ref[0, h].T[:, 1:2], h).astype(BF16)
            sqd[mine, :] = head_lanes(sq_ref[...], h)
        dqt[...] = jnp.zeros_like(dqt)

    here = pl.ds(pl.multiple_of(slot_of(j) * SEQ + kb * KB, KB), KB)
    dkv[here, D_S:] += dot(es_ref[0], dmz[...])
    for h in range(HEADS):
        lanes = slice(h * QB, h * QB + QB)
        for c in range(KB // 256):
            part = slice(c * 256, c * 256 + 256)
            d_probs = dot(sv_ref[part, :], dmt[h])
            s_exp, t_exp = es_ref[0, part, lanes].astype(F32), et_ref[0, part, lanes].astype(F32)
            d_scores = (d_probs - rows[h, 0:1, :]) * rows[h, 1:2, :] * s_exp - t_exp * rows[h, 2:3, :]
            ds[part, lanes] = d_scores.astype(BF16)
        own = slice(h * HEAD_S, h * HEAD_S + HEAD_S)
        dqt[own, :] += dot(skt_ref[own, :], ds[:, lanes])
    dkv[here, :D_S] += dot(ds[...], sqd[...])

    @pl.when(kb == pl.num_programs(1) - 1)
    def _():
        dq[pl.ds(pl.multiple_of(j * QB, QB), QB), :] = (dqt[...] * s_scale).T

    @pl.when((j == 2) & (kb == pl.num_programs(1) - 1))
    def _():
        qkv_w = wqkv_ref[...]
        dq_low = dq[...].astype(BF16)
        own = pl.ds(pl.multiple_of(first_block() * QB, QB), OWN)
        q_grad = dot_tn(first_ref[own, :], dq_low)
        own_part = dsum_ref[...] + dot_nt(dq_low, qkv_w[:, :D_S])
        kv_grad = jnp.zeros((D_S, 2 * D_S), F32)
        kv_bias = jnp.zeros((1, 2 * D_S), F32)
        for c in range(8):
            part = pl.ds(c * 512, 512)
            wide = dkv[part, :]
            low = jnp.concatenate([(wide[:, :D_S] * s_scale).astype(BF16), wide[:, D_S:].astype(BF16)], 1)
            kv_grad += dot_tn(first_ref[part, :], low)
            kv_bias += jnp.sum(low.astype(F32), 0, keepdims=True)
            dfirst[part, :] = dot_nt(low, qkv_w[:, D_S:])
        dfirst[own, :] += own_part
        in_grad = jnp.zeros((D_S, D_E), F32)
        in_bias = jnp.zeros((1, D_S), F32)
        two = has_two()
        emb_load.wait()
        for c in range(8):
            part = pl.ds(c * 512, 512)
            low = dfirst[part, :].astype(BF16)
            emb = emb_ref[part, :]
            if c >= 4:
                emb = jnp.where(two, emb, jnp.zeros_like(emb))
            in_grad += dot_tn(low, emb)
            in_bias += jnp.sum(low.astype(F32), 0, keepdims=True)
        flat[0:512, :] = in_grad.T
        flat[pl.ds(512, 128, stride=3), :] = q_grad
        flat[pl.ds(513, 128, stride=3), :] = kv_grad[:, :D_S]
        flat[pl.ds(514, 128, stride=3), :] = kv_grad[:, D_S:]
        vecs[0:1, :] = in_bias
        vecs[1:2, :] = jnp.sum(dq_low.astype(F32), 0, keepdims=True)
        vecs[2:3, :] = kv_bias[:, :D_S]
        vecs[3:4, :] = kv_bias[:, D_S:]
        pack_blocks(range(FIRST_EARLY // 2), flat, vecs, block_ref)
        kl = jnp.sum(kls[0:1, :], keepdims=True)
        corner = lax.broadcasted_iota(jnp.int32, (1, 128), 1) == 0
        send_rest(block_ref, buffers)
        update(block_ref, part_in[0:1, :] + jnp.where(corner, kl, 0.0), state_refs, made_ref, buffers)


def back(et, es, stat, smix, dmix, weight, sq, sv, skt, dsum, emb, first, wqkv, vgrad, part, late, *state):
    count = SEQ // KB
    place = lambda j, k: slot_of(j) * count + k
    dma = pltpu.SemaphoreType.DMA
    return pl.pallas_call(
        back_kernel,
        grid=(3, count),
        in_specs=[
            pl.BlockSpec((1, KB, HEADS * QB), lambda j, k: (j, k, 0)),
            pl.BlockSpec((1, KB, HEADS * QB), lambda j, k: (j, k, 0)),
            pl.BlockSpec((1, HEADS, 8, QB), lambda j, k: (j, 0, 0, 0)),
            pl.BlockSpec((1, D_S, QB), lambda j, k: (j, 0, 0)),
            pl.BlockSpec((QB, D_S), lambda j, k: (j, 0)),
            pl.BlockSpec((1, 1, QB), lambda j, k: (j, 0, 0)),
            pl.BlockSpec((QB, D_S), lambda j, k: (first_block() + j, 0)),
            pl.BlockSpec((KB, D_S), lambda j, k: (place(j, k), 0)),
            pl.BlockSpec((D_S, KB), lambda j, k: (0, place(j, k))),
            whole(OWN, D_S),
            pl.BlockSpec(memory_space=pl.ANY),
            whole(SLOTS, D_S),
            whole(D_S, 3 * D_S),
            whole(48, 128),
            whole(8, 128),
            pl.BlockSpec(memory_space=pl.ANY),
        ]
        + [whole(SHARD, 128), whole(1, 47)] * 3,
        out_specs=whole(3 * BLOCK + 8, 128),
        out_shape=jax.ShapeDtypeStruct((3 * BLOCK + 8, 128), F32),
        scratch_shapes=[
            pltpu.VMEM((SLOTS, 2 * D_S), F32),
            pltpu.VMEM((D_S, QB), F32),
            pltpu.VMEM((KB, HEADS * QB), BF16),
            pltpu.VMEM((OWN, D_S), F32),
            pltpu.VMEM((SLOTS, D_S), F32),
            pltpu.VMEM((HEADS, D_S, QB), BF16),
            pltpu.VMEM((HEADS * QB, D_S), BF16),
            pltpu.VMEM((HEADS * QB, D_S), BF16),
            pltpu.VMEM((HEADS, 8, QB), F32),
            pltpu.VMEM((5632, 128), F32),
            pltpu.VMEM((48, 128), F32),
            pltpu.VMEM((8, QB), F32),
            pltpu.VMEM((4, 2, 16, BLOCK, 128), BF16),
            pltpu.VMEM((SLOTS, D_E), BF16),
            dma,
            dma,
            pltpu.VMEM((3, BLOCK, 128), F32),
            pltpu.VMEM((4, 16, BLOCK, 128), BF16),
            pltpu.VMEM((BLOCK, 128), F32),
            pltpu.VMEM((64, BLOCK, 128), BF16),
            pltpu.VMEM((64, BLOCK, 128), BF16),
            pltpu.VMEM((2, 2, 8, 128), F32),
            pltpu.VMEM((2, 16, 8, 128), F32),
            pltpu.VMEM((2, 8, 8, 128), F32),
            dma((2, 6)),
            dma((64,)),
            dma((64,)),
            dma((2, 16)),
            dma((2, 16)),
            dma((2, 8)),
            dma((2, 8)),
        ],
        compiler_params=params(44, collective_id=1, has_side_effects=True),
        name="back",
    )(et, es, stat, smix, dmix, weight, sq, sv, skt, dsum, emb, first, wqkv, vgrad, part, late, *state)


def chip(k):
    dp, fs = lax.axis_index("dp"), lax.axis_index("fsdp")
    return (2 * ((dp // 2 + k // 16) % 4) + dp % 2, (fs + k) % 16)


def greet():
    dp, fs = lax.axis_index("dp"), lax.axis_index("fsdp")
    barrier = pltpu.get_barrier_semaphore()

    def signal(k, _):
        pl.semaphore_signal(barrier, inc=1, device_id=chip(k), device_id_type=MESH)
        return 0

    lax.fori_loop(1, 64, signal, 0)
    for k in range(4):
        other = (2 * ((dp // 2 + k) % 4) + 1 - dp % 2, fs)
        pl.semaphore_signal(barrier, inc=1, device_id=other, device_id_type=MESH)


FIRST_EARLY = 22


def pack_blocks(pairs, flat, vecs, block_ref):
    lane = lax.broadcasted_iota(jnp.int32, (1, 128), 1)
    rest = jnp.zeros((BLOCK - SHARD - 1, 128), F32)
    for pair in pairs:
        both = flat[88 * pair : 88 * pair + 88, :]
        for i in range(2):
            owner = 2 * pair + i
            row, shift = divmod(47 * owner, 128)
            entries = vecs[row : row + 1, :]
            if shift + 47 > 128:
                entries = jnp.where(lane >= shift, entries, vecs[row + 1 : row + 2, :])
            if shift:
                entries = pltpu.roll(entries, 128 - shift, 1)
            entries = jnp.where(lane < 47, entries, 0.0)
            mine = both[SHARD * i : SHARD * (i + 1)]
            block_ref[owner // 32, owner // 16 % 2, owner % 16] = jnp.concatenate([mine, entries, rest], 0).astype(BF16)


SPLIT = FIRST_EARLY - 16


def swap_copy(n, g_ref, half_in, half_sems):
    dp, fs = lax.axis_index("dp"), lax.axis_index("fsdp")
    core = dp % 2
    if n in (1, 2, 3):
        source, goal = g_ref.at[n, 1 - core], half_in.at[n]
    elif n == 0:
        source, goal = g_ref.at[0, 1, 0:SPLIT], half_in.at[0, 0:SPLIT]
    elif n == 4:
        source, goal = g_ref.at[0, 1, SPLIT:16], half_in.at[0, SPLIT:16]
    else:
        source, goal = g_ref.at[0, 0], half_in.at[0]
    return pltpu.make_async_remote_copy(
        source, goal, half_sems.at[0, n], half_sems.at[1, n], device_id=(dp + 1 - 2 * core, fs), device_id_type=MESH
    )


def swap_early(g_ref, buffers):
    half_in, half_sems = buffers[1], buffers[8]
    pl.semaphore_wait(pltpu.get_barrier_semaphore(), 67)
    for n in (1, 2, 3):
        swap_copy(n, g_ref, half_in, half_sems).start()

    @pl.when(lax.axis_index("dp") % 2 == 0)
    def _():
        swap_copy(4, g_ref, half_in, half_sems).start()


def block_copy(k, buffers):
    block_out, blocks_in, block_send, block_recv = buffers[3], buffers[4], buffers[9], buffers[10]
    dp, fs = lax.axis_index("dp"), lax.axis_index("fsdp")
    place = (dp // 2 + k // 16) % 4 * 16 + (fs + k) % 16
    return pltpu.make_async_remote_copy(
        block_out.at[place], blocks_in.at[k], block_send.at[k], block_recv.at[k], device_id=chip(k), device_id_type=MESH
    )


def is_early(place):
    return (place >= 16) | ((lax.axis_index("dp") % 2 == 1) & (place >= SPLIT))


def join_and_send(early, g_ref, buffers):
    half_in, block_out = buffers[1], buffers[3]
    dp, fs = lax.axis_index("dp"), lax.axis_index("fsdp")
    core = dp % 2

    def join(i, _):
        @pl.when(is_early(i) == early)
        def _():
            summed = g_ref[i // 16, core, i % 16].astype(F32) + half_in[i // 16, i % 16].astype(F32)
            block_out[i] = summed.astype(BF16)

        return 0

    lax.fori_loop(0, 64 if early else 16, join, 0)

    def start(k, _):
        place = (dp // 2 + k // 16) % 4 * 16 + (fs + k) % 16

        @pl.when(is_early(place) == early)
        def _():
            block_copy(k, buffers).start()

        return 0

    lax.fori_loop(1, 64, start, 0)


def send_early(g_ref, buffers):
    half_in, half_sems = buffers[1], buffers[8]
    core = lax.axis_index("dp") % 2
    for n in (1, 2, 3):
        swap_copy(n, g_ref, half_in, half_sems).wait()

    @pl.when(core == 0)
    def _():
        swap_copy(4, g_ref, half_in, half_sems).wait_send()

    @pl.when(core == 1)
    def _():
        swap_copy(4, g_ref, half_in, half_sems).wait_recv()

    join_and_send(True, g_ref, buffers)


def send_rest(g_ref, buffers):
    half_in, half_sems = buffers[1], buffers[8]
    core = lax.axis_index("dp") % 2

    @pl.when(core == 0)
    def _():
        swap_copy(0, g_ref, half_in, half_sems).start()
        swap_copy(5, g_ref, half_in, half_sems).wait_recv()
        swap_copy(0, g_ref, half_in, half_sems).wait_send()

    @pl.when(core == 1)
    def _():
        swap_copy(5, g_ref, half_in, half_sems).start()
        swap_copy(0, g_ref, half_in, half_sems).wait_recv()
        swap_copy(5, g_ref, half_in, half_sems).wait_send()

    join_and_send(False, g_ref, buffers)


def update(g_ref, part, state_refs, made_ref, buffers):
    master_mat, master_vec, first_mat, first_vec, second_mat, second_vec = state_refs
    (packs, half_in, mine, block_out, blocks_in, tile_out, tiles_f, tiles_d,
     half_sems, block_send, block_recv, f_send, f_recv, d_send, d_recv) = buffers
    dp, fs = lax.axis_index("dp"), lax.axis_index("fsdp")
    x, core = dp // 2, dp % 2
    packs[...] = jnp.zeros_like(packs)
    for i, (mat, vec) in enumerate([(master_mat, master_vec), (first_mat, first_vec), (second_mat, second_vec)]):
        packs[i, 0:SHARD, :] = mat[...]
        packs[i, SHARD : SHARD + 1, 0:47] = vec[...]
    mine[...] = g_ref[x, core, fs].astype(F32) + half_in[x, fs].astype(F32)

    def gather(k, _):
        block_copy(k, buffers).wait_recv()
        mine[...] += blocks_in[k].astype(F32)
        return 0

    lax.fori_loop(1, 64, gather, 0)

    row = lax.broadcasted_iota(jnp.int32, (BLOCK, 1), 0)
    place = (dp * 16 + fs) * SHARD + row
    is_matrix = row < SHARD
    bounds = [0]
    for rows in MAT_ROWS:
        bounds.append(bounds[-1] + rows)
    members = [is_matrix & (place >= bounds[i]) & (place < bounds[i + 1]) for i in range(6)]

    hops = lambda k: min(k, 4 - k)
    in_plane = sorted(range(1, 16), key=lambda k: -hops(k // 4) - hops(k % 4))
    along_x = sorted(range(1, 8), key=lambda k: -hops(k // 2) - k % 2)

    def everyone(tile, turn):
        tile_out[turn, 0] = tile
        tiles_d[turn, dp] = tile

        def f_copy(k):
            return pltpu.make_async_remote_copy(
                tile_out.at[turn, 1], tiles_f.at[turn, fs], f_send.at[turn, k], f_recv.at[turn, k],
                device_id=(dp, (fs // 4 + k // 4) % 4 * 4 + (fs + k) % 4), device_id_type=MESH,
            )

        def d_copy(k):
            return pltpu.make_async_remote_copy(
                tile_out.at[turn, 0], tiles_d.at[turn, dp], d_send.at[turn, k], d_recv.at[turn, k],
                device_id=((x + k // 2) % 4 * 2 + (core + k) % 2, fs), device_id_type=MESH,
            )

        for k in along_x:
            d_copy(k).start()
        for k in along_x:
            d_copy(k).wait_recv()
        total = tiles_d[turn, 0]
        for k in range(1, 8):
            total = total + tiles_d[turn, k]
        tile_out[turn, 1] = total
        tiles_f[turn, fs] = total
        for k in in_plane:
            f_copy(k).start()
        for k in in_plane:
            f_copy(k).wait_recv()
        total = tiles_f[turn, 0]
        for k in range(1, 16):
            total = total + tiles_f[turn, k]

        def sent():
            for k in along_x:
                d_copy(k).wait_send()
            for k in in_plane:
                f_copy(k).wait_send()

        return total, sent

    column = lambda v: jnp.sum(v, 0, keepdims=True)

    def tile_of(rows):
        return jnp.concatenate(rows + [jnp.zeros((8 - len(rows), 128), F32)] * (len(rows) < 8), 0)

    grad = mine[...]
    master = packs[0]
    squares = master * master
    tile, first_sent = everyone(
        tile_of([part, column(grad * grad)] + [column(jnp.where(members[i], squares, 0.0)) for i in range(6)]), 0
    )
    loss, count = tile[0:1, 0:1], tile[0:1, 1:2]
    sums = jnp.sum(tile, 1, keepdims=True)
    inverse = 1.0 / count
    norm = jnp.sqrt(sums[1:2]) * inverse
    factor = CLIP_NORM / jnp.maximum(norm, CLIP_NORM)
    grad = grad * inverse * factor
    first = BETA_ONE * packs[1] + (1.0 - BETA_ONE) * grad
    second = BETA_TWO * packs[2] + (1.0 - BETA_TWO) * grad * grad
    ratio = first / (1.0 - BETA_ONE**STEP) / (jnp.sqrt(second / (1.0 - BETA_TWO**STEP)) + ADAM_EPS)
    ratio = ratio + jnp.where(is_matrix, WEIGHT_DECAY * master, 0.0)
    squares = ratio * ratio
    steps, second_sent = everyone(tile_of([column(jnp.where(members[i], squares, 0.0)) for i in range(6)]), 1)
    made_ref[BLOCK : 2 * BLOCK, :] = first
    made_ref[2 * BLOCK : 3 * BLOCK, :] = second
    trusts = jnp.sqrt(sums[2:8]) / jnp.sqrt(jnp.sum(steps, 1, keepdims=True)[0:6])
    trust = jnp.ones((BLOCK, 1), F32)
    for i in range(6):
        trust = jnp.where(members[i], trusts[i : i + 1], trust)
    made_ref[0:BLOCK, :] = master - LEARN_RATE * (trust * ratio)
    lane = lax.broadcasted_iota(jnp.int32, (8, 128), 1)
    made_ref[3 * BLOCK :, :] = jnp.where(lane == 0, loss, jnp.where(lane == 1, count, norm))

    def block_sent(k, _):
        block_copy(k, buffers).wait_send()
        return 0

    lax.fori_loop(1, 64, block_sent, 0)
    first_sent()
    second_sent()


def finish_kernel(made, loss, count, norm, m0, m1, m2, v0, v1, v2):
    for i, (mat, vec) in enumerate(((m0, v0), (m1, v1), (m2, v2))):
        mat[...] = made[BLOCK * i : BLOCK * i + SHARD, :]
        vec[...] = made[BLOCK * i + SHARD : BLOCK * i + SHARD + 1, 0:47]
    for i, out in enumerate((loss, count, norm)):
        out[...] = made[3 * BLOCK : 3 * BLOCK + 1, i : i + 1]


def finish(made):
    vmem = pl.BlockSpec(memory_space=pltpu.VMEM)
    shape = lambda *dims: jax.ShapeDtypeStruct(dims, F32)
    return pl.pallas_call(
        finish_kernel,
        in_specs=[vmem],
        out_specs=[vmem] * 9,
        out_shape=[shape(1, 1)] * 3 + [shape(SHARD, 128)] * 3 + [shape(1, 47)] * 3,
        compiler_params=params(63),
        name="finish",
    )(made)


def per_device(
    token_ids,
    splits,
    valid_mask,
    embed_table,
    embed_proj,
    embed_bias,
    type_table,
    teach_in,
    teach_qkv,
    teach_att,
    teach_up,
    teach_down,
    teach_out,
    teach_bias,
    teach_gain,
    teach_shift,
    matrices,
    vectors,
    matrix_first,
    matrix_second,
    vector_first,
    vector_second,
):
    mat = lambda v: v.reshape(SHARD, 128)
    vec = lambda v: v.reshape(1, 47)
    rows_128 = lambda v: v.reshape(-1, 128)
    bias = rows_128(teach_bias)
    emb, t_keys, t_values, own_emb, hidden, t_queries, weights, packed = front(
        token_ids, embed_table, embed_table, valid_mask, splits, mat(matrices), vec(vectors), embed_proj, teach_in, teach_qkv,
        rows_128(embed_bias), type_table, bias,
    )
    first, s_q, s_k, s_v, s_kt, s_vt, in_w, qkv_w, att_w, up_w, down_w, out_w, vecs = student_in(emb, packed)
    et, es, t_mixed, s_mixed, stat = attend(t_queries, t_keys, t_values, s_q, s_k, s_vt, s_kt)
    target = teacher(
        t_mixed, hidden, own_emb, teach_att, teach_up, teach_down, teach_out, bias, rows_128(teach_gain), rows_128(teach_shift)
    )
    late, vgrads, d_sum, d_mixed, part = student(
        own_emb, s_mixed, target, weights, in_w, att_w, up_w, down_w, out_w, vecs
    )
    made = back(
        et, es, stat, s_mixed, d_mixed, weights, s_q, s_v, s_kt, d_sum, emb, first, qkv_w, vgrads, part, late,
        mat(matrices), vec(vectors), mat(matrix_first), vec(vector_first), mat(matrix_second), vec(vector_second),
    )
    loss, count, norm, m0, m1, m2, v0, v1, v2 = finish(made)
    flat = lambda v: v.reshape(-1)
    scalar = lambda v: v.reshape(())
    return (
        scalar(loss), scalar(count), scalar(norm), flat(m0), flat(m1), flat(m2), flat(v0), flat(v1), flat(v2),
    )


def solution(mesh):
    both = P(("dp", "fsdp"))
    return jax.shard_map(
        per_device,
        mesh=mesh,
        in_specs=(P("dp", "fsdp"), P("dp"), P("dp", "fsdp")) + (P(),) * 13 + (both,) * 6,
        out_specs=(P(), P(), P(), both, both, both, both, both, both),
        check_vma=False,
    )
```
